128 devices in a mesh: rep: 16 (over y, z_lo, core), shard: 8 (over z_hi, x).
Axes of the slice: x: 4, y: 4, z: 4 (z_hi: 2, z_lo: 2; z = z_hi * 2 + z_lo), core: 2. Of those that a mesh axis runs over, the one named last changes fastest.
Arguments:
- tokens: bfloat16 [24576, 1152], P(('rep', 'shard')), may hold values from -6 to 6
- lengths: int32 [16, 8], P('rep', 'shard'), may hold values from 128 to 192, as said below
- attn_gain: bfloat16 [1152], P('shard'), may hold values from 0.25 to 1.75
- w_query: bfloat16 [1152, 1024], P('shard'), may hold values from -0.1875 to 0.1875
- w_keyval: bfloat16 [1152, 512], P('shard'), may hold values from -0.1875 to 0.1875
- w_out: bfloat16 [1024, 1152], P('shard'), may hold values from -1.5 to 1.5
- mlp_gain: bfloat16 [1152], P('shard'), may hold values from 0.25 to 1.75
- w_gate: bfloat16 [1152, 6912], P('shard'), may hold values from -0.1875 to 0.1875
- w_up: bfloat16 [1152, 6912], P('shard'), may hold values from -0.1875 to 0.1875
- w_down: bfloat16 [6912, 1152], P('shard'), may hold values from -0.15625 to 0.15625
- cotangent: bfloat16 [24576, 1152], P(('rep', 'shard')), may hold values from -6 to 6
Outputs:
- outputs: bfloat16 [24576, 1152], P(('rep', 'shard'))
- grad_tokens: float32 [24576, 1152], P(('rep', 'shard'))
- grad_attn_gain: float32 [1152], P('shard')
- grad_w_query: float32 [1152, 1024], P('shard')
- grad_w_keyval: float32 [1152, 512], P('shard')
- grad_w_out: float32 [1024, 1152], P('shard')
- grad_mlp_gain: float32 [1152], P('shard')
- grad_w_gate: float32 [1152, 6912], P('shard')
- grad_w_up: float32 [1152, 6912], P('shard')
- grad_w_down: float32 [6912, 1152], P('shard')
The draws below stay inside these ranges and needn't reach their ends.
Inputs may be any that keep to these rules, and one draw needn't show every extreme that they name: lengths[r, s] counts the live slots at the start of the 192 slots of shard index s in sequence r; in every sequence one device has all 192 live and another has exactly 128.
All inputs are finite; a program needn't handle non-finite values.
Results may differ from the reference program's by a relative error of at most 0.025.
Values may be sent and summed in bfloat16 or wider, within the bound.
A program may use at most 256 MiB of HBM per device.

```python
import jax
import jax.numpy as jnp
from jax import lax

D = 1152
FF = 6912
H = 4
HD = 256
WINDOW = 512
TOK_DEV = 192
TOKENS = 24576
N_REP = 16
N_SHARD = 8


def draw_lengths(key, part):
    key = jax.random.fold_in(key, 11)
    count_key, order_key = jax.random.split(key)
    least_live = TOK_DEV * 2 // 3
    counts = jax.random.randint(count_key, (N_REP, N_SHARD), least_live, TOK_DEV + 1)
    orders = jax.vmap(lambda sub_key: jax.random.permutation(sub_key, N_SHARD))(jax.random.split(order_key, N_REP))
    counts = jnp.where(orders == 0, TOK_DEV, counts)
    counts = jnp.where(orders == 1, least_live, counts)
    return counts.astype(jnp.int32)


def block_levels(rng, extent, shards, least, high):
    loudness, own = 1.0, jax.random.fold_in(rng, 6)
    for position, shards_of in shards:
        heights = jnp.exp(jax.random.uniform(jax.random.fold_in(own, position), (shards_of,), jnp.float32, least / len(shards), high / len(shards)))
        loudness = loudness * jnp.repeat(heights, extent[position] // shards_of).reshape([-1 if axis == position else 1 for axis in range(len(extent))])
    return loudness


def noise(own_key, extent, scale, limit, cuts=(), held_as=jnp.bfloat16):
    array = jax.random.normal(own_key, extent, jnp.float32) * scale
    if len(cuts) > 0:
        array = block_levels(own_key, extent, cuts, -0.22, 0.18) * array
    return jnp.clip(array, min=-limit, max=limit).astype(held_as)


def setup_inputs(seed: int = 0) -> dict:
    splits = jax.random.split(jax.random.key(seed), 12)
    tokens = noise(splits[0], (TOKENS, D), 1.0, 6.0, ((0, 128),))
    lengths = draw_lengths(jax.random.fold_in(splits[11], 71), 0)
    attn_gain = jnp.clip(1.0 + 0.15 * jax.random.normal(splits[2], (D,), jnp.float32), 0.25, 1.75).astype(jnp.bfloat16)
    w_query = noise(splits[3], (D, H * HD), D ** -0.5, 0.1875, ((0, 8),))
    w_keyval = noise(splits[4], (D, 2 * HD), D ** -0.5, 0.1875, ((0, 8),))
    w_out = noise(splits[5], (H * HD, D), (max(H * HD // 64, 1)) ** -0.5, 1.5, ((0, 8),))
    mlp_gain = jnp.clip(1.0 + 0.15 * jax.random.normal(splits[6], (D,), jnp.float32), 0.25, 1.75).astype(jnp.bfloat16)
    w_gate = noise(splits[7], (D, FF), D ** -0.5, 0.1875, ((0, 8),))
    w_up = noise(splits[8], (D, FF), D ** -0.5, 0.1875, ((0, 8),))
    w_down = noise(splits[9], (FF, D), (FF // 4) ** -0.5, 0.15625, ((0, 8),))
    cotangent = noise(splits[10], (TOKENS, D), 1.0, 6.0, ((0, 128),))
    return dict(tokens=tokens, lengths=lengths, attn_gain=attn_gain, w_query=w_query, w_keyval=w_keyval, w_out=w_out, mlp_gain=mlp_gain, w_gate=w_gate, w_up=w_up, w_down=w_down, cotangent=cotangent)


@jax.custom_vjp
def low(v):
    return lax.optimization_barrier(v.astype(jnp.bfloat16)).astype(jnp.float32)

@jax.custom_vjp
def low_back(v):
    return v

def low_keep(v):
    return (low(v), None)

def low_pass(kept, grad):
    return (grad,)

def back_keep(v):
    return (v, None)

def back_low(kept, grad):
    return (low(grad),)
low.defvjp(low_keep, low_pass)
low_back.defvjp(back_keep, back_low)
EPSILON = 1e-06
MASKED = -1e+30
HIGHEST_MODE = lax.Precision.HIGHEST

def matmul(former, latter):
    return jnp.dot(former, latter, precision=HIGHEST_MODE)

def rotate(vectors, positions):
    half_size = vectors.shape[-1] // 2
    indices = jnp.arange(half_size).astype(jnp.float32)
    frequency = jnp.power(10000.0, -2.0 * indices / vectors.shape[-1])
    angles = positions.astype(jnp.float32)[:, None] * frequency[None, :]
    if vectors.ndim == 3:
        angles = angles[:, None, :]
    cosine = jnp.cos(angles)
    sine_part = jnp.sin(angles)
    first_half = vectors[..., :half_size]
    second_half = vectors[..., half_size:]
    return jnp.concatenate([first_half * cosine - second_half * sine_part, second_half * cosine + first_half * sine_part], axis=-1)

def rms_scaled(values):
    return values * lax.rsqrt(lax.optimization_barrier(jnp.mean(values * values, axis=1, keepdims=True)) + EPSILON)

def sequence_block(params, inputs, live_counts):
    attn_gain, w_query, w_keyval, w_out, mlp_gain, w_gate, w_up, w_down = params
    slots = jnp.arange(inputs.shape[0], dtype=jnp.int32)
    owner_slot = slots // TOK_DEV
    within = slots % TOK_DEV
    starts = (jnp.cumsum(live_counts) - live_counts).astype(jnp.int32)
    positions = starts[owner_slot] + within
    is_live = within < live_counts[owner_slot]
    keep_mask = is_live.astype(inputs.dtype)[:, None]
    normed1 = low(rms_scaled(inputs) * attn_gain)
    query_proj = low_back(matmul(normed1, w_query)).reshape(-1, H, HD)
    queries = low(rotate(query_proj, positions) * HD ** (-0.5))
    keyval_proj = low_back(matmul(normed1, w_keyval))
    keys = low(rotate(keyval_proj[:, :HD], positions))
    values = low(keyval_proj[:, HD:])
    raw_scores = low_back(jnp.einsum('thd,gd->htg', queries, keys, precision=HIGHEST_MODE))
    allowed = is_live[None, :] & (positions[None, :] <= positions[:, None]) & (positions[:, None] - positions[None, :] < WINDOW)
    probs = jax.nn.softmax(jnp.where(allowed[None], raw_scores, MASKED), axis=-1)
    attended = jnp.einsum('htg,gd->thd', low(probs), values, precision=HIGHEST_MODE)
    attended = low(low_back(attended)).reshape(inputs.shape[0], H * HD)
    middle = inputs + keep_mask * low_back(matmul(attended, w_out))
    normed2 = low(rms_scaled(middle) * mlp_gain)
    gate_pre = low_back(matmul(normed2, w_gate))
    up_pre = low_back(matmul(normed2, w_up))
    hidden = low(jax.nn.gelu(gate_pre, approximate=True) * up_pre)
    return middle + keep_mask * low_back(matmul(hidden, w_down))

def reference(tokens, lengths, attn_gain, w_query, w_keyval, w_out, mlp_gain, w_gate, w_up, w_down, cotangent):
    params = tuple((weight.astype(jnp.float32) for weight in (attn_gain, w_query, w_keyval, w_out, mlp_gain, w_gate, w_up, w_down)))
    grouped = tokens.astype(jnp.float32).reshape(N_REP, TOK_DEV * N_SHARD, D)

    def forward(weights, inputs):

        def group_step(group_pair):
            return sequence_block(weights, group_pair[0], group_pair[1])
        return lax.map(jax.checkpoint(group_step), (inputs, lengths))
    layer_out, pullback = jax.vjp(forward, params, grouped)
    weight_grads, input_grads = pullback(cotangent.astype(jnp.float32).reshape(layer_out.shape))
    return (layer_out.reshape(TOK_DEV * N_SHARD * N_REP, D).astype(jnp.bfloat16), input_grads.reshape(TOK_DEV * N_SHARD * N_REP, D), weight_grads[0], weight_grads[1], weight_grads[2], weight_grads[3], weight_grads[4], weight_grads[5], weight_grads[6], weight_grads[7])
```

```python
import functools

import jax
import jax.numpy as jnp
from jax import lax
from jax.experimental import pallas as pl
from jax.experimental.pallas import tpu as pltpu
from jax.sharding import PartitionSpec as P

MESH = pl.DeviceIdType.MESH
WINDOW = 512
EPSILON = 1e-06
MASKED = -1e30
VMEM_LIMIT = 60 * 2**20
FF_DEV = 864
FF_PAD = 896
PAIRS = FF_PAD // 128
BEHIND = 4


def matmul(former, latter):
    return jnp.dot(former, latter, preferred_element_type=jnp.float32)


def lead_product(former, latter):
    return lax.dot_general(
        former, latter, (((0,), (0,)), ((), ())), preferred_element_type=jnp.float32
    )


def trail_product(former, latter):
    return lax.dot_general(
        former, latter, (((1,), (1,)), ((), ())), preferred_element_type=jnp.float32
    )


class Place:
    def __init__(self):
        rep, shard = lax.axis_index("rep"), lax.axis_index("shard")
        self.rep, self.shard = rep, shard
        self.y, self.z_lo, self.core = rep // 4, (rep // 2) % 2, rep % 2
        self.z_hi, self.x = shard // 4, shard % 4

    def device(self, dx=0, dy=0, mirror=0, swap_lo=0, sibling=0):
        z_lo = (self.z_lo + mirror + swap_lo) % 2
        rep = (((self.y + dy) % 4) * 2 + z_lo) * 2 + (self.core + sibling) % 2
        return (rep, ((self.z_hi + mirror) % 2) * 4 + (self.x + dx) % 4)

    def shard_at(self, j, p):
        return ((self.z_hi + p) % 2) * 4 + (self.x + STEPS[j]) % 4


STEPS = (0, 1, 3, 2)


class Wire:
    def __init__(self, send_sems, recv_sems):
        self.send_sems, self.recv_sems, self.made = send_sems, recv_sems, []

    def copy(self, src, dst, device):
        k = len(self.made)
        made = pltpu.make_async_remote_copy(
            src_ref=src,
            dst_ref=dst,
            send_sem=self.send_sems.at[k],
            recv_sem=self.recv_sems.at[k],
            device_id=device,
            device_id_type=MESH,
        )
        self.made.append(made)
        return made

    def drain(self):
        for made in self.made:
            made.wait_send()


def greet(devices):
    barrier = pltpu.get_barrier_semaphore()
    for device in devices:
        pl.semaphore_signal(barrier, inc=1, device_id=device, device_id_type=MESH)
    pl.semaphore_wait(barrier, len(devices))


GATHER_HOPS = (
    ((0, 0), (0, 1), 0, 0, 1),
    ((0, 0), (2, 0), 0, 1, 0),
    ((0, 0), (1, 0), 0, 3, 0),
    ((0, 1), (2, 1), 0, 1, 0),
    ((0, 1), (1, 1), 0, 3, 0),
    ((2, 0), (3, 0), 1, 1, 0),
    ((1, 0), (3, 0), 2, 3, 0),
    ((2, 1), (3, 1), 1, 1, 0),
    ((1, 1), (3, 1), 2, 3, 0),
)


def gather_tree(wire, place, own, slot, cut, absolute):
    copies = []
    for source, target, part, dx, mirror in GATHER_HOPS:
        src = own if source == (0, 0) else slot(*source)
        dst = slot(*(source if absolute else target))
        copies.append(wire.copy(cut(src, part), cut(dst, part), place.device(dx=dx, mirror=mirror)))
    return copies


def spread_kernel(
    misc, qkv, wo, gu, gb, o_misc, o_qkv, o_wo, o_gu, o_gb, local_sems, send_sems, recv_sems
):
    place = Place()
    wire = Wire(send_sems, recv_sems)
    core = place.core
    others = [(j, p) for p in (0, 1) for j in range(4) if (j, p) != (0, 0)]
    group = [place.device(dx=STEPS[j], mirror=p) for j, p in others]
    sequence = [(place.rep, place.shard_at(j, p)) for j, p in others]
    sibling = place.device(sibling=1)
    me = place.shard
    greet([sibling] + group + [d for d, (j, p) in zip(sequence, others) if p == 1])

    def cut_qkv(ref, part):
        start, size = ((0, 768), (0, 384), (384, 384))[part]
        return ref.at[:, pl.ds(pl.multiple_of(core * 768 + start, 128), size)]

    def cut_wo(ref, part):
        start, size = ((0, 64), (0, 32), (32, 32))[part]
        return ref.at[pl.ds(pl.multiple_of(core * 64 + start, 32), size)]

    def cut_gb(ref, part):
        return ref if part == 0 else ref.at[pl.ds((part - 1) * 96, 96)]

    def cut_gu(ref):
        return ref.at[:, pl.ds(pl.multiple_of(core * FF_PAD, 128), FF_PAD)]

    locals_ = []
    for k, (src, dst) in enumerate(
        [
            (misc, o_misc.at[me]),
            (qkv, o_qkv.at[me]),
            (wo, o_wo.at[me]),
            (gu.at[me], o_gu.at[me]),
            (gb, o_gb.at[0, 0]),
        ]
    ):
        copy = pltpu.make_async_copy(src, dst, local_sems.at[k])
        copy.start()
        locals_.append(copy)

    slot_qkv = lambda j, p: o_qkv.at[place.shard_at(j, p)]
    slot_wo = lambda j, p: o_wo.at[place.shard_at(j, p)]
    slot_gb = lambda j, p: o_gb.at[j, p]
    misc_copies = [wire.copy(misc, o_misc.at[me], device) for device in sequence]
    trees = [
        gather_tree(wire, place, qkv, slot_qkv, cut_qkv, True),
        gather_tree(wire, place, wo, slot_wo, cut_wo, True),
        gather_tree(wire, place, gb, slot_gb, cut_gb, False),
    ]
    gu_copies = [
        wire.copy(cut_gu(gu.at[place.shard_at(j, p)]), cut_gu(o_gu.at[me]), device)
        for (j, p), device in zip(others, group)
    ]
    passed = {}
    for j, p in others:
        at = place.shard_at(j, p)
        passed[j, p] = [
            wire.copy(cut_qkv(o_qkv.at[at], 0), cut_qkv(o_qkv.at[at], 0), sibling),
            wire.copy(cut_wo(o_wo.at[at], 0), cut_wo(o_wo.at[at], 0), sibling),
        ]
    gu_passed = []
    for j, p in others:
        at = place.shard_at((0, 2, 1, 3)[j], p)
        gu_passed.append(wire.copy(cut_gu(o_gu.at[at]), cut_gu(o_gu.at[at]), sibling))

    for copy in misc_copies:
        copy.start()
    for tree in trees[:2]:
        for k in (0, 1, 2):
            tree[k].start()

    def then(k, nexts, slots):
        for tree in trees[:2]:
            tree[k].wait_recv()
            for n in nexts:
                tree[n].start()
        for s in slots:
            for copy in passed[s]:
                copy.start()

    then(0, (3, 4), [(0, 1)])
    then(1, (5,), [(2, 0)])
    then(2, (6,), [(1, 0)])
    then(3, (7,), [(2, 1)])
    then(4, (8,), [(1, 1)])
    for k in (0, 1, 2):
        trees[2][k].start()
    for copy in gu_copies:
        copy.start()
    then(5, (), [])
    then(6, (), [(3, 0)])
    then(7, (), [])
    then(8, (), [(3, 1)])
    gb_tree = trees[2]
    for k, nexts in ((0, (3, 4)), (1, (5,)), (2, (6,)), (3, (7,)), (4, (8,))):
        gb_tree[k].wait_recv()
        for n in nexts:
            gb_tree[n].start()
    for copy, onward in zip(gu_copies, gu_passed):
        copy.wait_recv()
        onward.start()
    for k in (5, 6, 7, 8):
        gb_tree[k].wait_recv()
    for copy in misc_copies + gu_passed + [c for cs in passed.values() for c in cs]:
        copy.wait_recv()
    for copy in locals_:
        copy.wait()
    wire.drain()


ANY = pl.BlockSpec(memory_space=pl.ANY)


def comm_params(collective_id):
    return pltpu.CompilerParams(
        collective_id=collective_id, has_side_effects=True, vmem_limit_bytes=VMEM_LIMIT
    )


def spread(misc, qkv, wo, gu, gb):
    shape = lambda *s: jax.ShapeDtypeStruct(s, jnp.bfloat16)
    return pl.pallas_call(
        spread_kernel,
        out_shape=(
            shape(8, *misc.shape),
            shape(8, *qkv.shape),
            shape(8, *wo.shape),
            shape(*gu.shape),
            shape(4, 2, *gb.shape),
        ),
        in_specs=[ANY] * 5,
        out_specs=(ANY,) * 5,
        scratch_shapes=[
            pltpu.SemaphoreType.DMA((5,)),
            pltpu.SemaphoreType.DMA((64,)),
            pltpu.SemaphoreType.DMA((64,)),
        ],
        compiler_params=comm_params(1),
        name="spread_weights",
    )(misc, qkv, wo, gu, gb)


def window_kernel(reverse, own, out, send_sems, recv_sems):
    rep, shard = lax.axis_index("rep"), lax.axis_index("shard")
    barrier = pltpu.get_barrier_semaphore()
    sign = -1 if reverse else 1

    def inside(i):
        return jnp.logical_and(shard + i >= 0, shard + i < 8)

    for i in range(1, BEHIND + 1):

        @pl.when(inside(-sign * i))
        def _():
            pl.semaphore_signal(
                barrier, inc=1, device_id=(rep, shard - sign * i), device_id_type=MESH
            )

    targets = jnp.minimum(shard if reverse else 7 - shard, BEHIND)

    @pl.when(targets > 0)
    def _():
        pl.semaphore_wait(barrier, targets)

    copies = []
    for i in range(1, BEHIND + 1):
        copy = pltpu.make_async_remote_copy(
            src_ref=own.at[i] if reverse else own,
            dst_ref=out.at[i - 1],
            send_sem=send_sems.at[i],
            recv_sem=recv_sems.at[i],
            device_id=(rep, shard + sign * i),
            device_id_type=MESH,
        )
        copies.append(copy)
        pl.when(inside(sign * i))(copy.start)
    for i, copy in enumerate(copies):
        pl.when(inside(-sign * (i + 1)))(copy.wait_recv)
        pl.when(inside(sign * (i + 1)))(copy.wait_send)


def window(own, reverse, collective_id, name):
    block = own.shape[-2:]
    return pl.pallas_call(
        functools.partial(window_kernel, reverse),
        out_shape=jax.ShapeDtypeStruct((BEHIND, *block), jnp.bfloat16),
        in_specs=[ANY],
        out_specs=ANY,
        scratch_shapes=[
            pltpu.SemaphoreType.DMA((BEHIND + 1,)),
            pltpu.SemaphoreType.DMA((BEHIND + 1,)),
        ],
        compiler_params=comm_params(collective_id),
        name=name,
    )(own)


class SumTree:
    def __init__(self, wire, place, slot, cut, half_a, half_b, from_m, from_p, from_z):
        self.slot, self.cut = slot, cut
        self.half_a, self.half_b, self.from_m, self.from_p = half_a, half_b, from_m, from_p
        self.from_z = from_z
        plus, minus = place.device(dx=1), place.device(dx=3)
        self.far, self.near = {}, {}
        for p in (0, 1):
            self.far[p] = (
                wire.copy(cut(slot(3, p), 1), half_a.at[p], plus),
                wire.copy(cut(slot(3, p), 2), half_b.at[p], minus),
            )
            self.near[p] = (
                wire.copy(slot(1, p), from_m.at[p], plus),
                wire.copy(slot(2, p), from_p.at[p], minus),
            )
        self.last = wire.copy(slot(0, 1), from_z, place.device(mirror=1))

    def send_far(self):
        for p in (0, 1):
            for copy in self.far[p]:
                copy.start()

    def send_near(self):
        for p in (0, 1):
            for copy, part, half, j in (
                (self.far[p][0], 1, self.half_a, 1),
                (self.far[p][1], 2, self.half_b, 2),
            ):
                copy.wait_recv()
                add_into(self.cut(self.slot(j, p), part), half.at[p])
                self.near[p][j - 1].start()

    def send_last(self):
        for p in (1, 0):
            for copy, source in zip(self.near[p], (self.from_m, self.from_p)):
                copy.wait_recv()
                add_into(self.slot(0, p), source.at[p])
            if p == 1:
                self.last.start()

    def finish(self):
        self.last.wait_recv()
        return self.slot(0, 0)[...].astype(jnp.float32) + self.from_z[...].astype(jnp.float32)


def add_into(target, source):
    target[...] = (target[...].astype(jnp.float32) + source[...].astype(jnp.float32)).astype(
        target.dtype
    )


ROOT = 0.7978845608028654
CUBE = 0.044715


def ff_kernel(
    own_n, gb_all, wgu_all, wd_all,
    o_gn, o_br, o_dgu, o_dd,
    nbuf, gb, wgu, wd, gh, hid, ggu, part_g, part_b, out_f32, dgu_tile,
    g_ha, g_hb, g_fm, g_fp, g_fz, b_ha, b_hb, b_fm, b_fp, b_fz,
    local_sems, send_sems, recv_sems,
):
    place = Place()
    wire = Wire(send_sems, recv_sems)
    loads = [
        pltpu.make_async_copy(src, dst, local_sems.at[k])
        for k, (src, dst) in enumerate(
            [(own_n, nbuf.at[0, 0]), (wd_all, wd), (gb_all, gb), (wgu_all, wgu)]
        )
    ]
    for load in loads:
        load.start()
    greet([place.device(dx=1), place.device(dx=3), place.device(mirror=1)])

    def cut(ref, part):
        return ref if part == 0 else ref.at[pl.ds((part - 1) * 96, 96)]

    slot_n = lambda j, p: nbuf.at[j, p]
    tree = gather_tree(wire, place, nbuf.at[0, 0], slot_n, cut, False)
    sum_g = SumTree(
        wire, place, lambda j, p: part_g.at[j, p], cut, g_ha, g_hb, g_fm, g_fp, g_fz
    )
    sum_b = SumTree(
        wire, place, lambda j, p: part_b.at[j, p], cut, b_ha, b_hb, b_fm, b_fp, b_fz
    )
    loads[0].wait()
    for k in (0, 1, 2):
        tree[k].start()
    loads[1].wait()
    loads[2].wait()

    def back_hidden(j):
        rows = jnp.concatenate([gb[j, 0], gb[j, 1]], axis=0)
        gh[j] = trail_product(rows, wd[...])

    def onward(k, nexts):
        tree[k].wait_recv()
        for n in nexts:
            tree[n].start()

    def forward(j):
        rows = jnp.concatenate([nbuf[j, 0], nbuf[j, 1]], axis=0)

        def tile(t, carry):
            columns = pl.ds(pl.multiple_of(t * 256, 256), 256)
            narrow = pl.ds(pl.multiple_of(t * 128, 128), 128)
            both = matmul(rows, wgu[:, columns])
            gate, up = both[:, :128], both[:, 128:]
            square = gate * gate
            curve = jnp.tanh(ROOT * gate * (1.0 + CUBE * square))
            half_up = 0.5 * (1.0 + curve)
            active = gate * half_up
            slope = half_up + 0.5 * gate * (1.0 - curve * curve) * (
                ROOT * (1.0 + 3.0 * CUBE * square)
            )
            back = gh[j, :, narrow]
            hid[j, :, narrow] = (active * up).astype(jnp.bfloat16)
            ggu[j, :, columns] = jnp.concatenate(
                [(back * up * slope).astype(jnp.bfloat16), (back * active).astype(jnp.bfloat16)],
                axis=1,
            )
            return carry

        lax.fori_loop(0, PAIRS, tile, 0)

    def back_normed(j):
        for start, size in ((0, 512), (512, 512), (1024, 128)):
            block = trail_product(ggu[j], wgu[start : start + size, :]).astype(jnp.bfloat16)
            part_g[j, 0, :, start : start + size] = block[:192]
            part_g[j, 1, :, start : start + size] = block[192:]

    def down(j):
        for start, size in ((0, 512), (512, 512), (1024, 128)):
            block = matmul(hid[j], wd[:, start : start + size]).astype(jnp.bfloat16)
            part_b[j, 0, :, start : start + size] = block[:192]
            part_b[j, 1, :, start : start + size] = block[192:]

    for j in range(4):
        back_hidden(j)
    onward(0, (3, 4))
    onward(1, (5,))
    onward(2, (6,))
    loads[3].wait()
    forward(0)
    onward(3, (7,))
    onward(4, (8,))
    forward(1)
    forward(2)
    for k in (5, 6, 7, 8):
        onward(k, ())
    forward(3)
    back_normed(3)
    sum_g.send_far()
    back_normed(1)
    back_normed(2)
    sum_g.send_near()
    down(3)
    sum_b.send_far()
    back_normed(0)
    down(1)
    down(2)
    sum_g.send_last()
    sum_b.send_near()
    down(0)

    hid_rows = hid.reshape(4 * 384, FF_PAD)
    ggu_rows = ggu.reshape(4 * 384, 2 * FF_PAD)
    n_rows = nbuf.reshape(4 * 384, 1152)
    gb_rows = gb.reshape(4 * 384, 1152)

    def grad_gu(t, carry):
        columns = pl.ds(pl.multiple_of(t * 256, 256), 256)
        dgu_tile[:, columns] = lead_product(n_rows[...], ggu_rows[:, columns]).astype(jnp.bfloat16)
        return carry

    lax.fori_loop(0, PAIRS, grad_gu, 0)
    store_gu = pltpu.make_async_copy(dgu_tile, o_dgu, local_sems.at[4])
    store_gu.start()

    part_dd = lead_product(hid_rows[...], gb_rows[...])
    wd[...] = part_dd.astype(jnp.bfloat16)
    store_d = pltpu.make_async_copy(wd, o_dd, local_sems.at[5])
    store_d.start()
    sum_b.send_last()
    out_f32[0] = sum_g.finish()
    out_f32[1] = sum_b.finish()
    stores = [
        store_gu,
        store_d,
        pltpu.make_async_copy(out_f32.at[0], o_gn, local_sems.at[6]),
        pltpu.make_async_copy(out_f32.at[1], o_br, local_sems.at[7]),
    ]
    for store in stores[2:]:
        store.start()
    for store in stores:
        store.wait()
    wire.drain()


def feed_forward(own_n, gb_all, wgu_all, wd_all):
    bf, f32 = jnp.bfloat16, jnp.float32
    vm = pltpu.VMEM
    tokens, width = own_n.shape
    sums = [
        vm((2, 96, width), bf),
        vm((2, 96, width), bf),
        vm((2, tokens, width), bf),
        vm((2, tokens, width), bf),
        vm((tokens, width), bf),
    ]
    return pl.pallas_call(
        ff_kernel,
        out_shape=(
            jax.ShapeDtypeStruct((tokens, width), f32),
            jax.ShapeDtypeStruct((tokens, width), f32),
            jax.ShapeDtypeStruct(wgu_all.shape, bf),
            jax.ShapeDtypeStruct(wd_all.shape, bf),
        ),
        in_specs=[ANY] * 4,
        out_specs=(ANY,) * 4,
        scratch_shapes=[
            vm((4, 2, tokens, width), bf),
            vm((4, 2, tokens, width), bf),
            vm(wgu_all.shape, bf),
            vm(wd_all.shape, bf),
            vm((4, 2 * tokens, FF_PAD), f32),
            vm((4, 2 * tokens, FF_PAD), bf),
            vm((4, 2 * tokens, 2 * FF_PAD), bf),
            vm((4, 2, tokens, width), bf),
            vm((4, 2, tokens, width), bf),
            vm((2, tokens, width), f32),
            vm(wgu_all.shape, bf),
        ]
        + sums
        + sums
        + [
            pltpu.SemaphoreType.DMA((8,)),
            pltpu.SemaphoreType.DMA((32,)),
            pltpu.SemaphoreType.DMA((32,)),
        ],
        compiler_params=comm_params(2),
        name="feed_forward",
    )(own_n, gb_all, wgu_all, wd_all)


def reduce_kernel(
    dgu, dd, dqkv, dwo, dgain,
    o_gu, o_d, o_qkv, o_wo, o_gain,
    h_gu, r_gu, f_gu, h_d, r_d, h_qkv, r_qkv, h_wo, r_wo, h_gain, r_gain,
    y_gu, y_d, y_qkv, y_wo, y_gain, p_gu, p_d, p_qkv, p_wo, p_gain, z_gu, z_d, z_qkv, z_wo, z_gain,
    qa, qb, qm, qp, qz, wa, wb, wm, wp, wz, ga, gb_, gm, gp, gz,
    local_sems, send_sems, recv_sems,
):
    place = Place()
    wire = Wire(send_sems, recv_sems)
    core, me, y = place.core, place.shard, place.y
    others = [(j, p) for p in (0, 1) for j in range(4) if (j, p) != (0, 0)]
    group = [place.device(dx=STEPS[j], mirror=p) for j, p in others]
    sibling = place.device(sibling=1)
    column = [place.device(dy=d) for d in (1, 3, 2)]
    low = place.device(swap_lo=1)

    def lanes(ref, which, size):
        start = pl.multiple_of(which * size, 128)
        return ref.at[..., pl.ds(start, size)]

    def gu_half(ref, which):
        return ref.at[:, :, pl.ds(pl.multiple_of(which * FF_PAD, 128), FF_PAD)]

    def d_half(ref, which):
        return ref.at[pl.ds(pl.multiple_of(which * 448, 16), 448)]

    def qkv_half(ref, which):
        return ref.at[:, :, pl.ds(pl.multiple_of(which * 768, 128), 768)]

    def wo_half(ref, which):
        return ref.at[:, pl.ds(pl.multiple_of(which * 64, 16), 64)]

    locals_ = []

    def local(src, dst):
        copy = pltpu.make_async_copy(src, dst, local_sems.at[len(locals_)])
        copy.start()
        locals_.append(copy)
        return copy

    mine = [
        local(gu_half(dgu, core), h_gu),
        local(d_half(dd, core), h_d),
        local(qkv_half(dqkv, core), h_qkv),
        local(wo_half(dwo, core), h_wo),
        local(dgain, h_gain),
    ]
    greet([sibling, low] + group + column)
    swaps = [
        wire.copy(gu_half(dgu, 1 - core), r_gu, sibling),
        wire.copy(qkv_half(dqkv, 1 - core), r_qkv, sibling),
        wire.copy(wo_half(dwo, 1 - core), r_wo, sibling),
        wire.copy(dgain, r_gain, sibling),
        wire.copy(d_half(dd, 1 - core), r_d, sibling),
    ]
    for swap in swaps:
        swap.start()
    for copy in mine:
        copy.wait()

    def summed(target, source, count):
        def one(i, carry):
            add_into(target.at[i], source.at[i])
            return carry

        lax.fori_loop(0, count, one, 0)

    swaps[0].wait_recv()
    summed(h_gu, r_gu, 8)
    swaps[0].wait_send()
    turn = [
        wire.copy(h_gu.at[place.shard_at(j, p)], f_gu.at[me], device)
        for (j, p), device in zip(others, group)
    ]
    for copy in turn:
        copy.start()
    f_gu[me] = h_gu[me]
    for swap in swaps[1:4]:
        swap.wait_recv()
    summed(h_qkv, r_qkv, 8)
    summed(h_wo, r_wo, 8)
    summed(h_gain, r_gain, 8)

    def cut_lanes(size):
        def cut(ref, part):
            return ref if part == 0 else ref.at[:, pl.ds((part - 1) * size, size)]

        return cut

    def cut_rows(size):
        def cut(ref, part):
            return ref if part == 0 else ref.at[pl.ds((part - 1) * size, size)]

        return cut

    at = place.shard_at
    sums = [
        SumTree(wire, place, lambda j, p: h_qkv.at[at(j, p)], cut_lanes(384), qa, qb, qm, qp, qz),
        SumTree(wire, place, lambda j, p: h_wo.at[at(j, p)], cut_rows(32), wa, wb, wm, wp, wz),
        SumTree(wire, place, lambda j, p: h_gain.at[at(j, p)], cut_lanes(128), ga, gb_, gm, gp, gz),
    ]
    for tree in sums:
        tree.send_far()
    swaps[4].wait_recv()
    add_into(h_d, r_d)

    def quarter_gu(ref, which):
        return ref.at[pl.ds(which * 2, 2)]

    def quarter_d(ref, which):
        return ref.at[pl.ds(pl.multiple_of(which * 112, 16), 112)]

    steps = (1, 3, 2)
    over_d = [
        wire.copy(quarter_d(h_d, (y + d) % 4), y_d.at[y], device)
        for d, device in zip(steps, column)
    ]
    for copy in over_d:
        copy.start()
    for tree in sums:
        tree.send_near()
    for copy in turn:
        copy.wait_recv()
    over_gu = [
        wire.copy(quarter_gu(f_gu, (y + d) % 4), y_gu.at[y], device)
        for d, device in zip(steps, column)
    ]
    for copy in over_gu:
        copy.start()
    y_gu[y] = quarter_gu(f_gu, y)[...]
    y_d[y] = quarter_d(h_d, y)[...]
    for tree in sums:
        tree.send_last()
    for tree, target in zip(sums, (y_qkv, y_wo, y_gain)):
        target[y] = tree.finish().astype(jnp.bfloat16)
    over_small = [
        [wire.copy(target.at[y], target.at[y], device) for device in column]
        for target in (y_qkv, y_wo, y_gain)
    ]
    for copies in over_small:
        for copy in copies:
            copy.start()

    def add_up(source):
        return (
            source[0].astype(jnp.float32)
            + source[1].astype(jnp.float32)
            + source[2].astype(jnp.float32)
            + source[3].astype(jnp.float32)
        )

    def across(copies, source, piece, other):
        for copy in copies:
            copy.wait_recv()
        piece[...] = add_up(source).astype(jnp.bfloat16)
        made = wire.copy(piece, other, low)
        made.start()
        return made

    crossings = [
        across(over_d, y_d, p_d, z_d),
        across(over_gu, y_gu, p_gu, z_gu),
        across(over_small[0], y_qkv, p_qkv, z_qkv),
        across(over_small[1], y_wo, p_wo, z_wo),
        across(over_small[2], y_gain, p_gain, z_gain),
    ]

    def settle(crossing, piece, other):
        crossing.wait_recv()
        crossing.wait_send()
        add_into(piece, other)

    def out_gu(which, half):
        return o_gu.at[
            pl.ds(which * 2, 2), :, pl.ds(pl.multiple_of(half * FF_PAD, 128), FF_PAD)
        ]

    def out_d(which, half):
        return o_d.at[pl.ds(pl.multiple_of(half * 448 + which * 112, 16), 112)]

    ends = []
    settle(crossings[0], p_d, z_d)
    back_d = [wire.copy(p_d, out_d(y, core), device) for device in column]
    ends.append(wire.copy(p_d, out_d(y, core), sibling))
    for copy in back_d + ends[-1:]:
        copy.start()
    local(p_d, out_d(y, core))
    settle(crossings[1], p_gu, z_gu)
    back_gu = [wire.copy(p_gu, out_gu(y, core), device) for device in column]
    ends.append(wire.copy(p_gu, out_gu(y, core), sibling))
    for copy in back_gu + ends[-1:]:
        copy.start()
    local(p_gu, out_gu(y, core))
    out_qkv = o_qkv.at[:, pl.ds(pl.multiple_of(core * 768, 128), 768)]
    out_wo = o_wo.at[pl.ds(pl.multiple_of(core * 64, 16), 64)]
    for crossing, piece, other, out in (
        (crossings[2], p_qkv, z_qkv, out_qkv),
        (crossings[3], p_wo, z_wo, out_wo),
    ):
        settle(crossing, piece, other)
        ends.append(wire.copy(piece, out, sibling))
        ends[-1].start()
        local(piece, out)
    settle(crossings[4], p_gain, z_gain)
    local(p_gain, o_gain)
    for backs, out in ((back_d, out_d), (back_gu, out_gu)):
        for d, copy in zip((3, 1, 2), backs):
            copy.wait_recv()
            which = (y + d) % 4
            ends.append(wire.copy(out(which, core), out(which, core), sibling))
            ends[-1].start()
    for copy in ends:
        copy.wait_recv()
    for copy in locals_[5:]:
        copy.wait()
    waited = [id(made) for made in swaps[:1] + crossings]
    for made in wire.made:
        if id(made) not in waited:
            made.wait_send()


def reduce_all(dgu, dd, dqkv, dwo, dgain):
    bf = jnp.bfloat16
    vm = lambda *s: pltpu.VMEM(s, bf)
    shape = lambda *s: jax.ShapeDtypeStruct(s, bf)
    h_gu, h_qkv, h_wo, h_gain, h_d = (8, 144, 896), (8, 144, 768), (8, 64, 1152), (8, 16, 256), (448, 1152)
    q_gu, q_d = (2, 144, 896), (112, 1152)
    unit = [h_qkv[1:], h_wo[1:], h_gain[1:]]
    halves = [(144, 384), (32, 1152), (16, 128)]
    trees = []
    for whole, half in zip(unit, halves):
        trees += [vm(2, *half), vm(2, *half), vm(2, *whole), vm(2, *whole), vm(*whole)]
    return pl.pallas_call(
        reduce_kernel,
        out_shape=(shape(8, 144, 1792), shape(896, 1152), shape(144, 1536), shape(128, 1152), shape(16, 256)),
        in_specs=[ANY] * 5,
        out_specs=(ANY,) * 5,
        scratch_shapes=[
            vm(*h_gu), vm(*h_gu), vm(*h_gu), vm(*h_d), vm(*h_d), vm(*h_qkv), vm(*h_qkv),
            vm(*h_wo), vm(*h_wo), vm(*h_gain), vm(*h_gain),
        ]
        + [vm(4, *s) for s in (q_gu, q_d, *unit)]
        + [vm(*s) for s in (q_gu, q_d, *unit)]
        + [vm(*s) for s in (q_gu, q_d, *unit)]
        + trees
        + [
            pltpu.SemaphoreType.DMA((12,)),
            pltpu.SemaphoreType.DMA((96,)),
            pltpu.SemaphoreType.DMA((96,)),
        ],
        compiler_params=comm_params(5),
        name="reduce_grads",
    )(dgu, dd, dqkv, dwo, dgain)


def rotate(vectors, cosine, sine_part):
    half_size = vectors.shape[-1] // 2
    first_half = vectors[..., :half_size]
    second_half = vectors[..., half_size:]
    return jnp.concatenate(
        [
            first_half * cosine - second_half * sine_part,
            second_half * cosine + first_half * sine_part,
        ],
        axis=-1,
    )


def norm_back(grad_normed, scaled, inverse, gain_values):
    grad_scaled = grad_normed * gain_values
    return inverse * (grad_scaled - scaled * jnp.mean(grad_scaled * scaled, axis=1, keepdims=True))


def pack_gate_up(w_gate, w_up):
    rows = w_gate.shape[0]

    def cut(weight):
        parts = weight.reshape(rows, 8, FF_DEV)
        return jnp.pad(parts, ((0, 0), (0, 0), (0, FF_PAD - FF_DEV))).reshape(rows, 8, PAIRS, 128)

    both = jnp.stack([cut(w_gate), cut(w_up)], axis=3)
    return both.transpose(1, 0, 2, 3, 4).reshape(8, rows, 2 * FF_PAD)


def unpack_gate_up(both):
    rows = both.shape[1]
    split = both.reshape(8, rows, PAIRS, 2, 128)

    def join(k):
        parts = split[:, :, :, k].reshape(8, rows, FF_PAD)[:, :, :FF_DEV]
        return parts.transpose(1, 0, 2).reshape(rows, 8 * FF_DEV).astype(jnp.float32)

    return join(0), join(1)


def gain_rows(*rows):
    made = jnp.stack([jnp.pad(row, ((0, 0), (0, 256 - row.shape[1]))) for row in rows], axis=1)
    return jnp.pad(made, ((0, 0), (0, 16 - len(rows)), (0, 0))).astype(jnp.bfloat16)


def on_device(
    tokens, lengths, attn_gain, w_query, w_keyval, w_out, mlp_gain, w_gate, w_up, w_down, cotangent
):
    row_count, width = tokens.shape
    head_size = w_keyval.shape[1] // 2
    heads_all = w_query.shape[1]
    head_count = heads_all // head_size
    scaling = head_size ** (-0.5)
    shard = lax.axis_index("shard")
    within = jnp.arange(row_count, dtype=jnp.int32)
    live_count = lengths[0, 0]
    keep_mask = (within < live_count).astype(jnp.float32)[:, None]
    grad_out = cotangent.astype(jnp.float32)
    grad_branch = (keep_mask * grad_out).astype(jnp.bfloat16)

    counts = jnp.full((1, 144), live_count, jnp.int32).astype(jnp.bfloat16)
    misc = gain_rows(attn_gain[None], mlp_gain[None], counts)[0]
    miscs, qkv_all, out_all, gu_all, branch_all = spread(
        misc,
        jnp.concatenate([w_query, w_keyval], axis=1),
        w_out,
        pack_gate_up(w_gate, w_up),
        grad_branch,
    )
    gain1 = miscs[:, 0, :144].reshape(width).astype(jnp.float32)
    gain2 = miscs[:, 1, :144].reshape(width).astype(jnp.float32)
    live_all = miscs[:, 2, 0].astype(jnp.int32)
    qkv_full = qkv_all.reshape(width, -1)
    out_full = out_all.reshape(heads_all, width)
    down_mine = jnp.pad(w_down, ((0, FF_PAD - FF_DEV), (0, 0)))

    starts = jnp.cumsum(live_all) - live_all
    offset = starts[shard]
    query_pos = offset + within
    back = shard - jnp.arange(BEHIND + 1)
    back_start = jnp.where(back >= 0, starts[jnp.maximum(back, 0)], 0)
    back_live = jnp.where(back >= 0, live_all[jnp.maximum(back, 0)], 0)
    key_pos = (back_start[:, None] + within[None]).reshape(-1)
    key_live = (within[None] < back_live[:, None]).reshape(-1)
    allowed = (
        key_live[None, :]
        & (key_pos[None, :] <= query_pos[:, None])
        & (query_pos[:, None] - key_pos[None, :] < WINDOW)
    )
    half_size = head_size // 2
    frequency = 10000.0 ** (-2.0 * jnp.arange(half_size, dtype=jnp.float32) / head_size)
    angles = query_pos.astype(jnp.float32)[:, None] * frequency[None, :]
    cosine = jnp.cos(angles)
    sine_part = jnp.sin(angles)
    heads_cos = cosine[:, None, :]
    heads_sin = sine_part[:, None, :]
    inputs = tokens.astype(jnp.float32)
    inverse1 = lax.rsqrt(jnp.mean(inputs * inputs, axis=1, keepdims=True) + EPSILON)
    scaled1 = inputs * inverse1
    normed1 = (scaled1 * gain1).astype(jnp.bfloat16)
    projected = matmul(normed1, qkv_full)
    queries = (
        rotate(
            projected[:, :heads_all].reshape(row_count, head_count, head_size),
            heads_cos,
            heads_sin,
        )
        * scaling
    ).astype(jnp.bfloat16)
    own_keys = rotate(
        projected[:, heads_all : heads_all + head_size], cosine, sine_part
    ).astype(jnp.bfloat16)
    own_values = projected[:, heads_all + head_size :].astype(jnp.bfloat16)
    own_kv = jnp.concatenate([own_keys, own_values], axis=1)
    behind = window(own_kv, False, 3, "keys_values")
    behind = jnp.where((back[1:] >= 0)[:, None, None], behind, 0)
    all_kv = jnp.concatenate([own_kv[None], behind], axis=0).reshape(-1, 2 * head_size)
    keys, values = all_kv[:, :head_size], all_kv[:, head_size:]

    raw_scores = jnp.einsum("thd,gd->htg", queries, keys, preferred_element_type=jnp.float32)
    scores = jnp.where(allowed[None], raw_scores, MASKED)
    row_max = jnp.max(scores, axis=-1, keepdims=True)
    raised = jnp.exp(scores - row_max)
    probs = raised / jnp.sum(raised, axis=-1, keepdims=True)
    probs_low = probs.astype(jnp.bfloat16)
    attended = jnp.einsum("htg,gd->thd", probs_low, values, preferred_element_type=jnp.float32)
    attended = attended.reshape(row_count, heads_all).astype(jnp.bfloat16)
    middle = inputs + keep_mask * matmul(attended, out_full)
    inverse2 = lax.rsqrt(jnp.mean(middle * middle, axis=1, keepdims=True) + EPSILON)
    scaled2 = middle * inverse2
    normed2 = (scaled2 * gain2).astype(jnp.bfloat16)

    grad_normed2, branch, grad_gu, grad_d = feed_forward(
        normed2, branch_all, gu_all.reshape(width, -1), down_mine
    )
    outputs = (middle + keep_mask * branch).astype(jnp.bfloat16)
    grad_gain2 = jnp.sum(grad_normed2 * scaled2, axis=0)
    grad_middle = grad_out + norm_back(grad_normed2, scaled2, inverse2, gain2)

    grad_attn = (keep_mask * grad_middle).astype(jnp.bfloat16)
    grad_out_w = lead_product(attended, grad_attn)
    grad_attended = (
        trail_product(grad_attn, out_full)
        .astype(jnp.bfloat16)
        .reshape(row_count, head_count, head_size)
    )
    grad_probs = jnp.einsum(
        "thd,gd->htg", grad_attended, values, preferred_element_type=jnp.float32
    )
    grad_values_all = jnp.einsum(
        "htg,thd->gd", probs_low, grad_attended, preferred_element_type=jnp.float32
    )
    row_delta = jnp.sum(probs * grad_probs, axis=-1, keepdims=True)
    grad_scores = (probs * (grad_probs - row_delta)).astype(jnp.bfloat16)
    grad_queries = jnp.einsum("htg,gd->thd", grad_scores, keys, preferred_element_type=jnp.float32)
    grad_keys_all = jnp.einsum(
        "htg,thd->gd", grad_scores, queries, preferred_element_type=jnp.float32
    )
    grad_kv_all = jnp.concatenate([grad_keys_all, grad_values_all], axis=1)
    grad_kv_all = grad_kv_all.reshape(BEHIND + 1, row_count, 2 * head_size)
    ahead = window(grad_kv_all.astype(jnp.bfloat16), True, 4, "grad_keys_values")
    is_ahead = (shard + 1 + jnp.arange(BEHIND) < 8)[:, None, None]
    grad_own_kv = grad_kv_all[0] + jnp.sum(
        jnp.where(is_ahead, ahead, 0).astype(jnp.float32), axis=0
    )
    grad_query_proj = (
        (rotate(grad_queries, heads_cos, -heads_sin) * scaling)
        .reshape(row_count, heads_all)
        .astype(jnp.bfloat16)
    )
    grad_keyval_proj = jnp.concatenate(
        [
            rotate(grad_own_kv[:, :head_size], cosine, -sine_part),
            grad_own_kv[:, head_size:],
        ],
        axis=1,
    ).astype(jnp.bfloat16)
    grad_proj = jnp.concatenate([grad_query_proj, grad_keyval_proj], axis=1)
    grad_qkv_w = lead_product(normed1, grad_proj)
    grad_normed1 = trail_product(grad_proj, qkv_full)
    grad_gain1 = jnp.sum(grad_normed1 * scaled1, axis=0)
    grad_inputs = grad_middle + norm_back(grad_normed1, scaled1, inverse1, gain1)

    sum_gu, sum_d, sum_qkv, sum_wo, sum_gain = reduce_all(
        grad_gu.reshape(8, 144, -1),
        grad_d,
        grad_qkv_w.astype(jnp.bfloat16).reshape(8, 144, -1),
        grad_out_w.astype(jnp.bfloat16).reshape(8, 128, width),
        gain_rows(grad_gain1.reshape(8, 144), grad_gain2.reshape(8, 144)),
    )
    grad_gate_w, grad_up_w = unpack_gate_up(sum_gu)
    sum_qkv = sum_qkv.astype(jnp.float32)
    return (
        outputs,
        grad_inputs,
        sum_gain[0, :144].astype(jnp.float32),
        sum_qkv[:, :heads_all],
        sum_qkv[:, heads_all:],
        sum_wo.astype(jnp.float32),
        sum_gain[1, :144].astype(jnp.float32),
        grad_gate_w,
        grad_up_w,
        sum_d[:FF_DEV].astype(jnp.float32),
    )


def solution(mesh):
    placed = (
        P(("rep", "shard"), None),
        P("rep", "shard"),
        P("shard"),
        P("shard", None),
        P("shard", None),
        P("shard", None),
        P("shard"),
        P("shard", None),
        P("shard", None),
        P("shard", None),
        P(("rep", "shard"), None),
    )
    return jax.shard_map(
        on_device,
        mesh=mesh,
        in_specs=placed,
        out_specs=(
            P(("rep", "shard"), None),
            P(("rep", "shard"), None),
            P("shard"),
            P("shard", None),
            P("shard", None),
            P("shard", None),
            P("shard"),
            P("shard", None),
            P("shard", None),
            P("shard", None),
        ),
        check_vma=False,
    )
```

```python
import functools

import jax
import jax.numpy as jnp
from jax import lax
from jax.experimental import pallas as pl
from jax.experimental.pallas import tpu as pltpu
from jax.sharding import PartitionSpec as P

MESH = pl.DeviceIdType.MESH
WINDOW = 512
EPSILON = 1e-06
MASKED = -1e30
VMEM_LIMIT = 60 * 2**20
FF_DEV = 864
FF_PAD = 896
PAIRS = FF_PAD // 128
BEHIND = 4


def matmul(former, latter):
    return jnp.dot(former, latter, preferred_element_type=jnp.float32)


def lead_product(former, latter):
    return lax.dot_general(
        former, latter, (((0,), (0,)), ((), ())), preferred_element_type=jnp.float32
    )


def trail_product(former, latter):
    return lax.dot_general(
        former, latter, (((1,), (1,)), ((), ())), preferred_element_type=jnp.float32
    )


class Place:
    def __init__(self):
        rep, shard = lax.axis_index("rep"), lax.axis_index("shard")
        self.rep, self.shard = rep, shard
        self.y, self.z_lo, self.core = rep // 4, (rep // 2) % 2, rep % 2
        self.z_hi, self.x = shard // 4, shard % 4

    def device(self, dx=0, dy=0, mirror=0, swap_lo=0, sibling=0):
        z_lo = (self.z_lo + mirror + swap_lo) % 2
        rep = (((self.y + dy) % 4) * 2 + z_lo) * 2 + (self.core + sibling) % 2
        return (rep, ((self.z_hi + mirror) % 2) * 4 + (self.x + dx) % 4)

    def shard_at(self, j, p):
        return ((self.z_hi + p) % 2) * 4 + (self.x + STEPS[j]) % 4


STEPS = (0, 1, 3, 2)


class Wire:
    def __init__(self, send_sems, recv_sems):
        self.send_sems, self.recv_sems, self.made = send_sems, recv_sems, []

    def copy(self, src, dst, device):
        k = len(self.made)
        made = pltpu.make_async_remote_copy(
            src_ref=src,
            dst_ref=dst,
            send_sem=self.send_sems.at[k],
            recv_sem=self.recv_sems.at[k],
            device_id=device,
            device_id_type=MESH,
        )
        self.made.append(made)
        return made

    def drain(self):
        for made in self.made:
            made.wait_send()


def greet(devices):
    barrier = pltpu.get_barrier_semaphore()
    for device in devices:
        pl.semaphore_signal(barrier, inc=1, device_id=device, device_id_type=MESH)
    pl.semaphore_wait(barrier, len(devices))


HOPS = (
    ((0, 0), (0, 1), 0, 0, 1),
    ((0, 0), (2, 0), 0, 1, 0),
    ((0, 0), (1, 0), 0, 3, 0),
    ((0, 1), (2, 1), 1, 1, 0),
    ((0, 1), (1, 1), 1, 3, 0),
    ((2, 0), (3, 0), 1, 1, 0),
    ((1, 0), (3, 0), 2, 3, 0),
    ((2, 0), (2, 1), 2, 0, 1),
    ((1, 0), (1, 1), 2, 0, 1),
    ((2, 1), (3, 1), 1, 1, 0),
    ((1, 1), (3, 1), 2, 3, 0),
)
ONWARD = {0: (3, 4), 1: (5, 7), 2: (6, 8), 3: (9,), 8: (10,)}
WHOLE = {0: (0, 1), 1: (2, 0), 2: (1, 0), 6: (3, 0), 7: (2, 1), 8: (1, 1), 10: (3, 1)}
ORDER = (0, 1, 2, 3, 4, 8, 7, 5, 6, 9, 10)


def gather_tree(wire, place, own, slot, cut, absolute):
    copies = []
    for source, target, part, dx, mirror in HOPS:
        src = own if source == (0, 0) else slot(*source)
        dst = slot(*(source if absolute else target))
        copies.append(wire.copy(cut(src, part), cut(dst, part), place.device(dx=dx, mirror=mirror)))
    return copies


def arrive(tree, k):
    tree[k].wait_recv()
    for n in ONWARD.get(k, ()):
        tree[n].start()


def add_into(target, source):
    target[...] = (target[...].astype(jnp.float32) + source[...].astype(jnp.float32)).astype(
        target.dtype
    )


class SumTree:
    def __init__(self, wire, place, slot, cut, whole, half):
        self.slot, self.cut = slot, cut
        self.copies, self.landed = [], []
        for k, (source, target, part, dx, mirror) in enumerate(HOPS):
            landing = whole.at[k] if k < 3 else half.at[k - 3]
            device = place.device(dx=(4 - dx) % 4, mirror=mirror)
            self.landed.append(landing)
            self.copies.append(wire.copy(cut(slot(*target), part), landing, device))

    def start(self, *hops):
        for k in hops:
            self.copies[k].start()

    def absorb(self, *hops):
        for k in hops:
            source, _, part, _, _ = HOPS[k]
            self.copies[k].wait_recv()
            add_into(self.cut(self.slot(*source), part), self.landed[k])

    def send_far(self):
        self.start(10, 9, 6, 5)

    def send_near(self):
        self.start(4, 7)
        self.absorb(10)
        self.start(8)
        self.absorb(9)
        self.start(3)
        self.absorb(6, 5)

    def send_next(self):
        self.absorb(8)
        self.start(2)
        self.absorb(7)
        self.start(1)

    def send_last(self):
        self.absorb(3, 4)
        self.start(0)

    def finish(self):
        total = self.slot(0, 0)[...].astype(jnp.float32)
        for k in (2, 1, 0):
            self.copies[k].wait_recv()
            total = total + self.landed[k][...].astype(jnp.float32)
        return total


def front_kernel(
    tokens, cot, misc, freq, w_query, w_keyval, w_out, w_gate, w_up,
    o_misc, o_qkv, o_wo, o_gu, o_gb, o_normed1, o_q, o_kv, o_probs, o_att, o_middle, o_normed2,
    x_ref, cot_ref, miscs, freq_ref, wqkv, wo, gate, up, packed, gb_own, normed1, q_ref, kv_ref,
    bias, probs, att, middle, normed2,
    local_sems, send_sems, recv_sems,
):
    place = Place()
    wire = Wire(send_sems, recv_sems)
    core, me, y = place.core, place.shard, place.y
    rows, width = tokens.shape
    at = place.shard_at
    others = [(j, p) for p in (0, 1) for j in range(4) if (j, p) != (0, 0)]
    group = [place.device(dx=STEPS[j], mirror=p) for j, p in others]
    sequence = [(place.rep, at(j, p)) for j, p in others]
    sibling = place.device(sibling=1)
    steps = (1, 3, 2)
    column = [place.device(dy=d) for d in steps]
    locals_ = []

    def local(src, dst):
        copy = pltpu.make_async_copy(src, dst, local_sems.at[len(locals_)])
        copy.start()
        locals_.append(copy)
        return copy

    load_x = local(tokens, x_ref)
    load_cot = local(cot, cot_ref)
    load_misc = local(misc, miscs.at[me])
    load_freq = local(freq, freq_ref)
    load_gate = local(w_gate, gate)
    load_up = local(w_up, up)
    load_own = [
        local(w_query, wqkv.at[me, :, pl.ds(0, 1024)]),
        local(w_keyval, wqkv.at[me, :, pl.ds(1024, 512)]),
        local(w_out, wo.at[me]),
    ]
    greet([sibling] + group + [d for d, (j, p) in zip(sequence, others) if p == 1] + column)

    def lanes_from(base, size):
        def cut(ref, part):
            start, count = ((0, size), (0, size // 2), (size // 2, size // 2))[part]
            start = pl.multiple_of(core * size + (base + start), 128)
            return ref.at[:, pl.ds(start, count)]

        return cut

    def cut_wo(ref, part):
        start, size = ((0, 64), (0, 32), (32, 32))[part]
        return ref.at[pl.ds(pl.multiple_of(core * 64 + start, 32), size)]

    def cut_gb(ref, part):
        return ref if part == 0 else ref.at[pl.ds((part - 1) * 96, 96)]

    def cut_gu(ref):
        return ref.at[:, pl.ds(pl.multiple_of(core * FF_PAD, 128), FF_PAD)]

    cut_q, cut_kv = lanes_from(0, 512), lanes_from(1024, 256)
    slot_qkv = lambda j, p: wqkv.at[at(j, p)]
    slot_wo = lambda j, p: wo.at[at(j, p)]
    slot_gb = lambda j, p: o_gb.at[j, p]
    misc_copies = [wire.copy(misc, miscs.at[me], device) for device in sequence]
    for copy in misc_copies:
        copy.start()
    for load in load_own:
        load.wait()
    own = wqkv.at[me]
    trees = [
        gather_tree(wire, place, own, slot_qkv, cut_q, True),
        gather_tree(wire, place, own, slot_qkv, cut_kv, True),
        gather_tree(wire, place, wo.at[me], slot_wo, cut_wo, True),
    ]
    cuts = [cut_q, cut_kv, cut_wo]
    slots = [slot_qkv, slot_qkv, slot_wo]
    passes = [
        {k: wire.copy(cut(slot(*jp), 0), cut(slot(*jp), 0), sibling) for k, jp in WHOLE.items()}
        for cut, slot in zip(cuts, slots)
    ]
    for tree in trees:
        for k in (0, 1, 2):
            tree[k].start()

    load_x.wait()
    inputs = x_ref[...].astype(jnp.float32)
    inverse1 = lax.rsqrt(jnp.mean(inputs * inputs, axis=1, keepdims=True) + EPSILON)
    middle[...] = inputs * inverse1
    load_gate.wait()
    load_up.wait()
    for d in range(8):
        for t in range(PAIRS):
            start = FF_DEV * d + 128 * t
            size = min(128, FF_DEV - 128 * t)
            for k, weight in enumerate((gate, up)):
                block = weight[:, start : start + size]
                if size < 128:
                    block = jnp.concatenate(
                        [block, jnp.zeros((block.shape[0], 128 - size), block.dtype)], axis=1
                    )
                packed[d, :, 256 * t + 128 * k : 256 * t + 128 * (k + 1)] = block

    def attn(*hops):
        for k in hops:
            for tree, onward in zip(trees, passes):
                arrive(tree, k)
                if k in onward:
                    onward[k].start()

    attn(0, 1, 2)
    load_cot.wait()
    load_misc.wait()
    load_freq.wait()
    live_col = (
        lax.broadcasted_iota(jnp.int32, (rows, 1), 0).astype(jnp.float32)
        < miscs[me].astype(jnp.float32)[2:3, :1]
    )
    gb_own[...] = jnp.where(live_col, cot_ref[...].astype(jnp.float32), 0.0).astype(jnp.bfloat16)
    attn(3, 4, 8, 7)
    gb_tree = gather_tree(wire, place, gb_own, slot_gb, cut_gb, False)
    for k in (0, 1, 2):
        gb_tree[k].start()
    local(gb_own, o_gb.at[0, 0])

    z_of = lambda p: (place.z_hi + p) % 2
    shard_from = lambda d, p: z_of(p) * 4 + (place.x + y + d) % 4
    turn = []
    for p in (0, 1):
        target = z_of(p) * 4 + (place.x - y + 4) % 4
        turn.append(
            wire.copy(
                cut_gu(packed.at[target]), cut_gu(o_gu.at[me]), place.device(dx=4 - y, mirror=p)
            )
        )
    away, home = y > 0, y == 0
    keep_own = pltpu.make_async_copy(
        cut_gu(packed.at[me]), cut_gu(o_gu.at[me]), local_sems.at[len(locals_)]
    )
    locals_.append(None)
    turn[1].start()
    pl.when(away)(turn[0].start)
    pl.when(home)(keep_own.start)
    attn(5, 6, 9, 10)

    for copy in misc_copies:
        copy.wait_recv()
    as_float = [miscs[s].astype(jnp.float32) for s in range(8)]
    gain1 = jnp.concatenate([m[0:1, :144] for m in as_float], axis=1)
    gain2 = jnp.concatenate([m[1:2, :144] for m in as_float], axis=1)
    normed = (middle[...] * gain1).astype(jnp.bfloat16)
    normed1[...] = normed
    for k in WHOLE:
        passes[0][k].wait_recv()
        passes[1][k].wait_recv()
    live = [m[2:3, :1] for m in as_float]
    start_of = []
    for i in range(BEHIND + 1):
        total = jnp.zeros((1, 1), jnp.float32)
        for s in range(8):
            total = total + jnp.where(s < me - i, 1.0, 0.0) * live[s]
        start_of.append(total)
    row = lax.broadcasted_iota(jnp.int32, (rows, 1), 0).astype(jnp.float32)
    query_pos = start_of[0] + row
    angles = query_pos * freq_ref[0:1, :]
    cosine, sine_part = jnp.cos(angles), jnp.sin(angles)
    weights = wqkv.reshape(width, 1536)

    def turned(vectors):
        first, second = vectors[:, :128], vectors[:, 128:]
        return jnp.concatenate(
            [first * cosine - second * sine_part, second * cosine + first * sine_part], axis=1
        )

    projected = matmul(normed, weights[:, 1024:1536])
    kv_ref[0, :, :256] = turned(projected[:, :256]).astype(jnp.bfloat16)
    kv_ref[0, :, 256:] = projected[:, 256:].astype(jnp.bfloat16)
    sends = [
        wire.copy(kv_ref.at[0], kv_ref.at[i], (place.rep, jnp.minimum(me + i, 7)))
        for i in range(1, BEHIND + 1)
    ]
    for i, copy in enumerate(sends):
        pl.when(me + (i + 1) < 8)(copy.start)

        @pl.when(me < i + 1)
        def _():
            kv_ref[i + 1] = jnp.zeros(kv_ref.shape[1:], kv_ref.dtype)

    scaling = 256 ** (-0.5)
    for h in range(4):
        heads = matmul(normed, weights[:, 256 * h : 256 * (h + 1)])
        q_ref[h] = (turned(heads) * scaling).astype(jnp.bfloat16)

    index = lax.broadcasted_iota(jnp.int32, (1, (BEHIND + 1) * rows), 1)
    key_pos = jnp.zeros(index.shape, jnp.float32)
    key_live = jnp.zeros(index.shape, jnp.float32)
    for i in range(BEHIND + 1):
        inside = jnp.logical_and(index >= i * rows, index < (i + 1) * rows)
        within = (index - i * rows).astype(jnp.float32)
        live_i = jnp.zeros((1, 1), jnp.float32)
        for s in range(8):
            live_i = live_i + jnp.where(me - i == s, 1.0, 0.0) * live[s]
        key_pos = jnp.where(inside, start_of[i] + within, key_pos)
        key_live = jnp.where(inside, jnp.where(within < live_i, 1.0, 0.0), key_live)
    ahead = query_pos - key_pos
    allowed = jnp.logical_and(
        jnp.logical_and(ahead >= 0.0, ahead < float(WINDOW)), key_live > 0.5
    )
    bias[...] = jnp.where(allowed, 0.0, MASKED)

    for k in ORDER[:5]:
        arrive(gb_tree, k)
    pl.when(away)(turn[0].wait_recv)
    turn[1].wait_recv()
    pl.when(home)(keep_own.wait)
    over = []
    for d, device in zip(steps, column):
        for p in (0, 1):
            held = cut_gu(o_gu.at[shard_from(0, p)])
            over.append(wire.copy(held, held, device))
            over[-1].start()
    gu_passes = []

    def pass_gu(d, p):
        held = cut_gu(o_gu.at[shard_from(d, p)])
        gu_passes.append(wire.copy(held, held, sibling))
        gu_passes[-1].start()

    for p in (0, 1):
        pass_gu(0, p)
    for i, copy in enumerate(sends):
        pl.when(me >= i + 1)(copy.wait_recv)

    all_kv = kv_ref.reshape((BEHIND + 1) * rows, 512)
    for h in range(4):
        scores = trail_product(q_ref[h], all_kv[:, :256]) + bias[...]
        raised = jnp.exp(scores - jnp.max(scores, axis=1, keepdims=True))
        share = raised * (1.0 / jnp.sum(raised, axis=1, keepdims=True))
        probs[h] = share
        att[:, 256 * h : 256 * (h + 1)] = matmul(
            share.astype(jnp.bfloat16), all_kv[:, 256:]
        ).astype(jnp.bfloat16)
        if h == 1:
            for k in ORDER[5:]:
                arrive(gb_tree, k)
    for k in WHOLE:
        passes[2][k].wait_recv()
    keep = jnp.where(live_col, 1.0, 0.0)
    mid = x_ref[...].astype(jnp.float32) + keep * matmul(att[...], wo.reshape(1024, width)[...])
    middle[...] = mid
    inverse2 = lax.rsqrt(jnp.mean(mid * mid, axis=1, keepdims=True) + EPSILON)
    normed2[...] = (mid * inverse2 * gain2).astype(jnp.bfloat16)
    for src, dst in (
        (miscs, o_misc),
        (wqkv, o_qkv),
        (wo, o_wo),
        (normed1, o_normed1),
        (q_ref, o_q),
        (kv_ref, o_kv),
        (probs, o_probs),
        (att, o_att),
        (middle, o_middle),
        (normed2, o_normed2),
    ):
        local(src, dst)
    for i, (d, p) in enumerate([(d, p) for d in (3, 1, 2) for p in (0, 1)]):
        over[i].wait_recv()
        pass_gu(d, p)
    for copy in gu_passes:
        copy.wait_recv()
    waited = [id(copy) for copy in sends] + [id(turn[0])]
    for copy in locals_[9:]:
        if copy is not None:
            copy.wait()
    pl.when(away)(turn[0].wait_send)
    for i, copy in enumerate(sends):
        pl.when(me + (i + 1) < 8)(copy.wait_send)
    for copy in wire.made:
        if id(copy) not in waited:
            copy.wait_send()


ANY = pl.BlockSpec(memory_space=pl.ANY)


def comm_params(collective_id):
    return pltpu.CompilerParams(
        collective_id=collective_id, has_side_effects=True, vmem_limit_bytes=VMEM_LIMIT
    )


def front(tokens, cot, misc, freq, w_query, w_keyval, w_out, w_gate, w_up):
    bf, f32 = jnp.bfloat16, jnp.float32
    rows, width = tokens.shape
    keys = (BEHIND + 1) * rows
    outs = [
        ((8, 16, 256), bf),
        ((8, 144, 1536), bf),
        ((8, 128, width), bf),
        ((8, 144, 2 * FF_PAD), bf),
        ((4, 2, rows, width), bf),
        ((rows, width), bf),
        ((4, rows, 256), bf),
        ((BEHIND + 1, rows, 512), bf),
        ((4, rows, keys), f32),
        ((rows, 1024), bf),
        ((rows, width), f32),
        ((rows, width), bf),
    ]
    scratch = [
        ((rows, width), bf),
        ((rows, width), bf),
        ((8, 16, 256), bf),
        ((8, 128), f32),
        ((8, 144, 1536), bf),
        ((8, 128, width), bf),
        (w_gate.shape, bf),
        (w_up.shape, bf),
        ((8, 144, 2 * FF_PAD), bf),
        ((rows, width), bf),
        ((rows, width), bf),
        ((4, rows, 256), bf),
        ((BEHIND + 1, rows, 512), bf),
        ((rows, keys), f32),
        ((4, rows, keys), f32),
        ((rows, 1024), bf),
        ((rows, width), f32),
        ((rows, width), bf),
    ]
    return pl.pallas_call(
        front_kernel,
        out_shape=tuple(jax.ShapeDtypeStruct(*o) for o in outs),
        in_specs=[ANY] * 9,
        out_specs=(ANY,) * len(outs),
        scratch_shapes=[pltpu.VMEM(*v) for v in scratch]
        + [
            pltpu.SemaphoreType.DMA((32,)),
            pltpu.SemaphoreType.DMA((112,)),
            pltpu.SemaphoreType.DMA((112,)),
        ],
        compiler_params=comm_params(1),
        name="attention_forward",
    )(tokens, cot, misc, freq, w_query, w_keyval, w_out, w_gate, w_up)


def unpack_kernel(both, gate, up):
    for d in range(8):
        for t in range(PAIRS):
            size = min(128, FF_DEV - 128 * t)
            start = FF_DEV * d + 128 * t
            for k, out in enumerate((gate, up)):
                block = both[d, :, 256 * t + 128 * k : 256 * t + 128 * k + size]
                out[:, start : start + size] = block.astype(jnp.float32)


def unpack_gate_up(both):
    rows = both.shape[1]
    out = jax.ShapeDtypeStruct((rows, 8 * FF_DEV), jnp.float32)
    spec = pl.BlockSpec((16, 8 * FF_DEV), lambda i: (i, 0))
    return pl.pallas_call(
        unpack_kernel,
        grid=(rows // 16,),
        out_shape=(out, out),
        in_specs=[pl.BlockSpec((8, 16, 2 * FF_PAD), lambda i: (0, i, 0))],
        out_specs=(spec, spec),
        compiler_params=pltpu.CompilerParams(vmem_limit_bytes=VMEM_LIMIT),
        name="unpack_gate_up",
    )(both)


def window_kernel(reverse, own, out, send_sems, recv_sems):
    rep, shard = lax.axis_index("rep"), lax.axis_index("shard")
    barrier = pltpu.get_barrier_semaphore()
    sign = -1 if reverse else 1

    def inside(i):
        return jnp.logical_and(shard + i >= 0, shard + i < 8)

    for i in range(1, BEHIND + 1):

        @pl.when(inside(-sign * i))
        def _():
            pl.semaphore_signal(
                barrier, inc=1, device_id=(rep, shard - sign * i), device_id_type=MESH
            )

    targets = jnp.minimum(shard if reverse else 7 - shard, BEHIND)

    @pl.when(targets > 0)
    def _():
        pl.semaphore_wait(barrier, targets)

    copies = []
    for i in range(1, BEHIND + 1):
        copy = pltpu.make_async_remote_copy(
            src_ref=own.at[i] if reverse else own,
            dst_ref=out.at[i - 1],
            send_sem=send_sems.at[i],
            recv_sem=recv_sems.at[i],
            device_id=(rep, shard + sign * i),
            device_id_type=MESH,
        )
        copies.append(copy)
        pl.when(inside(sign * i))(copy.start)
    for i, copy in enumerate(copies):
        pl.when(inside(-sign * (i + 1)))(copy.wait_recv)
        pl.when(inside(sign * (i + 1)))(copy.wait_send)


def window(own, reverse, collective_id, name):
    block = own.shape[-2:]
    return pl.pallas_call(
        functools.partial(window_kernel, reverse),
        out_shape=jax.ShapeDtypeStruct((BEHIND, *block), jnp.bfloat16),
        in_specs=[ANY],
        out_specs=ANY,
        scratch_shapes=[
            pltpu.SemaphoreType.DMA((BEHIND + 1,)),
            pltpu.SemaphoreType.DMA((BEHIND + 1,)),
        ],
        compiler_params=comm_params(collective_id),
        name=name,
    )(own)


ROOT = 0.7978845608028654
CUBE = 0.044715


def ff_kernel(
    own_n, gb_all, wgu_all, wd_all,
    o_gn, o_br, o_dgu, o_dd,
    nbuf, gb, wgu, wd, gh, hid, ggu, part_g, part_b, out_f32, dgu_tile,
    g_whole, g_half, b_whole, b_half,
    local_sems, send_sems, recv_sems,
):
    place = Place()
    wire = Wire(send_sems, recv_sems)
    loads = [
        pltpu.make_async_copy(src, dst, local_sems.at[k])
        for k, (src, dst) in enumerate(
            [(own_n, nbuf.at[0, 0]), (wd_all, wd), (gb_all, gb), (wgu_all, wgu)]
        )
    ]
    for load in loads:
        load.start()
    greet([place.device(dx=1), place.device(dx=3), place.device(mirror=1)])

    def cut(ref, part):
        return ref if part == 0 else ref.at[pl.ds((part - 1) * 96, 96)]

    slot_n = lambda j, p: nbuf.at[j, p]
    tree = gather_tree(wire, place, nbuf.at[0, 0], slot_n, cut, False)
    sum_g = SumTree(wire, place, lambda j, p: part_g.at[j, p], cut, g_whole, g_half)
    sum_b = SumTree(wire, place, lambda j, p: part_b.at[j, p], cut, b_whole, b_half)
    loads[0].wait()
    for k in (0, 1, 2):
        tree[k].start()
    loads[1].wait()
    loads[2].wait()

    def back_hidden(j):
        rows = jnp.concatenate([gb[j, 0], gb[j, 1]], axis=0)
        gh[j] = trail_product(rows, wd[...])

    def forward(j):
        rows = jnp.concatenate([nbuf[j, 0], nbuf[j, 1]], axis=0)

        def tile(t, carry):
            columns = pl.ds(pl.multiple_of(t * 256, 256), 256)
            narrow = pl.ds(pl.multiple_of(t * 128, 128), 128)
            both = matmul(rows, wgu[:, columns])
            gate, up = both[:, :128], both[:, 128:]
            square = gate * gate
            curve = jnp.tanh(ROOT * gate * (1.0 + CUBE * square))
            half_up = 0.5 * (1.0 + curve)
            active = gate * half_up
            slope = half_up + 0.5 * gate * (1.0 - curve * curve) * (
                ROOT * (1.0 + 3.0 * CUBE * square)
            )
            back = gh[j, :, narrow]
            hid[j, :, narrow] = (active * up).astype(jnp.bfloat16)
            ggu[j, :, columns] = jnp.concatenate(
                [(back * up * slope).astype(jnp.bfloat16), (back * active).astype(jnp.bfloat16)],
                axis=1,
            )
            return carry

        lax.fori_loop(0, PAIRS, tile, 0)

    def back_normed(j):
        for start, size in ((0, 512), (512, 512), (1024, 128)):
            block = trail_product(ggu[j], wgu[start : start + size, :]).astype(jnp.bfloat16)
            part_g[j, 0, :, start : start + size] = block[:192]
            part_g[j, 1, :, start : start + size] = block[192:]

    def down(j):
        for start, size in ((0, 512), (512, 512), (1024, 128)):
            block = matmul(hid[j], wd[:, start : start + size]).astype(jnp.bfloat16)
            part_b[j, 0, :, start : start + size] = block[:192]
            part_b[j, 1, :, start : start + size] = block[192:]

    for j in range(4):
        back_hidden(j)
    for k in (0, 1, 2):
        arrive(tree, k)
    loads[3].wait()
    forward(0)
    for k in (3, 4, 8, 7):
        arrive(tree, k)
    forward(1)
    forward(2)
    for k in (5, 6, 9, 10):
        arrive(tree, k)
    forward(3)
    back_normed(3)
    sum_g.send_far()
    back_normed(1)
    back_normed(2)
    sum_g.send_near()
    down(3)
    sum_g.send_next()
    sum_b.send_far()
    back_normed(0)
    sum_g.send_last()
    down(1)
    down(2)
    sum_b.send_near()
    down(0)
    sum_b.send_next()

    hid_rows = hid.reshape(4 * 384, FF_PAD)
    ggu_rows = ggu.reshape(4 * 384, 2 * FF_PAD)
    n_rows = nbuf.reshape(4 * 384, 1152)
    gb_rows = gb.reshape(4 * 384, 1152)

    def grad_gu(t, carry):
        columns = pl.ds(pl.multiple_of(t * 256, 256), 256)
        dgu_tile[:, columns] = lead_product(n_rows[...], ggu_rows[:, columns]).astype(jnp.bfloat16)
        return carry

    lax.fori_loop(0, PAIRS, grad_gu, 0)
    store_gu = pltpu.make_async_copy(dgu_tile, o_dgu, local_sems.at[4])
    store_gu.start()

    part_dd = lead_product(hid_rows[...], gb_rows[...])
    wd[...] = part_dd.astype(jnp.bfloat16)
    store_d = pltpu.make_async_copy(wd, o_dd, local_sems.at[5])
    store_d.start()
    sum_b.send_last()
    out_f32[0] = sum_g.finish()
    out_f32[1] = sum_b.finish()
    stores = [
        store_gu,
        store_d,
        pltpu.make_async_copy(out_f32.at[0], o_gn, local_sems.at[6]),
        pltpu.make_async_copy(out_f32.at[1], o_br, local_sems.at[7]),
    ]
    for store in stores[2:]:
        store.start()
    for store in stores:
        store.wait()
    wire.drain()


def feed_forward(own_n, gb_all, wgu_all, wd_all):
    bf, f32 = jnp.bfloat16, jnp.float32
    vm = pltpu.VMEM
    tokens, width = own_n.shape
    sums = [vm((3, tokens, width), bf), vm((8, tokens // 2, width), bf)]
    return pl.pallas_call(
        ff_kernel,
        out_shape=(
            jax.ShapeDtypeStruct((tokens, width), f32),
            jax.ShapeDtypeStruct((tokens, width), f32),
            jax.ShapeDtypeStruct(wgu_all.shape, bf),
            jax.ShapeDtypeStruct(wd_all.shape, bf),
        ),
        in_specs=[ANY] * 4,
        out_specs=(ANY,) * 4,
        scratch_shapes=[
            vm((4, 2, tokens, width), bf),
            vm((4, 2, tokens, width), bf),
            vm(wgu_all.shape, bf),
            vm(wd_all.shape, bf),
            vm((4, 2 * tokens, FF_PAD), f32),
            vm((4, 2 * tokens, FF_PAD), bf),
            vm((4, 2 * tokens, 2 * FF_PAD), bf),
            vm((4, 2, tokens, width), bf),
            vm((4, 2, tokens, width), bf),
            vm((2, tokens, width), f32),
            vm(wgu_all.shape, bf),
        ]
        + sums
        + sums
        + [
            pltpu.SemaphoreType.DMA((8,)),
            pltpu.SemaphoreType.DMA((40,)),
            pltpu.SemaphoreType.DMA((40,)),
        ],
        compiler_params=comm_params(2),
        name="feed_forward",
    )(own_n, gb_all, wgu_all, wd_all)


def reduce_kernel(
    dgu, dd, dqkv, dwo, dgain,
    o_gu, o_d, o_qkv, o_wo, o_gain,
    h_gu, r_gu, f_gu, h_d, r_d, h_qkv, r_qkv, h_wo, r_wo, h_gain, r_gain,
    y_gu, y_d, y_qkv, y_wo, y_gain, p_gu, p_d, p_qkv, p_wo, p_gain, z_gu, z_d, z_qkv, z_wo, z_gain,
    q_whole, q_half, w_whole, w_half, g_whole, g_half,
    local_sems, send_sems, recv_sems,
):
    place = Place()
    wire = Wire(send_sems, recv_sems)
    core, me, y = place.core, place.shard, place.y
    others = [(j, p) for p in (0, 1) for j in range(4) if (j, p) != (0, 0)]
    group = [place.device(dx=STEPS[j], mirror=p) for j, p in others]
    sibling = place.device(sibling=1)
    column = [place.device(dy=d) for d in (1, 3, 2)]
    low = place.device(swap_lo=1)

    def lanes(ref, which, size):
        start = pl.multiple_of(which * size, 128)
        return ref.at[..., pl.ds(start, size)]

    def gu_half(ref, which):
        return ref.at[:, :, pl.ds(pl.multiple_of(which * FF_PAD, 128), FF_PAD)]

    def d_half(ref, which):
        return ref.at[pl.ds(pl.multiple_of(which * 448, 16), 448)]

    def qkv_half(ref, which):
        return ref.at[:, :, pl.ds(pl.multiple_of(which * 768, 128), 768)]

    def wo_half(ref, which):
        return ref.at[:, pl.ds(pl.multiple_of(which * 64, 16), 64)]

    locals_ = []

    def local(src, dst):
        copy = pltpu.make_async_copy(src, dst, local_sems.at[len(locals_)])
        copy.start()
        locals_.append(copy)
        return copy

    mine = [
        local(gu_half(dgu, core), h_gu),
        local(d_half(dd, core), h_d),
        local(qkv_half(dqkv, core), h_qkv),
        local(wo_half(dwo, core), h_wo),
        local(dgain, h_gain),
    ]
    greet([sibling, low] + group + column)
    swaps = [
        wire.copy(gu_half(dgu, 1 - core), r_gu, sibling),
        wire.copy(qkv_half(dqkv, 1 - core), r_qkv, sibling),
        wire.copy(wo_half(dwo, 1 - core), r_wo, sibling),
        wire.copy(dgain, r_gain, sibling),
        wire.copy(d_half(dd, 1 - core), r_d, sibling),
    ]
    for swap in swaps:
        swap.start()
    for copy in mine:
        copy.wait()

    def summed(target, source, count):
        def one(i, carry):
            add_into(target.at[i], source.at[i])
            return carry

        lax.fori_loop(0, count, one, 0)

    swaps[0].wait_recv()
    summed(h_gu, r_gu, 8)
    swaps[0].wait_send()
    turn = [
        wire.copy(h_gu.at[place.shard_at(j, p)], f_gu.at[me], device)
        for (j, p), device in zip(others, group)
    ]
    for copy in turn:
        copy.start()
    f_gu[me] = h_gu[me]
    for swap in swaps[1:4]:
        swap.wait_recv()
    summed(h_qkv, r_qkv, 8)
    summed(h_wo, r_wo, 8)
    summed(h_gain, r_gain, 8)

    def cut_lanes(size):
        def cut(ref, part):
            return ref if part == 0 else ref.at[:, pl.ds((part - 1) * size, size)]

        return cut

    def cut_rows(size):
        def cut(ref, part):
            return ref if part == 0 else ref.at[pl.ds((part - 1) * size, size)]

        return cut

    at = place.shard_at
    sums = [
        SumTree(wire, place, lambda j, p: h_qkv.at[at(j, p)], cut_lanes(384), q_whole, q_half),
        SumTree(wire, place, lambda j, p: h_wo.at[at(j, p)], cut_rows(32), w_whole, w_half),
        SumTree(wire, place, lambda j, p: h_gain.at[at(j, p)], cut_lanes(128), g_whole, g_half),
    ]
    for tree in sums:
        tree.send_far()
    swaps[4].wait_recv()
    add_into(h_d, r_d)

    def quarter_gu(ref, which):
        return ref.at[pl.ds(which * 2, 2)]

    def quarter_d(ref, which):
        return ref.at[pl.ds(pl.multiple_of(which * 112, 16), 112)]

    steps = (1, 3, 2)
    over_d = [
        wire.copy(quarter_d(h_d, (y + d) % 4), y_d.at[y], device)
        for d, device in zip(steps, column)
    ]
    for copy in over_d:
        copy.start()
    for tree in sums:
        tree.send_near()
    for copy in turn:
        copy.wait_recv()
    over_gu = [
        wire.copy(quarter_gu(f_gu, (y + d) % 4), y_gu.at[y], device)
        for d, device in zip(steps, column)
    ]
    for copy in over_gu:
        copy.start()
    y_gu[y] = quarter_gu(f_gu, y)[...]
    y_d[y] = quarter_d(h_d, y)[...]
    for tree in sums:
        tree.send_next()
    for tree in sums:
        tree.send_last()
    for tree, target in zip(sums, (y_qkv, y_wo, y_gain)):
        target[y] = tree.finish().astype(jnp.bfloat16)
    over_small = [
        [wire.copy(target.at[y], target.at[y], device) for device in column]
        for target in (y_qkv, y_wo, y_gain)
    ]
    for copies in over_small:
        for copy in copies:
            copy.start()

    def add_up(source):
        return (
            source[0].astype(jnp.float32)
            + source[1].astype(jnp.float32)
            + source[2].astype(jnp.float32)
            + source[3].astype(jnp.float32)
        )

    def across(copies, source, piece, other):
        for copy in copies:
            copy.wait_recv()
        piece[...] = add_up(source).astype(jnp.bfloat16)
        made = wire.copy(piece, other, low)
        made.start()
        return made

    crossings = [
        across(over_d, y_d, p_d, z_d),
        across(over_gu, y_gu, p_gu, z_gu),
        across(over_small[0], y_qkv, p_qkv, z_qkv),
        across(over_small[1], y_wo, p_wo, z_wo),
        across(over_small[2], y_gain, p_gain, z_gain),
    ]

    def settle(crossing, piece, other):
        crossing.wait_recv()
        crossing.wait_send()
        add_into(piece, other)

    def out_gu(which, half):
        return o_gu.at[
            pl.ds(which * 2, 2), :, pl.ds(pl.multiple_of(half * FF_PAD, 128), FF_PAD)
        ]

    def out_d(which, half):
        return o_d.at[pl.ds(pl.multiple_of(half * 448 + which * 112, 16), 112)]

    ends = []
    settle(crossings[0], p_d, z_d)
    back_d = [wire.copy(p_d, out_d(y, core), device) for device in column]
    ends.append(wire.copy(p_d, out_d(y, core), sibling))
    for copy in back_d + ends[-1:]:
        copy.start()
    local(p_d, out_d(y, core))
    settle(crossings[1], p_gu, z_gu)
    back_gu = [wire.copy(p_gu, out_gu(y, core), device) for device in column]
    ends.append(wire.copy(p_gu, out_gu(y, core), sibling))
    for copy in back_gu + ends[-1:]:
        copy.start()
    local(p_gu, out_gu(y, core))
    out_qkv = o_qkv.at[:, pl.ds(pl.multiple_of(core * 768, 128), 768)]
    out_wo = o_wo.at[pl.ds(pl.multiple_of(core * 64, 16), 64)]
    for crossing, piece, other, out in (
        (crossings[2], p_qkv, z_qkv, out_qkv),
        (crossings[3], p_wo, z_wo, out_wo),
    ):
        settle(crossing, piece, other)
        ends.append(wire.copy(piece, out, sibling))
        ends[-1].start()
        local(piece, out)
    settle(crossings[4], p_gain, z_gain)
    local(p_gain, o_gain)
    for backs, out in ((back_d, out_d), (back_gu, out_gu)):
        for d, copy in zip((3, 1, 2), backs):
            copy.wait_recv()
            which = (y + d) % 4
            ends.append(wire.copy(out(which, core), out(which, core), sibling))
            ends[-1].start()
    for copy in ends:
        copy.wait_recv()
    for copy in locals_[5:]:
        copy.wait()
    waited = [id(made) for made in swaps[:1] + crossings]
    for made in wire.made:
        if id(made) not in waited:
            made.wait_send()


def reduce_all(dgu, dd, dqkv, dwo, dgain):
    bf = jnp.bfloat16
    vm = lambda *s: pltpu.VMEM(s, bf)
    shape = lambda *s: jax.ShapeDtypeStruct(s, bf)
    h_gu, h_qkv, h_wo, h_gain, h_d = (8, 144, 896), (8, 144, 768), (8, 64, 1152), (8, 16, 256), (448, 1152)
    q_gu, q_d = (2, 144, 896), (112, 1152)
    unit = [h_qkv[1:], h_wo[1:], h_gain[1:]]
    halves = [(144, 384), (32, 1152), (16, 128)]
    trees = []
    for whole, half in zip(unit, halves):
        trees += [vm(3, *whole), vm(8, *half)]
    return pl.pallas_call(
        reduce_kernel,
        out_shape=(shape(8, 144, 1792), shape(896, 1152), shape(144, 1536), shape(128, 1152), shape(16, 256)),
        in_specs=[ANY] * 5,
        out_specs=(ANY,) * 5,
        scratch_shapes=[
            vm(*h_gu), vm(*h_gu), vm(*h_gu), vm(*h_d), vm(*h_d), vm(*h_qkv), vm(*h_qkv),
            vm(*h_wo), vm(*h_wo), vm(*h_gain), vm(*h_gain),
        ]
        + [vm(4, *s) for s in (q_gu, q_d, *unit)]
        + [vm(*s) for s in (q_gu, q_d, *unit)]
        + [vm(*s) for s in (q_gu, q_d, *unit)]
        + trees
        + [
            pltpu.SemaphoreType.DMA((12,)),
            pltpu.SemaphoreType.DMA((96,)),
            pltpu.SemaphoreType.DMA((96,)),
        ],
        compiler_params=comm_params(5),
        name="reduce_grads",
    )(dgu, dd, dqkv, dwo, dgain)


def rotate(vectors, cosine, sine_part):
    half_size = vectors.shape[-1] // 2
    first_half = vectors[..., :half_size]
    second_half = vectors[..., half_size:]
    return jnp.concatenate(
        [
            first_half * cosine - second_half * sine_part,
            second_half * cosine + first_half * sine_part,
        ],
        axis=-1,
    )


def norm_back(grad_normed, scaled, inverse, gain_values):
    grad_scaled = grad_normed * gain_values
    return inverse * (grad_scaled - scaled * jnp.mean(grad_scaled * scaled, axis=1, keepdims=True))


def gain_rows(*rows):
    made = jnp.stack([jnp.pad(row, ((0, 0), (0, 256 - row.shape[1]))) for row in rows], axis=1)
    return jnp.pad(made, ((0, 0), (0, 16 - len(rows)), (0, 0))).astype(jnp.bfloat16)


def on_device(
    tokens, lengths, attn_gain, w_query, w_keyval, w_out, mlp_gain, w_gate, w_up, w_down, cotangent
):
    row_count, width = tokens.shape
    head_size = w_keyval.shape[1] // 2
    heads_all = w_query.shape[1]
    head_count = heads_all // head_size
    scaling = head_size ** (-0.5)
    shard = lax.axis_index("shard")
    within = jnp.arange(row_count, dtype=jnp.int32)
    live_count = lengths[0, 0]
    keep_mask = (within < live_count).astype(jnp.float32)[:, None]
    grad_out = cotangent.astype(jnp.float32)

    counts = jnp.full((1, 144), live_count, jnp.int32).astype(jnp.bfloat16)
    misc = gain_rows(attn_gain[None], mlp_gain[None], counts)[0]
    half_size = head_size // 2
    frequency = 10000.0 ** (-2.0 * jnp.arange(half_size, dtype=jnp.float32) / head_size)
    (
        miscs, qkv_all, out_all, gu_all, branch_all,
        normed1, queries, all_kv, probs, attended, middle, normed2,
    ) = front(
        tokens, cotangent, misc, jnp.tile(frequency[None], (8, 1)),
        w_query, w_keyval, w_out, w_gate, w_up,
    )
    gain1 = miscs[:, 0, :144].reshape(width).astype(jnp.float32)
    gain2 = miscs[:, 1, :144].reshape(width).astype(jnp.float32)
    live_all = miscs[:, 2, 0].astype(jnp.int32)
    qkv_full = qkv_all.reshape(width, -1)
    out_full = out_all.reshape(heads_all, width)
    down_mine = jnp.pad(w_down, ((0, FF_PAD - FF_DEV), (0, 0)))
    starts = jnp.cumsum(live_all) - live_all
    query_pos = starts[shard] + within
    angles = query_pos.astype(jnp.float32)[:, None] * frequency[None, :]
    cosine = jnp.cos(angles)
    sine_part = jnp.sin(angles)
    heads_cos = cosine[:, None, :]
    heads_sin = sine_part[:, None, :]
    inputs = tokens.astype(jnp.float32)
    inverse1 = lax.rsqrt(jnp.mean(inputs * inputs, axis=1, keepdims=True) + EPSILON)
    scaled1 = inputs * inverse1
    inverse2 = lax.rsqrt(jnp.mean(middle * middle, axis=1, keepdims=True) + EPSILON)
    scaled2 = middle * inverse2
    flat_kv = all_kv.reshape(-1, 2 * head_size)
    keys, values = flat_kv[:, :head_size], flat_kv[:, head_size:]
    probs_low = probs.astype(jnp.bfloat16)

    grad_normed2, branch, grad_gu, grad_d = feed_forward(
        normed2, branch_all, gu_all.reshape(width, -1), down_mine
    )
    outputs = (middle + keep_mask * branch).astype(jnp.bfloat16)
    grad_gain2 = jnp.sum(grad_normed2 * scaled2, axis=0)
    grad_middle = grad_out + norm_back(grad_normed2, scaled2, inverse2, gain2)

    grad_attn = (keep_mask * grad_middle).astype(jnp.bfloat16)
    grad_out_w = lead_product(attended, grad_attn)
    grad_attended = (
        trail_product(grad_attn, out_full)
        .astype(jnp.bfloat16)
        .reshape(row_count, head_count, head_size)
    )
    grad_probs = jnp.einsum(
        "thd,gd->htg", grad_attended, values, preferred_element_type=jnp.float32
    )
    grad_values_all = jnp.einsum(
        "htg,thd->gd", probs_low, grad_attended, preferred_element_type=jnp.float32
    )
    row_delta = jnp.sum(probs * grad_probs, axis=-1, keepdims=True)
    grad_scores = (probs * (grad_probs - row_delta)).astype(jnp.bfloat16)
    grad_queries = jnp.einsum("htg,gd->thd", grad_scores, keys, preferred_element_type=jnp.float32)
    grad_keys_all = jnp.einsum(
        "htg,htd->gd", grad_scores, queries, preferred_element_type=jnp.float32
    )
    grad_kv_all = jnp.concatenate([grad_keys_all, grad_values_all], axis=1)
    grad_kv_all = grad_kv_all.reshape(BEHIND + 1, row_count, 2 * head_size)
    ahead = window(grad_kv_all.astype(jnp.bfloat16), True, 4, "grad_keys_values")
    is_ahead = (shard + 1 + jnp.arange(BEHIND) < 8)[:, None, None]
    grad_own_kv = grad_kv_all[0] + jnp.sum(
        jnp.where(is_ahead, ahead, 0).astype(jnp.float32), axis=0
    )
    grad_query_proj = (
        (rotate(grad_queries, heads_cos, -heads_sin) * scaling)
        .reshape(row_count, heads_all)
        .astype(jnp.bfloat16)
    )
    grad_keyval_proj = jnp.concatenate(
        [
            rotate(grad_own_kv[:, :head_size], cosine, -sine_part),
            grad_own_kv[:, head_size:],
        ],
        axis=1,
    ).astype(jnp.bfloat16)
    grad_proj = jnp.concatenate([grad_query_proj, grad_keyval_proj], axis=1)
    grad_qkv_w = lead_product(normed1, grad_proj)
    grad_normed1 = trail_product(grad_proj, qkv_full)
    grad_gain1 = jnp.sum(grad_normed1 * scaled1, axis=0)
    grad_inputs = grad_middle + norm_back(grad_normed1, scaled1, inverse1, gain1)

    sum_gu, sum_d, sum_qkv, sum_wo, sum_gain = reduce_all(
        grad_gu.reshape(8, 144, -1),
        grad_d,
        grad_qkv_w.astype(jnp.bfloat16).reshape(8, 144, -1),
        grad_out_w.astype(jnp.bfloat16).reshape(8, 128, width),
        gain_rows(grad_gain1.reshape(8, 144), grad_gain2.reshape(8, 144)),
    )
    grad_gate_w, grad_up_w = unpack_gate_up(sum_gu)
    sum_qkv = sum_qkv.astype(jnp.float32)
    return (
        outputs,
        grad_inputs,
        sum_gain[0, :144].astype(jnp.float32),
        sum_qkv[:, :heads_all],
        sum_qkv[:, heads_all:],
        sum_wo.astype(jnp.float32),
        sum_gain[1, :144].astype(jnp.float32),
        grad_gate_w,
        grad_up_w,
        sum_d[:FF_DEV].astype(jnp.float32),
    )


def solution(mesh):
    placed = (
        P(("rep", "shard"), None),
        P("rep", "shard"),
        P("shard"),
        P("shard", None),
        P("shard", None),
        P("shard", None),
        P("shard"),
        P("shard", None),
        P("shard", None),
        P("shard", None),
        P(("rep", "shard"), None),
    )
    return jax.shard_map(
        on_device,
        mesh=mesh,
        in_specs=placed,
        out_specs=(
            P(("rep", "shard"), None),
            P(("rep", "shard"), None),
            P("shard"),
            P("shard", None),
            P("shard", None),
            P("shard", None),
            P("shard"),
            P("shard", None),
            P("shard", None),
            P("shard", None),
        ),
        check_vma=False,
    )
```

```python
import functools

import jax
import jax.numpy as jnp
from jax import lax
from jax.experimental import pallas as pl
from jax.experimental.pallas import tpu as pltpu
from jax.sharding import PartitionSpec as P

MESH = pl.DeviceIdType.MESH
WINDOW = 512
EPSILON = 1e-06
MASKED = -1e30
VMEM_LIMIT = 60 * 2**20
FF_DEV = 864
FF_PAD = 896
PAIRS = FF_PAD // 128
BEHIND = 4


def matmul(former, latter):
    return jnp.dot(former, latter, preferred_element_type=jnp.float32)


def lead_product(former, latter):
    return lax.dot_general(
        former, latter, (((0,), (0,)), ((), ())), preferred_element_type=jnp.float32
    )


def trail_product(former, latter):
    return lax.dot_general(
        former, latter, (((1,), (1,)), ((), ())), preferred_element_type=jnp.float32
    )


class Place:
    def __init__(self):
        rep, shard = lax.axis_index("rep"), lax.axis_index("shard")
        self.rep, self.shard = rep, shard
        self.y, self.z_lo, self.core = rep // 4, (rep // 2) % 2, rep % 2
        self.z_hi, self.x = shard // 4, shard % 4

    def device(self, dx=0, dy=0, mirror=0, swap_lo=0, sibling=0):
        z_lo = (self.z_lo + mirror + swap_lo) % 2
        rep = (((self.y + dy) % 4) * 2 + z_lo) * 2 + (self.core + sibling) % 2
        return (rep, ((self.z_hi + mirror) % 2) * 4 + (self.x + dx) % 4)

    def over_group(self, dx, mirror):
        return self.device(dx=dx, mirror=mirror)

    def shard_at(self, j, p):
        return ((self.z_hi + p) % 2) * 4 + (self.x + STEPS[j]) % 4


STEPS = (0, 1, 3, 2)


class Wire:
    def __init__(self, send_sems, recv_sems):
        self.send_sems, self.recv_sems, self.made = send_sems, recv_sems, []

    def copy(self, src, dst, device):
        k = len(self.made)
        made = pltpu.make_async_remote_copy(
            src_ref=src,
            dst_ref=dst,
            send_sem=self.send_sems.at[k],
            recv_sem=self.recv_sems.at[k],
            device_id=device,
            device_id_type=MESH,
        )
        self.made.append(made)
        return made

    def drain(self):
        for made in self.made:
            made.wait_send()


def greet(devices):
    barrier = pltpu.get_barrier_semaphore()
    for device in devices:
        pl.semaphore_signal(barrier, inc=1, device_id=device, device_id_type=MESH)
    pl.semaphore_wait(barrier, len(devices))


HOPS = (
    ((0, 0), (0, 1), 0, 0, 1),
    ((0, 0), (2, 0), 0, 1, 0),
    ((0, 0), (1, 0), 0, 3, 0),
    ((0, 1), (2, 1), 1, 1, 0),
    ((0, 1), (1, 1), 1, 3, 0),
    ((2, 0), (3, 0), 1, 1, 0),
    ((1, 0), (3, 0), 2, 3, 0),
    ((2, 0), (2, 1), 2, 0, 1),
    ((1, 0), (1, 1), 2, 0, 1),
    ((2, 1), (3, 1), 1, 1, 0),
    ((1, 1), (3, 1), 2, 3, 0),
)
ONWARD = {0: (3, 4), 1: (5, 7), 2: (6, 8), 3: (9,), 8: (10,)}
WHOLE = {0: (0, 1), 1: (2, 0), 2: (1, 0), 6: (3, 0), 7: (2, 1), 8: (1, 1), 10: (3, 1)}
ORDER = (0, 1, 2, 3, 4, 8, 7, 5, 6, 9, 10)
RING = (
    ((0, 0), (2, 0), 0, 1, 0),
    ((0, 0), (1, 0), 0, 3, 0),
    ((2, 0), (3, 0), 1, 1, 0),
    ((1, 0), (3, 0), 2, 3, 0),
)
RING_ONWARD = {0: (2,), 1: (3,)}


def gather_tree(wire, device_of, hops, own, slot, cut, absolute):
    copies = []
    for source, target, part, dx, mirror in hops:
        src = own if source == (0, 0) else slot(*source)
        dst = slot(*(source if absolute else target))
        copies.append(wire.copy(cut(src, part), cut(dst, part), device_of(dx, mirror)))
    return copies


def arrive(tree, k, after=ONWARD):
    tree[k].wait_recv()
    for n in after.get(k, ()):
        tree[n].start()


def add_into(target, source):
    target[...] = (target[...].astype(jnp.float32) + source[...].astype(jnp.float32)).astype(
        target.dtype
    )


class SumTree:
    def __init__(self, wire, device_of, hops, slot, cut, landings):
        self.hops, self.slot, self.cut, self.landings = hops, slot, cut, landings
        self.copies = [
            wire.copy(cut(slot(*target), part), landing, device_of((4 - dx) % 4, mirror))
            for (_, target, part, dx, mirror), landing in zip(hops, landings)
        ]

    def start(self, *hops):
        for k in hops:
            self.copies[k].start()

    def absorb(self, *hops):
        for k in hops:
            source, _, part, _, _ = self.hops[k]
            self.copies[k].wait_recv()
            add_into(self.cut(self.slot(*source), part), self.landings[k])

    def send_near(self):
        self.start(4, 7)
        self.absorb(10)
        self.start(8)
        self.absorb(9)
        self.start(3)
        self.absorb(6, 5)

    def send_next(self):
        self.absorb(8)
        self.start(2)
        self.absorb(7)
        self.start(1)

    def send_last(self):
        self.absorb(3, 4)
        self.start(0)

    def finish(self):
        total = self.slot(0, 0)[...].astype(jnp.float32)
        for k in (2, 1, 0):
            self.copies[k].wait_recv()
            total = total + self.landings[k][...].astype(jnp.float32)
        return total


def front_kernel(
    tokens, cot, misc, freq, w_query, w_keyval, w_out, w_gate, w_up,
    o_misc, o_qkv, o_wo, o_gu, o_gb, o_normed1, o_q, o_kv, o_probs, o_att, o_middle, o_normed2, o_rope,
    x_ref, cot_ref, miscs, freq_ref, wqkv, wo, gate, up, packed, gb_own, normed1, q_ref, kv_ref,
    bias, probs, att, middle, normed2, rope,
    local_sems, send_sems, recv_sems,
):
    place = Place()
    wire = Wire(send_sems, recv_sems)
    core, me, y = place.core, place.shard, place.y
    rows, width = tokens.shape
    at = place.shard_at
    others = [(j, p) for p in (0, 1) for j in range(4) if (j, p) != (0, 0)]
    group = [place.device(dx=STEPS[j], mirror=p) for j, p in others]
    sequence = [(place.rep, at(j, p)) for j, p in others]
    sibling = place.device(sibling=1)
    steps = (1, 3, 2)
    column = [place.device(dy=d) for d in steps]
    locals_ = []

    def local(src, dst):
        copy = pltpu.make_async_copy(src, dst, local_sems.at[len(locals_)])
        copy.start()
        locals_.append(copy)
        return copy

    load_x = local(tokens, x_ref)
    load_cot = local(cot, cot_ref)
    load_misc = local(misc, miscs.at[me])
    load_freq = local(freq, freq_ref)
    load_gate = local(w_gate, gate)
    load_up = local(w_up, up)
    load_own = [
        local(w_query, wqkv.at[me, :, pl.ds(0, 1024)]),
        local(w_keyval, wqkv.at[me, :, pl.ds(1024, 512)]),
        local(w_out, wo.at[me]),
    ]
    greet([sibling] + group + [d for d, (j, p) in zip(sequence, others) if p == 1] + column)

    def lanes_from(base, size):
        def cut(ref, part):
            start, count = ((0, size), (0, size // 2), (size // 2, size // 2))[part]
            start = pl.multiple_of(core * size + (base + start), 128)
            return ref.at[:, pl.ds(start, count)]

        return cut

    def cut_wo(ref, part):
        start, size = ((0, 64), (0, 32), (32, 32))[part]
        return ref.at[pl.ds(pl.multiple_of(core * 64 + start, 32), size)]

    def cut_gb(ref, part):
        return ref if part == 0 else ref.at[pl.ds((part - 1) * 96, 96)]

    def cut_gu(ref):
        return ref.at[:, pl.ds(pl.multiple_of(core * FF_PAD, 128), FF_PAD)]

    cut_q, cut_kv = lanes_from(0, 512), lanes_from(1024, 256)
    slot_qkv = lambda j, p: wqkv.at[at(j, p)]
    slot_wo = lambda j, p: wo.at[at(j, p)]
    slot_gb = lambda j, p: o_gb.at[j, p]
    misc_copies = [wire.copy(misc, miscs.at[me], device) for device in sequence]
    for copy in misc_copies:
        copy.start()
    for load in load_own:
        load.wait()
    own = wqkv.at[me]
    trees = [
        gather_tree(wire, place.over_group, HOPS, own, slot_qkv, cut_q, True),
        gather_tree(wire, place.over_group, HOPS, own, slot_qkv, cut_kv, True),
        gather_tree(wire, place.over_group, HOPS, wo.at[me], slot_wo, cut_wo, True),
    ]
    cuts = [cut_q, cut_kv, cut_wo]
    slots = [slot_qkv, slot_qkv, slot_wo]
    passes = [
        {k: wire.copy(cut(slot(*jp), 0), cut(slot(*jp), 0), sibling) for k, jp in WHOLE.items()}
        for cut, slot in zip(cuts, slots)
    ]
    for tree in trees:
        for k in (0, 1, 2):
            tree[k].start()

    load_x.wait()
    inputs = x_ref[...].astype(jnp.float32)
    inverse1 = lax.rsqrt(jnp.mean(inputs * inputs, axis=1, keepdims=True) + EPSILON)
    middle[...] = inputs * inverse1
    load_gate.wait()
    load_up.wait()
    for d in range(8):
        for t in range(PAIRS):
            start = FF_DEV * d + 128 * t
            size = min(128, FF_DEV - 128 * t)
            for k, weight in enumerate((gate, up)):
                block = weight[:, start : start + size]
                if size < 128:
                    block = jnp.concatenate(
                        [block, jnp.zeros((block.shape[0], 128 - size), block.dtype)], axis=1
                    )
                packed[d, :, 256 * t + 128 * k : 256 * t + 128 * (k + 1)] = block

    def attn(*hops):
        for k in hops:
            for tree, onward in zip(trees, passes):
                arrive(tree, k)
                if k in onward:
                    onward[k].start()

    attn(0, 1, 2)
    load_cot.wait()
    load_misc.wait()
    load_freq.wait()
    live_col = (
        lax.broadcasted_iota(jnp.int32, (rows, 1), 0).astype(jnp.float32)
        < miscs[me].astype(jnp.float32)[2:3, :1]
    )
    gb_own[...] = jnp.where(live_col, cot_ref[...].astype(jnp.float32), 0.0).astype(jnp.bfloat16)
    attn(3, 4, 8, 7)
    gb_tree = gather_tree(wire, place.over_group, HOPS, gb_own, slot_gb, cut_gb, False)
    for k in (0, 1, 2):
        gb_tree[k].start()
    local(gb_own, o_gb.at[0, 0])

    z_of = lambda p: (place.z_hi + p) % 2
    shard_from = lambda d, p: z_of(p) * 4 + (place.x + y + d) % 4
    turn = []
    for p in (0, 1):
        target = z_of(p) * 4 + (place.x - y + 4) % 4
        turn.append(
            wire.copy(
                cut_gu(packed.at[target]), cut_gu(o_gu.at[me]), place.device(dx=4 - y, mirror=p)
            )
        )
    away, home = y > 0, y == 0
    keep_own = pltpu.make_async_copy(
        cut_gu(packed.at[me]), cut_gu(o_gu.at[me]), local_sems.at[len(locals_)]
    )
    locals_.append(None)
    turn[1].start()
    pl.when(away)(turn[0].start)
    pl.when(home)(keep_own.start)
    attn(5, 6, 9, 10)

    for copy in misc_copies:
        copy.wait_recv()
    as_float = [miscs[s].astype(jnp.float32) for s in range(8)]
    gain1 = jnp.concatenate([m[0:1, :144] for m in as_float], axis=1)
    gain2 = jnp.concatenate([m[1:2, :144] for m in as_float], axis=1)
    normed = (middle[...] * gain1).astype(jnp.bfloat16)
    normed1[...] = normed
    for k in WHOLE:
        passes[0][k].wait_recv()
        passes[1][k].wait_recv()
    live = [m[2:3, :1] for m in as_float]
    start_of = []
    for i in range(BEHIND + 1):
        total = jnp.zeros((1, 1), jnp.float32)
        for s in range(8):
            total = total + jnp.where(s < me - i, 1.0, 0.0) * live[s]
        start_of.append(total)
    row = lax.broadcasted_iota(jnp.int32, (rows, 1), 0).astype(jnp.float32)
    query_pos = start_of[0] + row
    angles = query_pos * freq_ref[0:1, :]
    cosine, sine_part = jnp.cos(angles), jnp.sin(angles)
    rope[:, :128] = cosine
    rope[:, 128:] = sine_part
    weights = wqkv.reshape(width, 1536)

    def turned(vectors):
        first, second = vectors[:, :128], vectors[:, 128:]
        return jnp.concatenate(
            [first * cosine - second * sine_part, second * cosine + first * sine_part], axis=1
        )

    projected = matmul(normed, weights[:, 1024:1536])
    kv_ref[0, :, :256] = turned(projected[:, :256]).astype(jnp.bfloat16)
    kv_ref[0, :, 256:] = projected[:, 256:].astype(jnp.bfloat16)
    sends = [
        wire.copy(kv_ref.at[0], kv_ref.at[i], (place.rep, jnp.minimum(me + i, 7)))
        for i in range(1, BEHIND + 1)
    ]
    for i, copy in enumerate(sends):
        pl.when(me + (i + 1) < 8)(copy.start)

        @pl.when(me < i + 1)
        def _():
            kv_ref[i + 1] = jnp.zeros(kv_ref.shape[1:], kv_ref.dtype)

    scaling = 256 ** (-0.5)
    for h in range(4):
        heads = matmul(normed, weights[:, 256 * h : 256 * (h + 1)])
        q_ref[h] = (turned(heads) * scaling).astype(jnp.bfloat16)

    index = lax.broadcasted_iota(jnp.int32, (1, (BEHIND + 1) * rows), 1)
    key_pos = jnp.zeros(index.shape, jnp.float32)
    key_live = jnp.zeros(index.shape, jnp.float32)
    for i in range(BEHIND + 1):
        inside = jnp.logical_and(index >= i * rows, index < (i + 1) * rows)
        within = (index - i * rows).astype(jnp.float32)
        live_i = jnp.zeros((1, 1), jnp.float32)
        for s in range(8):
            live_i = live_i + jnp.where(me - i == s, 1.0, 0.0) * live[s]
        key_pos = jnp.where(inside, start_of[i] + within, key_pos)
        key_live = jnp.where(inside, jnp.where(within < live_i, 1.0, 0.0), key_live)
    ahead = query_pos - key_pos
    allowed = jnp.logical_and(
        jnp.logical_and(ahead >= 0.0, ahead < float(WINDOW)), key_live > 0.5
    )
    bias[...] = jnp.where(allowed, 0.0, MASKED)

    for k in ORDER[:5]:
        arrive(gb_tree, k)
    pl.when(away)(turn[0].wait_recv)
    turn[1].wait_recv()
    pl.when(home)(keep_own.wait)
    over = []
    for d, device in zip(steps, column):
        for p in (0, 1):
            held = cut_gu(o_gu.at[shard_from(0, p)])
            over.append(wire.copy(held, held, device))
            over[-1].start()
    gu_passes = []

    def pass_gu(d, p):
        held = cut_gu(o_gu.at[shard_from(d, p)])
        gu_passes.append(wire.copy(held, held, sibling))
        gu_passes[-1].start()

    for p in (0, 1):
        pass_gu(0, p)
    for i, copy in enumerate(sends):
        pl.when(me >= i + 1)(copy.wait_recv)

    all_kv = kv_ref.reshape((BEHIND + 1) * rows, 512)
    for h in range(4):
        scores = trail_product(q_ref[h], all_kv[:, :256]) + bias[...]
        raised = jnp.exp(scores - jnp.max(scores, axis=1, keepdims=True))
        share = raised * (1.0 / jnp.sum(raised, axis=1, keepdims=True))
        probs[h] = share
        att[:, 256 * h : 256 * (h + 1)] = matmul(
            share.astype(jnp.bfloat16), all_kv[:, 256:]
        ).astype(jnp.bfloat16)
        if h == 1:
            for k in ORDER[5:]:
                arrive(gb_tree, k)
    for k in WHOLE:
        passes[2][k].wait_recv()
    keep = jnp.where(live_col, 1.0, 0.0)
    mid = x_ref[...].astype(jnp.float32) + keep * matmul(att[...], wo.reshape(1024, width)[...])
    middle[...] = mid
    inverse2 = lax.rsqrt(jnp.mean(mid * mid, axis=1, keepdims=True) + EPSILON)
    normed2[...] = (mid * inverse2 * gain2).astype(jnp.bfloat16)
    for src, dst in (
        (miscs, o_misc),
        (wqkv, o_qkv),
        (wo, o_wo),
        (normed1, o_normed1),
        (q_ref, o_q),
        (kv_ref, o_kv),
        (probs, o_probs),
        (att, o_att),
        (middle, o_middle),
        (normed2, o_normed2),
        (rope, o_rope),
    ):
        local(src, dst)
    for i, (d, p) in enumerate([(d, p) for d in (3, 1, 2) for p in (0, 1)]):
        over[i].wait_recv()
        pass_gu(d, p)
    for copy in gu_passes:
        copy.wait_recv()
    waited = [id(copy) for copy in sends] + [id(turn[0])]
    for copy in locals_[9:]:
        if copy is not None:
            copy.wait()
    pl.when(away)(turn[0].wait_send)
    for i, copy in enumerate(sends):
        pl.when(me + (i + 1) < 8)(copy.wait_send)
    for copy in wire.made:
        if id(copy) not in waited:
            copy.wait_send()


ANY = pl.BlockSpec(memory_space=pl.ANY)


def comm_params(collective_id):
    return pltpu.CompilerParams(
        collective_id=collective_id, has_side_effects=True, vmem_limit_bytes=VMEM_LIMIT
    )


def front(tokens, cot, misc, freq, w_query, w_keyval, w_out, w_gate, w_up):
    bf, f32 = jnp.bfloat16, jnp.float32
    rows, width = tokens.shape
    keys = (BEHIND + 1) * rows
    outs = [
        ((8, 16, 256), bf),
        ((8, 144, 1536), bf),
        ((8, 128, width), bf),
        ((8, 144, 2 * FF_PAD), bf),
        ((4, 2, rows, width), bf),
        ((rows, width), bf),
        ((4, rows, 256), bf),
        ((BEHIND + 1, rows, 512), bf),
        ((4, rows, keys), f32),
        ((rows, 1024), bf),
        ((rows, width), f32),
        ((rows, width), bf),
        ((rows, 256), f32),
    ]
    scratch = [
        ((rows, width), bf),
        ((rows, width), bf),
        ((8, 16, 256), bf),
        ((8, 128), f32),
        ((8, 144, 1536), bf),
        ((8, 128, width), bf),
        (w_gate.shape, bf),
        (w_up.shape, bf),
        ((8, 144, 2 * FF_PAD), bf),
        ((rows, width), bf),
        ((rows, width), bf),
        ((4, rows, 256), bf),
        ((BEHIND + 1, rows, 512), bf),
        ((rows, keys), f32),
        ((4, rows, keys), f32),
        ((rows, 1024), bf),
        ((rows, width), f32),
        ((rows, width), bf),
        ((rows, 256), f32),
    ]
    return pl.pallas_call(
        front_kernel,
        out_shape=tuple(jax.ShapeDtypeStruct(*o) for o in outs),
        in_specs=[ANY] * 9,
        out_specs=(ANY,) * len(outs),
        scratch_shapes=[pltpu.VMEM(*v) for v in scratch]
        + [
            pltpu.SemaphoreType.DMA((32,)),
            pltpu.SemaphoreType.DMA((112,)),
            pltpu.SemaphoreType.DMA((112,)),
        ],
        compiler_params=comm_params(1),
        name="attention_forward",
    )(tokens, cot, misc, freq, w_query, w_keyval, w_out, w_gate, w_up)


def unpack_kernel(both, gate, up):
    for d in range(8):
        for t in range(PAIRS):
            size = min(128, FF_DEV - 128 * t)
            start = FF_DEV * d + 128 * t
            for k, out in enumerate((gate, up)):
                half, rest = divmod(256 * t + 128 * k, FF_PAD)
                block = both[half, rest // 256, d, :, rest % 256 : rest % 256 + size]
                out[:, start : start + size] = block.astype(jnp.float32)


def unpack_gate_up(both):
    rows = both.shape[3]
    out = jax.ShapeDtypeStruct((rows, 8 * FF_DEV), jnp.float32)
    spec = pl.BlockSpec((16, 8 * FF_DEV), lambda i: (i, 0))
    return pl.pallas_call(
        unpack_kernel,
        grid=(rows // 16,),
        out_shape=(out, out),
        in_specs=[pl.BlockSpec((2, 4, 8, 16, 256), lambda i: (0, 0, 0, i, 0))],
        out_specs=(spec, spec),
        compiler_params=pltpu.CompilerParams(vmem_limit_bytes=VMEM_LIMIT),
        name="unpack_gate_up",
    )(both)


ROOT = 0.7978845608028654
CUBE = 0.044715


def ff_kernel(
    own_n, gb_all, wgu_all, wd_all,
    o_gn, o_pb, o_dgu, o_pd,
    nbuf, gb, wgu, wd, gh, hid, ggu, part_g, part_b, out_f32, dgu_tile,
    g_whole, g_half, dd, r_d, d_whole, d_half_a, d_half_b, z_d,
    local_sems, send_sems, recv_sems,
):
    place = Place()
    wire = Wire(send_sems, recv_sems)
    loads = [
        pltpu.make_async_copy(src, dst, local_sems.at[k])
        for k, (src, dst) in enumerate(
            [(own_n, nbuf.at[0, 0]), (wd_all, wd), (gb_all, gb), (wgu_all, wgu)]
        )
    ]
    for load in loads:
        load.start()
    core, y = place.core, place.y
    sibling, low = place.device(sibling=1), place.device(swap_lo=1)
    greet(
        [place.device(dx=1), place.device(dx=3), place.device(mirror=1), sibling, low]
        + [place.device(dy=1), place.device(dy=3)]
    )

    def cut(ref, part):
        return ref if part == 0 else ref.at[pl.ds((part - 1) * 96, 96)]

    slot_n = lambda j, p: nbuf.at[j, p]
    tree = gather_tree(wire, place.over_group, HOPS, nbuf.at[0, 0], slot_n, cut, False)
    sum_g = SumTree(
        wire, place.over_group, HOPS, lambda j, p: part_g.at[j, p], cut,
        [g_whole.at[k] for k in range(3)] + [g_half.at[k] for k in range(8)],
    )

    def cut_d(ref, part):
        start, size = ((0, 1152), (0, 640), (640, 512))[part]
        return ref.at[:, pl.ds(start, size)]

    quarter_d = dd.at[core, y]
    swap_d = wire.copy(dd.at[1 - core], r_d, sibling)
    sum_d = SumTree(
        wire, lambda dx, mirror: place.device(dy=dx), RING,
        lambda j, p: dd.at[core, (y + STEPS[j]) % 4], cut_d,
        [d_whole.at[0], d_whole.at[1], d_half_a, d_half_b],
    )
    cross_d = wire.copy(quarter_d, z_d, low)
    loads[0].wait()
    for k in (0, 1, 2):
        tree[k].start()
    loads[1].wait()
    loads[2].wait()

    def back_hidden(j):
        rows = jnp.concatenate([gb[j, 0], gb[j, 1]], axis=0)
        gh[j] = trail_product(rows, wd[...])

    def forward(j):
        rows = jnp.concatenate([nbuf[j, 0], nbuf[j, 1]], axis=0)

        def tile(t, carry):
            columns = pl.ds(pl.multiple_of(t * 256, 256), 256)
            narrow = pl.ds(pl.multiple_of(t * 128, 128), 128)
            both = matmul(rows, wgu[:, columns])
            gate, up = both[:, :128], both[:, 128:]
            square = gate * gate
            curve = jnp.tanh(ROOT * gate * (1.0 + CUBE * square))
            half_up = 0.5 * (1.0 + curve)
            active = gate * half_up
            slope = half_up + 0.5 * gate * (1.0 - curve * curve) * (
                ROOT * (1.0 + 3.0 * CUBE * square)
            )
            back = gh[j, :, narrow]
            hid[j, :, narrow] = (active * up).astype(jnp.bfloat16)
            ggu[j, :, columns] = jnp.concatenate(
                [(back * up * slope).astype(jnp.bfloat16), (back * active).astype(jnp.bfloat16)],
                axis=1,
            )
            return carry

        lax.fori_loop(0, PAIRS, tile, 0)

    def back_normed(j):
        for start, size in ((0, 512), (512, 512), (1024, 128)):
            block = trail_product(ggu[j], wgu[start : start + size, :]).astype(jnp.bfloat16)
            part_g[j, 0, :, start : start + size] = block[:192]
            part_g[j, 1, :, start : start + size] = block[192:]

    def down(j):
        for start, size in ((0, 512), (512, 512), (1024, 128)):
            block = matmul(hid[j], wd[:, start : start + size]).astype(jnp.bfloat16)
            part_b[j, 0, :, start : start + size] = block[:192]
            part_b[j, 1, :, start : start + size] = block[192:]

    for j in range(4):
        back_hidden(j)
    for k in (0, 1, 2):
        arrive(tree, k)
    loads[3].wait()
    forward(0)
    for k in (3, 4, 8, 7):
        arrive(tree, k)
    forward(1)
    forward(2)
    for k in (5, 6, 9, 10):
        arrive(tree, k)
    forward(3)
    back_normed(3)
    sum_g.start(10, 9, 6, 5)
    back_normed(1)
    back_normed(2)

    hid_rows = hid.reshape(4 * 384, FF_PAD)
    ggu_rows = ggu.reshape(4 * 384, 2 * FF_PAD)
    n_rows = nbuf.reshape(4 * 384, 1152)
    gb_rows = gb.reshape(4 * 384, 1152)
    dd_rows = dd.reshape(FF_PAD, 1152)
    for start, size in ((0, 512), (512, 512), (1024, 128)):
        dd_rows[:, start : start + size] = lead_product(
            hid_rows[...], gb_rows[:, start : start + size]
        ).astype(jnp.bfloat16)
    swap_d.start()
    sum_g.send_near()
    back_normed(0)
    down(0)
    swap_d.wait_recv()

    def add_d(i, carry):
        add_into(dd.at[core, i], r_d.at[i])
        return carry

    lax.fori_loop(0, 4, add_d, 0)
    sum_d.start(2, 3)
    down(1)
    sum_g.send_next()
    down(2)
    down(3)
    store_b = pltpu.make_async_copy(part_b, o_pb, local_sems.at[5])
    store_b.start()

    def grad_gu(t, carry):
        columns = pl.ds(pl.multiple_of(t * 256, 256), 256)
        dgu_tile[:, columns] = lead_product(n_rows[...], ggu_rows[:, columns]).astype(jnp.bfloat16)
        return carry

    lax.fori_loop(0, 3, grad_gu, 0)
    sum_d.absorb(2, 3)
    sum_d.start(0, 1)
    sum_g.send_last()
    lax.fori_loop(3, PAIRS, grad_gu, 0)
    store_gu = pltpu.make_async_copy(dgu_tile, o_dgu, local_sems.at[4])
    store_gu.start()
    sum_d.absorb(0, 1)
    cross_d.start()
    out_f32[...] = sum_g.finish()
    store_g = pltpu.make_async_copy(out_f32, o_gn, local_sems.at[6])
    store_g.start()
    cross_d.wait_recv()
    cross_d.wait_send()
    add_into(quarter_d, z_d)
    store_d = pltpu.make_async_copy(quarter_d, o_pd, local_sems.at[7])
    store_d.start()
    for store in (store_b, store_gu, store_g, store_d):
        store.wait()
    for copy in wire.made:
        if copy is not cross_d:
            copy.wait_send()


def feed_forward(own_n, gb_all, wgu_all, wd_all):
    bf, f32 = jnp.bfloat16, jnp.float32
    vm = pltpu.VMEM
    tokens, width = own_n.shape
    sums = [vm((3, tokens, width), bf), vm((8, tokens // 2, width), bf)]
    return pl.pallas_call(
        ff_kernel,
        out_shape=(
            jax.ShapeDtypeStruct((tokens, width), f32),
            jax.ShapeDtypeStruct((4, 2, tokens, width), bf),
            jax.ShapeDtypeStruct(wgu_all.shape, bf),
            jax.ShapeDtypeStruct((112, width), bf),
        ),
        in_specs=[ANY] * 4,
        out_specs=(ANY,) * 4,
        scratch_shapes=[
            vm((4, 2, tokens, width), bf),
            vm((4, 2, tokens, width), bf),
            vm(wgu_all.shape, bf),
            vm(wd_all.shape, bf),
            vm((4, 2 * tokens, FF_PAD), f32),
            vm((4, 2 * tokens, FF_PAD), bf),
            vm((4, 2 * tokens, 2 * FF_PAD), bf),
            vm((4, 2, tokens, width), bf),
            vm((4, 2, tokens, width), bf),
            vm((tokens, width), f32),
            vm(wgu_all.shape, bf),
        ]
        + sums
        + [
            vm((2, 4, 112, width), bf),
            vm((4, 112, width), bf),
            vm((2, 112, width), bf),
            vm((112, 640), bf),
            vm((112, 512), bf),
            vm((112, width), bf),
        ]
        + [
            pltpu.SemaphoreType.DMA((8,)),
            pltpu.SemaphoreType.DMA((40,)),
            pltpu.SemaphoreType.DMA((40,)),
        ],
        compiler_params=comm_params(2),
        name="feed_forward",
    )(own_n, gb_all, wgu_all, wd_all)


def back_kernel(
    dgu, p_d, part_b_all, gn2_all, middle_all, miscs_all, tokens, cot, rope_all, q_all, kv_all,
    probs_all, att_all, wqkv_all, wo_all, normed1_all,
    o_gu, o_d, o_qkv, o_wo, o_out, o_grad,
    h_gu, r_gu, gu_whole, gu_half, z_gu, f_gu, piece_d,
    part_b, b_whole, b_half, gn2, middle, miscs, x_ref, cot_ref, rope, q_ref, kv_ref, probs, att,
    wqkv, wo, normed1, dq, r_qkv, q_whole, q_half, dwo, r_wo, w_whole, w_half,
    h_gain, r_gain, g_whole, g_half, gkv, kv_out, kv_in, gproj, gmid, out_bf,
    s_qkv, y_qkv, z_qkv, s_wo, y_wo, z_wo,
    local_sems, send_sems, recv_sems,
):
    place = Place()
    wire = Wire(send_sems, recv_sems)
    core, me, y, rep = place.core, place.shard, place.y, place.rep
    rows, width = tokens.shape
    at = place.shard_at
    others = [(j, p) for p in (0, 1) for j in range(4) if (j, p) != (0, 0)]
    group = [place.device(dx=STEPS[j], mirror=p) for j, p in others]
    sequence = [(rep, at(j, 1)) for j in range(4)]
    sibling = place.device(sibling=1)
    column = [place.device(dy=d) for d in (1, 3, 2)]
    low = place.device(swap_lo=1)
    locals_ = []

    def local(src, dst):
        copy = pltpu.make_async_copy(src, dst, local_sems.at[len(locals_)])
        copy.start()
        locals_.append(copy)
        return copy

    def gu_part(ref, half, q):
        size = 256 if q < 3 else 128
        return ref.at[:, :, pl.ds(pl.multiple_of(half * FF_PAD + 256 * q, 128), size)]

    def landed(ref, q):
        return ref.at[q] if q < 3 else ref.at[q, :, :, pl.ds(0, 128)]

    load_gu = [local(gu_part(dgu, core, q), landed(h_gu, q)) for q in range(4)]
    load_d = local(p_d, piece_d)
    load_b = local(part_b_all, part_b)
    loads = [
        local(src, dst)
        for src, dst in (
            (gn2_all, gn2),
            (middle_all, middle),
            (miscs_all, miscs),
            (tokens, x_ref),
            (cot, cot_ref),
            (att_all, att),
            (wo_all, wo),
        )
    ]
    loads_heads = [
        local(src, dst)
        for src, dst in ((q_all, q_ref), (kv_all, kv_ref), (probs_all, probs), (rope_all, rope))
    ]
    loads_last = [local(src, dst) for src, dst in ((normed1_all, normed1), (wqkv_all, wqkv))]
    loaded = len(locals_)
    h_gu[3, :, :, 128:] = jnp.zeros((8, 144, 128), jnp.bfloat16)
    r_gu[3, :, :, 128:] = jnp.zeros((8, 144, 128), jnp.bfloat16)
    greet([sibling, low] + group + column + sequence)

    swap_gu = [wire.copy(gu_part(dgu, 1 - core, q), landed(r_gu, q), sibling) for q in range(4)]
    for copy in swap_gu:
        copy.start()

    def cut_d(ref, part):
        start, size = ((0, width), (0, 640), (640, 512))[part]
        return ref.at[:, pl.ds(start, size)]

    def over_y(dx, mirror):
        return place.device(dy=dx)

    load_d.wait()
    slot_d = lambda j, p: o_d.at[core, (y + STEPS[j]) % 4]
    tree_d = gather_tree(wire, over_y, RING, piece_d, slot_d, cut_d, True)
    pass_d = {
        jp: wire.copy(piece_d if jp == (0, 0) else slot_d(*jp), slot_d(*jp), sibling)
        for jp in ((0, 0), (2, 0), (1, 0), (3, 0))
    }
    for copy in (tree_d[0], tree_d[1], pass_d[0, 0]):
        copy.start()
    local(piece_d, slot_d(0, 0))

    def cut_rows96(ref, part):
        return ref if part == 0 else ref.at[pl.ds((part - 1) * 96, 96)]

    sum_b = SumTree(
        wire, place.over_group, HOPS, lambda j, p: part_b.at[j, p], cut_rows96,
        [b_whole.at[k] for k in range(3)] + [b_half.at[k] for k in range(8)],
    )
    load_b.wait()
    sum_b.start(10, 9, 6, 5)

    for load in loads:
        load.wait()
    as_float = [miscs[s].astype(jnp.float32) for s in range(8)]
    gain1 = jnp.concatenate([m[0:1, :144] for m in as_float], axis=1)
    gain2 = jnp.concatenate([m[1:2, :144] for m in as_float], axis=1)
    row = lax.broadcasted_iota(jnp.int32, (rows, 1), 0).astype(jnp.float32)
    keep = jnp.where(row < miscs[me].astype(jnp.float32)[2:3, :1], 1.0, 0.0)
    mid = middle[...]
    inverse2 = lax.rsqrt(jnp.mean(mid * mid, axis=1, keepdims=True) + EPSILON)
    scaled2 = mid * inverse2
    grad2 = gn2[...]
    grad_gain2 = jnp.sum(grad2 * scaled2, axis=0, keepdims=True)
    grad2 = grad2 * gain2
    grad_mid = cot_ref[...].astype(jnp.float32) + inverse2 * (
        grad2 - scaled2 * jnp.mean(grad2 * scaled2, axis=1, keepdims=True)
    )
    gmid[...] = grad_mid
    grad_attn = (keep * grad_mid).astype(jnp.bfloat16)
    for start in range(0, width, 384):
        block = lead_product(att[...], grad_attn[:, start : start + 384]).astype(jnp.bfloat16)
        block = block.reshape(8, 2, 64, 384)
        dwo[0, :, :, start : start + 384] = block[:, 0]
        dwo[1, :, :, start : start + 384] = block[:, 1]
    swap_wo = wire.copy(dwo.at[1 - core], r_wo, sibling)
    swap_wo.start()
    grad_att = trail_product(grad_attn, wo.reshape(1024, width)[...]).astype(jnp.bfloat16)

    def added(target, source, count):
        def one(i, carry):
            add_into(target.at[i], source.at[i])
            return carry

        lax.fori_loop(0, count, one, 0)

    for copy in load_gu:
        copy.wait()
    for copy in swap_gu:
        copy.wait_recv()
    added(h_gu.reshape(32, 144, 256), r_gu.reshape(32, 144, 256), 32)

    def cut_lead(ref, part):
        return ref if part == 0 else ref.at[pl.ds((part - 1) * 4, 4)]

    quarter = h_gu.at[y]
    sum_gu = SumTree(
        wire, over_y, RING, lambda j, p: h_gu.at[(y + STEPS[j]) % 4], cut_lead,
        [gu_whole.at[0], gu_whole.at[1], gu_half.at[0], gu_half.at[1]],
    )
    sum_gu.start(2, 3)

    for load in loads_heads:
        load.wait()
    keys = (BEHIND + 1) * rows
    all_kv = kv_ref.reshape(keys, 512)
    flat = gkv.reshape(keys, 512)
    cosine, sine_part = rope[:, :128], rope[:, 128:]
    scaling = 256 ** (-0.5)

    def turned_back(vectors):
        first, second = vectors[:, :128], vectors[:, 128:]
        return jnp.concatenate(
            [first * cosine + second * sine_part, second * cosine - first * sine_part], axis=1
        )

    for h in range(4):
        share = probs[h]
        share_low = share.astype(jnp.bfloat16)
        grad_h = grad_att[:, 256 * h : 256 * (h + 1)]
        grad_probs = trail_product(grad_h, all_kv[:, 256:])
        delta = jnp.sum(share * grad_probs, axis=1, keepdims=True)
        grad_scores = (share * (grad_probs - delta)).astype(jnp.bfloat16)
        grad_keys = lead_product(grad_scores, q_ref[h])
        grad_values = lead_product(share_low, grad_h)
        if h == 0:
            flat[:, :256] = grad_keys
            flat[:, 256:] = grad_values
        else:
            flat[:, :256] += grad_keys
            flat[:, 256:] += grad_values
        grad_q = matmul(grad_scores, all_kv[:, :256])
        gproj[:, 256 * h : 256 * (h + 1)] = (turned_back(grad_q) * scaling).astype(jnp.bfloat16)
    sends = []
    for i in range(1, BEHIND + 1):
        kv_out[i - 1] = gkv[i].astype(jnp.bfloat16)
        sends.append(
            wire.copy(kv_out.at[i - 1], kv_in.at[i - 1], (rep, jnp.maximum(me - i, 0)))
        )
        pl.when(me >= i)(sends[-1].start)

        @pl.when(me + i > 7)
        def _():
            kv_in[i - 1] = jnp.zeros(kv_in.shape[1:], kv_in.dtype)

    for k in (0, 1):
        arrive(tree_d, k, RING_ONWARD)
        pass_d[((2, 0), (1, 0))[k]].start()
    swap_wo.wait_recv()
    added(dwo.at[core], r_wo, 8)

    def cut_wo(ref, part):
        return ref if part == 0 else ref.at[pl.ds((part - 1) * 32, 32)]

    def cut_lanes(size):
        def cut(ref, part):
            return ref if part == 0 else ref.at[:, pl.ds((part - 1) * size, size)]

        return cut

    sum_wo = SumTree(
        wire, place.over_group, HOPS, lambda j, p: dwo.at[core, at(j, p)], cut_wo,
        [w_whole.at[k] for k in range(3)] + [w_half.at[k] for k in range(8)],
    )
    sum_wo.start(10, 9, 6, 5)
    sum_gu.absorb(2, 3)
    sum_gu.start(0, 1)
    sum_b.send_near()

    grad_kv = gkv[0]
    for i, copy in enumerate(sends):
        pl.when(me + (i + 1) <= 7)(copy.wait_recv)
        grad_kv = grad_kv + kv_in[i].astype(jnp.float32)
    gproj[:, 1024:1280] = turned_back(grad_kv[:, :256]).astype(jnp.bfloat16)
    gproj[:, 1280:1536] = grad_kv[:, 256:].astype(jnp.bfloat16)
    for load in loads_last:
        load.wait()
    dq_rows = dq.reshape(2, width, 768)
    for t in range(6):
        dq_rows[t // 3, :, 256 * (t % 3) : 256 * (t % 3 + 1)] = lead_product(
            normed1[...], gproj[:, 256 * t : 256 * (t + 1)]
        ).astype(jnp.bfloat16)
    swap_qkv = wire.copy(dq.at[1 - core], r_qkv, sibling)
    swap_qkv.start()
    for k in (2, 3):
        arrive(tree_d, k, RING_ONWARD)
    pass_d[3, 0].start()
    inputs = x_ref[...].astype(jnp.float32)
    inverse1 = lax.rsqrt(jnp.mean(inputs * inputs, axis=1, keepdims=True) + EPSILON)
    scaled1 = inputs * inverse1
    grad1 = trail_product(gproj[...], wqkv.reshape(width, 1536)[...])
    grad_gain1 = jnp.sum(grad1 * scaled1, axis=0, keepdims=True)
    grad1 = grad1 * gain1
    gmid[...] += inverse1 * (grad1 - scaled1 * jnp.mean(grad1 * scaled1, axis=1, keepdims=True))
    local(gmid, o_grad)
    for s in range(8):
        cols = slice(144 * s, 144 * (s + 1))
        both = jnp.concatenate(
            [grad_gain1[:, cols], grad_gain2[:, cols], jnp.zeros((14, 144), jnp.float32)], axis=0
        )
        both = jnp.concatenate([both, jnp.zeros((16, 112), jnp.float32)], axis=1)
        h_gain[0, s] = both.astype(jnp.bfloat16)
        h_gain[1, s] = both.astype(jnp.bfloat16)
    swap_gain = wire.copy(h_gain.at[1], r_gain, sibling)
    swap_gain.start()

    sum_gu.absorb(0, 1)
    cross_gu = wire.copy(quarter, z_gu, low)
    cross_gu.start()
    sum_b.send_next()
    swap_qkv.wait_recv()
    added(dq.at[core], r_qkv, 8)
    swap_gain.wait_recv()
    added(h_gain.at[0], r_gain, 8)
    sum_q = SumTree(
        wire, place.over_group, HOPS, lambda j, p: dq.at[core, at(j, p)], cut_lanes(384),
        [q_whole.at[k] for k in range(3)] + [q_half.at[k] for k in range(8)],
    )
    sum_gain = SumTree(
        wire, place.over_group, HOPS, lambda j, p: h_gain.at[0, at(j, p)], cut_lanes(128),
        [g_whole.at[k] for k in range(3)] + [g_half.at[k] for k in range(8)],
    )
    sum_q.start(10, 9, 6, 5)
    sum_gain.start(10, 9, 6, 5)
    sum_wo.send_near()
    sum_b.send_last()
    cross_gu.wait_recv()
    cross_gu.wait_send()
    added(quarter, z_gu, 8)
    turn = [
        wire.copy(h_gu.at[y, at(j, p)], f_gu.at[me], device)
        for (j, p), device in zip(others, group)
    ]
    for copy in turn:
        copy.start()
    f_gu[me] = h_gu[y, me]
    trees = [sum_q, sum_wo, sum_gain]
    sum_wo.send_next()
    sum_q.send_near()
    sum_gain.send_near()
    sum_q.send_next()
    sum_gain.send_next()
    for tree in trees:
        tree.send_last()

    for copy in turn:
        copy.wait_recv()
    slot_gu = lambda j, p: o_gu.at[core, (y + STEPS[j]) % 4]
    tree_gu = gather_tree(wire, over_y, RING, f_gu, slot_gu, cut_lead, True)
    pass_gu = {
        jp: wire.copy(f_gu if jp == (0, 0) else slot_gu(*jp), slot_gu(*jp), sibling)
        for jp in ((0, 0), (2, 0), (1, 0), (3, 0))
    }
    for copy in (tree_gu[0], tree_gu[1], pass_gu[0, 0]):
        copy.start()
    local(f_gu, slot_gu(0, 0))

    total = sum_wo.finish().astype(jnp.bfloat16)
    s_wo[...] = total.reshape(4, 16, width)
    total = sum_q.finish().astype(jnp.bfloat16)
    for q in range(3):
        s_qkv[q] = total[:, 256 * q : 256 * (q + 1)]
    s_qkv[3] = jnp.concatenate(
        [sum_gain.finish(), jnp.zeros((128, 256), jnp.float32)], axis=0
    ).astype(jnp.bfloat16)
    steps = (1, 3, 2)
    over = [
        wire.copy(source.at[(y + d) % 4], landing.at[i], device)
        for source, landing in ((s_wo, y_wo), (s_qkv, y_qkv))
        for i, (d, device) in enumerate(zip(steps, column))
    ]
    for copy in over:
        copy.start()
    out = sum_b.finish()
    out_bf[...] = (middle[...] + keep * out).astype(jnp.bfloat16)
    local(out_bf, o_out)
    for copy in over:
        copy.wait_recv()
    crossings = []
    for source, landing, other in ((s_wo, y_wo, z_wo), (s_qkv, y_qkv, z_qkv)):
        mine = source[y].astype(jnp.float32)
        for i in range(3):
            mine = mine + landing[i].astype(jnp.float32)
        source[y] = mine.astype(jnp.bfloat16)
        crossings.append(wire.copy(source.at[y], other, low))
        crossings[-1].start()
    for k in (0, 1):
        arrive(tree_gu, k, RING_ONWARD)
        pass_gu[((2, 0), (1, 0))[k]].start()
    backs = []
    for crossing, source, other, out_ref in zip(crossings, (s_wo, s_qkv), (z_wo, z_qkv), (o_wo, o_qkv)):
        crossing.wait_recv()
        crossing.wait_send()
        add_into(source.at[y], other)
        back = [wire.copy(source.at[y], out_ref.at[core, y], device) for device in column]
        ends = [wire.copy(source.at[y], out_ref.at[core, y], sibling)]
        for copy in back + ends:
            copy.start()
        local(source.at[y], out_ref.at[core, y])
        backs.append((back, ends, out_ref))
    for back, ends, out_ref in backs:
        for d, copy in zip((3, 1, 2), back):
            copy.wait_recv()
            held = out_ref.at[core, (y + d) % 4]
            ends.append(wire.copy(held, held, sibling))
            ends[-1].start()
    for k in (2, 3):
        arrive(tree_gu, k, RING_ONWARD)
    pass_gu[3, 0].start()
    for copy in list(pass_d.values()) + list(pass_gu.values()) + backs[0][1] + backs[1][1]:
        copy.wait_recv()
    for copy in locals_[loaded:]:
        copy.wait()
    for i, copy in enumerate(sends):
        pl.when(me >= i + 1)(copy.wait_send)
    waited = [id(copy) for copy in sends + crossings + [cross_gu]]
    for copy in wire.made:
        if id(copy) not in waited:
            copy.wait_send()


def back(*args):
    bf, f32 = jnp.bfloat16, jnp.float32
    width = 1152
    rows = args[6].shape[0]
    outs = [
        ((2, 4, 8, 144, 256), bf),
        ((2, 4, 112, width), bf),
        ((2, 4, 144, 256), bf),
        ((2, 4, 16, width), bf),
        ((rows, width), bf),
        ((rows, width), f32),
    ]
    scratch = [
        ((4, 8, 144, 256), bf),
        ((4, 8, 144, 256), bf),
        ((2, 8, 144, 256), bf),
        ((2, 4, 144, 256), bf),
        ((8, 144, 256), bf),
        ((8, 144, 256), bf),
        ((112, width), bf),
        ((4, 2, rows, width), bf),
        ((3, rows, width), bf),
        ((8, rows // 2, width), bf),
    ]
    scratch += [(a.shape, a.dtype) for a in args[3:16]]
    scratch += [
        ((2, 8, 144, 768), bf),
        ((8, 144, 768), bf),
        ((3, 144, 768), bf),
        ((8, 144, 384), bf),
        ((2, 8, 64, width), bf),
        ((8, 64, width), bf),
        ((3, 64, width), bf),
        ((8, 32, width), bf),
        ((2, 8, 16, 256), bf),
        ((8, 16, 256), bf),
        ((3, 16, 256), bf),
        ((8, 16, 128), bf),
        ((BEHIND + 1, rows, 512), f32),
        ((BEHIND, rows, 512), bf),
        ((BEHIND, rows, 512), bf),
        ((rows, 1536), bf),
        ((rows, width), f32),
        ((rows, width), bf),
        ((4, 144, 256), bf),
        ((3, 144, 256), bf),
        ((144, 256), bf),
        ((4, 16, width), bf),
        ((3, 16, width), bf),
        ((16, width), bf),
    ]
    return pl.pallas_call(
        back_kernel,
        out_shape=tuple(jax.ShapeDtypeStruct(*o) for o in outs),
        in_specs=[ANY] * 16,
        out_specs=(ANY,) * len(outs),
        scratch_shapes=[pltpu.VMEM(*v) for v in scratch]
        + [
            pltpu.SemaphoreType.DMA((40,)),
            pltpu.SemaphoreType.DMA((128,)),
            pltpu.SemaphoreType.DMA((128,)),
        ],
        compiler_params=comm_params(3),
        name="attention_backward",
    )(*args)


def gain_rows(*rows):
    made = jnp.stack([jnp.pad(row, ((0, 0), (0, 256 - row.shape[1]))) for row in rows], axis=1)
    return jnp.pad(made, ((0, 0), (0, 16 - len(rows)), (0, 0))).astype(jnp.bfloat16)


def on_device(
    tokens, lengths, attn_gain, w_query, w_keyval, w_out, mlp_gain, w_gate, w_up, w_down, cotangent
):
    width = tokens.shape[1]
    heads_all = w_query.shape[1]
    live_count = lengths[0, 0]
    counts = jnp.full((1, 144), live_count, jnp.int32).astype(jnp.bfloat16)
    misc = gain_rows(attn_gain[None], mlp_gain[None], counts)[0]
    frequency = 10000.0 ** (-2.0 * jnp.arange(128, dtype=jnp.float32) / 256)
    (
        miscs, qkv_all, out_all, gu_all, branch_all,
        normed1, queries, all_kv, probs, attended, middle, normed2, rope,
    ) = front(
        tokens, cotangent, misc, jnp.tile(frequency[None], (8, 1)),
        w_query, w_keyval, w_out, w_gate, w_up,
    )
    down_mine = jnp.pad(w_down, ((0, FF_PAD - FF_DEV), (0, 0)))
    grad_normed2, branch, grad_gu, grad_d = feed_forward(
        normed2, branch_all, gu_all.reshape(width, -1), down_mine
    )
    sum_gu, sum_d, sum_qkv, sum_wo, outputs, grad_inputs = back(
        grad_gu.reshape(8, 144, -1), grad_d, branch, grad_normed2, middle, miscs, tokens, cotangent,
        rope, queries, all_kv, probs, attended, qkv_all, out_all, normed1,
    )
    grad_gate_w, grad_up_w = unpack_gate_up(sum_gu)
    grad_qkv = sum_qkv[:, :3].transpose(2, 0, 1, 3).reshape(144, 1536).astype(jnp.float32)
    gains = sum_qkv[0, 3].astype(jnp.float32)
    return (
        outputs,
        grad_inputs,
        gains[0, :144],
        grad_qkv[:, :heads_all],
        grad_qkv[:, heads_all:],
        sum_wo.reshape(128, width).astype(jnp.float32),
        gains[1, :144],
        grad_gate_w,
        grad_up_w,
        sum_d.reshape(FF_PAD, width)[:FF_DEV].astype(jnp.float32),
    )


def solution(mesh):
    placed = (
        P(("rep", "shard"), None),
        P("rep", "shard"),
        P("shard"),
        P("shard", None),
        P("shard", None),
        P("shard", None),
        P("shard"),
        P("shard", None),
        P("shard", None),
        P("shard", None),
        P(("rep", "shard"), None),
    )
    return jax.shard_map(
        on_device,
        mesh=mesh,
        in_specs=placed,
        out_specs=(
            P(("rep", "shard"), None),
            P(("rep", "shard"), None),
            P("shard"),
            P("shard", None),
            P("shard", None),
            P("shard", None),
            P("shard"),
            P("shard", None),
            P("shard", None),
            P("shard", None),
        ),
        check_vma=False,
    )
```

```python
import functools

import jax
import jax.numpy as jnp
import numpy as np
from jax import lax
from jax.experimental import pallas as pl
from jax.experimental.pallas import tpu as pltpu
from jax.sharding import PartitionSpec as P

MESH = pl.DeviceIdType.MESH
WINDOW = 512
EPSILON = 1e-06
MASKED = -1e30
VMEM_LIMIT = 60 * 2**20
FF_DEV = 864
FF_PAD = 896
PAIRS = FF_PAD // 128
BEHIND = 4


def matmul(former, latter):
    return jnp.dot(former, latter, preferred_element_type=jnp.float32)


def lead_product(former, latter):
    return lax.dot_general(
        former, latter, (((0,), (0,)), ((), ())), preferred_element_type=jnp.float32
    )


def trail_product(former, latter):
    return lax.dot_general(
        former, latter, (((1,), (1,)), ((), ())), preferred_element_type=jnp.float32
    )


class Place:
    def __init__(self):
        rep, shard = lax.axis_index("rep"), lax.axis_index("shard")
        self.rep, self.shard = rep, shard
        self.y, self.z_lo, self.core = rep // 4, (rep // 2) % 2, rep % 2
        self.z_hi, self.x = shard // 4, shard % 4

    def device(self, dx=0, dy=0, mirror=0, swap_lo=0, sibling=0):
        z_lo = (self.z_lo + mirror + swap_lo) % 2
        rep = (((self.y + dy) % 4) * 2 + z_lo) * 2 + (self.core + sibling) % 2
        return (rep, ((self.z_hi + mirror) % 2) * 4 + (self.x + dx) % 4)

    def over_group(self, dx, mirror):
        return self.device(dx=dx, mirror=mirror)

    def shard_at(self, j, p):
        return ((self.z_hi + p) % 2) * 4 + (self.x + STEPS[j]) % 4


STEPS = (0, 1, 3, 2)


class Wire:
    def __init__(self, send_sems, recv_sems):
        self.send_sems, self.recv_sems, self.made = send_sems, recv_sems, []

    def copy(self, src, dst, device):
        k = len(self.made)
        made = pltpu.make_async_remote_copy(
            src_ref=src,
            dst_ref=dst,
            send_sem=self.send_sems.at[k],
            recv_sem=self.recv_sems.at[k],
            device_id=device,
            device_id_type=MESH,
        )
        self.made.append(made)
        return made

    def drain(self):
        for made in self.made:
            made.wait_send()


def greet(devices):
    barrier = pltpu.get_barrier_semaphore()
    for device in devices:
        pl.semaphore_signal(barrier, inc=1, device_id=device, device_id_type=MESH)
    pl.semaphore_wait(barrier, len(devices))


HOPS = (
    ((0, 0), (0, 1), 0, 0, 1),
    ((0, 0), (2, 0), 0, 1, 0),
    ((0, 0), (1, 0), 0, 3, 0),
    ((0, 1), (2, 1), 1, 1, 0),
    ((0, 1), (1, 1), 1, 3, 0),
    ((2, 0), (3, 0), 1, 1, 0),
    ((1, 0), (3, 0), 2, 3, 0),
    ((2, 0), (2, 1), 2, 0, 1),
    ((1, 0), (1, 1), 2, 0, 1),
    ((2, 1), (3, 1), 1, 1, 0),
    ((1, 1), (3, 1), 2, 3, 0),
)
ONWARD = {0: (3, 4), 1: (5, 7), 2: (6, 8), 3: (9,), 8: (10,)}
WHOLE = {0: (0, 1), 1: (2, 0), 2: (1, 0), 6: (3, 0), 7: (2, 1), 8: (1, 1), 10: (3, 1)}
ORDER = (0, 1, 2, 3, 4, 8, 7, 5, 6, 9, 10)
RING = (
    ((0, 0), (2, 0), 0, 1, 0),
    ((0, 0), (1, 0), 0, 3, 0),
    ((2, 0), (3, 0), 1, 1, 0),
    ((1, 0), (3, 0), 2, 3, 0),
)
RING_ONWARD = {0: (2,), 1: (3,)}


def gather_tree(wire, device_of, hops, own, slot, cut, absolute):
    copies = []
    for source, target, part, dx, mirror in hops:
        src = own if source == (0, 0) else slot(*source)
        dst = slot(*(source if absolute else target))
        copies.append(wire.copy(cut(src, part), cut(dst, part), device_of(dx, mirror)))
    return copies


def arrive(tree, k, after=ONWARD):
    tree[k].wait_recv()
    for n in after.get(k, ()):
        tree[n].start()


def add_into(target, source):
    target[...] = (target[...].astype(jnp.float32) + source[...].astype(jnp.float32)).astype(
        target.dtype
    )


class SumTree:
    def __init__(self, wire, device_of, hops, slot, cut, landings):
        self.hops, self.slot, self.cut, self.landings = hops, slot, cut, landings
        self.copies = [
            wire.copy(cut(slot(*target), part), landing, device_of((4 - dx) % 4, mirror))
            for (_, target, part, dx, mirror), landing in zip(hops, landings)
        ]

    def start(self, *hops):
        for k in hops:
            self.copies[k].start()

    def absorb(self, *hops):
        for k in hops:
            source, _, part, _, _ = self.hops[k]
            self.copies[k].wait_recv()
            add_into(self.cut(self.slot(*source), part), self.landings[k])

    def send_near(self):
        self.start(4, 7)
        self.absorb(10)
        self.start(8)
        self.absorb(9)
        self.start(3)
        self.absorb(6, 5)

    def send_next(self):
        self.absorb(8)
        self.start(2)
        self.absorb(7)
        self.start(1)

    def send_last(self):
        self.absorb(3, 4)
        self.start(0)

    def finish(self):
        total = self.slot(0, 0)[...].astype(jnp.float32)
        for k in (2, 1, 0):
            self.copies[k].wait_recv()
            total = total + self.landings[k][...].astype(jnp.float32)
        return total


def front_kernel(
    tokens, cot, misc, freq, w_query, w_keyval, w_out, w_gate, w_up,
    o_misc, o_qkv, o_wo, o_gu, o_gb, o_normed1, o_q, o_kv, o_probs, o_att, o_middle, o_normed2, o_rope,
    x_ref, cot_ref, miscs, freq_ref, wqkv, wo, gate, up, packed, gb_own, normed1, q_ref, kv_ref,
    bias, probs, att, middle, normed2, rope,
    local_sems, send_sems, recv_sems,
):
    place = Place()
    wire = Wire(send_sems, recv_sems)
    core, me, y = place.core, place.shard, place.y
    rows, width = tokens.shape
    at = place.shard_at
    others = [(j, p) for p in (0, 1) for j in range(4) if (j, p) != (0, 0)]
    group = [place.device(dx=STEPS[j], mirror=p) for j, p in others]
    sequence = [(place.rep, at(j, p)) for j, p in others]
    sibling = place.device(sibling=1)
    column = [place.device(dy=d) for d in (1, 3, 2)]
    locals_ = []

    def local(src, dst):
        copy = pltpu.make_async_copy(src, dst, local_sems.at[len(locals_)])
        copy.start()
        locals_.append(copy)
        return copy

    load_x = local(tokens, x_ref)
    load_cot = local(cot, cot_ref)
    load_misc = local(misc, miscs.at[me])
    load_freq = local(freq, freq_ref)
    load_gate = local(w_gate, gate)
    load_up = local(w_up, up)
    load_own = [
        local(w_query, wqkv.at[me, :, pl.ds(0, 1024)]),
        local(w_keyval, wqkv.at[me, :, pl.ds(1024, 512)]),
        local(w_out, wo.at[me]),
    ]
    greet([sibling] + group + [d for d, (j, p) in zip(sequence, others) if p == 1] + column)

    def lanes_from(base, size):
        def cut(ref, part):
            start, count = ((0, size), (0, size // 2), (size // 2, size // 2))[part]
            start = pl.multiple_of(core * size + (base + start), 128)
            return ref.at[:, pl.ds(start, count)]

        return cut

    def cut_wo(ref, part):
        start, size = ((0, 64), (0, 32), (32, 32))[part]
        return ref.at[pl.ds(pl.multiple_of(core * 64 + start, 32), size)]

    def cut_gb(ref, part):
        return ref if part == 0 else ref.at[pl.ds((part - 1) * 96, 96)]

    def cut_gu(ref):
        return ref.at[:, pl.ds(pl.multiple_of(core * FF_PAD, 128), FF_PAD)]

    cut_q, cut_kv = lanes_from(0, 512), lanes_from(1024, 256)
    slot_qkv = lambda j, p: wqkv.at[at(j, p)]
    slot_wo = lambda j, p: wo.at[at(j, p)]
    slot_gb = lambda j, p: o_gb.at[j, p]
    misc_copies = [wire.copy(misc, miscs.at[me], device) for device in sequence]
    for copy in misc_copies:
        copy.start()
    for load in load_own:
        load.wait()
    own = wqkv.at[me]
    trees = [
        gather_tree(wire, place.over_group, HOPS, own, slot_qkv, cut_q, True),
        gather_tree(wire, place.over_group, HOPS, own, slot_qkv, cut_kv, True),
        gather_tree(wire, place.over_group, HOPS, wo.at[me], slot_wo, cut_wo, True),
    ]
    cuts = [cut_q, cut_kv, cut_wo]
    slots = [slot_qkv, slot_qkv, slot_wo]
    passes = [
        {k: wire.copy(cut(slot(*jp), 0), cut(slot(*jp), 0), sibling) for k, jp in WHOLE.items()}
        for cut, slot in zip(cuts, slots)
    ]
    for tree in trees:
        for k in (0, 1, 2):
            tree[k].start()

    load_x.wait()
    inputs = x_ref[...].astype(jnp.float32)
    inverse1 = lax.rsqrt(jnp.mean(inputs * inputs, axis=1, keepdims=True) + EPSILON)
    middle[...] = inputs * inverse1
    load_gate.wait()
    load_up.wait()
    for d in range(8):
        for t in range(PAIRS):
            start = FF_DEV * d + 128 * t
            size = min(128, FF_DEV - 128 * t)
            for k, weight in enumerate((gate, up)):
                block = weight[:, start : start + size]
                if size < 128:
                    block = jnp.concatenate(
                        [block, jnp.zeros((block.shape[0], 128 - size), block.dtype)], axis=1
                    )
                packed[d, :, 256 * t + 128 * k : 256 * t + 128 * (k + 1)] = block

    def attn(*hops):
        for k in hops:
            for tree, onward in zip(trees, passes):
                arrive(tree, k)
                if k in onward:
                    onward[k].start()

    z_of = lambda p: (place.z_hi + p) % 2
    shard_from = lambda d, p: z_of(p) * 4 + (place.x + y + d) % 4
    turn = []
    for p in (0, 1):
        target = z_of(p) * 4 + (place.x - y + 4) % 4
        turn.append(
            wire.copy(
                cut_gu(packed.at[target]), cut_gu(o_gu.at[me]), place.device(dx=4 - y, mirror=p)
            )
        )
    away, home = y > 0, y == 0
    keep_own = pltpu.make_async_copy(
        cut_gu(packed.at[me]), cut_gu(o_gu.at[me]), local_sems.at[len(locals_)]
    )
    locals_.append(None)
    turn[1].start()
    pl.when(away)(turn[0].start)
    pl.when(home)(keep_own.start)

    def over_y(dx, mirror):
        return place.device(dy=dx)

    def cut_block(ref, part):
        start, size = ((0, 144), (0, 80), (80, 64))[part]
        return ref.at[pl.ds(start, size), pl.ds(pl.multiple_of(core * FF_PAD, 128), FF_PAD)]

    gu_slots = [lambda j, _, p=p: o_gu.at[shard_from(STEPS[j], p)] for p in (0, 1)]
    gu_trees = [
        gather_tree(wire, over_y, RING, slot(0, 0), slot, cut_block, True) for slot in gu_slots
    ]
    gu_passes = {
        (j, p): wire.copy(
            cut_gu(o_gu.at[shard_from(STEPS[j], p)]),
            cut_gu(o_gu.at[shard_from(STEPS[j], p)]),
            sibling,
        )
        for j in range(4)
        for p in (0, 1)
    }

    def over(k, j):
        for p in (0, 1):
            arrive(gu_trees[p], k, RING_ONWARD)
            if j:
                gu_passes[j, p].start()

    attn(0, 1, 2)
    load_cot.wait()
    load_misc.wait()
    load_freq.wait()
    live_col = (
        lax.broadcasted_iota(jnp.int32, (rows, 1), 0).astype(jnp.float32)
        < miscs[me].astype(jnp.float32)[2:3, :1]
    )
    gb_own[...] = jnp.where(live_col, cot_ref[...].astype(jnp.float32), 0.0).astype(jnp.bfloat16)
    gb_tree = gather_tree(wire, place.over_group, HOPS, gb_own, slot_gb, cut_gb, False)
    attn(3, 4, 8, 7)
    pl.when(away)(turn[0].wait_recv)
    turn[1].wait_recv()
    pl.when(home)(keep_own.wait)
    for p in (0, 1):
        gu_trees[p][0].start()
        gu_trees[p][1].start()
        gu_passes[0, p].start()
    for k in (0, 1, 2):
        gb_tree[k].start()
    local(gb_own, o_gb.at[0, 0])
    attn(5, 6, 9, 10)

    for copy in misc_copies:
        copy.wait_recv()
    as_float = [miscs[s].astype(jnp.float32) for s in range(8)]
    gain1 = jnp.concatenate([m[0:1, :144] for m in as_float], axis=1)
    gain2 = jnp.concatenate([m[1:2, :144] for m in as_float], axis=1)
    normed = (middle[...] * gain1).astype(jnp.bfloat16)
    normed1[...] = normed
    for k in WHOLE:
        passes[0][k].wait_recv()
        passes[1][k].wait_recv()
    live = [m[2:3, :1] for m in as_float]
    start_of = []
    for i in range(BEHIND + 1):
        total = jnp.zeros((1, 1), jnp.float32)
        for s in range(8):
            total = total + jnp.where(s < me - i, 1.0, 0.0) * live[s]
        start_of.append(total)
    row = lax.broadcasted_iota(jnp.int32, (rows, 1), 0).astype(jnp.float32)
    query_pos = start_of[0] + row
    angles = query_pos * freq_ref[0:1, :]
    cosine, sine_part = jnp.cos(angles), jnp.sin(angles)
    rope[:, :128] = cosine
    rope[:, 128:] = sine_part
    weights = wqkv.reshape(width, 1536)

    def turned(vectors):
        first, second = vectors[:, :128], vectors[:, 128:]
        return jnp.concatenate(
            [first * cosine - second * sine_part, second * cosine + first * sine_part], axis=1
        )

    projected = matmul(normed, weights[:, 1024:1536])
    kv_ref[0, :, :256] = turned(projected[:, :256]).astype(jnp.bfloat16)
    kv_ref[0, :, 256:] = projected[:, 256:].astype(jnp.bfloat16)
    sends = [
        wire.copy(kv_ref.at[0], kv_ref.at[i], (place.rep, jnp.minimum(me + i, 7)))
        for i in range(1, BEHIND + 1)
    ]
    for i, copy in enumerate(sends):
        pl.when(me + (i + 1) < 8)(copy.start)

        @pl.when(me < i + 1)
        def _():
            kv_ref[i + 1] = jnp.zeros(kv_ref.shape[1:], kv_ref.dtype)

    scaling = 256 ** (-0.5)
    for h in range(4):
        heads = matmul(normed, weights[:, 256 * h : 256 * (h + 1)])
        q_ref[h] = (turned(heads) * scaling).astype(jnp.bfloat16)

    index = lax.broadcasted_iota(jnp.int32, (1, (BEHIND + 1) * rows), 1)
    key_pos = jnp.zeros(index.shape, jnp.float32)
    key_live = jnp.zeros(index.shape, jnp.float32)
    for i in range(BEHIND + 1):
        inside = jnp.logical_and(index >= i * rows, index < (i + 1) * rows)
        within = (index - i * rows).astype(jnp.float32)
        live_i = jnp.zeros((1, 1), jnp.float32)
        for s in range(8):
            live_i = live_i + jnp.where(me - i == s, 1.0, 0.0) * live[s]
        key_pos = jnp.where(inside, start_of[i] + within, key_pos)
        key_live = jnp.where(inside, jnp.where(within < live_i, 1.0, 0.0), key_live)
    ahead = query_pos - key_pos
    allowed = jnp.logical_and(
        jnp.logical_and(ahead >= 0.0, ahead < float(WINDOW)), key_live > 0.5
    )
    bias[...] = jnp.where(allowed, 0.0, MASKED)

    over(0, 2)
    over(1, 1)
    for k in ORDER[:3]:
        arrive(gb_tree, k)
    for i, copy in enumerate(sends):
        pl.when(me >= i + 1)(copy.wait_recv)

    all_kv = kv_ref.reshape((BEHIND + 1) * rows, 512)
    for h in range(4):
        scores = trail_product(q_ref[h], all_kv[:, :256]) + bias[...]
        raised = jnp.exp(scores - jnp.max(scores, axis=1, keepdims=True))
        share = raised * (1.0 / jnp.sum(raised, axis=1, keepdims=True))
        probs[h] = share
        att[:, 256 * h : 256 * (h + 1)] = matmul(
            share.astype(jnp.bfloat16), all_kv[:, 256:]
        ).astype(jnp.bfloat16)
        if h == 1:
            for k in ORDER[3:7]:
                arrive(gb_tree, k)
    for k in WHOLE:
        passes[2][k].wait_recv()
    keep = jnp.where(live_col, 1.0, 0.0)
    mid = x_ref[...].astype(jnp.float32) + keep * matmul(att[...], wo.reshape(1024, width)[...])
    middle[...] = mid
    inverse2 = lax.rsqrt(jnp.mean(mid * mid, axis=1, keepdims=True) + EPSILON)
    normed2[...] = (mid * inverse2 * gain2).astype(jnp.bfloat16)
    for src, dst in (
        (miscs, o_misc),
        (wqkv, o_qkv),
        (wo, o_wo),
        (normed1, o_normed1),
        (q_ref, o_q),
        (kv_ref, o_kv),
        (probs, o_probs),
        (att, o_att),
        (middle, o_middle),
        (normed2, o_normed2),
        (rope, o_rope),
    ):
        local(src, dst)
    over(2, 0)
    over(3, 3)
    for k in ORDER[7:]:
        arrive(gb_tree, k)
    for copy in gu_passes.values():
        copy.wait_recv()
    waited = [id(copy) for copy in sends] + [id(turn[0])]
    for copy in locals_[9:]:
        if copy is not None:
            copy.wait()
    pl.when(away)(turn[0].wait_send)
    for i, copy in enumerate(sends):
        pl.when(me + (i + 1) < 8)(copy.wait_send)
    for copy in wire.made:
        if id(copy) not in waited:
            copy.wait_send()


ANY = pl.BlockSpec(memory_space=pl.ANY)


def comm_params(collective_id):
    return pltpu.CompilerParams(
        collective_id=collective_id, has_side_effects=True, vmem_limit_bytes=VMEM_LIMIT
    )


def front(tokens, cot, misc, freq, w_query, w_keyval, w_out, w_gate, w_up):
    bf, f32 = jnp.bfloat16, jnp.float32
    rows, width = tokens.shape
    keys = (BEHIND + 1) * rows
    outs = [
        ((8, 16, 256), bf),
        ((8, 144, 1536), bf),
        ((8, 128, width), bf),
        ((8, 144, 2 * FF_PAD), bf),
        ((4, 2, rows, width), bf),
        ((rows, width), bf),
        ((4, rows, 256), bf),
        ((BEHIND + 1, rows, 512), bf),
        ((4, rows, keys), f32),
        ((rows, 1024), bf),
        ((rows, width), f32),
        ((rows, width), bf),
        ((rows, 256), f32),
    ]
    scratch = [
        ((rows, width), bf),
        ((rows, width), bf),
        ((8, 16, 256), bf),
        ((8, 128), f32),
        ((8, 144, 1536), bf),
        ((8, 128, width), bf),
        (w_gate.shape, bf),
        (w_up.shape, bf),
        ((8, 144, 2 * FF_PAD), bf),
        ((rows, width), bf),
        ((rows, width), bf),
        ((4, rows, 256), bf),
        ((BEHIND + 1, rows, 512), bf),
        ((rows, keys), f32),
        ((4, rows, keys), f32),
        ((rows, 1024), bf),
        ((rows, width), f32),
        ((rows, width), bf),
        ((rows, 256), f32),
    ]
    return pl.pallas_call(
        front_kernel,
        out_shape=tuple(jax.ShapeDtypeStruct(*o) for o in outs),
        in_specs=[ANY] * 9,
        out_specs=(ANY,) * len(outs),
        scratch_shapes=[pltpu.VMEM(*v) for v in scratch]
        + [
            pltpu.SemaphoreType.DMA((32,)),
            pltpu.SemaphoreType.DMA((112,)),
            pltpu.SemaphoreType.DMA((112,)),
        ],
        compiler_params=comm_params(1),
        name="attention_forward",
    )(tokens, cot, misc, freq, w_query, w_keyval, w_out, w_gate, w_up)


def unpack_kernel(both, gate, up):
    for d in range(8):
        for t in range(PAIRS):
            size = min(128, FF_DEV - 128 * t)
            start = FF_DEV * d + 128 * t
            for k, out in enumerate((gate, up)):
                half, q, first = (k, 3, 0) if t == 3 else (t // 4, t % 4, 128 * k)
                block = both[half, q, d, :, first : first + size]
                out[:, start : start + size] = block.astype(jnp.float32)


def unpack_gate_up(both):
    rows = both.shape[3]
    out = jax.ShapeDtypeStruct((rows, 8 * FF_DEV), jnp.float32)
    spec = pl.BlockSpec((16, 8 * FF_DEV), lambda i: (i, 0))
    return pl.pallas_call(
        unpack_kernel,
        grid=(rows // 16,),
        out_shape=(out, out),
        in_specs=[pl.BlockSpec((2, 4, 8, 16, 256), lambda i: (0, 0, 0, i, 0))],
        out_specs=(spec, spec),
        compiler_params=pltpu.CompilerParams(vmem_limit_bytes=VMEM_LIMIT),
        name="unpack_gate_up",
    )(both)


ROOT = 0.7978845608028654
CUBE = 0.044715


def ff_kernel(
    own_n, gb_all, wgu_all, wd_all,
    o_gn, o_pb, o_pgu, o_pd,
    nbuf, gb, wgu, wd, gh, hid, ggu, part_g, part_b, out_f32, dgu,
    g_whole, g_half, dd, r_d, d_whole, d_half_a, d_half_b, z_d,
    r_gu, n_turned,
    local_sems, send_sems, recv_sems,
):
    place = Place()
    wire = Wire(send_sems, recv_sems)
    loads = [
        pltpu.make_async_copy(src, dst, local_sems.at[k])
        for k, (src, dst) in enumerate(
            [(own_n, nbuf.at[0, 0]), (wd_all, wd.at[pl.ds(0, FF_DEV)]), (gb_all, gb), (wgu_all, wgu)]
        )
    ]
    for load in loads:
        load.start()
    core, y = place.core, place.y
    sibling, low = place.device(sibling=1), place.device(swap_lo=1)
    greet(
        [place.device(dx=1), place.device(dx=3), place.device(mirror=1), sibling, low]
        + [place.device(dy=1), place.device(dy=3)]
    )

    def cut(ref, part):
        return ref if part == 0 else ref.at[pl.ds((part - 1) * 96, 96)]

    slot_n = lambda j, p: nbuf.at[j, p]
    tree = gather_tree(wire, place.over_group, HOPS, nbuf.at[0, 0], slot_n, cut, False)
    sum_g = SumTree(
        wire, place.over_group, HOPS, lambda j, p: part_g.at[j, p], cut,
        [g_whole.at[k] for k in range(3)] + [g_half.at[k] for k in range(8)],
    )

    def cut_d(ref, part):
        start, size = ((0, 1152), (0, 640), (640, 512))[part]
        return ref.at[:, pl.ds(start, size)]

    quarter_d = dd.at[core, y]
    swap_d = wire.copy(dd.at[1 - core], r_d, sibling)
    sum_d = SumTree(
        wire, lambda dx, mirror: place.device(dy=dx), RING,
        lambda j, p: dd.at[core, (y + STEPS[j]) % 4], cut_d,
        [d_whole.at[0], d_whole.at[1], d_half_a, d_half_b],
    )
    cross_d = wire.copy(quarter_d, z_d, low)

    swap_gu = wire.copy(dgu.at[1 - core], r_gu, sibling)
    loads[0].wait()
    for k in (0, 1, 2):
        tree[k].start()
    wd[FF_DEV:] = jnp.zeros((FF_PAD - FF_DEV, wd.shape[1]), wd.dtype)
    loads[1].wait()
    loads[2].wait()

    def back_hidden(j):
        rows = jnp.concatenate([gb[j, 0], gb[j, 1]], axis=0)
        gh[j] = trail_product(rows, wd[...])

    def forward(j):
        rows = jnp.concatenate([nbuf[j, 0], nbuf[j, 1]], axis=0)

        def tile(t, carry):
            columns = pl.ds(pl.multiple_of(t * 256, 256), 256)
            narrow = pl.ds(pl.multiple_of(t * 128, 128), 128)
            both = matmul(rows, wgu[:, columns])
            gate, up = both[:, :128], both[:, 128:]
            square = gate * gate
            curve = jnp.tanh(ROOT * gate * (1.0 + CUBE * square))
            half_up = 0.5 * (1.0 + curve)
            active = gate * half_up
            slope = half_up + 0.5 * gate * (1.0 - curve * curve) * (
                ROOT * (1.0 + 3.0 * CUBE * square)
            )
            back = gh[j, :, narrow]
            hid[j, :, narrow] = (active * up).astype(jnp.bfloat16)
            ggu[j, :, columns] = jnp.concatenate(
                [(back * up * slope).astype(jnp.bfloat16), (back * active).astype(jnp.bfloat16)],
                axis=1,
            )
            return carry

        lax.fori_loop(0, PAIRS, tile, 0)

    def back_normed(j):
        for start, size in ((0, 512), (512, 512), (1024, 128)):
            block = trail_product(ggu[j], wgu[start : start + size, :]).astype(jnp.bfloat16)
            part_g[j, 0, :, start : start + size] = block[:192]
            part_g[j, 1, :, start : start + size] = block[192:]

    def down(j):
        for start, size in ((0, 512), (512, 512), (1024, 128)):
            block = matmul(hid[j], wd[:, start : start + size]).astype(jnp.bfloat16)
            part_b[j, 0, :, start : start + size] = block[:192]
            part_b[j, 1, :, start : start + size] = block[192:]

    hid_rows = hid.reshape(4 * 384, FF_PAD)
    ggu_rows = ggu.reshape(4 * 384, 2 * FF_PAD)
    gb_rows = gb.reshape(4 * 384, 1152)
    dd_rows = dd.reshape(FF_PAD, 1152)
    dgu_rows = dgu.reshape(2, 4, 1152, 256)

    def turn_rows(j):
        rows = jnp.concatenate([nbuf[j, 0], nbuf[j, 1]], axis=0)
        n_turned[:, 384 * j : 384 * (j + 1)] = rows.T

    def grad_half(half):
        def tile(q, carry):
            columns = pl.ds(pl.multiple_of((half * 4 + q) * 256, 256), 256)
            dgu_rows[half, q] = matmul(n_turned[...], ggu_rows[:, columns]).astype(jnp.bfloat16)
            return carry

        lax.fori_loop(0, 3, tile, 0)

    dgu[:, 3, :, :, 128:] = jnp.zeros((2, 8, 144, 128), jnp.bfloat16)
    for j in range(4):
        back_hidden(j)
    for k in (0, 1, 2):
        arrive(tree, k)
    loads[3].wait()
    forward(0)
    turn_rows(0)
    for k in (3, 4, 8, 7):
        arrive(tree, k)
    forward(1)
    forward(2)
    turn_rows(1)
    turn_rows(2)
    for k in (5, 6, 9, 10):
        arrive(tree, k)
    forward(3)
    back_normed(3)
    sum_g.start(10, 9, 6, 5)
    back_normed(1)
    back_normed(2)
    for start, size in ((0, 512), (512, 512), (1024, 128)):
        dd_rows[:, start : start + size] = lead_product(
            hid_rows[...], gb_rows[:, start : start + size]
        ).astype(jnp.bfloat16)
    swap_d.start()
    sum_g.send_near()
    back_normed(0)
    turn_rows(3)
    middle_tile = matmul(n_turned[...], ggu_rows[:, 768:1024]).astype(jnp.bfloat16)
    dgu_rows[0, 3, :, :128] = middle_tile[:, :128]
    dgu_rows[1, 3, :, :128] = middle_tile[:, 128:]
    swap_d.wait_recv()

    def add_d(i, carry):
        add_into(dd.at[core, i], r_d.at[i])
        return carry

    lax.fori_loop(0, 4, add_d, 0)
    sum_d.start(2, 3)
    sum_g.send_next()
    sum_g.send_last()
    grad_half(1 - core)
    swap_gu.start()
    sum_d.absorb(2, 3)
    sum_d.start(0, 1)
    grad_half(core)
    down(0)
    down(1)
    sum_d.absorb(0, 1)
    cross_d.start()
    down(2)
    down(3)
    store_b = pltpu.make_async_copy(part_b, o_pb, local_sems.at[5])
    store_b.start()
    swap_gu.wait_recv()

    def add_gu(i, carry):
        add_into(dgu.reshape(2, 32, 144, 256).at[core, i], r_gu.reshape(32, 144, 256).at[i])
        return carry

    lax.fori_loop(0, 32, add_gu, 0)
    store_gu = pltpu.make_async_copy(dgu.at[core], o_pgu, local_sems.at[4])
    store_gu.start()
    cross_d.wait_recv()
    cross_d.wait_send()
    add_into(quarter_d, z_d)
    store_d = pltpu.make_async_copy(quarter_d, o_pd, local_sems.at[7])
    store_d.start()
    out_f32[...] = sum_g.finish()
    store_g = pltpu.make_async_copy(out_f32, o_gn, local_sems.at[6])
    store_g.start()
    for store in (store_b, store_gu, store_g, store_d):
        store.wait()
    for copy in wire.made:
        if copy is not cross_d:
            copy.wait_send()


def feed_forward(own_n, gb_all, wgu_all, wd_all):
    bf, f32 = jnp.bfloat16, jnp.float32
    vm = pltpu.VMEM
    tokens, width = own_n.shape
    sums = [vm((3, tokens, width), bf), vm((8, tokens // 2, width), bf)]
    return pl.pallas_call(
        ff_kernel,
        out_shape=(
            jax.ShapeDtypeStruct((tokens, width), f32),
            jax.ShapeDtypeStruct((4, 2, tokens, width), bf),
            jax.ShapeDtypeStruct((4, 8, 144, 256), bf),
            jax.ShapeDtypeStruct((112, width), bf),
        ),
        in_specs=[ANY] * 4,
        out_specs=(ANY,) * 4,
        scratch_shapes=[
            vm((4, 2, tokens, width), bf),
            vm((4, 2, tokens, width), bf),
            vm(wgu_all.shape, bf),
            vm((FF_PAD, width), bf),
            vm((4, 2 * tokens, FF_PAD), f32),
            vm((4, 2 * tokens, FF_PAD), bf),
            vm((4, 2 * tokens, 2 * FF_PAD), bf),
            vm((4, 2, tokens, width), bf),
            vm((4, 2, tokens, width), bf),
            vm((tokens, width), f32),
            vm((2, 4, 8, 144, 256), bf),
        ]
        + sums
        + [
            vm((2, 4, 112, width), bf),
            vm((4, 112, width), bf),
            vm((2, 112, width), bf),
            vm((112, 640), bf),
            vm((112, 512), bf),
            vm((112, width), bf),
            vm((4, 8, 144, 256), bf),
            vm((width, 8 * tokens), bf),
        ]
        + [
            pltpu.SemaphoreType.DMA((8,)),
            pltpu.SemaphoreType.DMA((40,)),
            pltpu.SemaphoreType.DMA((40,)),
        ],
        compiler_params=comm_params(2),
        name="feed_forward",
    )(own_n, gb_all, wgu_all, wd_all)


def back_kernel(
    p_gu, p_d, part_b_all, gn2_all, middle_all, miscs_all, tokens, cot, rope_all, q_all, kv_all,
    probs_all, att_all, wqkv_all, wo_all, normed1_all,
    o_gu, o_d, o_q, o_kv, o_wo, o_out, o_grad,
    h_gu, gu_whole, gu_half, z_gu, f_gu, piece_d,
    part_b, b_whole, b_half, gn2, middle, miscs, x_ref, cot_ref, rope, q_ref, kv_ref, probs, att,
    wqkv, wo, normed1, dq, r_q, q_whole, q_half, dkv, r_kv, kv_whole, kv_half,
    dwo, r_wo, w_whole, w_half,
    h_gain, r_gain, g_whole, g_half, gkv, kv_out, kv_in, gproj, gmid, out_bf,
    s_wo, y_wo, z_wo, s_q, y_q, z_q, s_kv, y_kv, z_kv,
    local_sems, send_sems, recv_sems,
):
    place = Place()
    wire = Wire(send_sems, recv_sems)
    core, me, y, rep = place.core, place.shard, place.y, place.rep
    rows, width = tokens.shape
    at = place.shard_at
    others = [(j, p) for p in (0, 1) for j in range(4) if (j, p) != (0, 0)]
    group = [place.device(dx=STEPS[j], mirror=p) for j, p in others]
    sequence = [(rep, at(j, 1)) for j in range(4)]
    sibling = place.device(sibling=1)
    column = [place.device(dy=d) for d in (1, 3, 2)]
    low = place.device(swap_lo=1)
    locals_ = []

    def local(src, dst):
        copy = pltpu.make_async_copy(src, dst, local_sems.at[len(locals_)])
        copy.start()
        locals_.append(copy)
        return copy

    loads = [
        local(src, dst)
        for src, dst in (
            (miscs_all, miscs),
            (gn2_all, gn2),
            (middle_all, middle),
            (cot, cot_ref),
            (att_all, att),
            (wo_all, wo),
        )
    ]
    load_gu = local(p_gu, h_gu)
    greet([sibling, low] + group + column + sequence)
    loads_heads = [
        local(src, dst)
        for src, dst in ((q_all, q_ref), (kv_all, kv_ref), (probs_all, probs), (rope_all, rope))
    ]
    load_d = local(p_d, piece_d)
    load_b = local(part_b_all, part_b)
    load_x = local(tokens, x_ref)
    load_n = local(normed1_all, normed1)
    load_w = local(wqkv_all, wqkv)
    loaded = len(locals_)

    def over_y(dx, mirror):
        return place.device(dy=dx)

    def cut_lead(ref, part):
        return ref if part == 0 else ref.at[pl.ds((part - 1) * 4, 4)]

    def cut_rows(size):
        def cut(ref, part):
            return ref if part == 0 else ref.at[pl.ds((part - 1) * size, size)]

        return cut

    def cut_lanes(size):
        def cut(ref, part):
            return ref if part == 0 else ref.at[:, pl.ds((part - 1) * size, size)]

        return cut

    def cut_d(ref, part):
        start, size = ((0, width), (0, 640), (640, 512))[part]
        return ref.at[:, pl.ds(start, size)]

    def added(target, source, count):
        def one(i, carry):
            add_into(target.at[i], source.at[i])
            return carry

        lax.fori_loop(0, count, one, 0)

    chunks = [pl.ds(0, 80), pl.ds(80, 64)]
    sums_gu = [
        SumTree(
            wire, over_y, RING,
            lambda j, p, c=c: h_gu.at[(y + STEPS[j]) % 4, :, c], cut_lead,
            [gu_whole.at[0, :, c], gu_whole.at[1, :, c], gu_half.at[0, :, c], gu_half.at[1, :, c]],
        )
        for c in chunks
    ]
    quarters = [h_gu.at[y, :, c] for c in chunks]
    crossings_gu = [wire.copy(h_gu.at[y, :, c], z_gu.at[:, c], low) for c in chunks]
    turns = [
        [
            wire.copy(h_gu.at[y, at(j, p), c], f_gu.at[me, c], device)
            for (j, p), device in zip(others, group)
        ]
        for c in chunks
    ]
    slots_gu = [lambda j, p, c=c: o_gu.at[core, (y + STEPS[j]) % 4, :, c] for c in chunks]
    trees_gu = [
        gather_tree(wire, over_y, RING, f_gu.at[:, c], slot, cut_lead, True)
        for c, slot in zip(chunks, slots_gu)
    ]
    passes_gu = [
        [
            wire.copy(f_gu.at[:, c] if j == 0 else slot(j, 0), slot(j, 0), sibling)
            for j in range(4)
        ]
        for c, slot in zip(chunks, slots_gu)
    ]

    def cross(i):
        sums_gu[i].absorb(0, 1)
        crossings_gu[i].start()

    def turn(i):
        crossings_gu[i].wait_recv()
        crossings_gu[i].wait_send()
        added(quarters[i], z_gu.at[:, chunks[i]], 8)
        for copy in turns[i]:
            copy.start()
        f_gu[me, chunks[i]] = h_gu[y, me, chunks[i]]

    def spread(i):
        for copy in turns[i]:
            copy.wait_recv()
        for copy in (trees_gu[i][0], trees_gu[i][1], passes_gu[i][0]):
            copy.start()
        local(f_gu.at[:, chunks[i]], slots_gu[i](0, 0))

    def spread_on(i, k):
        arrive(trees_gu[i], k, RING_ONWARD)
        if k != 2:
            passes_gu[i][(2, 1, None, 3)[k]].start()

    load_gu.wait()
    sums_gu[0].start(2, 3)
    sums_gu[1].start(2, 3)

    for load in loads:
        load.wait()
    as_float = [miscs[s].astype(jnp.float32) for s in range(8)]
    gain1 = jnp.concatenate([m[0:1, :144] for m in as_float], axis=1)
    gain2 = jnp.concatenate([m[1:2, :144] for m in as_float], axis=1)
    row = lax.broadcasted_iota(jnp.int32, (rows, 1), 0).astype(jnp.float32)
    keep = jnp.where(row < miscs[me].astype(jnp.float32)[2:3, :1], 1.0, 0.0)
    mid = middle[...]
    inverse2 = lax.rsqrt(jnp.mean(mid * mid, axis=1, keepdims=True) + EPSILON)
    scaled2 = mid * inverse2
    grad2 = gn2[...]
    grad_gain2 = jnp.sum(grad2 * scaled2, axis=0, keepdims=True)
    grad2 = grad2 * gain2
    grad_mid = cot_ref[...].astype(jnp.float32) + inverse2 * (
        grad2 - scaled2 * jnp.mean(grad2 * scaled2, axis=1, keepdims=True)
    )
    gmid[...] = grad_mid
    grad_attn = (keep * grad_mid).astype(jnp.bfloat16)
    for start in range(0, width, 384):
        block = lead_product(att[...], grad_attn[:, start : start + 384]).astype(jnp.bfloat16)
        block = block.reshape(8, 2, 64, 384)
        dwo[0, :, :, start : start + 384] = block[:, 0]
        dwo[1, :, :, start : start + 384] = block[:, 1]
    swap_wo = wire.copy(dwo.at[1 - core], r_wo, sibling)
    swap_wo.start()
    grad_att = trail_product(grad_attn, wo.reshape(1024, width)[...]).astype(jnp.bfloat16)

    sum_b = SumTree(
        wire, place.over_group, HOPS, lambda j, p: part_b.at[j, p], cut_rows(96),
        [b_whole.at[k] for k in range(3)] + [b_half.at[k] for k in range(8)],
    )
    load_b.wait()
    sum_b.start(10, 9, 6, 5)
    for tree in sums_gu:
        tree.absorb(2, 3)
        tree.start(0, 1)

    for load in loads_heads:
        load.wait()
    keys = (BEHIND + 1) * rows
    all_kv = kv_ref.reshape(keys, 512)
    flat = gkv.reshape(keys, 512)
    cosine, sine_part = rope[:, :128], rope[:, 128:]
    scaling = 256 ** (-0.5)

    def turned_back(vectors):
        first, second = vectors[:, :128], vectors[:, 128:]
        return jnp.concatenate(
            [first * cosine + second * sine_part, second * cosine - first * sine_part], axis=1
        )

    for h in range(4):
        share = probs[h]
        share_low = share.astype(jnp.bfloat16)
        grad_h = grad_att[:, 256 * h : 256 * (h + 1)]
        grad_probs = trail_product(grad_h, all_kv[:, 256:])
        delta = jnp.sum(share * grad_probs, axis=1, keepdims=True)
        grad_scores = (share * (grad_probs - delta)).astype(jnp.bfloat16)
        grad_keys = lead_product(grad_scores, q_ref[h])
        grad_values = lead_product(share_low, grad_h)
        if h == 0:
            flat[:, :256] = grad_keys
            flat[:, 256:] = grad_values
        else:
            flat[:, :256] += grad_keys
            flat[:, 256:] += grad_values
        grad_q = matmul(grad_scores, all_kv[:, :256])
        gproj[:, 256 * h : 256 * (h + 1)] = (turned_back(grad_q) * scaling).astype(jnp.bfloat16)
    sends = []
    for i in range(1, BEHIND + 1):
        kv_out[i - 1] = gkv[i].astype(jnp.bfloat16)
        sends.append(
            wire.copy(kv_out.at[i - 1], kv_in.at[i - 1], (rep, jnp.maximum(me - i, 0)))
        )
        pl.when(me >= i)(sends[-1].start)

        @pl.when(me + i > 7)
        def _():
            kv_in[i - 1] = jnp.zeros(kv_in.shape[1:], kv_in.dtype)

    load_n.wait()
    dq_rows = dq.reshape(2, width, 512)
    for t in range(4):
        dq_rows[t // 2, :, 256 * (t % 2) : 256 * (t % 2 + 1)] = lead_product(
            normed1[...], gproj[:, 256 * t : 256 * (t + 1)]
        ).astype(jnp.bfloat16)
    swap_q = wire.copy(dq.at[1 - core], r_q, sibling)
    swap_q.start()
    cross(0)
    swap_wo.wait_recv()
    added(dwo.at[core], r_wo, 8)
    sum_wo = SumTree(
        wire, place.over_group, HOPS, lambda j, p: dwo.at[core, at(j, p)], cut_rows(32),
        [w_whole.at[k] for k in range(3)] + [w_half.at[k] for k in range(8)],
    )
    sum_wo.start(10, 9, 6, 5)
    swap_q.wait_recv()
    added(dq.at[core], r_q, 8)
    sum_q = SumTree(
        wire, place.over_group, HOPS, lambda j, p: dq.at[core, at(j, p)], cut_lanes(256),
        [q_whole.at[k] for k in range(3)] + [q_half.at[k] for k in range(8)],
    )
    sum_q.start(10, 9, 6, 5)

    load_d.wait()
    slot_d = lambda j, p: o_d.at[core, (y + STEPS[j]) % 4]
    tree_d = gather_tree(wire, over_y, RING, piece_d, slot_d, cut_d, True)
    pass_d = [
        wire.copy(piece_d if j == 0 else slot_d(j, 0), slot_d(j, 0), sibling) for j in range(4)
    ]
    for copy in (tree_d[0], tree_d[1], pass_d[0]):
        copy.start()
    local(piece_d, slot_d(0, 0))
    cross(1)
    sum_wo.send_near()
    turn(0)

    grad_kv = gkv[0]
    for i, copy in enumerate(sends):
        pl.when(me + (i + 1) <= 7)(copy.wait_recv)
        grad_kv = grad_kv + kv_in[i].astype(jnp.float32)
    gproj[:, 1024:1280] = turned_back(grad_kv[:, :256]).astype(jnp.bfloat16)
    gproj[:, 1280:1536] = grad_kv[:, 256:].astype(jnp.bfloat16)
    dkv_rows = dkv.reshape(2, width, 256)
    for t in range(2):
        dkv_rows[t] = lead_product(
            normed1[...], gproj[:, 1024 + 256 * t : 1280 + 256 * t]
        ).astype(jnp.bfloat16)
    swap_kv = wire.copy(dkv.at[1 - core], r_kv, sibling)
    swap_kv.start()
    sum_wo.send_next()
    sum_q.send_near()
    turn(1)
    load_x.wait()
    load_w.wait()
    inputs = x_ref[...].astype(jnp.float32)
    inverse1 = lax.rsqrt(jnp.mean(inputs * inputs, axis=1, keepdims=True) + EPSILON)
    scaled1 = inputs * inverse1
    grad1 = trail_product(gproj[...], wqkv.reshape(width, 1536)[...])
    grad_gain1 = jnp.sum(grad1 * scaled1, axis=0, keepdims=True)
    grad1 = grad1 * gain1
    gmid[...] += inverse1 * (grad1 - scaled1 * jnp.mean(grad1 * scaled1, axis=1, keepdims=True))
    local(gmid, o_grad)
    for s in range(8):
        cols = slice(144 * s, 144 * (s + 1))
        both = jnp.concatenate(
            [grad_gain1[:, cols], grad_gain2[:, cols], jnp.zeros((14, 144), jnp.float32)], axis=0
        )
        both = jnp.concatenate([both, jnp.zeros((16, 112), jnp.float32)], axis=1)
        h_gain[0, s] = both.astype(jnp.bfloat16)
        h_gain[1, s] = both.astype(jnp.bfloat16)
    swap_gain = wire.copy(h_gain.at[1], r_gain, sibling)
    swap_gain.start()
    swap_kv.wait_recv()
    added(dkv.at[core], r_kv, 8)
    sum_kv = SumTree(
        wire, place.over_group, HOPS, lambda j, p: dkv.at[core, at(j, p)], cut_lanes(128),
        [kv_whole.at[k] for k in range(3)] + [kv_half.at[k] for k in range(8)],
    )
    sum_kv.start(10, 9, 6, 5)
    swap_gain.wait_recv()
    added(h_gain.at[0], r_gain, 8)
    sum_gain = SumTree(
        wire, place.over_group, HOPS, lambda j, p: h_gain.at[0, at(j, p)], cut_lanes(128),
        [g_whole.at[k] for k in range(3)] + [g_half.at[k] for k in range(8)],
    )
    sum_gain.start(10, 9, 6, 5)
    spread(0)
    sum_wo.send_last()
    sum_q.send_next()
    sum_q.send_last()
    sum_kv.send_near()
    sum_gain.send_near()
    spread(1)
    for k in (0, 1):
        arrive(tree_d, k, RING_ONWARD)
        pass_d[(2, 1)[k]].start()
    sum_b.send_near()
    sum_kv.send_next()
    sum_gain.send_next()
    sum_kv.send_last()
    sum_gain.send_last()
    for k in (0, 1):
        spread_on(0, k)

    def over_column(source, landing):
        copies = [
            wire.copy(source.at[(y + d) % 4], landing.at[i], device)
            for i, (d, device) in enumerate(zip((1, 3, 2), column))
        ]
        for copy in copies:
            copy.start()
        return copies

    def over_low(copies, source, landing, other):
        for copy in copies:
            copy.wait_recv()
        mine = source[y].astype(jnp.float32)
        for i in range(3):
            mine = mine + landing[i].astype(jnp.float32)
        source[y] = mine.astype(jnp.bfloat16)
        crossing = wire.copy(source.at[y], other, low)
        crossing.start()
        return crossing

    def to_all(crossing, source, other, slot):
        crossing.wait_recv()
        crossing.wait_send()
        add_into(source.at[y], other)
        made = [wire.copy(source.at[y], slot(core, y), device) for device in column + [sibling]]
        for copy in made:
            copy.start()
        local(source.at[y], slot(core, y))
        return made

    def pass_on(made, slot):
        ends = [made[3]]
        for d, copy in zip((3, 1, 2), made):
            copy.wait_recv()
            held = slot(core, (y + d) % 4)
            ends.append(wire.copy(held, held, sibling))
            ends[-1].start()
        return ends

    slot_wo = lambda c, q: o_wo.at[c, q]
    slot_q = lambda c, q: o_q.at[:, pl.ds(pl.multiple_of(c * 512 + q * 128, 128), 128)]
    slot_kv = lambda c, q: o_kv.at[c, q]
    s_wo[...] = sum_wo.finish().astype(jnp.bfloat16).reshape(4, 16, width)
    over_wo = over_column(s_wo, y_wo)
    total = sum_q.finish().astype(jnp.bfloat16)
    for q in range(4):
        s_q[q] = total[:, 128 * q : 128 * (q + 1)]
    over_q = over_column(s_q, y_q)
    for k in (0, 1):
        spread_on(1, k)
    sum_b.send_next()
    cross_wo = over_low(over_wo, s_wo, y_wo, z_wo)
    cross_q = over_low(over_q, s_q, y_q, z_q)
    total = sum_kv.finish().astype(jnp.bfloat16)
    s_kv[0] = total[:, :128]
    s_kv[1] = total[:, 128:]
    total = sum_gain.finish()
    s_kv[2] = jnp.concatenate(
        [total[:, :128], total[:, 128:], jnp.zeros((112, 128), jnp.float32)], axis=0
    ).astype(jnp.bfloat16)
    s_kv[3] = jnp.zeros((144, 128), jnp.bfloat16)
    over_kv = over_column(s_kv, y_kv)
    sum_b.send_last()
    for k in (2, 3):
        arrive(tree_d, k, RING_ONWARD)
    pass_d[3].start()
    all_wo = to_all(cross_wo, s_wo, z_wo, slot_wo)
    all_q = to_all(cross_q, s_q, z_q, slot_q)
    cross_kv = over_low(over_kv, s_kv, y_kv, z_kv)
    for k in (2, 3):
        spread_on(0, k)
    all_kv_sum = to_all(cross_kv, s_kv, z_kv, slot_kv)
    ends = pass_on(all_wo, slot_wo) + pass_on(all_q, slot_q)
    for k in (2, 3):
        spread_on(1, k)
    out_bf[...] = (middle[...] + keep * sum_b.finish()).astype(jnp.bfloat16)
    local(out_bf, o_out)
    ends += pass_on(all_kv_sum, slot_kv)
    for copy in pass_d + passes_gu[0] + passes_gu[1] + ends:
        copy.wait_recv()
    for copy in locals_[loaded:]:
        copy.wait()
    for i, copy in enumerate(sends):
        pl.when(me >= i + 1)(copy.wait_send)
    waited = [id(copy) for copy in sends + crossings_gu + [cross_wo, cross_q, cross_kv]]
    for copy in wire.made:
        if id(copy) not in waited:
            copy.wait_send()


def back(*args):
    bf, f32 = jnp.bfloat16, jnp.float32
    width = 1152
    rows = args[6].shape[0]
    outs = [
        ((2, 4, 8, 144, 256), bf),
        ((2, 4, 112, width), bf),
        ((144, 1024), bf),
        ((2, 4, 144, 128), bf),
        ((2, 4, 16, width), bf),
        ((rows, width), bf),
        ((rows, width), f32),
    ]
    scratch = [
        ((4, 8, 144, 256), bf),
        ((2, 8, 144, 256), bf),
        ((2, 4, 144, 256), bf),
        ((8, 144, 256), bf),
        ((8, 144, 256), bf),
        ((112, width), bf),
        ((4, 2, rows, width), bf),
        ((3, rows, width), bf),
        ((8, rows // 2, width), bf),
    ]
    scratch += [(a.shape, a.dtype) for a in args[3:16]]
    for whole, half in (
        ((144, 512), (144, 256)),
        ((144, 256), (144, 128)),
        ((64, width), (32, width)),
        ((16, 256), (16, 128)),
    ):
        scratch += [((2, 8, *whole), bf), ((8, *whole), bf), ((3, *whole), bf), ((8, *half), bf)]
    scratch += [
        ((BEHIND + 1, rows, 512), f32),
        ((BEHIND, rows, 512), bf),
        ((BEHIND, rows, 512), bf),
        ((rows, 1536), bf),
        ((rows, width), f32),
        ((rows, width), bf),
    ]
    for piece in ((16, width), (144, 128), (144, 128)):
        scratch += [((4, *piece), bf), ((3, *piece), bf), (piece, bf)]
    return pl.pallas_call(
        back_kernel,
        out_shape=tuple(jax.ShapeDtypeStruct(*o) for o in outs),
        in_specs=[ANY] * 16,
        out_specs=(ANY,) * len(outs),
        scratch_shapes=[pltpu.VMEM(*v) for v in scratch]
        + [
            pltpu.SemaphoreType.DMA((40,)),
            pltpu.SemaphoreType.DMA((176,)),
            pltpu.SemaphoreType.DMA((176,)),
        ],
        compiler_params=comm_params(3),
        name="attention_backward",
    )(*args)


def on_device(
    tokens, lengths, attn_gain, w_query, w_keyval, w_out, mlp_gain, w_gate, w_up, w_down, cotangent
):
    width = tokens.shape[1]
    heads_all = w_query.shape[1]
    live_count = lengths[0, 0]
    row = lax.broadcasted_iota(jnp.int32, (16, 256), 0)
    wide = lambda gain: jnp.pad(gain, (0, 112))[None]
    misc = jnp.where(
        row == 0,
        wide(attn_gain),
        jnp.where(row == 1, wide(mlp_gain), live_count.astype(jnp.bfloat16)),
    )
    frequency = np.power(10000.0, -2.0 * np.arange(128) / 256).astype(np.float32)
    (
        miscs, qkv_all, out_all, gu_all, branch_all,
        normed1, queries, all_kv, probs, attended, middle, normed2, rope,
    ) = front(
        tokens, cotangent, misc, jnp.asarray(np.tile(frequency[None], (8, 1))),
        w_query, w_keyval, w_out, w_gate, w_up,
    )
    grad_normed2, branch, grad_gu, grad_d = feed_forward(
        normed2, branch_all, gu_all.reshape(width, -1), w_down
    )
    sum_gu, sum_d, sum_q, sum_kv, sum_wo, outputs, grad_inputs = back(
        grad_gu, grad_d, branch, grad_normed2, middle, miscs, tokens, cotangent,
        rope, queries, all_kv, probs, attended, qkv_all, out_all, normed1,
    )
    grad_gate_w, grad_up_w = unpack_gate_up(sum_gu)
    gains = jnp.concatenate([sum_kv[0, 2, :2], sum_kv[0, 2, 16:18]], axis=1).astype(jnp.float32)
    grad_kv = sum_kv[:, :2].transpose(2, 0, 1, 3).reshape(144, 512).astype(jnp.float32)
    return (
        outputs,
        grad_inputs,
        gains[0, :144],
        sum_q.astype(jnp.float32),
        grad_kv,
        sum_wo.reshape(128, width).astype(jnp.float32),
        gains[1, :144],
        grad_gate_w,
        grad_up_w,
        sum_d.reshape(FF_PAD, width)[:FF_DEV].astype(jnp.float32),
    )


def solution(mesh):
    placed = (
        P(("rep", "shard"), None),
        P("rep", "shard"),
        P("shard"),
        P("shard", None),
        P("shard", None),
        P("shard", None),
        P("shard"),
        P("shard", None),
        P("shard", None),
        P("shard", None),
        P(("rep", "shard"), None),
    )
    return jax.shard_map(
        on_device,
        mesh=mesh,
        in_specs=placed,
        out_specs=(
            P(("rep", "shard"), None),
            P(("rep", "shard"), None),
            P("shard"),
            P("shard", None),
            P("shard", None),
            P("shard", None),
            P("shard"),
            P("shard", None),
            P("shard", None),
            P("shard", None),
        ),
        check_vma=False,
    )
```

```python
import functools

import jax
import jax.numpy as jnp
import numpy as np
from jax import lax
from jax.experimental import pallas as pl
from jax.experimental.pallas import tpu as pltpu
from jax.sharding import PartitionSpec as P

MESH = pl.DeviceIdType.MESH
WINDOW = 512
EPSILON = 1e-06
MASKED = -1e30
VMEM_LIMIT = 60 * 2**20
FF_DEV = 864
FF_PAD = 896
PAIRS = FF_PAD // 128
BEHIND = 4


def matmul(former, latter):
    return jnp.dot(former, latter, preferred_element_type=jnp.float32)


def lead_product(former, latter):
    return lax.dot_general(
        former, latter, (((0,), (0,)), ((), ())), preferred_element_type=jnp.float32
    )


def trail_product(former, latter):
    return lax.dot_general(
        former, latter, (((1,), (1,)), ((), ())), preferred_element_type=jnp.float32
    )


class Place:
    def __init__(self):
        rep, shard = lax.axis_index("rep"), lax.axis_index("shard")
        self.rep, self.shard = rep, shard
        self.y, self.z_lo, self.core = rep // 4, (rep // 2) % 2, rep % 2
        self.z_hi, self.x = shard // 4, shard % 4

    def device(self, dx=0, dy=0, mirror=0, swap_lo=0, sibling=0):
        z_lo = (self.z_lo + mirror + swap_lo) % 2
        rep = (((self.y + dy) % 4) * 2 + z_lo) * 2 + (self.core + sibling) % 2
        return (rep, ((self.z_hi + mirror) % 2) * 4 + (self.x + dx) % 4)

    def over_group(self, dx, mirror):
        return self.device(dx=dx, mirror=mirror)

    def shard_at(self, j, p):
        return ((self.z_hi + p) % 2) * 4 + (self.x + STEPS[j]) % 4


STEPS = (0, 1, 3, 2)


class Wire:
    def __init__(self, send_sems, recv_sems):
        self.send_sems, self.recv_sems, self.made = send_sems, recv_sems, []

    def copy(self, src, dst, device):
        k = len(self.made)
        made = pltpu.make_async_remote_copy(
            src_ref=src,
            dst_ref=dst,
            send_sem=self.send_sems.at[k],
            recv_sem=self.recv_sems.at[k],
            device_id=device,
            device_id_type=MESH,
        )
        self.made.append(made)
        return made

    def drain(self):
        for made in self.made:
            made.wait_send()


def greet(devices):
    barrier = pltpu.get_barrier_semaphore()
    for device in devices:
        pl.semaphore_signal(barrier, inc=1, device_id=device, device_id_type=MESH)
    pl.semaphore_wait(barrier, len(devices))


HOPS = (
    ((0, 0), (0, 1), 1, 0, 1),
    ((0, 0), (0, 1), 2, 0, 1),
    ((0, 0), (2, 0), 1, 1, 0),
    ((0, 0), (2, 0), 2, 1, 0),
    ((0, 0), (1, 0), 1, 3, 0),
    ((0, 0), (1, 0), 2, 3, 0),
    ((0, 1), (2, 1), 1, 1, 0),
    ((0, 1), (1, 1), 1, 3, 0),
    ((2, 0), (3, 0), 1, 1, 0),
    ((1, 0), (3, 0), 2, 3, 0),
    ((2, 0), (2, 1), 2, 0, 1),
    ((1, 0), (1, 1), 2, 0, 1),
    ((2, 1), (3, 1), 1, 1, 0),
    ((1, 1), (3, 1), 2, 3, 0),
)
FIRST = (0, 2, 5, 1, 3, 4)
ONWARD = {0: (6, 7), 2: (8,), 3: (10,), 5: (9, 11), 6: (12,), 11: (13,)}
SERVE = (0, 2, 5, 3, 11, 6, 1, 4, 7, 8, 9, 10, 12, 13)
WHOLE = {1: (0, 1), 3: (2, 0), 4: (1, 0), 7: (1, 1), 9: (3, 0), 10: (2, 1), 13: (3, 1)}
HOPS_FAR = tuple(HOPS[k] for k in (13, 12, 9, 8))
RING = (
    ((0, 0), (2, 0), 0, 1, 0),
    ((0, 0), (1, 0), 0, 3, 0),
    ((2, 0), (3, 0), 1, 1, 0),
    ((1, 0), (3, 0), 2, 3, 0),
)
RING_ONWARD = {0: (2,), 1: (3,)}


def gather_tree(wire, device_of, hops, own, slot, cut, absolute):
    copies = []
    for source, target, part, dx, mirror in hops:
        src = own if source == (0, 0) else slot(*source)
        dst = slot(*(source if absolute else target))
        copies.append(wire.copy(cut(src, part), cut(dst, part), device_of(dx, mirror)))
    return copies


def arrive(tree, k, after=ONWARD):
    tree[k].wait_recv()
    for n in after.get(k, ()):
        tree[n].start()


def add_into(target, source):
    target[...] = (target[...].astype(jnp.float32) + source[...].astype(jnp.float32)).astype(
        target.dtype
    )


class SumTree:
    def __init__(self, wire, device_of, hops, slot, cut, landings):
        self.hops, self.slot, self.cut, self.landings = hops, slot, cut, landings
        self.copies = [
            wire.copy(cut(slot(*target), part), landing, device_of((4 - dx) % 4, mirror))
            for (_, target, part, dx, mirror), landing in zip(hops, landings)
        ]

    def start(self, *hops):
        for k in hops:
            self.copies[k].start()

    def absorb(self, *hops):
        for k in hops:
            source, _, part, _, _ = self.hops[k]
            self.copies[k].wait_recv()
            add_into(self.cut(self.slot(*source), part), self.landings[k])

    def send_far(self):
        self.start(13, 12, 9, 8)

    def send_mid(self):
        self.start(7, 4, 10)

    def send_near(self):
        self.absorb(13)
        self.start(11)
        self.absorb(12)
        self.start(6)
        self.absorb(8)
        self.start(2)

    def send_next(self):
        self.absorb(9, 11)
        self.start(5)
        self.absorb(10)
        self.start(3)

    def send_last(self):
        self.absorb(6, 7)
        self.start(0)

    def finish(self, axis):
        halves = []
        for part in (1, 2):
            total = self.cut(self.slot(0, 0), part)[...].astype(jnp.float32)
            for k in (4, 2, 0):
                self.copies[k + part - 1].wait_recv()
                total = total + self.landings[k + part - 1][...].astype(jnp.float32)
            halves.append(total)
        return jnp.concatenate(halves, axis=axis)


def front_kernel(
    tokens, cot, misc, freq, w_query, w_keyval, w_out, w_gate, w_up,
    o_misc, o_qkv, o_wo, o_gu, o_gb, o_normed1, o_q, o_kv, o_probs, o_att, o_middle, o_normed2, o_rope,
    x_ref, cot_ref, miscs, freq_ref, wqkv, wo, gate, up, packed, gb_own, normed1, q_ref, kv_ref,
    bias, probs, att, middle, normed2, rope,
    local_sems, send_sems, recv_sems,
):
    place = Place()
    wire = Wire(send_sems, recv_sems)
    core, me, y = place.core, place.shard, place.y
    rows, width = tokens.shape
    at = place.shard_at
    others = [(j, p) for p in (0, 1) for j in range(4) if (j, p) != (0, 0)]
    group = [place.device(dx=STEPS[j], mirror=p) for j, p in others]
    sequence = [(place.rep, at(j, p)) for j, p in others]
    sibling = place.device(sibling=1)
    column = [place.device(dy=d) for d in (1, 3, 2)]
    locals_ = []

    def local(src, dst):
        copy = pltpu.make_async_copy(src, dst, local_sems.at[len(locals_)])
        copy.start()
        locals_.append(copy)
        return copy

    load_x = local(tokens, x_ref)
    load_cot = local(cot, cot_ref)
    load_misc = local(misc, miscs.at[me])
    load_freq = local(freq, freq_ref)
    load_gate = local(w_gate, gate)
    load_up = local(w_up, up)
    load_own = [
        local(w_query, wqkv.at[me, :, pl.ds(0, 1024)]),
        local(w_keyval, wqkv.at[me, :, pl.ds(1024, 512)]),
        local(w_out, wo.at[me]),
    ]
    greet([sibling] + group + [d for d, (j, p) in zip(sequence, others) if p == 1] + column)

    def lanes_from(base, size):
        def cut(ref, part):
            start, count = ((0, size), (0, size // 2), (size // 2, size // 2))[part]
            start = pl.multiple_of(core * size + (base + start), 128)
            return ref.at[:, pl.ds(start, count)]

        return cut

    def cut_wo(ref, part):
        start, size = ((0, 64), (0, 32), (32, 32))[part]
        return ref.at[pl.ds(pl.multiple_of(core * 64 + start, 32), size)]

    def cut_gb(ref, part):
        return ref if part == 0 else ref.at[pl.ds((part - 1) * 96, 96)]

    def cut_gu(ref):
        return ref.at[:, pl.ds(pl.multiple_of(core * FF_PAD, 128), FF_PAD)]

    cut_q, cut_kv = lanes_from(0, 512), lanes_from(1024, 256)
    slot_qkv = lambda j, p: wqkv.at[at(j, p)]
    slot_wo = lambda j, p: wo.at[at(j, p)]
    slot_gb = lambda j, p: o_gb.at[j, p]
    misc_copies = [wire.copy(misc, miscs.at[me], device) for device in sequence]
    for copy in misc_copies:
        copy.start()
    for load in load_own:
        load.wait()
    own = wqkv.at[me]
    trees = [
        gather_tree(wire, place.over_group, HOPS, own, slot_qkv, cut_q, True),
        gather_tree(wire, place.over_group, HOPS, own, slot_qkv, cut_kv, True),
        gather_tree(wire, place.over_group, HOPS, wo.at[me], slot_wo, cut_wo, True),
    ]
    cuts = [cut_q, cut_kv, cut_wo]
    slots = [slot_qkv, slot_qkv, slot_wo]
    passes = [
        {k: wire.copy(cut(slot(*jp), 0), cut(slot(*jp), 0), sibling) for k, jp in WHOLE.items()}
        for cut, slot in zip(cuts, slots)
    ]
    for tree in trees:
        for k in FIRST:
            tree[k].start()

    load_x.wait()
    inputs = x_ref[...].astype(jnp.float32)
    inverse1 = lax.rsqrt(jnp.mean(inputs * inputs, axis=1, keepdims=True) + EPSILON)
    middle[...] = inputs * inverse1
    load_gate.wait()
    load_up.wait()
    for d in range(8):
        for t in range(PAIRS):
            start = FF_DEV * d + 128 * t
            size = min(128, FF_DEV - 128 * t)
            for k, weight in enumerate((gate, up)):
                block = weight[:, start : start + size]
                if size < 128:
                    block = jnp.concatenate(
                        [block, jnp.zeros((block.shape[0], 128 - size), block.dtype)], axis=1
                    )
                packed[d, :, 256 * t + 128 * k : 256 * t + 128 * (k + 1)] = block

    def attn(*hops):
        for k in hops:
            for tree, onward in zip(trees, passes):
                arrive(tree, k)
                if k in onward:
                    onward[k].start()

    z_of = lambda p: (place.z_hi + p) % 2
    shard_from = lambda d, p: z_of(p) * 4 + (place.x + y + d) % 4
    turn = []
    for p in (0, 1):
        target = z_of(p) * 4 + (place.x - y + 4) % 4
        turn.append(
            wire.copy(
                cut_gu(packed.at[target]), cut_gu(o_gu.at[me]), place.device(dx=4 - y, mirror=p)
            )
        )
    away, home = y > 0, y == 0
    keep_own = pltpu.make_async_copy(
        cut_gu(packed.at[me]), cut_gu(o_gu.at[me]), local_sems.at[len(locals_)]
    )
    locals_.append(None)
    turn[1].start()
    pl.when(away)(turn[0].start)
    pl.when(home)(keep_own.start)

    def over_y(dx, mirror):
        return place.device(dy=dx)

    def cut_block(ref, part):
        start, size = ((0, 144), (0, 80), (80, 64))[part]
        return ref.at[pl.ds(start, size), pl.ds(pl.multiple_of(core * FF_PAD, 128), FF_PAD)]

    gu_slots = [lambda j, _, p=p: o_gu.at[shard_from(STEPS[j], p)] for p in (0, 1)]
    gu_trees = [
        gather_tree(wire, over_y, RING, slot(0, 0), slot, cut_block, True) for slot in gu_slots
    ]
    gu_passes = {
        (j, p): wire.copy(
            cut_gu(o_gu.at[shard_from(STEPS[j], p)]),
            cut_gu(o_gu.at[shard_from(STEPS[j], p)]),
            sibling,
        )
        for j in range(4)
        for p in (0, 1)
    }

    def over(k, j):
        for p in (0, 1):
            arrive(gu_trees[p], k, RING_ONWARD)
            if j:
                gu_passes[j, p].start()

    attn(0, 2, 5)
    load_cot.wait()
    load_misc.wait()
    load_freq.wait()
    live_col = (
        lax.broadcasted_iota(jnp.int32, (rows, 1), 0).astype(jnp.float32)
        < miscs[me].astype(jnp.float32)[2:3, :1]
    )
    gb_own[...] = jnp.where(live_col, cot_ref[...].astype(jnp.float32), 0.0).astype(jnp.bfloat16)
    gb_tree = gather_tree(wire, place.over_group, HOPS, gb_own, slot_gb, cut_gb, False)
    attn(3, 11, 6)
    pl.when(away)(turn[0].wait_recv)
    turn[1].wait_recv()
    pl.when(home)(keep_own.wait)
    for p in (0, 1):
        gu_trees[p][0].start()
        gu_trees[p][1].start()
        gu_passes[0, p].start()
    for k in FIRST:
        gb_tree[k].start()
    local(gb_own, o_gb.at[0, 0])
    attn(1, 4, 7, 8, 9, 10, 12, 13)

    for copy in misc_copies:
        copy.wait_recv()
    as_float = [miscs[s].astype(jnp.float32) for s in range(8)]
    gain1 = jnp.concatenate([m[0:1, :144] for m in as_float], axis=1)
    gain2 = jnp.concatenate([m[1:2, :144] for m in as_float], axis=1)
    normed = (middle[...] * gain1).astype(jnp.bfloat16)
    normed1[...] = normed
    for k in WHOLE:
        passes[0][k].wait_recv()
        passes[1][k].wait_recv()
    live = [m[2:3, :1] for m in as_float]
    start_of = []
    for i in range(BEHIND + 1):
        total = jnp.zeros((1, 1), jnp.float32)
        for s in range(8):
            total = total + jnp.where(s < me - i, 1.0, 0.0) * live[s]
        start_of.append(total)
    row = lax.broadcasted_iota(jnp.int32, (rows, 1), 0).astype(jnp.float32)
    query_pos = start_of[0] + row
    angles = query_pos * freq_ref[0:1, :]
    cosine, sine_part = jnp.cos(angles), jnp.sin(angles)
    rope[:, :128] = cosine
    rope[:, 128:] = sine_part
    weights = wqkv.reshape(width, 1536)

    def turned(vectors):
        first, second = vectors[:, :128], vectors[:, 128:]
        return jnp.concatenate(
            [first * cosine - second * sine_part, second * cosine + first * sine_part], axis=1
        )

    projected = matmul(normed, weights[:, 1024:1536])
    kv_ref[0, :, :256] = turned(projected[:, :256]).astype(jnp.bfloat16)
    kv_ref[0, :, 256:] = projected[:, 256:].astype(jnp.bfloat16)
    x, upper = place.x, place.z_hi == 1
    cross_kv = wire.copy(kv_ref.at[0], kv_ref.at[BEHIND], (place.rep, at(0, 1)))
    near_kv, far_kv = [], []
    for i in range(1, BEHIND):
        target = (place.rep, 4 * place.z_hi + (x + i) % 4)
        near_kv.append(wire.copy(kv_ref.at[0], kv_ref.at[i], target))
        far_kv.append(wire.copy(kv_ref.at[BEHIND], kv_ref.at[i], target))
    pl.when(jnp.logical_not(upper))(cross_kv.start)
    for i, copy in enumerate(near_kv):
        pl.when(x + (i + 1) < 4)(copy.start)
    for i in range(1, BEHIND + 1):

        @pl.when(me < i)
        def _():
            kv_ref[i] = jnp.zeros(kv_ref.shape[1:], kv_ref.dtype)

    def pass_kv():
        pl.when(upper)(cross_kv.wait_recv)
        for i, copy in enumerate(far_kv):
            pl.when(jnp.logical_and(upper, x + (i + 1) > 3))(copy.start)

    def have_kv():
        for i, (near, far) in enumerate(zip(near_kv, far_kv)):
            pl.when(x >= i + 1)(near.wait_recv)
            pl.when(jnp.logical_and(upper, x < i + 1))(far.wait_recv)

    scaling = 256 ** (-0.5)
    for h in range(4):
        heads = matmul(normed, weights[:, 256 * h : 256 * (h + 1)])
        q_ref[h] = (turned(heads) * scaling).astype(jnp.bfloat16)

    index = lax.broadcasted_iota(jnp.int32, (1, (BEHIND + 1) * rows), 1)
    key_pos = jnp.zeros(index.shape, jnp.float32)
    key_live = jnp.zeros(index.shape, jnp.float32)
    for i in range(BEHIND + 1):
        inside = jnp.logical_and(index >= i * rows, index < (i + 1) * rows)
        within = (index - i * rows).astype(jnp.float32)
        live_i = jnp.zeros((1, 1), jnp.float32)
        for s in range(8):
            live_i = live_i + jnp.where(me - i == s, 1.0, 0.0) * live[s]
        key_pos = jnp.where(inside, start_of[i] + within, key_pos)
        key_live = jnp.where(inside, jnp.where(within < live_i, 1.0, 0.0), key_live)
    ahead = query_pos - key_pos
    allowed = jnp.logical_and(
        jnp.logical_and(ahead >= 0.0, ahead < float(WINDOW)), key_live > 0.5
    )
    bias[...] = jnp.where(allowed, 0.0, MASKED)
    pass_kv()

    over(0, 2)
    over(1, 1)
    for k in SERVE[:4]:
        arrive(gb_tree, k)
    have_kv()
    all_kv = kv_ref.reshape((BEHIND + 1) * rows, 512)
    for h in range(4):
        scores = trail_product(q_ref[h], all_kv[:, :256]) + bias[...]
        raised = jnp.exp(scores - jnp.max(scores, axis=1, keepdims=True))
        share = raised * (1.0 / jnp.sum(raised, axis=1, keepdims=True))
        probs[h] = share
        att[:, 256 * h : 256 * (h + 1)] = matmul(
            share.astype(jnp.bfloat16), all_kv[:, 256:]
        ).astype(jnp.bfloat16)
        if h == 1:
            for k in SERVE[4:6]:
                arrive(gb_tree, k)
    for k in WHOLE:
        passes[2][k].wait_recv()
    keep = jnp.where(live_col, 1.0, 0.0)
    mid = x_ref[...].astype(jnp.float32) + keep * matmul(att[...], wo.reshape(1024, width)[...])
    middle[...] = mid
    inverse2 = lax.rsqrt(jnp.mean(mid * mid, axis=1, keepdims=True) + EPSILON)
    normed2[...] = (mid * inverse2 * gain2).astype(jnp.bfloat16)
    for src, dst in (
        (miscs, o_misc),
        (wqkv, o_qkv),
        (wo, o_wo),
        (normed1, o_normed1),
        (q_ref, o_q),
        (kv_ref, o_kv),
        (probs, o_probs),
        (att, o_att),
        (middle, o_middle),
        (normed2, o_normed2),
        (rope, o_rope),
    ):
        local(src, dst)
    over(2, 0)
    over(3, 3)
    for k in SERVE[6:]:
        arrive(gb_tree, k)
    for copy in gu_passes.values():
        copy.wait_recv()
    waited = [id(copy) for copy in near_kv + far_kv + [cross_kv, turn[0]]]
    for copy in locals_[9:]:
        if copy is not None:
            copy.wait()
    pl.when(away)(turn[0].wait_send)
    pl.when(jnp.logical_not(upper))(cross_kv.wait_send)
    for i, (near, far) in enumerate(zip(near_kv, far_kv)):
        pl.when(x + (i + 1) < 4)(near.wait_send)
        pl.when(jnp.logical_and(upper, x + (i + 1) > 3))(far.wait_send)
    for copy in wire.made:
        if id(copy) not in waited:
            copy.wait_send()


ANY = pl.BlockSpec(memory_space=pl.ANY)


def comm_params(collective_id):
    return pltpu.CompilerParams(
        collective_id=collective_id, has_side_effects=True, vmem_limit_bytes=VMEM_LIMIT
    )


def front(tokens, cot, misc, freq, w_query, w_keyval, w_out, w_gate, w_up):
    bf, f32 = jnp.bfloat16, jnp.float32
    rows, width = tokens.shape
    keys = (BEHIND + 1) * rows
    outs = [
        ((8, 16, 256), bf),
        ((8, 144, 1536), bf),
        ((8, 128, width), bf),
        ((8, 144, 2 * FF_PAD), bf),
        ((4, 2, rows, width), bf),
        ((rows, width), bf),
        ((4, rows, 256), bf),
        ((BEHIND + 1, rows, 512), bf),
        ((4, rows, keys), f32),
        ((rows, 1024), bf),
        ((rows, width), f32),
        ((rows, width), bf),
        ((rows, 256), f32),
    ]
    scratch = [
        ((rows, width), bf),
        ((rows, width), bf),
        ((8, 16, 256), bf),
        ((8, 128), f32),
        ((8, 144, 1536), bf),
        ((8, 128, width), bf),
        (w_gate.shape, bf),
        (w_up.shape, bf),
        ((8, 144, 2 * FF_PAD), bf),
        ((rows, width), bf),
        ((rows, width), bf),
        ((4, rows, 256), bf),
        ((BEHIND + 1, rows, 512), bf),
        ((rows, keys), f32),
        ((4, rows, keys), f32),
        ((rows, 1024), bf),
        ((rows, width), f32),
        ((rows, width), bf),
        ((rows, 256), f32),
    ]
    return pl.pallas_call(
        front_kernel,
        out_shape=tuple(jax.ShapeDtypeStruct(*o) for o in outs),
        in_specs=[ANY] * 9,
        out_specs=(ANY,) * len(outs),
        scratch_shapes=[pltpu.VMEM(*v) for v in scratch]
        + [
            pltpu.SemaphoreType.DMA((32,)),
            pltpu.SemaphoreType.DMA((136,)),
            pltpu.SemaphoreType.DMA((136,)),
        ],
        compiler_params=comm_params(1),
        name="attention_forward",
    )(tokens, cot, misc, freq, w_query, w_keyval, w_out, w_gate, w_up)


def finish_kernel(both, d_in, q_in, kv_in, wo_in, gate, up, d_out, q_out, kv_out, wo_out):
    for k, out in enumerate((gate, up)):
        parts = []
        for d in range(8):
            for t in range(PAIRS):
                half, q, first = (k, 3, 0) if t == 3 else (t // 4, t % 4, 128 * k)
                size = min(128, FF_DEV - 128 * t)
                parts.append(both[half, q, d, :, first : first + size])
        out[...] = jnp.concatenate(parts, axis=1).astype(jnp.float32)
    d_out[...] = d_in[...].astype(jnp.float32)
    q_out[...] = q_in[...].astype(jnp.float32)
    for c in range(2):
        for q in range(2):
            start = 256 * c + 128 * q
            kv_out[:, start : start + 128] = kv_in[c, q].astype(jnp.float32)

    @pl.when(pl.program_id(0) == 0)
    def _():
        wo_out[...] = wo_in[...].astype(jnp.float32)


def finish(both, d_in, q_in, kv_in, wo_in):
    rows, width = both.shape[3], d_in.shape[1]
    steps = rows // 16
    shapes = [(rows, 8 * FF_DEV)] * 2 + [(FF_DEV, width), (rows, 1024), (rows, 512), wo_in.shape]
    blocks = [(16, 8 * FF_DEV)] * 2 + [(FF_DEV // steps, width), (16, 1024), (16, 512)]
    by_row = lambda i: (i, 0)
    fixed = pl.BlockSpec(wo_in.shape, lambda i: (0, 0))
    return pl.pallas_call(
        finish_kernel,
        grid=(steps,),
        out_shape=[jax.ShapeDtypeStruct(shape, jnp.float32) for shape in shapes],
        in_specs=[
            pl.BlockSpec((2, 4, 8, 16, 256), lambda i: (0, 0, 0, i, 0)),
            pl.BlockSpec((FF_DEV // steps, width), by_row),
            pl.BlockSpec((16, 1024), by_row),
            pl.BlockSpec((2, 4, 16, 128), lambda i: (0, 0, i, 0)),
            fixed,
        ],
        out_specs=[pl.BlockSpec(block, by_row) for block in blocks] + [fixed],
        compiler_params=pltpu.CompilerParams(vmem_limit_bytes=VMEM_LIMIT),
        name="finish",
    )(both, d_in, q_in, kv_in, wo_in)


ROOT = 0.7978845608028654
CUBE = 0.044715


def ff_kernel(
    own_n, gb_all, wgu_all, wd_all,
    o_gn, o_pb, o_pgu, o_pd,
    nbuf, gb, wgu, wd, gh, hid, ggu, part_g, part_b, out_f32, dgu,
    g_half, dd, r_d, d_whole, d_half_a, d_half_b, z_d,
    r_gu, gu_half, n_turned, b_half,
    local_sems, send_sems, recv_sems,
):
    place = Place()
    wire = Wire(send_sems, recv_sems)
    loads = [
        pltpu.make_async_copy(src, dst, local_sems.at[k])
        for k, (src, dst) in enumerate(
            [(own_n, nbuf.at[0, 0]), (wd_all, wd.at[pl.ds(0, FF_DEV)]), (gb_all, gb), (wgu_all, wgu)]
        )
    ]
    for load in loads:
        load.start()
    core, y = place.core, place.y
    sibling, low = place.device(sibling=1), place.device(swap_lo=1)
    greet(
        [place.device(dx=1), place.device(dx=3), place.device(mirror=1), sibling, low]
        + [place.device(dy=1), place.device(dy=3)]
    )

    def cut(ref, part):
        return ref if part == 0 else ref.at[pl.ds((part - 1) * 96, 96)]

    slot_n = lambda j, p: nbuf.at[j, p]
    tree = gather_tree(wire, place.over_group, HOPS, nbuf.at[0, 0], slot_n, cut, False)
    sum_g = SumTree(
        wire, place.over_group, HOPS, lambda j, p: part_g.at[j, p], cut,
        [g_half.at[k] for k in range(14)],
    )

    def cut_d(ref, part):
        start, size = ((0, 1152), (0, 640), (640, 512))[part]
        return ref.at[:, pl.ds(start, size)]

    quarter_d = dd.at[core, y]
    swap_d = wire.copy(dd.at[1 - core], r_d, sibling)
    sum_d = SumTree(
        wire, lambda dx, mirror: place.device(dy=dx), RING,
        lambda j, p: dd.at[core, (y + STEPS[j]) % 4], cut_d,
        [d_whole.at[0], d_whole.at[1], d_half_a, d_half_b],
    )
    cross_d = wire.copy(quarter_d, z_d, low)

    def cut_lead(ref, part):
        return ref if part == 0 else ref.at[pl.ds((part - 1) * 4, 4)]

    swap_gu = wire.copy(dgu.at[1 - core], r_gu, sibling)
    far_b = SumTree(
        wire, place.over_group, HOPS_FAR, lambda j, p: part_b.at[j, p], cut,
        [b_half.at[k] for k in range(4)],
    )
    far_gu = [
        wire.copy(
            cut_lead(dgu.at[core, (y + 2) % 4], part),
            gu_half.at[part - 1],
            place.device(dy=(3, 1)[part - 1]),
        )
        for part in (1, 2)
    ]
    loads[0].wait()
    for k in FIRST:
        tree[k].start()
    wd[FF_DEV:] = jnp.zeros((FF_PAD - FF_DEV, wd.shape[1]), wd.dtype)
    loads[1].wait()
    loads[2].wait()

    def back_hidden(j):
        rows = jnp.concatenate([gb[j, 0], gb[j, 1]], axis=0)
        gh[j] = trail_product(rows, wd[...])

    def forward(j):
        rows = jnp.concatenate([nbuf[j, 0], nbuf[j, 1]], axis=0)

        def tile(t, carry):
            columns = pl.ds(pl.multiple_of(t * 256, 256), 256)
            narrow = pl.ds(pl.multiple_of(t * 128, 128), 128)
            both = matmul(rows, wgu[:, columns])
            gate, up = both[:, :128], both[:, 128:]
            square = gate * gate
            curve = jnp.tanh(ROOT * gate * (1.0 + CUBE * square))
            half_up = 0.5 * (1.0 + curve)
            active = gate * half_up
            slope = half_up + 0.5 * gate * (1.0 - curve * curve) * (
                ROOT * (1.0 + 3.0 * CUBE * square)
            )
            back = gh[j, :, narrow]
            hid[j, :, narrow] = (active * up).astype(jnp.bfloat16)
            ggu[j, :, columns] = jnp.concatenate(
                [(back * up * slope).astype(jnp.bfloat16), (back * active).astype(jnp.bfloat16)],
                axis=1,
            )
            return carry

        lax.fori_loop(0, PAIRS, tile, 0)

    def back_normed(j):
        for start, size in ((0, 512), (512, 512), (1024, 128)):
            block = trail_product(ggu[j], wgu[start : start + size, :]).astype(jnp.bfloat16)
            part_g[j, 0, :, start : start + size] = block[:192]
            part_g[j, 1, :, start : start + size] = block[192:]

    def down(j):
        for start, size in ((0, 512), (512, 512), (1024, 128)):
            block = matmul(hid[j], wd[:, start : start + size]).astype(jnp.bfloat16)
            part_b[j, 0, :, start : start + size] = block[:192]
            part_b[j, 1, :, start : start + size] = block[192:]

    hid_rows = hid.reshape(4 * 384, FF_PAD)
    ggu_rows = ggu.reshape(4 * 384, 2 * FF_PAD)
    gb_rows = gb.reshape(4 * 384, 1152)
    dd_rows = dd.reshape(FF_PAD, 1152)
    dgu_rows = dgu.reshape(2, 4, 1152, 256)

    def turn_rows(j):
        rows = jnp.concatenate([nbuf[j, 0], nbuf[j, 1]], axis=0)
        n_turned[:, 384 * j : 384 * (j + 1)] = rows.T

    def grad_half(half):
        def tile(q, carry):
            columns = pl.ds(pl.multiple_of((half * 4 + q) * 256, 256), 256)
            dgu_rows[half, q] = matmul(n_turned[...], ggu_rows[:, columns]).astype(jnp.bfloat16)
            return carry

        lax.fori_loop(0, 3, tile, 0)

    dgu[:, 3, :, :, 128:] = jnp.zeros((2, 8, 144, 128), jnp.bfloat16)
    back_hidden(0)
    back_hidden(1)
    back_hidden(2)
    for k in SERVE[:3]:
        arrive(tree, k)
    back_hidden(3)
    for k in SERVE[3:7]:
        arrive(tree, k)
    loads[3].wait()
    forward(0)
    turn_rows(0)
    for k in SERVE[7:9]:
        arrive(tree, k)
    forward(1)
    for k in SERVE[9:12]:
        arrive(tree, k)
    forward(2)
    turn_rows(1)
    turn_rows(2)
    for k in SERVE[12:]:
        arrive(tree, k)
    forward(3)
    back_normed(3)
    sum_g.send_far()
    back_normed(1)
    back_normed(2)
    sum_g.send_mid()
    for start, size in ((0, 512), (512, 512), (1024, 128)):
        dd_rows[:, start : start + size] = lead_product(
            hid_rows[...], gb_rows[:, start : start + size]
        ).astype(jnp.bfloat16)
    swap_d.start()
    sum_g.send_near()
    back_normed(0)
    sum_g.start(1)
    turn_rows(3)
    middle_tile = matmul(n_turned[...], ggu_rows[:, 768:1024]).astype(jnp.bfloat16)
    dgu_rows[0, 3, :, :128] = middle_tile[:, :128]
    dgu_rows[1, 3, :, :128] = middle_tile[:, 128:]
    down(3)
    swap_d.wait_recv()

    def add_d(i, carry):
        add_into(dd.at[core, i], r_d.at[i])
        return carry

    lax.fori_loop(0, 4, add_d, 0)
    sum_d.start(2, 3)
    sum_g.send_next()
    grad_half(1 - core)
    swap_gu.start()
    sum_g.send_last()
    far_b.start(0, 1, 2, 3)
    sum_d.absorb(2, 3)
    sum_d.start(0, 1)
    grad_half(core)
    down(0)
    swap_gu.wait_recv()

    def add_gu(i, carry):
        add_into(dgu.reshape(2, 32, 144, 256).at[core, i], r_gu.reshape(32, 144, 256).at[i])
        return carry

    lax.fori_loop(0, 32, add_gu, 0)
    for copy in far_gu:
        copy.start()
    sum_d.absorb(0, 1)
    cross_d.start()
    down(1)
    down(2)
    out_f32[...] = sum_g.finish(0)
    store_g = pltpu.make_async_copy(out_f32, o_gn, local_sems.at[6])
    store_g.start()
    cross_d.wait_recv()
    cross_d.wait_send()
    add_into(quarter_d, z_d)
    store_d = pltpu.make_async_copy(quarter_d, o_pd, local_sems.at[7])
    store_d.start()
    far_b.absorb(0, 1, 2, 3)
    store_b = pltpu.make_async_copy(part_b, o_pb, local_sems.at[5])
    store_b.start()
    for part, j in ((1, 2), (2, 1)):
        far_gu[part - 1].wait_recv()
        add_into(
            cut_lead(dgu.at[core, (y + STEPS[j]) % 4], part), gu_half.at[part - 1]
        )
    store_gu = pltpu.make_async_copy(dgu.at[core], o_pgu, local_sems.at[4])
    store_gu.start()
    for store in (store_b, store_gu, store_g, store_d):
        store.wait()
    for copy in wire.made:
        if copy is not cross_d:
            copy.wait_send()


def feed_forward(own_n, gb_all, wgu_all, wd_all):
    bf, f32 = jnp.bfloat16, jnp.float32
    vm = pltpu.VMEM
    tokens, width = own_n.shape
    sums = [vm((14, tokens // 2, width), bf)]
    return pl.pallas_call(
        ff_kernel,
        out_shape=(
            jax.ShapeDtypeStruct((tokens, width), f32),
            jax.ShapeDtypeStruct((4, 2, tokens, width), bf),
            jax.ShapeDtypeStruct((4, 8, 144, 256), bf),
            jax.ShapeDtypeStruct((112, width), bf),
        ),
        in_specs=[ANY] * 4,
        out_specs=(ANY,) * 4,
        scratch_shapes=[
            vm((4, 2, tokens, width), bf),
            vm((4, 2, tokens, width), bf),
            vm(wgu_all.shape, bf),
            vm((FF_PAD, width), bf),
            vm((4, 2 * tokens, FF_PAD), f32),
            vm((4, 2 * tokens, FF_PAD), bf),
            vm((4, 2 * tokens, 2 * FF_PAD), bf),
            vm((4, 2, tokens, width), bf),
            vm((4, 2, tokens, width), bf),
            vm((tokens, width), f32),
            vm((2, 4, 8, 144, 256), bf),
        ]
        + sums
        + [
            vm((2, 4, 112, width), bf),
            vm((4, 112, width), bf),
            vm((2, 112, width), bf),
            vm((112, 640), bf),
            vm((112, 512), bf),
            vm((112, width), bf),
            vm((4, 8, 144, 256), bf),
            vm((2, 4, 144, 256), bf),
            vm((width, 8 * tokens), bf),
            vm((4, tokens // 2, width), bf),
        ]
        + [
            pltpu.SemaphoreType.DMA((8,)),
            pltpu.SemaphoreType.DMA((48,)),
            pltpu.SemaphoreType.DMA((48,)),
        ],
        compiler_params=comm_params(2),
        name="feed_forward",
    )(own_n, gb_all, wgu_all, wd_all)


def back_kernel(
    p_gu, p_d, part_b_all, gn2_all, middle_all, miscs_all, tokens, cot, rope_all, q_all, kv_all,
    probs_all, att_all, wqkv_all, wo_all, normed1_all,
    o_gu, o_d, o_q, o_kv, o_wo, o_out, o_grad,
    h_gu, gu_whole, z_gu, f_gu, piece_d,
    part_b, b_half, gn2, middle, miscs, x_ref, cot_ref, rope, q_ref, kv_ref, probs, att,
    wqkv, wo, normed1, dq, r_q, q_half, dkv, r_kv, kv_parts, dwo, r_wo, w_half,
    gkv, kv_out, kv_in, gproj, gmid, out_bf,
    s_wo, y_wo, z_wo, s_q, y_q, z_q, s_kv, y_kv, z_kv,
    local_sems, send_sems, recv_sems,
):
    place = Place()
    wire = Wire(send_sems, recv_sems)
    core, me, y, rep = place.core, place.shard, place.y, place.rep
    rows, width = tokens.shape
    at = place.shard_at
    others = [(j, p) for p in (0, 1) for j in range(4) if (j, p) != (0, 0)]
    group = [place.device(dx=STEPS[j], mirror=p) for j, p in others]
    sequence = [(rep, at(j, 1)) for j in range(4)]
    sibling = place.device(sibling=1)
    column = [place.device(dy=d) for d in (1, 3, 2)]
    low = place.device(swap_lo=1)
    locals_ = []

    def local(src, dst):
        copy = pltpu.make_async_copy(src, dst, local_sems.at[len(locals_)])
        copy.start()
        locals_.append(copy)
        return copy

    loads = [
        local(src, dst)
        for src, dst in (
            (miscs_all, miscs),
            (gn2_all, gn2),
            (middle_all, middle),
            (cot, cot_ref),
            (att_all, att),
            (wo_all, wo),
        )
    ]
    load_gu = local(p_gu, h_gu)
    load_d = local(p_d, piece_d)
    load_b = local(part_b_all, part_b)
    both_cores = [place.device(dy=d, sibling=1) for d in (1, 3, 2)]
    greet([sibling, low] + group + column + sequence + both_cores)
    loads_heads = [
        local(src, dst)
        for src, dst in ((q_all, q_ref), (kv_all, kv_ref), (probs_all, probs), (rope_all, rope))
    ]
    load_x = local(tokens, x_ref)
    load_n = local(normed1_all, normed1)
    load_w = local(wqkv_all, wqkv)
    loaded = len(locals_)

    def over_y(dx, mirror):
        return place.device(dy=dx)

    def cut_lead(ref, part):
        return ref if part == 0 else ref.at[pl.ds((part - 1) * 4, 4)]

    def cut_rows(size):
        def cut(ref, part):
            return ref if part == 0 else ref.at[pl.ds((part - 1) * size, size)]

        return cut

    def cut_lanes(size):
        def cut(ref, part):
            return ref if part == 0 else ref.at[:, pl.ds((part - 1) * size, size)]

        return cut

    def cut_d(ref, part):
        start, size = ((0, width), (0, 640), (640, 512))[part]
        return ref.at[:, pl.ds(start, size)]

    def added(target, source, count):
        def one(i, carry):
            add_into(target.at[i], source.at[i])
            return carry

        lax.fori_loop(0, count, one, 0)

    chunks = [pl.ds(0, 80), pl.ds(80, 64)]
    near_gu = [
        [
            wire.copy(
                h_gu.at[(y + STEPS[j]) % 4, :, c],
                gu_whole.at[k, :, c],
                place.device(dy=(3, 1)[k]),
            )
            for k, j in enumerate((2, 1))
        ]
        for c in chunks
    ]
    quarters = [h_gu.at[y, :, c] for c in chunks]
    crossings_gu = [wire.copy(h_gu.at[y, :, c], z_gu.at[:, c], low) for c in chunks]
    turns = [
        [
            wire.copy(h_gu.at[y, at(j, p), c], f_gu.at[me, c], device)
            for (j, p), device in zip(others, group)
        ]
        for c in chunks
    ]
    slots_gu = [lambda j, p, c=c: o_gu.at[core, (y + STEPS[j]) % 4, :, c] for c in chunks]
    trees_gu = [
        gather_tree(wire, over_y, RING, f_gu.at[:, c], slot, cut_lead, True)
        for c, slot in zip(chunks, slots_gu)
    ]
    passes_gu = [
        [
            wire.copy(f_gu.at[:, c] if j == 0 else slot(j, 0), slot(j, 0), sibling)
            for j in range(4)
        ]
        for c, slot in zip(chunks, slots_gu)
    ]

    def cross(i):
        for k, copy in enumerate(near_gu[i]):
            copy.wait_recv()
            added(quarters[i], gu_whole.at[k, :, chunks[i]], 8)
        crossings_gu[i].start()

    def turn(i):
        crossings_gu[i].wait_recv()
        crossings_gu[i].wait_send()
        added(quarters[i], z_gu.at[:, chunks[i]], 8)
        for copy in turns[i]:
            copy.start()
        f_gu[me, chunks[i]] = h_gu[y, me, chunks[i]]

    def spread(i):
        for copy in turns[i]:
            copy.wait_recv()
        for copy in (trees_gu[i][0], trees_gu[i][1], passes_gu[i][0]):
            copy.start()
        local(f_gu.at[:, chunks[i]], slots_gu[i](0, 0))

    def spread_on(i, k):
        arrive(trees_gu[i], k, RING_ONWARD)
        if k != 2:
            passes_gu[i][(2, 1, None, 3)[k]].start()

    load_gu.wait()
    for copy in near_gu[0] + near_gu[1]:
        copy.start()

    sum_b = SumTree(
        wire, place.over_group, HOPS, lambda j, p: part_b.at[j, p], cut_rows(96),
        [b_half.at[k] for k in range(14)],
    )
    load_b.wait()
    sum_b.start(7, 6, 4, 2, 11, 10, 1)

    load_d.wait()
    slot_d = lambda j, p: o_d.at[core, (y + STEPS[j]) % 4]
    tree_d = gather_tree(wire, over_y, RING, piece_d, slot_d, cut_d, True)
    pass_d = [
        wire.copy(piece_d if j == 0 else slot_d(j, 0), slot_d(j, 0), sibling) for j in range(4)
    ]

    for load in loads:
        load.wait()
    as_float = [miscs[s].astype(jnp.float32) for s in range(8)]
    gain1 = jnp.concatenate([m[0:1, :144] for m in as_float], axis=1)
    gain2 = jnp.concatenate([m[1:2, :144] for m in as_float], axis=1)
    row = lax.broadcasted_iota(jnp.int32, (rows, 1), 0).astype(jnp.float32)
    keep = jnp.where(row < miscs[me].astype(jnp.float32)[2:3, :1], 1.0, 0.0)
    mid = middle[...]
    inverse2 = lax.rsqrt(jnp.mean(mid * mid, axis=1, keepdims=True) + EPSILON)
    scaled2 = mid * inverse2
    grad2 = gn2[...]
    grad_gain2 = jnp.sum(grad2 * scaled2, axis=0, keepdims=True)
    grad2 = grad2 * gain2
    grad_mid = cot_ref[...].astype(jnp.float32) + inverse2 * (
        grad2 - scaled2 * jnp.mean(grad2 * scaled2, axis=1, keepdims=True)
    )
    gmid[...] = grad_mid
    grad_attn = (keep * grad_mid).astype(jnp.bfloat16)
    for start in range(0, width, 384):
        block = lead_product(att[...], grad_attn[:, start : start + 384]).astype(jnp.bfloat16)
        block = block.reshape(8, 2, 64, 384)
        dwo[0, :, :, start : start + 384] = block[:, 0]
        dwo[1, :, :, start : start + 384] = block[:, 1]
    swap_wo = wire.copy(dwo.at[1 - core], r_wo, sibling)
    swap_wo.start()
    grad_att = trail_product(grad_attn, wo.reshape(1024, width)[...]).astype(jnp.bfloat16)

    for load in loads_heads:
        load.wait()
    keys = (BEHIND + 1) * rows
    all_kv = kv_ref.reshape(keys, 512)
    flat = gkv.reshape(keys, 512)
    cosine, sine_part = rope[:, :128], rope[:, 128:]
    scaling = 256 ** (-0.5)

    def turned_back(vectors):
        first, second = vectors[:, :128], vectors[:, 128:]
        return jnp.concatenate(
            [first * cosine + second * sine_part, second * cosine - first * sine_part], axis=1
        )

    for h in range(4):
        share = probs[h]
        share_low = share.astype(jnp.bfloat16)
        grad_h = grad_att[:, 256 * h : 256 * (h + 1)]
        grad_probs = trail_product(grad_h, all_kv[:, 256:])
        delta = jnp.sum(share * grad_probs, axis=1, keepdims=True)
        grad_scores = (share * (grad_probs - delta)).astype(jnp.bfloat16)
        grad_keys = lead_product(grad_scores, q_ref[h])
        grad_values = lead_product(share_low, grad_h)
        if h == 0:
            flat[:, :256] = grad_keys
            flat[:, 256:] = grad_values
        else:
            flat[:, :256] += grad_keys
            flat[:, 256:] += grad_values
        grad_q = matmul(grad_scores, all_kv[:, :256])
        gproj[:, 256 * h : 256 * (h + 1)] = (turned_back(grad_q) * scaling).astype(jnp.bfloat16)
        if h == 1:
            cross(0)
            for copy in (tree_d[0], tree_d[1], pass_d[0]):
                copy.start()
            local(piece_d, slot_d(0, 0))
    x, upper = place.x, place.z_hi == 1
    sends = []
    for i in range(1, BEHIND):
        kv_out[i - 1] = gkv[i].astype(jnp.bfloat16)
        target = (rep, 4 * place.z_hi + (x + (4 - i)) % 4)
        sends.append(wire.copy(kv_out.at[i - 1], kv_in.at[i - 1], target))
        pl.when(jnp.logical_or(upper, x >= i))(sends[-1].start)

        @pl.when(jnp.logical_not(jnp.logical_or(upper, x + i <= 3)))
        def _():
            kv_in[i - 1] = jnp.zeros(kv_in.shape[1:], kv_in.dtype)

    plane_kv = wire.copy(kv_out.at[BEHIND - 1], kv_in.at[BEHIND - 1], (rep, at(0, 1)))

    @pl.when(upper)
    def _():
        kv_in[BEHIND - 1] = jnp.zeros(kv_in.shape[1:], kv_in.dtype)

    def collect_kv():
        through = gkv[BEHIND]
        for i, copy in enumerate(sends):
            pl.when(jnp.logical_or(upper, x + (i + 1) <= 3))(copy.wait_recv)
            through = through + jnp.where(x + (i + 1) > 3, 1.0, 0.0) * kv_in[i].astype(jnp.float32)
        kv_out[BEHIND - 1] = through.astype(jnp.bfloat16)
        pl.when(upper)(plane_kv.start)

    load_n.wait()
    dq_rows = dq.reshape(2, width, 512)
    for t in range(4):
        dq_rows[t // 2, :, 256 * (t % 2) : 256 * (t % 2 + 1)] = lead_product(
            normed1[...], gproj[:, 256 * t : 256 * (t + 1)]
        ).astype(jnp.bfloat16)
    swap_q = wire.copy(dq.at[1 - core], r_q, sibling)
    swap_q.start()
    swap_wo.wait_recv()
    added(dwo.at[core], r_wo, 8)
    sum_wo = SumTree(
        wire, place.over_group, HOPS, lambda j, p: dwo.at[core, at(j, p)], cut_rows(32),
        [w_half.at[k] for k in range(14)],
    )
    sum_wo.send_far()
    sum_wo.send_mid()
    sum_wo.start(1)
    cross(1)
    collect_kv()
    load_x.wait()
    load_w.wait()
    weights = wqkv.reshape(width, 1536)
    gn2[...] = trail_product(gproj[:, :1024], weights[:, :1024])
    swap_q.wait_recv()
    added(dq.at[core], r_q, 8)
    sum_q = SumTree(
        wire, place.over_group, HOPS, lambda j, p: dq.at[core, at(j, p)], cut_lanes(256),
        [q_half.at[k] for k in range(14)],
    )
    sum_q.send_far()
    sum_q.send_mid()
    sum_q.start(1)
    turn(0)

    pl.when(jnp.logical_not(upper))(plane_kv.wait_recv)
    grad_kv = gkv[0] + kv_in[BEHIND - 1].astype(jnp.float32)
    for i in range(BEHIND - 1):
        grad_kv = grad_kv + jnp.where(x + (i + 1) <= 3, 1.0, 0.0) * kv_in[i].astype(jnp.float32)
    gproj[:, 1024:1280] = turned_back(grad_kv[:, :256]).astype(jnp.bfloat16)
    gproj[:, 1280:1536] = grad_kv[:, 256:].astype(jnp.bfloat16)
    for t in range(2):
        dkv[t, :, :144] = (
            lead_product(normed1[...], gproj[:, 1024 + 256 * t : 1280 + 256 * t])
            .astype(jnp.bfloat16)
            .reshape(8, 144, 256)
        )
    inputs = x_ref[...].astype(jnp.float32)
    inverse1 = lax.rsqrt(jnp.mean(inputs * inputs, axis=1, keepdims=True) + EPSILON)
    scaled1 = inputs * inverse1
    grad1 = gn2[...] + trail_product(gproj[:, 1024:], weights[:, 1024:])
    grad_gain1 = jnp.sum(grad1 * scaled1, axis=0, keepdims=True)
    for s in range(8):
        cols = slice(144 * s, 144 * (s + 1))
        both = jnp.concatenate(
            [grad_gain1[:, cols], grad_gain2[:, cols], jnp.zeros((14, 144), jnp.float32)], axis=0
        )
        both = jnp.concatenate([both, jnp.zeros((16, 112), jnp.float32)], axis=1)
        dkv[0, s, 144:] = both.astype(jnp.bfloat16)
        dkv[1, s, 144:] = both.astype(jnp.bfloat16)
    swap_kv = wire.copy(dkv.at[1 - core], r_kv, sibling)
    swap_kv.start()
    turn(1)
    sum_wo.send_near()
    swap_kv.wait_recv()
    added(dkv.at[core], r_kv, 8)
    direct_kv = [
        wire.copy(dkv.at[core, at(j, p)], kv_parts.at[i], device)
        for i, ((j, p), device) in enumerate(zip(others, group))
    ]
    for copy in direct_kv:
        copy.start()
    spread(0)
    grad1 = grad1 * gain1
    gmid[...] += inverse1 * (grad1 - scaled1 * jnp.mean(grad1 * scaled1, axis=1, keepdims=True))
    local(gmid, o_grad)
    for k in (0, 1):
        arrive(tree_d, k, RING_ONWARD)
        pass_d[(2, 1)[k]].start()
    spread(1)
    sum_q.send_near()
    sum_wo.send_next()
    sum_wo.send_last()
    sum_q.send_next()
    sum_q.send_last()
    for k in (0, 1):
        spread_on(0, k)
    sum_b.absorb(10)
    sum_b.start(3)
    sum_b.absorb(11)
    sum_b.start(5)
    sum_b.send_last()

    def over_column(source, landing):
        copies = [
            wire.copy(source.at[(y + d) % 4], landing.at[i], device)
            for i, (d, device) in enumerate(zip((1, 3, 2), column))
        ]
        for copy in copies:
            copy.start()
        return copies

    def over_low(copies, source, landing, other):
        for copy in copies:
            copy.wait_recv()
        mine = source[y].astype(jnp.float32)
        for i in range(3):
            mine = mine + landing[i].astype(jnp.float32)
        source[y] = mine.astype(jnp.bfloat16)
        crossing = wire.copy(source.at[y], other, low)
        crossing.start()
        return crossing

    def to_all(crossing, source, other, slot):
        crossing.wait_recv()
        crossing.wait_send()
        add_into(source.at[y], other)
        made = [wire.copy(source.at[y], slot(core, y), device) for device in column + [sibling]]
        for copy in made:
            copy.start()
        local(source.at[y], slot(core, y))
        return made

    def to_both(crossing, source, other, slot):
        made = to_all(crossing, source, other, slot)
        made += [
            wire.copy(source.at[y], slot(core, y), place.device(dy=d, sibling=1)) for d in (1, 3, 2)
        ]
        for copy in made[4:]:
            copy.start()
        return made

    def pass_on(made, slot):
        ends = [made[3]]
        for d, copy in zip((3, 1, 2), made):
            copy.wait_recv()
            held = slot(core, (y + d) % 4)
            ends.append(wire.copy(held, held, sibling))
            ends[-1].start()
        return ends

    slot_wo = lambda c, q: o_wo.at[c, q]
    slot_q = lambda c, q: o_q.at[:, pl.ds(pl.multiple_of(c * 512 + q * 128, 128), 128)]
    slot_kv = lambda c, q: o_kv.at[c, q]
    s_wo[...] = sum_wo.finish(0).astype(jnp.bfloat16).reshape(4, 16, width)
    over_wo = over_column(s_wo, y_wo)
    total = sum_q.finish(1).astype(jnp.bfloat16)
    for q in range(4):
        s_q[q] = total[:, 128 * q : 128 * (q + 1)]
    over_q = over_column(s_q, y_q)
    for k in (0, 1):
        spread_on(1, k)
    cross_wo = over_low(over_wo, s_wo, y_wo, z_wo)
    cross_q = over_low(over_q, s_q, y_q, z_q)
    total = dkv[core, me].astype(jnp.float32)
    for i, copy in enumerate(direct_kv):
        copy.wait_recv()
        total = total + kv_parts[i].astype(jnp.float32)
    s_kv[0] = total[:144, :128].astype(jnp.bfloat16)
    s_kv[1] = total[:144, 128:].astype(jnp.bfloat16)
    s_kv[2] = jnp.concatenate(
        [total[144:, :128], total[144:, 128:], jnp.zeros((112, 128), jnp.float32)], axis=0
    ).astype(jnp.bfloat16)
    s_kv[3] = jnp.zeros((144, 128), jnp.bfloat16)
    over_kv = over_column(s_kv, y_kv)
    for k in (2, 3):
        arrive(tree_d, k, RING_ONWARD)
    pass_d[3].start()
    all_wo = to_all(cross_wo, s_wo, z_wo, slot_wo)
    all_q = to_all(cross_q, s_q, z_q, slot_q)
    cross_kv = over_low(over_kv, s_kv, y_kv, z_kv)
    for k in (2, 3):
        spread_on(0, k)
    all_kv_sum = to_both(cross_kv, s_kv, z_kv, slot_kv)
    ends = pass_on(all_wo, slot_wo) + pass_on(all_q, slot_q)
    for k in (2, 3):
        spread_on(1, k)
    out_bf[...] = (middle[...] + keep * sum_b.finish(0)).astype(jnp.bfloat16)
    local(out_bf, o_out)
    ends += all_kv_sum
    for copy in pass_d + passes_gu[0] + passes_gu[1] + ends:
        copy.wait_recv()
    for copy in locals_[loaded:]:
        copy.wait()
    for i, copy in enumerate(sends):
        pl.when(jnp.logical_or(upper, x >= i + 1))(copy.wait_send)
    pl.when(upper)(plane_kv.wait_send)
    waited = [id(copy) for copy in sends + [plane_kv] + crossings_gu + [cross_wo, cross_q, cross_kv]]
    waited += [id(sum_b.copies[k]) for k in (8, 9, 12, 13)]
    for copy in wire.made:
        if id(copy) not in waited:
            copy.wait_send()


def back(*args):
    bf, f32 = jnp.bfloat16, jnp.float32
    width = 1152
    rows = args[6].shape[0]
    outs = [
        ((2, 4, 8, 144, 256), bf),
        ((2, 4, 112, width), bf),
        ((144, 1024), bf),
        ((2, 4, 144, 128), bf),
        ((2, 4, 16, width), bf),
        ((rows, width), bf),
        ((rows, width), f32),
    ]
    scratch = [
        ((4, 8, 144, 256), bf),
        ((2, 8, 144, 256), bf),
        ((8, 144, 256), bf),
        ((8, 144, 256), bf),
        ((112, width), bf),
        ((4, 2, rows, width), bf),
        ((14, rows // 2, width), bf),
    ]
    scratch += [(a.shape, a.dtype) for a in args[3:16]]
    for whole, parts in (
        ((144, 512), (14, 144, 256)),
        ((160, 256), (7, 160, 256)),
        ((64, width), (14, 32, width)),
    ):
        scratch += [((2, 8, *whole), bf), ((8, *whole), bf), (parts, bf)]
    scratch += [
        ((BEHIND + 1, rows, 512), f32),
        ((BEHIND, rows, 512), bf),
        ((BEHIND, rows, 512), bf),
        ((rows, 1536), bf),
        ((rows, width), f32),
        ((rows, width), bf),
    ]
    for piece in ((16, width), (144, 128), (144, 128)):
        scratch += [((4, *piece), bf), ((3, *piece), bf), (piece, bf)]
    return pl.pallas_call(
        back_kernel,
        out_shape=tuple(jax.ShapeDtypeStruct(*o) for o in outs),
        in_specs=[ANY] * 16,
        out_specs=(ANY,) * len(outs),
        scratch_shapes=[pltpu.VMEM(*v) for v in scratch]
        + [
            pltpu.SemaphoreType.DMA((40,)),
            pltpu.SemaphoreType.DMA((176,)),
            pltpu.SemaphoreType.DMA((176,)),
        ],
        compiler_params=comm_params(3),
        name="attention_backward",
    )(*args)


def on_device(
    tokens, lengths, attn_gain, w_query, w_keyval, w_out, mlp_gain, w_gate, w_up, w_down, cotangent
):
    width = tokens.shape[1]
    live_count = lengths[0, 0]
    row = lax.broadcasted_iota(jnp.int32, (16, 256), 0)
    wide = lambda gain: jnp.pad(gain, (0, 112))[None]
    misc = jnp.where(
        row == 0,
        wide(attn_gain),
        jnp.where(row == 1, wide(mlp_gain), live_count.astype(jnp.bfloat16)),
    )
    frequency = np.power(10000.0, -2.0 * np.arange(128) / 256).astype(np.float32)
    (
        miscs, qkv_all, out_all, gu_all, branch_all,
        normed1, queries, all_kv, probs, attended, middle, normed2, rope,
    ) = front(
        tokens, cotangent, misc, jnp.asarray(np.tile(frequency[None], (8, 1))),
        w_query, w_keyval, w_out, w_gate, w_up,
    )
    grad_normed2, branch, grad_gu, grad_d = feed_forward(
        normed2, branch_all, gu_all.reshape(width, -1), w_down
    )
    sum_gu, sum_d, sum_q, sum_kv, sum_wo, outputs, grad_inputs = back(
        grad_gu, grad_d, branch, grad_normed2, middle, miscs, tokens, cotangent,
        rope, queries, all_kv, probs, attended, qkv_all, out_all, normed1,
    )
    grad_gate_w, grad_up_w, grad_down, grad_q, grad_kv, grad_wo = finish(
        sum_gu, sum_d.reshape(FF_PAD, width), sum_q, sum_kv, sum_wo.reshape(128, width)
    )
    gains = sum_kv[0, 2]
    gains = jnp.concatenate([gains[:2], gains[16:18, :16]], axis=1).astype(jnp.float32)
    return (
        outputs,
        grad_inputs,
        gains[0],
        grad_q,
        grad_kv,
        grad_wo,
        gains[1],
        grad_gate_w,
        grad_up_w,
        grad_down,
    )


def solution(mesh):
    placed = (
        P(("rep", "shard"), None),
        P("rep", "shard"),
        P("shard"),
        P("shard", None),
        P("shard", None),
        P("shard", None),
        P("shard"),
        P("shard", None),
        P("shard", None),
        P("shard", None),
        P(("rep", "shard"), None),
    )
    return jax.shard_map(
        on_device,
        mesh=mesh,
        in_specs=placed,
        out_specs=(
            P(("rep", "shard"), None),
            P(("rep", "shard"), None),
            P("shard"),
            P("shard", None),
            P("shard", None),
            P("shard", None),
            P("shard"),
            P("shard", None),
            P("shard", None),
            P("shard", None),
        ),
        check_vma=False,
    )
```

```python
import functools

import jax
import jax.numpy as jnp
import numpy as np
from jax import lax
from jax.experimental import pallas as pl
from jax.experimental.pallas import tpu as pltpu
from jax.sharding import PartitionSpec as P

MESH = pl.DeviceIdType.MESH
WINDOW = 512
EPSILON = 1e-06
MASKED = -1e30
VMEM_LIMIT = 60 * 2**20
FF_DEV = 864
FF_PAD = 896
PAIRS = FF_PAD // 128
BEHIND = 4


def matmul(former, latter):
    return jnp.dot(former, latter, preferred_element_type=jnp.float32)


def lead_product(former, latter):
    return lax.dot_general(
        former, latter, (((0,), (0,)), ((), ())), preferred_element_type=jnp.float32
    )


def trail_product(former, latter):
    return lax.dot_general(
        former, latter, (((1,), (1,)), ((), ())), preferred_element_type=jnp.float32
    )


class Place:
    def __init__(self):
        rep, shard = lax.axis_index("rep"), lax.axis_index("shard")
        self.rep, self.shard = rep, shard
        self.y, self.z_lo, self.core = rep // 4, (rep // 2) % 2, rep % 2
        self.z_hi, self.x = shard // 4, shard % 4

    def device(self, dx=0, dy=0, mirror=0, swap_lo=0, sibling=0):
        z_lo = (self.z_lo + mirror + swap_lo) % 2
        rep = (((self.y + dy) % 4) * 2 + z_lo) * 2 + (self.core + sibling) % 2
        return (rep, ((self.z_hi + mirror) % 2) * 4 + (self.x + dx) % 4)

    def over_group(self, dx, mirror):
        return self.device(dx=dx, mirror=mirror)

    def shard_at(self, j, p):
        return ((self.z_hi + p) % 2) * 4 + (self.x + STEPS[j]) % 4


STEPS = (0, 1, 3, 2)


class Wire:
    def __init__(self, send_sems, recv_sems):
        self.send_sems, self.recv_sems, self.made = send_sems, recv_sems, []

    def copy(self, src, dst, device):
        k = len(self.made)
        made = pltpu.make_async_remote_copy(
            src_ref=src,
            dst_ref=dst,
            send_sem=self.send_sems.at[k],
            recv_sem=self.recv_sems.at[k],
            device_id=device,
            device_id_type=MESH,
        )
        self.made.append(made)
        return made

    def drain(self):
        for made in self.made:
            made.wait_send()


def greet(devices):
    barrier = pltpu.get_barrier_semaphore()
    for device in devices:
        pl.semaphore_signal(barrier, inc=1, device_id=device, device_id_type=MESH)
    pl.semaphore_wait(barrier, len(devices))


HOPS = (
    ((0, 0), (0, 1), 1, 0, 1),
    ((0, 0), (0, 1), 2, 0, 1),
    ((0, 0), (2, 0), 1, 1, 0),
    ((0, 0), (2, 0), 2, 1, 0),
    ((0, 0), (1, 0), 1, 3, 0),
    ((0, 0), (1, 0), 2, 3, 0),
    ((0, 1), (2, 1), 1, 1, 0),
    ((0, 1), (1, 1), 1, 3, 0),
    ((2, 0), (3, 0), 1, 1, 0),
    ((1, 0), (3, 0), 2, 3, 0),
    ((2, 0), (2, 1), 2, 0, 1),
    ((1, 0), (1, 1), 2, 0, 1),
    ((2, 1), (3, 1), 1, 1, 0),
    ((1, 1), (3, 1), 2, 3, 0),
)
FIRST = (0, 2, 5, 1, 3, 4)
ONWARD = {0: (6, 7), 2: (8,), 3: (10,), 5: (9, 11), 6: (12,), 11: (13,)}
SERVE = (0, 2, 5, 3, 11, 6, 1, 4, 7, 8, 9, 10, 12, 13)
WHOLE = {1: (0, 1), 3: (2, 0), 4: (1, 0), 7: (1, 1), 9: (3, 0), 10: (2, 1), 13: (3, 1)}
HOPS_FAR = tuple(HOPS[k] for k in (13, 12, 9, 8))
RING = (
    ((0, 0), (2, 0), 0, 1, 0),
    ((0, 0), (1, 0), 0, 3, 0),
    ((2, 0), (3, 0), 1, 1, 0),
    ((1, 0), (3, 0), 2, 3, 0),
)
RING_ONWARD = {0: (2,), 1: (3,)}


def gather_tree(wire, device_of, hops, own, slot, cut, absolute):
    copies = []
    for source, target, part, dx, mirror in hops:
        src = own if source == (0, 0) else slot(*source)
        dst = slot(*(source if absolute else target))
        copies.append(wire.copy(cut(src, part), cut(dst, part), device_of(dx, mirror)))
    return copies


def arrive(tree, k, after=ONWARD):
    tree[k].wait_recv()
    for n in after.get(k, ()):
        tree[n].start()


def add_into(target, source):
    target[...] = (target[...].astype(jnp.float32) + source[...].astype(jnp.float32)).astype(
        target.dtype
    )


class SumTree:
    def __init__(self, wire, device_of, hops, slot, cut, landings):
        self.hops, self.slot, self.cut, self.landings = hops, slot, cut, landings
        self.copies = [
            wire.copy(cut(slot(*target), part), landing, device_of((4 - dx) % 4, mirror))
            for (_, target, part, dx, mirror), landing in zip(hops, landings)
        ]

    def start(self, *hops):
        for k in hops:
            self.copies[k].start()

    def absorb(self, *hops):
        for k in hops:
            source, _, part, _, _ = self.hops[k]
            self.copies[k].wait_recv()
            add_into(self.cut(self.slot(*source), part), self.landings[k])

    def send_far(self):
        self.start(13, 12, 9, 8)

    def send_mid(self):
        self.start(7, 4, 10)

    def send_near(self):
        self.absorb(13)
        self.start(11)
        self.absorb(12)
        self.start(6)
        self.absorb(8)
        self.start(2)

    def send_next(self):
        self.absorb(9, 11)
        self.start(5)
        self.absorb(10)
        self.start(3)

    def send_last(self):
        self.absorb(6, 7)
        self.start(0)

    def finish(self, axis):
        halves = []
        for part in (1, 2):
            total = self.cut(self.slot(0, 0), part)[...].astype(jnp.float32)
            for k in (4, 2, 0):
                self.copies[k + part - 1].wait_recv()
                total = total + self.landings[k + part - 1][...].astype(jnp.float32)
            halves.append(total)
        return jnp.concatenate(halves, axis=axis)


def front_kernel(
    tokens, cot, misc, freq, w_query, w_keyval, w_out, w_gate, w_up,
    o_misc, o_qkv, o_wo, o_gu, o_gb, o_normed1, o_q, o_kv, o_probs, o_att, o_middle, o_normed2, o_rope,
    x_ref, cot_ref, miscs, freq_ref, wqkv, wo, gate, up, packed, gb_own, normed1, q_ref, kv_ref,
    bias, probs, att, middle, normed2, rope,
    local_sems, send_sems, recv_sems,
):
    place = Place()
    wire = Wire(send_sems, recv_sems)
    core, me, y = place.core, place.shard, place.y
    rows, width = tokens.shape
    at = place.shard_at
    others = [(j, p) for p in (0, 1) for j in range(4) if (j, p) != (0, 0)]
    group = [place.device(dx=STEPS[j], mirror=p) for j, p in others]
    sequence = [(place.rep, at(j, p)) for j, p in others]
    sibling = place.device(sibling=1)
    column = [place.device(dy=d) for d in (1, 3, 2)]
    locals_ = []

    def local(src, dst):
        copy = pltpu.make_async_copy(src, dst, local_sems.at[len(locals_)])
        copy.start()
        locals_.append(copy)
        return copy

    load_x = local(tokens, x_ref)
    load_cot = local(cot, cot_ref)
    load_misc = local(misc, miscs.at[me])
    load_freq = local(freq, freq_ref)
    load_gate = local(w_gate, gate)
    load_up = local(w_up, up)
    load_own = [
        local(w_query, wqkv.at[me, :, pl.ds(0, 1024)]),
        local(w_keyval, wqkv.at[me, :, pl.ds(1024, 512)]),
        local(w_out, wo.at[me]),
    ]
    greet([sibling] + group + [d for d, (j, p) in zip(sequence, others) if p == 1] + column)

    def lanes_from(base, size):
        def cut(ref, part):
            start, count = ((0, size), (0, size // 2), (size // 2, size // 2))[part]
            start = pl.multiple_of(core * size + (base + start), 128)
            return ref.at[:, pl.ds(start, count)]

        return cut

    def cut_wo(ref, part):
        start, size = ((0, 64), (0, 32), (32, 32))[part]
        return ref.at[pl.ds(pl.multiple_of(core * 64 + start, 32), size)]

    def cut_gb(ref, part):
        return ref if part == 0 else ref.at[pl.ds((part - 1) * 96, 96)]

    def cut_gu(ref):
        return ref.at[:, pl.ds(pl.multiple_of(core * FF_PAD, 128), FF_PAD)]

    cut_q, cut_kv = lanes_from(0, 512), lanes_from(1024, 256)
    slot_qkv = lambda j, p: wqkv.at[at(j, p)]
    slot_wo = lambda j, p: wo.at[at(j, p)]
    slot_gb = lambda j, p: o_gb.at[j, p]
    misc_copies = [wire.copy(misc, miscs.at[me], device) for device in sequence]
    for copy in misc_copies:
        copy.start()
    for load in load_own:
        load.wait()
    own = wqkv.at[me]
    trees = [
        gather_tree(wire, place.over_group, HOPS, own, slot_qkv, cut_q, True),
        gather_tree(wire, place.over_group, HOPS, own, slot_qkv, cut_kv, True),
        gather_tree(wire, place.over_group, HOPS, wo.at[me], slot_wo, cut_wo, True),
    ]
    cuts = [cut_q, cut_kv, cut_wo]
    slots = [slot_qkv, slot_qkv, slot_wo]
    passes = [
        {k: wire.copy(cut(slot(*jp), 0), cut(slot(*jp), 0), sibling) for k, jp in WHOLE.items()}
        for cut, slot in zip(cuts, slots)
    ]
    for tree in trees:
        for k in FIRST:
            tree[k].start()

    load_x.wait()
    inputs = x_ref[...].astype(jnp.float32)
    inverse1 = lax.rsqrt(jnp.mean(inputs * inputs, axis=1, keepdims=True) + EPSILON)
    middle[...] = inputs * inverse1
    load_gate.wait()
    load_up.wait()
    for d in range(8):
        for t in range(PAIRS):
            start = FF_DEV * d + 128 * t
            size = min(128, FF_DEV - 128 * t)
            for k, weight in enumerate((gate, up)):
                block = weight[:, start : start + size]
                if size < 128:
                    block = jnp.concatenate(
                        [block, jnp.zeros((block.shape[0], 128 - size), block.dtype)], axis=1
                    )
                packed[d, :, 256 * t + 128 * k : 256 * t + 128 * (k + 1)] = block

    def attn(*hops):
        for k in hops:
            for tree, onward in zip(trees, passes):
                arrive(tree, k)
                if k in onward:
                    onward[k].start()

    z_of = lambda p: (place.z_hi + p) % 2
    shard_from = lambda d, p: z_of(p) * 4 + (place.x + y + d) % 4
    turn = []
    for p in (0, 1):
        target = z_of(p) * 4 + (place.x - y + 4) % 4
        turn.append(
            wire.copy(
                cut_gu(packed.at[target]), cut_gu(o_gu.at[me]), place.device(dx=4 - y, mirror=p)
            )
        )
    away, home = y > 0, y == 0
    keep_own = pltpu.make_async_copy(
        cut_gu(packed.at[me]), cut_gu(o_gu.at[me]), local_sems.at[len(locals_)]
    )
    locals_.append(None)
    turn[1].start()
    pl.when(away)(turn[0].start)
    pl.when(home)(keep_own.start)

    def over_y(dx, mirror):
        return place.device(dy=dx)

    def cut_block(ref, part):
        start, size = ((0, 144), (0, 80), (80, 64))[part]
        return ref.at[pl.ds(start, size), pl.ds(pl.multiple_of(core * FF_PAD, 128), FF_PAD)]

    gu_slots = [lambda j, _, p=p: o_gu.at[shard_from(STEPS[j], p)] for p in (0, 1)]
    gu_trees = [
        gather_tree(wire, over_y, RING, slot(0, 0), slot, cut_block, True) for slot in gu_slots
    ]
    gu_passes = {
        (j, p): wire.copy(
            cut_gu(o_gu.at[shard_from(STEPS[j], p)]),
            cut_gu(o_gu.at[shard_from(STEPS[j], p)]),
            sibling,
        )
        for j in range(4)
        for p in (0, 1)
    }

    def over(k, j):
        for p in (0, 1):
            arrive(gu_trees[p], k, RING_ONWARD)
            if j:
                gu_passes[j, p].start()

    attn(0, 2, 5)
    load_cot.wait()
    load_misc.wait()
    load_freq.wait()
    live_col = (
        lax.broadcasted_iota(jnp.int32, (rows, 1), 0).astype(jnp.float32)
        < miscs[me].astype(jnp.float32)[2:3, :1]
    )
    gb_own[...] = jnp.where(live_col, cot_ref[...].astype(jnp.float32), 0.0).astype(jnp.bfloat16)
    gb_tree = gather_tree(wire, place.over_group, HOPS, gb_own, slot_gb, cut_gb, False)
    attn(3, 11, 6)
    pl.when(away)(turn[0].wait_recv)
    turn[1].wait_recv()
    pl.when(home)(keep_own.wait)
    for p in (0, 1):
        gu_trees[p][0].start()
        gu_trees[p][1].start()
        gu_passes[0, p].start()
    for k in FIRST:
        gb_tree[k].start()
    local(gb_own, o_gb.at[0, 0])
    attn(1, 4, 7, 8, 9, 10, 12, 13)

    for copy in misc_copies:
        copy.wait_recv()
    as_float = [miscs[s].astype(jnp.float32) for s in range(8)]
    gain1 = jnp.concatenate([m[0:1, :144] for m in as_float], axis=1)
    gain2 = jnp.concatenate([m[1:2, :144] for m in as_float], axis=1)
    normed = (middle[...] * gain1).astype(jnp.bfloat16)
    normed1[...] = normed
    for k in WHOLE:
        passes[0][k].wait_recv()
        passes[1][k].wait_recv()
    live = [m[2:3, :1] for m in as_float]
    start_of = []
    for i in range(BEHIND + 1):
        total = jnp.zeros((1, 1), jnp.float32)
        for s in range(8):
            total = total + jnp.where(s < me - i, 1.0, 0.0) * live[s]
        start_of.append(total)
    row = lax.broadcasted_iota(jnp.int32, (rows, 1), 0).astype(jnp.float32)
    query_pos = start_of[0] + row
    angles = query_pos * freq_ref[0:1, :]
    cosine, sine_part = jnp.cos(angles), jnp.sin(angles)
    rope[:, :128] = cosine
    rope[:, 128:] = sine_part
    weights = wqkv.reshape(width, 1536)

    def turned(vectors):
        first, second = vectors[:, :128], vectors[:, 128:]
        return jnp.concatenate(
            [first * cosine - second * sine_part, second * cosine + first * sine_part], axis=1
        )

    projected = matmul(normed, weights[:, 1024:1536])
    kv_ref[0, :, :256] = turned(projected[:, :256]).astype(jnp.bfloat16)
    kv_ref[0, :, 256:] = projected[:, 256:].astype(jnp.bfloat16)
    x, upper = place.x, place.z_hi == 1
    cross_kv = wire.copy(kv_ref.at[0], kv_ref.at[BEHIND], (place.rep, at(0, 1)))
    near_kv, far_kv = [], []
    for i in range(1, BEHIND):
        target = (place.rep, 4 * place.z_hi + (x + i) % 4)
        near_kv.append(wire.copy(kv_ref.at[0], kv_ref.at[i], target))
        far_kv.append(wire.copy(kv_ref.at[BEHIND], kv_ref.at[i], target))
    pl.when(jnp.logical_not(upper))(cross_kv.start)
    for i, copy in enumerate(near_kv):
        pl.when(x + (i + 1) < 4)(copy.start)
    for i in range(1, BEHIND + 1):

        @pl.when(me < i)
        def _():
            kv_ref[i] = jnp.zeros(kv_ref.shape[1:], kv_ref.dtype)

    def pass_kv():
        pl.when(upper)(cross_kv.wait_recv)
        for i, copy in enumerate(far_kv):
            pl.when(jnp.logical_and(upper, x + (i + 1) > 3))(copy.start)

    def have_kv():
        for i, (near, far) in enumerate(zip(near_kv, far_kv)):
            pl.when(x >= i + 1)(near.wait_recv)
            pl.when(jnp.logical_and(upper, x < i + 1))(far.wait_recv)

    scaling = 256 ** (-0.5)
    for h in range(4):
        heads = matmul(normed, weights[:, 256 * h : 256 * (h + 1)])
        q_ref[h] = (turned(heads) * scaling).astype(jnp.bfloat16)

    index = lax.broadcasted_iota(jnp.int32, (1, (BEHIND + 1) * rows), 1)
    key_pos = jnp.zeros(index.shape, jnp.float32)
    key_live = jnp.zeros(index.shape, jnp.float32)
    for i in range(BEHIND + 1):
        inside = jnp.logical_and(index >= i * rows, index < (i + 1) * rows)
        within = (index - i * rows).astype(jnp.float32)
        live_i = jnp.zeros((1, 1), jnp.float32)
        for s in range(8):
            live_i = live_i + jnp.where(me - i == s, 1.0, 0.0) * live[s]
        key_pos = jnp.where(inside, start_of[i] + within, key_pos)
        key_live = jnp.where(inside, jnp.where(within < live_i, 1.0, 0.0), key_live)
    ahead = query_pos - key_pos
    allowed = jnp.logical_and(
        jnp.logical_and(ahead >= 0.0, ahead < float(WINDOW)), key_live > 0.5
    )
    bias[...] = jnp.where(allowed, 0.0, MASKED)
    pass_kv()

    over(0, 2)
    over(1, 1)
    for k in SERVE[:4]:
        arrive(gb_tree, k)
    have_kv()
    all_kv = kv_ref.reshape((BEHIND + 1) * rows, 512)
    for h in range(4):
        scores = trail_product(q_ref[h], all_kv[:, :256]) + bias[...]
        raised = jnp.exp(scores - jnp.max(scores, axis=1, keepdims=True))
        share = raised * (1.0 / jnp.sum(raised, axis=1, keepdims=True))
        probs[h] = share
        att[:, 256 * h : 256 * (h + 1)] = matmul(
            share.astype(jnp.bfloat16), all_kv[:, 256:]
        ).astype(jnp.bfloat16)
        if h == 1:
            for k in SERVE[4:6]:
                arrive(gb_tree, k)
    for k in WHOLE:
        passes[2][k].wait_recv()
    keep = jnp.where(live_col, 1.0, 0.0)
    mid = x_ref[...].astype(jnp.float32) + keep * matmul(att[...], wo.reshape(1024, width)[...])
    middle[...] = mid
    inverse2 = lax.rsqrt(jnp.mean(mid * mid, axis=1, keepdims=True) + EPSILON)
    normed2[...] = (mid * inverse2 * gain2).astype(jnp.bfloat16)
    for src, dst in (
        (miscs, o_misc),
        (wqkv, o_qkv),
        (wo, o_wo),
        (normed1, o_normed1),
        (q_ref, o_q),
        (kv_ref, o_kv),
        (probs, o_probs),
        (att, o_att),
        (middle, o_middle),
        (normed2, o_normed2),
        (rope, o_rope),
    ):
        local(src, dst)
    over(2, 0)
    over(3, 3)
    for k in SERVE[6:]:
        arrive(gb_tree, k)
    for copy in gu_passes.values():
        copy.wait_recv()
    waited = [id(copy) for copy in near_kv + far_kv + [cross_kv, turn[0]]]
    for copy in locals_[9:]:
        if copy is not None:
            copy.wait()
    pl.when(away)(turn[0].wait_send)
    pl.when(jnp.logical_not(upper))(cross_kv.wait_send)
    for i, (near, far) in enumerate(zip(near_kv, far_kv)):
        pl.when(x + (i + 1) < 4)(near.wait_send)
        pl.when(jnp.logical_and(upper, x + (i + 1) > 3))(far.wait_send)
    for copy in wire.made:
        if id(copy) not in waited:
            copy.wait_send()


ANY = pl.BlockSpec(memory_space=pl.ANY)


def comm_params(collective_id):
    return pltpu.CompilerParams(
        collective_id=collective_id, has_side_effects=True, vmem_limit_bytes=VMEM_LIMIT
    )


def front(tokens, cot, misc, freq, w_query, w_keyval, w_out, w_gate, w_up):
    bf, f32 = jnp.bfloat16, jnp.float32
    rows, width = tokens.shape
    keys = (BEHIND + 1) * rows
    outs = [
        ((8, 16, 256), bf),
        ((8, 144, 1536), bf),
        ((8, 128, width), bf),
        ((8, 144, 2 * FF_PAD), bf),
        ((4, 2, rows, width), bf),
        ((rows, width), bf),
        ((4, rows, 256), bf),
        ((BEHIND + 1, rows, 512), bf),
        ((4, rows, keys), f32),
        ((rows, 1024), bf),
        ((rows, width), f32),
        ((rows, width), bf),
        ((rows, 256), f32),
    ]
    scratch = [
        ((rows, width), bf),
        ((rows, width), bf),
        ((8, 16, 256), bf),
        ((8, 128), f32),
        ((8, 144, 1536), bf),
        ((8, 128, width), bf),
        (w_gate.shape, bf),
        (w_up.shape, bf),
        ((8, 144, 2 * FF_PAD), bf),
        ((rows, width), bf),
        ((rows, width), bf),
        ((4, rows, 256), bf),
        ((BEHIND + 1, rows, 512), bf),
        ((rows, keys), f32),
        ((4, rows, keys), f32),
        ((rows, 1024), bf),
        ((rows, width), f32),
        ((rows, width), bf),
        ((rows, 256), f32),
    ]
    return pl.pallas_call(
        front_kernel,
        out_shape=tuple(jax.ShapeDtypeStruct(*o) for o in outs),
        in_specs=[ANY] * 9,
        out_specs=(ANY,) * len(outs),
        scratch_shapes=[pltpu.VMEM(*v) for v in scratch]
        + [
            pltpu.SemaphoreType.DMA((32,)),
            pltpu.SemaphoreType.DMA((136,)),
            pltpu.SemaphoreType.DMA((136,)),
        ],
        compiler_params=comm_params(1),
        name="attention_forward",
    )(tokens, cot, misc, freq, w_query, w_keyval, w_out, w_gate, w_up)


def finish_kernel(both, d_in, q_in, kv_in, wo_in, gate, up, d_out, q_out, kv_out, wo_out):
    for k, out in enumerate((gate, up)):
        parts = []
        for d in range(8):
            for t in range(PAIRS):
                half, q, first = (k, 3, 0) if t == 3 else (t // 4, t % 4, 128 * k)
                size = min(128, FF_DEV - 128 * t)
                parts.append(both[half, q, d, :, first : first + size])
        out[...] = jnp.concatenate(parts, axis=1).astype(jnp.float32)
    d_out[...] = d_in[...].astype(jnp.float32)
    q_out[...] = q_in[...].astype(jnp.float32)
    for c in range(2):
        for q in range(2):
            start = 256 * c + 128 * q
            kv_out[:, start : start + 128] = kv_in[c, q].astype(jnp.float32)

    @pl.when(pl.program_id(0) == 0)
    def _():
        wo_out[...] = wo_in[...].astype(jnp.float32)


def finish(both, d_in, q_in, kv_in, wo_in):
    rows, width = both.shape[3], d_in.shape[1]
    steps = rows // 16
    shapes = [(rows, 8 * FF_DEV)] * 2 + [(FF_DEV, width), (rows, 1024), (rows, 512), wo_in.shape]
    blocks = [(16, 8 * FF_DEV)] * 2 + [(FF_DEV // steps, width), (16, 1024), (16, 512)]
    by_row = lambda i: (i, 0)
    fixed = pl.BlockSpec(wo_in.shape, lambda i: (0, 0))
    return pl.pallas_call(
        finish_kernel,
        grid=(steps,),
        out_shape=[jax.ShapeDtypeStruct(shape, jnp.float32) for shape in shapes],
        in_specs=[
            pl.BlockSpec((2, 4, 8, 16, 256), lambda i: (0, 0, 0, i, 0)),
            pl.BlockSpec((FF_DEV // steps, width), by_row),
            pl.BlockSpec((16, 1024), by_row),
            pl.BlockSpec((2, 4, 16, 128), lambda i: (0, 0, i, 0)),
            fixed,
        ],
        out_specs=[pl.BlockSpec(block, by_row) for block in blocks] + [fixed],
        compiler_params=pltpu.CompilerParams(vmem_limit_bytes=VMEM_LIMIT),
        name="finish",
    )(both, d_in, q_in, kv_in, wo_in)


ROOT = 0.7978845608028654
CUBE = 0.044715


def ff_kernel(
    own_n, gb_all, wgu_all, wd_all,
    o_gn, o_pb, o_pgu, o_pd,
    nbuf, gb, wgu, wd, gh, hid, ggu, part_g, part_b, out_f32, dgu,
    g_half, dd, r_d, d_whole, d_half_a, d_half_b, z_d,
    r_gu, gu_half, n_turned, b_half,
    local_sems, send_sems, recv_sems,
):
    place = Place()
    wire = Wire(send_sems, recv_sems)
    loads = [
        pltpu.make_async_copy(src, dst, local_sems.at[k])
        for k, (src, dst) in enumerate(
            [(own_n, nbuf.at[0, 0]), (wd_all, wd.at[pl.ds(0, FF_DEV)]), (gb_all, gb), (wgu_all, wgu)]
        )
    ]
    for load in loads:
        load.start()
    core, y = place.core, place.y
    sibling, low = place.device(sibling=1), place.device(swap_lo=1)
    greet(
        [place.device(dx=1), place.device(dx=3), place.device(mirror=1), sibling, low]
        + [place.device(dy=1), place.device(dy=3)]
    )

    def cut(ref, part):
        return ref if part == 0 else ref.at[pl.ds((part - 1) * 96, 96)]

    slot_n = lambda j, p: nbuf.at[j, p]
    tree = gather_tree(wire, place.over_group, HOPS, nbuf.at[0, 0], slot_n, cut, False)
    sum_g = SumTree(
        wire, place.over_group, HOPS, lambda j, p: part_g.at[j, p], cut,
        [g_half.at[k] for k in range(14)],
    )

    def cut_d(ref, part):
        start, size = ((0, 1152), (0, 640), (640, 512))[part]
        return ref.at[:, pl.ds(start, size)]

    quarter_d = dd.at[core, y]
    swap_d = wire.copy(dd.at[1 - core], r_d, sibling)
    sum_d = SumTree(
        wire, lambda dx, mirror: place.device(dy=dx), RING,
        lambda j, p: dd.at[core, (y + STEPS[j]) % 4], cut_d,
        [d_whole.at[0], d_whole.at[1], d_half_a, d_half_b],
    )
    cross_d = wire.copy(quarter_d, z_d, low)

    def cut_lead(ref, part):
        return ref if part == 0 else ref.at[pl.ds((part - 1) * 4, 4)]

    swap_gu = wire.copy(dgu.at[1 - core], r_gu, sibling)
    far_b = SumTree(
        wire, place.over_group, HOPS_FAR, lambda j, p: part_b.at[j, p], cut,
        [b_half.at[k] for k in range(4)],
    )
    far_gu = [
        wire.copy(
            cut_lead(dgu.at[core, (y + 2) % 4], part),
            gu_half.at[part - 1],
            place.device(dy=(3, 1)[part - 1]),
        )
        for part in (1, 2)
    ]
    loads[0].wait()
    for k in FIRST:
        tree[k].start()
    wd[FF_DEV:] = jnp.zeros((FF_PAD - FF_DEV, wd.shape[1]), wd.dtype)
    loads[1].wait()
    loads[2].wait()

    def back_hidden(j):
        rows = jnp.concatenate([gb[j, 0], gb[j, 1]], axis=0)
        gh[j] = trail_product(rows, wd[...])

    def forward(j, first=0, count=384):
        blocks = [nbuf[j, p] for p in (0, 1) if first <= 192 * p < first + count]
        rows = jnp.concatenate(blocks, axis=0) if len(blocks) > 1 else blocks[0]
        span = pl.ds(first, count)

        def tile(t, carry):
            columns = pl.ds(pl.multiple_of(t * 256, 256), 256)
            narrow = pl.ds(pl.multiple_of(t * 128, 128), 128)
            both = matmul(rows, wgu[:, columns])
            gate, up = both[:, :128], both[:, 128:]
            square = gate * gate
            curve = jnp.tanh(gate * (ROOT + ROOT * CUBE * square))
            half_up = 0.5 + 0.5 * curve
            active = gate * half_up
            slope = half_up + active * (1.0 - curve) * (ROOT + 3.0 * ROOT * CUBE * square)
            back = gh[j, span, narrow]
            hid[j, span, narrow] = (active * up).astype(jnp.bfloat16)
            ggu[j, span, columns] = jnp.concatenate(
                [(back * up * slope).astype(jnp.bfloat16), (back * active).astype(jnp.bfloat16)],
                axis=1,
            )
            return carry

        lax.fori_loop(0, PAIRS, tile, 0, unroll=True)

    def back_normed(j, first=0, count=384):
        for start, size in ((0, 512), (512, 512), (1024, 128)):
            block = trail_product(
                ggu[j, first : first + count], wgu[start : start + size, :]
            ).astype(jnp.bfloat16)
            for p in (0, 1):
                if first <= 192 * p < first + count:
                    low = 192 * p - first
                    part_g[j, p, :, start : start + size] = block[low : low + 192]

    def down(j):
        for start, size in ((0, 512), (512, 512), (1024, 128)):
            block = matmul(hid[j], wd[:, start : start + size]).astype(jnp.bfloat16)
            part_b[j, 0, :, start : start + size] = block[:192]
            part_b[j, 1, :, start : start + size] = block[192:]

    hid_rows = hid.reshape(4 * 384, FF_PAD)
    ggu_rows = ggu.reshape(4 * 384, 2 * FF_PAD)
    gb_rows = gb.reshape(4 * 384, 1152)
    dd_rows = dd.reshape(FF_PAD, 1152)
    dgu_rows = dgu.reshape(2, 4, 1152, 256)

    def turn_rows(j):
        rows = jnp.concatenate([nbuf[j, 0], nbuf[j, 1]], axis=0)
        n_turned[:, 384 * j : 384 * (j + 1)] = rows.T

    def grad_half(half):
        def tile(q, carry):
            columns = pl.ds(pl.multiple_of((half * 4 + q) * 256, 256), 256)
            dgu_rows[half, q] = matmul(n_turned[...], ggu_rows[:, columns]).astype(jnp.bfloat16)
            return carry

        lax.fori_loop(0, 3, tile, 0)

    dgu[:, 3, :, :, 128:] = jnp.zeros((2, 8, 144, 128), jnp.bfloat16)
    back_hidden(0)
    back_hidden(1)
    back_hidden(2)
    for k in SERVE[:3]:
        arrive(tree, k)
    back_hidden(3)
    for k in SERVE[3:7]:
        arrive(tree, k)
    loads[3].wait()
    forward(0)
    turn_rows(0)
    for k in SERVE[7:9]:
        arrive(tree, k)
    forward(1)
    for k in SERVE[9:12]:
        arrive(tree, k)
    forward(2)
    turn_rows(1)
    turn_rows(2)
    forward(3, 0, 192)
    back_normed(3, 0, 192)
    sum_g.start(9, 8)
    for k in SERVE[12:]:
        arrive(tree, k)
    forward(3, 192, 192)
    back_normed(3, 192, 192)
    sum_g.start(13, 12)
    back_normed(1)
    back_normed(2)
    sum_g.send_mid()
    for start, size in ((0, 512), (512, 512), (1024, 128)):
        dd_rows[:, start : start + size] = lead_product(
            hid_rows[...], gb_rows[:, start : start + size]
        ).astype(jnp.bfloat16)
    swap_d.start()
    sum_g.send_near()
    back_normed(0)
    sum_g.start(1)
    turn_rows(3)
    middle_tile = matmul(n_turned[...], ggu_rows[:, 768:1024]).astype(jnp.bfloat16)
    dgu_rows[0, 3, :, :128] = middle_tile[:, :128]
    dgu_rows[1, 3, :, :128] = middle_tile[:, 128:]
    down(3)
    swap_d.wait_recv()

    def add_d(i, carry):
        add_into(dd.at[core, i], r_d.at[i])
        return carry

    lax.fori_loop(0, 4, add_d, 0)
    sum_d.start(2, 3)
    sum_g.send_next()
    grad_half(1 - core)
    swap_gu.start()
    sum_g.send_last()
    far_b.start(0, 1, 2, 3)
    sum_d.absorb(2, 3)
    sum_d.start(0, 1)
    grad_half(core)
    down(0)
    swap_gu.wait_recv()

    def add_gu(i, carry):
        add_into(dgu.reshape(2, 32, 144, 256).at[core, i], r_gu.reshape(32, 144, 256).at[i])
        return carry

    lax.fori_loop(0, 32, add_gu, 0)
    for copy in far_gu:
        copy.start()
    sum_d.absorb(0, 1)
    cross_d.start()
    down(1)
    down(2)
    out_f32[...] = sum_g.finish(0)
    store_g = pltpu.make_async_copy(out_f32, o_gn, local_sems.at[6])
    store_g.start()
    cross_d.wait_recv()
    cross_d.wait_send()
    add_into(quarter_d, z_d)
    store_d = pltpu.make_async_copy(quarter_d, o_pd, local_sems.at[7])
    store_d.start()
    far_b.absorb(0, 1, 2, 3)
    store_b = pltpu.make_async_copy(part_b, o_pb, local_sems.at[5])
    store_b.start()
    for part, j in ((1, 2), (2, 1)):
        far_gu[part - 1].wait_recv()
        add_into(
            cut_lead(dgu.at[core, (y + STEPS[j]) % 4], part), gu_half.at[part - 1]
        )
    store_gu = pltpu.make_async_copy(dgu.at[core], o_pgu, local_sems.at[4])
    store_gu.start()
    for store in (store_b, store_gu, store_g, store_d):
        store.wait()
    for copy in wire.made:
        if copy is not cross_d:
            copy.wait_send()


def feed_forward(own_n, gb_all, wgu_all, wd_all):
    bf, f32 = jnp.bfloat16, jnp.float32
    vm = pltpu.VMEM
    tokens, width = own_n.shape
    sums = [vm((14, tokens // 2, width), bf)]
    return pl.pallas_call(
        ff_kernel,
        out_shape=(
            jax.ShapeDtypeStruct((tokens, width), f32),
            jax.ShapeDtypeStruct((4, 2, tokens, width), bf),
            jax.ShapeDtypeStruct((4, 8, 144, 256), bf),
            jax.ShapeDtypeStruct((112, width), bf),
        ),
        in_specs=[ANY] * 4,
        out_specs=(ANY,) * 4,
        scratch_shapes=[
            vm((4, 2, tokens, width), bf),
            vm((4, 2, tokens, width), bf),
            vm(wgu_all.shape, bf),
            vm((FF_PAD, width), bf),
            vm((4, 2 * tokens, FF_PAD), f32),
            vm((4, 2 * tokens, FF_PAD), bf),
            vm((4, 2 * tokens, 2 * FF_PAD), bf),
            vm((4, 2, tokens, width), bf),
            vm((4, 2, tokens, width), bf),
            vm((tokens, width), f32),
            vm((2, 4, 8, 144, 256), bf),
        ]
        + sums
        + [
            vm((2, 4, 112, width), bf),
            vm((4, 112, width), bf),
            vm((2, 112, width), bf),
            vm((112, 640), bf),
            vm((112, 512), bf),
            vm((112, width), bf),
            vm((4, 8, 144, 256), bf),
            vm((2, 4, 144, 256), bf),
            vm((width, 8 * tokens), bf),
            vm((4, tokens // 2, width), bf),
        ]
        + [
            pltpu.SemaphoreType.DMA((8,)),
            pltpu.SemaphoreType.DMA((48,)),
            pltpu.SemaphoreType.DMA((48,)),
        ],
        compiler_params=comm_params(2),
        name="feed_forward",
    )(own_n, gb_all, wgu_all, wd_all)


def back_kernel(
    p_gu, p_d, part_b_all, gn2_all, middle_all, miscs_all, tokens, cot, rope_all, q_all, kv_all,
    probs_all, att_all, wqkv_all, wo_all, normed1_all,
    o_gu, o_d, o_q, o_kv, o_wo, o_out, o_grad,
    h_gu, gu_whole, z_gu, f_gu, piece_d,
    part_b, b_half, gn2, middle, miscs, x_ref, cot_ref, rope, q_ref, kv_ref, probs, att,
    wqkv, wo, normed1, dq, r_q, q_parts, dkv, r_kv, kv_parts, dwo, r_wo, w_half,
    gkv, kv_out, kv_in, gproj, gmid, out_bf,
    s_wo, y_wo, z_wo, s_q, y_q, z_q, s_kv, y_kv, z_kv,
    local_sems, send_sems, recv_sems,
):
    place = Place()
    wire = Wire(send_sems, recv_sems)
    core, me, y, rep = place.core, place.shard, place.y, place.rep
    rows, width = tokens.shape
    at = place.shard_at
    others = [(j, p) for p in (0, 1) for j in range(4) if (j, p) != (0, 0)]
    group = [place.device(dx=STEPS[j], mirror=p) for j, p in others]
    sequence = [(rep, at(j, 1)) for j in range(4)]
    sibling = place.device(sibling=1)
    column = [place.device(dy=d) for d in (1, 3, 2)]
    low = place.device(swap_lo=1)
    locals_ = []

    def local(src, dst):
        copy = pltpu.make_async_copy(src, dst, local_sems.at[len(locals_)])
        copy.start()
        locals_.append(copy)
        return copy

    loads = [
        local(src, dst)
        for src, dst in (
            (miscs_all, miscs),
            (gn2_all, gn2),
            (middle_all, middle),
            (cot, cot_ref),
            (att_all, att),
            (wo_all, wo),
        )
    ]
    load_gu = local(p_gu, h_gu)
    load_d = local(p_d, piece_d)
    load_b = local(part_b_all, part_b)
    both_cores = [place.device(dy=d, sibling=1) for d in (1, 3, 2)]
    greet([sibling, low] + group + column + sequence + both_cores)
    loads_heads = [
        local(src, dst)
        for src, dst in ((q_all, q_ref), (kv_all, kv_ref), (probs_all, probs), (rope_all, rope))
    ]
    load_x = local(tokens, x_ref)
    load_n = local(normed1_all, normed1)
    load_w = local(wqkv_all, wqkv)
    loaded = len(locals_)

    def over_y(dx, mirror):
        return place.device(dy=dx)

    def cut_lead(ref, part):
        return ref if part == 0 else ref.at[pl.ds((part - 1) * 4, 4)]

    def cut_rows(size):
        def cut(ref, part):
            return ref if part == 0 else ref.at[pl.ds((part - 1) * size, size)]

        return cut

    def cut_lanes(size):
        def cut(ref, part):
            return ref if part == 0 else ref.at[:, pl.ds((part - 1) * size, size)]

        return cut

    def cut_d(ref, part):
        start, size = ((0, width), (0, 640), (640, 512))[part]
        return ref.at[:, pl.ds(start, size)]

    def added(target, source, count):
        def one(i, carry):
            add_into(target.at[i], source.at[i])
            return carry

        lax.fori_loop(0, count, one, 0)

    chunks = [pl.ds(0, 80), pl.ds(80, 64)]
    near_gu = [
        [
            wire.copy(
                h_gu.at[(y + STEPS[j]) % 4, :, c],
                gu_whole.at[k, :, c],
                place.device(dy=(3, 1)[k]),
            )
            for k, j in enumerate((2, 1))
        ]
        for c in chunks
    ]
    quarters = [h_gu.at[y, :, c] for c in chunks]
    crossings_gu = [wire.copy(h_gu.at[y, :, c], z_gu.at[:, c], low) for c in chunks]
    turns = [
        [
            wire.copy(h_gu.at[y, at(j, p), c], f_gu.at[me, c], device)
            for (j, p), device in zip(others, group)
        ]
        for c in chunks
    ]
    slots_gu = [lambda j, p, c=c: o_gu.at[core, (y + STEPS[j]) % 4, :, c] for c in chunks]
    trees_gu = [
        gather_tree(wire, over_y, RING, f_gu.at[:, c], slot, cut_lead, True)
        for c, slot in zip(chunks, slots_gu)
    ]
    passes_gu = [
        [
            wire.copy(f_gu.at[:, c] if j == 0 else slot(j, 0), slot(j, 0), sibling)
            for j in range(4)
        ]
        for c, slot in zip(chunks, slots_gu)
    ]

    def cross(i):
        for k, copy in enumerate(near_gu[i]):
            copy.wait_recv()
            added(quarters[i], gu_whole.at[k, :, chunks[i]], 8)
        crossings_gu[i].start()

    def turn(i):
        crossings_gu[i].wait_recv()
        crossings_gu[i].wait_send()
        added(quarters[i], z_gu.at[:, chunks[i]], 8)
        for copy in turns[i]:
            copy.start()
        f_gu[me, chunks[i]] = h_gu[y, me, chunks[i]]

    def spread(i):
        for copy in turns[i]:
            copy.wait_recv()
        for copy in (trees_gu[i][0], trees_gu[i][1], passes_gu[i][0]):
            copy.start()
        local(f_gu.at[:, chunks[i]], slots_gu[i](0, 0))

    def spread_on(i, k):
        arrive(trees_gu[i], k, RING_ONWARD)
        if k != 2:
            passes_gu[i][(2, 1, None, 3)[k]].start()

    load_gu.wait()
    for copy in near_gu[0] + near_gu[1]:
        copy.start()

    sum_b = SumTree(
        wire, place.over_group, HOPS, lambda j, p: part_b.at[j, p], cut_rows(96),
        [b_half.at[k] for k in range(14)],
    )
    load_b.wait()
    sum_b.start(7, 6, 4, 2, 11, 10, 1)

    load_d.wait()
    slot_d = lambda j, p: o_d.at[core, (y + STEPS[j]) % 4]
    tree_d = gather_tree(wire, over_y, RING, piece_d, slot_d, cut_d, True)
    pass_d = [
        wire.copy(piece_d if j == 0 else slot_d(j, 0), slot_d(j, 0), sibling) for j in range(4)
    ]

    for load in loads:
        load.wait()
    as_float = [miscs[s].astype(jnp.float32) for s in range(8)]
    gain1 = jnp.concatenate([m[0:1, :144] for m in as_float], axis=1)
    gain2 = jnp.concatenate([m[1:2, :144] for m in as_float], axis=1)
    row = lax.broadcasted_iota(jnp.int32, (rows, 1), 0).astype(jnp.float32)
    keep = jnp.where(row < miscs[me].astype(jnp.float32)[2:3, :1], 1.0, 0.0)
    mid = middle[...]
    inverse2 = lax.rsqrt(jnp.mean(mid * mid, axis=1, keepdims=True) + EPSILON)
    scaled2 = mid * inverse2
    grad2 = gn2[...]
    grad_gain2 = jnp.sum(grad2 * scaled2, axis=0, keepdims=True)
    grad2 = grad2 * gain2
    grad_mid = cot_ref[...].astype(jnp.float32) + inverse2 * (
        grad2 - scaled2 * jnp.mean(grad2 * scaled2, axis=1, keepdims=True)
    )
    gmid[...] = grad_mid
    grad_attn = (keep * grad_mid).astype(jnp.bfloat16)
    for start in range(0, width, 384):
        block = lead_product(att[...], grad_attn[:, start : start + 384]).astype(jnp.bfloat16)
        block = block.reshape(8, 2, 64, 384)
        dwo[0, :, :, start : start + 384] = block[:, 0]
        dwo[1, :, :, start : start + 384] = block[:, 1]
    swap_wo = wire.copy(dwo.at[1 - core], r_wo, sibling)
    swap_wo.start()
    grad_att = trail_product(grad_attn, wo.reshape(1024, width)[...]).astype(jnp.bfloat16)

    for load in loads_heads:
        load.wait()
    keys = (BEHIND + 1) * rows
    all_kv = kv_ref.reshape(keys, 512)
    flat = gkv.reshape(keys, 512)
    cosine, sine_part = rope[:, :128], rope[:, 128:]
    scaling = 256 ** (-0.5)

    def turned_back(vectors):
        first, second = vectors[:, :128], vectors[:, 128:]
        return jnp.concatenate(
            [first * cosine + second * sine_part, second * cosine - first * sine_part], axis=1
        )

    for h in range(4):
        share = probs[h]
        share_low = share.astype(jnp.bfloat16)
        grad_h = grad_att[:, 256 * h : 256 * (h + 1)]
        grad_probs = trail_product(grad_h, all_kv[:, 256:])
        delta = jnp.sum(share * grad_probs, axis=1, keepdims=True)
        grad_scores = (share * (grad_probs - delta)).astype(jnp.bfloat16)
        grad_keys = lead_product(grad_scores, q_ref[h])
        grad_values = lead_product(share_low, grad_h)
        if h == 0:
            flat[:, :256] = grad_keys
            flat[:, 256:] = grad_values
        else:
            flat[:, :256] += grad_keys
            flat[:, 256:] += grad_values
        grad_q = matmul(grad_scores, all_kv[:, :256])
        gproj[:, 256 * h : 256 * (h + 1)] = (turned_back(grad_q) * scaling).astype(jnp.bfloat16)
        if h == 1:
            cross(0)
            for copy in (tree_d[0], tree_d[1], pass_d[0]):
                copy.start()
            local(piece_d, slot_d(0, 0))
    x, upper = place.x, place.z_hi == 1
    sends = []
    for i in range(1, BEHIND):
        kv_out[i - 1] = gkv[i].astype(jnp.bfloat16)
        target = (rep, 4 * place.z_hi + (x + (4 - i)) % 4)
        sends.append(wire.copy(kv_out.at[i - 1], kv_in.at[i - 1], target))
        pl.when(jnp.logical_or(upper, x >= i))(sends[-1].start)

        @pl.when(jnp.logical_not(jnp.logical_or(upper, x + i <= 3)))
        def _():
            kv_in[i - 1] = jnp.zeros(kv_in.shape[1:], kv_in.dtype)

    plane_kv = wire.copy(kv_out.at[BEHIND - 1], kv_in.at[BEHIND - 1], (rep, at(0, 1)))

    @pl.when(upper)
    def _():
        kv_in[BEHIND - 1] = jnp.zeros(kv_in.shape[1:], kv_in.dtype)

    def collect_kv():
        through = gkv[BEHIND]
        for i, copy in enumerate(sends):
            pl.when(jnp.logical_or(upper, x + (i + 1) <= 3))(copy.wait_recv)
            through = through + jnp.where(x + (i + 1) > 3, 1.0, 0.0) * kv_in[i].astype(jnp.float32)
        kv_out[BEHIND - 1] = through.astype(jnp.bfloat16)
        pl.when(upper)(plane_kv.start)

    load_n.wait()
    dq_rows = dq.reshape(2, width, 512)
    for t in range(4):
        dq_rows[t // 2, :, 256 * (t % 2) : 256 * (t % 2 + 1)] = lead_product(
            normed1[...], gproj[:, 256 * t : 256 * (t + 1)]
        ).astype(jnp.bfloat16)
    swap_q = wire.copy(dq.at[1 - core], r_q, sibling)
    swap_q.start()
    cross(1)
    swap_wo.wait_recv()
    added(dwo.at[core], r_wo, 8)
    sum_wo = SumTree(
        wire, place.over_group, HOPS, lambda j, p: dwo.at[core, at(j, p)], cut_rows(32),
        [w_half.at[k] for k in range(14)],
    )
    sum_wo.send_far()
    sum_wo.send_mid()
    sum_wo.start(1)
    load_x.wait()
    load_w.wait()
    weights = wqkv.reshape(width, 1536)
    gn2[...] = trail_product(gproj[:, :1024], weights[:, :1024])
    turn(0)
    swap_q.wait_recv()
    added(dq.at[core], r_q, 8)
    direct_q = [
        wire.copy(dq.at[core, at(j, p)], q_parts.at[i], device)
        for i, ((j, p), device) in enumerate(zip(others, group))
    ]
    for copy in direct_q:
        copy.start()
    collect_kv()
    turn(1)
    sum_wo.send_near()
    spread(0)

    pl.when(jnp.logical_not(upper))(plane_kv.wait_recv)
    grad_kv = gkv[0] + kv_in[BEHIND - 1].astype(jnp.float32)
    for i in range(BEHIND - 1):
        grad_kv = grad_kv + jnp.where(x + (i + 1) <= 3, 1.0, 0.0) * kv_in[i].astype(jnp.float32)
    gproj[:, 1024:1280] = turned_back(grad_kv[:, :256]).astype(jnp.bfloat16)
    gproj[:, 1280:1536] = grad_kv[:, 256:].astype(jnp.bfloat16)
    for t in range(2):
        dkv[t, :, :144] = (
            lead_product(normed1[...], gproj[:, 1024 + 256 * t : 1280 + 256 * t])
            .astype(jnp.bfloat16)
            .reshape(8, 144, 256)
        )
    inputs = x_ref[...].astype(jnp.float32)
    inverse1 = lax.rsqrt(jnp.mean(inputs * inputs, axis=1, keepdims=True) + EPSILON)
    scaled1 = inputs * inverse1
    grad1 = gn2[...] + trail_product(gproj[:, 1024:], weights[:, 1024:])
    grad_gain1 = jnp.sum(grad1 * scaled1, axis=0, keepdims=True)
    for s in range(8):
        cols = slice(144 * s, 144 * (s + 1))
        both = jnp.concatenate(
            [grad_gain1[:, cols], grad_gain2[:, cols], jnp.zeros((14, 144), jnp.float32)], axis=0
        )
        both = jnp.concatenate([both, jnp.zeros((16, 112), jnp.float32)], axis=1)
        dkv[0, s, 144:] = both.astype(jnp.bfloat16)
        dkv[1, s, 144:] = both.astype(jnp.bfloat16)
    swap_kv = wire.copy(dkv.at[1 - core], r_kv, sibling)
    swap_kv.start()
    spread(1)
    sum_wo.send_next()
    def over_column(source, landing):
        copies = [
            wire.copy(source.at[(y + d) % 4], landing.at[i], device)
            for i, (d, device) in enumerate(zip((1, 3, 2), column))
        ]
        for copy in copies:
            copy.start()
        return copies

    def over_low(copies, source, landing, other):
        for copy in copies:
            copy.wait_recv()
        mine = source[y].astype(jnp.float32)
        for i in range(3):
            mine = mine + landing[i].astype(jnp.float32)
        source[y] = mine.astype(jnp.bfloat16)
        crossing = wire.copy(source.at[y], other, low)
        crossing.start()
        return crossing

    def to_all(crossing, source, other, slot):
        crossing.wait_recv()
        crossing.wait_send()
        add_into(source.at[y], other)
        made = [wire.copy(source.at[y], slot(core, y), device) for device in column + [sibling]]
        for copy in made:
            copy.start()
        local(source.at[y], slot(core, y))
        return made

    def to_both(crossing, source, other, slot):
        made = to_all(crossing, source, other, slot)
        made += [
            wire.copy(source.at[y], slot(core, y), place.device(dy=d, sibling=1)) for d in (1, 3, 2)
        ]
        for copy in made[4:]:
            copy.start()
        return made

    def pass_on(made, slot):
        ends = [made[3]]
        for d, copy in zip((3, 1, 2), made):
            copy.wait_recv()
            held = slot(core, (y + d) % 4)
            ends.append(wire.copy(held, held, sibling))
            ends[-1].start()
        return ends

    slot_wo = lambda c, q: o_wo.at[c, q]
    slot_q = lambda c, q: o_q.at[:, pl.ds(pl.multiple_of(c * 512 + q * 128, 128), 128)]
    slot_kv = lambda c, q: o_kv.at[c, q]
    swap_kv.wait_recv()
    added(dkv.at[core], r_kv, 8)
    direct_kv = [
        wire.copy(dkv.at[core, at(j, p)], kv_parts.at[i], device)
        for i, ((j, p), device) in enumerate(zip(others, group))
    ]
    for copy in direct_kv:
        copy.start()
    sum_wo.send_last()
    grad1 = grad1 * gain1
    gmid[...] += inverse1 * (grad1 - scaled1 * jnp.mean(grad1 * scaled1, axis=1, keepdims=True))
    local(gmid, o_grad)
    total = dq[core, me].astype(jnp.float32)
    for i, copy in enumerate(direct_q):
        copy.wait_recv()
        total = total + q_parts[i].astype(jnp.float32)
    for q in range(4):
        s_q[q] = total[:, 128 * q : 128 * (q + 1)].astype(jnp.bfloat16)
    over_q = over_column(s_q, y_q)
    for k in (0, 1):
        arrive(tree_d, k, RING_ONWARD)
        pass_d[(2, 1)[k]].start()
    s_wo[...] = sum_wo.finish(0).astype(jnp.bfloat16).reshape(4, 16, width)
    over_wo = over_column(s_wo, y_wo)
    for k in (0, 1):
        spread_on(0, k)
    cross_q = over_low(over_q, s_q, y_q, z_q)
    sum_b.absorb(10)
    sum_b.start(3)
    sum_b.absorb(11)
    sum_b.start(5)
    sum_b.send_last()
    cross_wo = over_low(over_wo, s_wo, y_wo, z_wo)
    total = dkv[core, me].astype(jnp.float32)
    for i, copy in enumerate(direct_kv):
        copy.wait_recv()
        total = total + kv_parts[i].astype(jnp.float32)
    s_kv[0] = total[:144, :128].astype(jnp.bfloat16)
    s_kv[1] = total[:144, 128:].astype(jnp.bfloat16)
    s_kv[2] = jnp.concatenate(
        [total[144:, :128], total[144:, 128:], jnp.zeros((112, 128), jnp.float32)], axis=0
    ).astype(jnp.bfloat16)
    s_kv[3] = jnp.zeros((144, 128), jnp.bfloat16)
    over_kv = over_column(s_kv, y_kv)
    all_q = to_all(cross_q, s_q, z_q, slot_q)
    all_wo = to_all(cross_wo, s_wo, z_wo, slot_wo)
    for k in (0, 1):
        spread_on(1, k)
    cross_kv = over_low(over_kv, s_kv, y_kv, z_kv)
    for k in (2, 3):
        arrive(tree_d, k, RING_ONWARD)
    pass_d[3].start()
    ends = pass_on(all_q, slot_q) + pass_on(all_wo, slot_wo)
    all_kv_sum = to_both(cross_kv, s_kv, z_kv, slot_kv)
    for i in (0, 1):
        for k in (2, 3):
            spread_on(i, k)
    out_bf[...] = (middle[...] + keep * sum_b.finish(0)).astype(jnp.bfloat16)
    local(out_bf, o_out)
    ends += all_kv_sum
    for copy in pass_d + passes_gu[0] + passes_gu[1] + ends:
        copy.wait_recv()
    for copy in locals_[loaded:]:
        copy.wait()
    for i, copy in enumerate(sends):
        pl.when(jnp.logical_or(upper, x >= i + 1))(copy.wait_send)
    pl.when(upper)(plane_kv.wait_send)
    waited = [id(copy) for copy in sends + [plane_kv] + crossings_gu + [cross_wo, cross_q, cross_kv]]
    waited += [id(sum_b.copies[k]) for k in (8, 9, 12, 13)]
    for copy in wire.made:
        if id(copy) not in waited:
            copy.wait_send()


def back(*args):
    bf, f32 = jnp.bfloat16, jnp.float32
    width = 1152
    rows = args[6].shape[0]
    outs = [
        ((2, 4, 8, 144, 256), bf),
        ((2, 4, 112, width), bf),
        ((144, 1024), bf),
        ((2, 4, 144, 128), bf),
        ((2, 4, 16, width), bf),
        ((rows, width), bf),
        ((rows, width), f32),
    ]
    scratch = [
        ((4, 8, 144, 256), bf),
        ((2, 8, 144, 256), bf),
        ((8, 144, 256), bf),
        ((8, 144, 256), bf),
        ((112, width), bf),
        ((4, 2, rows, width), bf),
        ((14, rows // 2, width), bf),
    ]
    scratch += [(a.shape, a.dtype) for a in args[3:16]]
    for whole, parts in (
        ((144, 512), (7, 144, 512)),
        ((160, 256), (7, 160, 256)),
        ((64, width), (14, 32, width)),
    ):
        scratch += [((2, 8, *whole), bf), ((8, *whole), bf), (parts, bf)]
    scratch += [
        ((BEHIND + 1, rows, 512), f32),
        ((BEHIND, rows, 512), bf),
        ((BEHIND, rows, 512), bf),
        ((rows, 1536), bf),
        ((rows, width), f32),
        ((rows, width), bf),
    ]
    for piece in ((16, width), (144, 128), (144, 128)):
        scratch += [((4, *piece), bf), ((3, *piece), bf), (piece, bf)]
    return pl.pallas_call(
        back_kernel,
        out_shape=tuple(jax.ShapeDtypeStruct(*o) for o in outs),
        in_specs=[ANY] * 16,
        out_specs=(ANY,) * len(outs),
        scratch_shapes=[pltpu.VMEM(*v) for v in scratch]
        + [
            pltpu.SemaphoreType.DMA((40,)),
            pltpu.SemaphoreType.DMA((176,)),
            pltpu.SemaphoreType.DMA((176,)),
        ],
        compiler_params=comm_params(3),
        name="attention_backward",
    )(*args)


def on_device(
    tokens, lengths, attn_gain, w_query, w_keyval, w_out, mlp_gain, w_gate, w_up, w_down, cotangent
):
    width = tokens.shape[1]
    live_count = lengths[0, 0]
    row = lax.broadcasted_iota(jnp.int32, (16, 256), 0)
    wide = lambda gain: jnp.pad(gain, (0, 112))[None]
    misc = jnp.where(
        row == 0,
        wide(attn_gain),
        jnp.where(row == 1, wide(mlp_gain), live_count.astype(jnp.bfloat16)),
    )
    frequency = np.power(10000.0, -2.0 * np.arange(128) / 256).astype(np.float32)
    (
        miscs, qkv_all, out_all, gu_all, branch_all,
        normed1, queries, all_kv, probs, attended, middle, normed2, rope,
    ) = front(
        tokens, cotangent, misc, jnp.asarray(np.tile(frequency[None], (8, 1))),
        w_query, w_keyval, w_out, w_gate, w_up,
    )
    grad_normed2, branch, grad_gu, grad_d = feed_forward(
        normed2, branch_all, gu_all.reshape(width, -1), w_down
    )
    sum_gu, sum_d, sum_q, sum_kv, sum_wo, outputs, grad_inputs = back(
        grad_gu, grad_d, branch, grad_normed2, middle, miscs, tokens, cotangent,
        rope, queries, all_kv, probs, attended, qkv_all, out_all, normed1,
    )
    grad_gate_w, grad_up_w, grad_down, grad_q, grad_kv, grad_wo = finish(
        sum_gu, sum_d.reshape(FF_PAD, width), sum_q, sum_kv, sum_wo.reshape(128, width)
    )
    gains = sum_kv[0, 2]
    gains = jnp.concatenate([gains[:2], gains[16:18, :16]], axis=1).astype(jnp.float32)
    return (
        outputs,
        grad_inputs,
        gains[0],
        grad_q,
        grad_kv,
        grad_wo,
        gains[1],
        grad_gate_w,
        grad_up_w,
        grad_down,
    )


def solution(mesh):
    placed = (
        P(("rep", "shard"), None),
        P("rep", "shard"),
        P("shard"),
        P("shard", None),
        P("shard", None),
        P("shard", None),
        P("shard"),
        P("shard", None),
        P("shard", None),
        P("shard", None),
        P(("rep", "shard"), None),
    )
    return jax.shard_map(
        on_device,
        mesh=mesh,
        in_specs=placed,
        out_specs=(
            P(("rep", "shard"), None),
            P(("rep", "shard"), None),
            P("shard"),
            P("shard", None),
            P("shard", None),
            P("shard", None),
            P("shard"),
            P("shard", None),
            P("shard", None),
            P("shard", None),
        ),
        check_vma=False,
    )
```

```python
import functools

import jax
import jax.numpy as jnp
import numpy as np
from jax import lax
from jax.experimental import pallas as pl
from jax.experimental.pallas import tpu as pltpu
from jax.sharding import PartitionSpec as P

MESH = pl.DeviceIdType.MESH
WINDOW = 512
EPSILON = 1e-06
MASKED = -1e30
VMEM_LIMIT = 60 * 2**20
FF_DEV = 864
FF_PAD = 896
PAIRS = FF_PAD // 128
BEHIND = 4


def matmul(former, latter):
    return jnp.dot(former, latter, preferred_element_type=jnp.float32)


def lead_product(former, latter):
    return lax.dot_general(
        former, latter, (((0,), (0,)), ((), ())), preferred_element_type=jnp.float32
    )


def trail_product(former, latter):
    return lax.dot_general(
        former, latter, (((1,), (1,)), ((), ())), preferred_element_type=jnp.float32
    )


class Place:
    def __init__(self):
        rep, shard = lax.axis_index("rep"), lax.axis_index("shard")
        self.rep, self.shard = rep, shard
        self.y, self.z_lo, self.core = rep // 4, (rep // 2) % 2, rep % 2
        self.z_hi, self.x = shard // 4, shard % 4

    def device(self, dx=0, dy=0, mirror=0, swap_lo=0, sibling=0):
        z_lo = (self.z_lo + mirror + swap_lo) % 2
        rep = (((self.y + dy) % 4) * 2 + z_lo) * 2 + (self.core + sibling) % 2
        return (rep, ((self.z_hi + mirror) % 2) * 4 + (self.x + dx) % 4)

    def over_group(self, dx, mirror):
        return self.device(dx=dx, mirror=mirror)

    def shard_at(self, j, p):
        return ((self.z_hi + p) % 2) * 4 + (self.x + STEPS[j]) % 4


STEPS = (0, 1, 3, 2)


class Wire:
    def __init__(self, send_sems, recv_sems):
        self.send_sems, self.recv_sems, self.made = send_sems, recv_sems, []

    def copy(self, src, dst, device):
        k = len(self.made)
        made = pltpu.make_async_remote_copy(
            src_ref=src,
            dst_ref=dst,
            send_sem=self.send_sems.at[k],
            recv_sem=self.recv_sems.at[k],
            device_id=device,
            device_id_type=MESH,
        )
        self.made.append(made)
        return made

    def drain(self):
        for made in self.made:
            made.wait_send()


def greet(devices):
    barrier = pltpu.get_barrier_semaphore()
    for device in devices:
        pl.semaphore_signal(barrier, inc=1, device_id=device, device_id_type=MESH)
    pl.semaphore_wait(barrier, len(devices))


HOPS = (
    ((0, 0), (0, 1), 1, 0, 1),
    ((0, 0), (0, 1), 2, 0, 1),
    ((0, 0), (2, 0), 1, 1, 0),
    ((0, 0), (2, 0), 2, 1, 0),
    ((0, 0), (1, 0), 1, 3, 0),
    ((0, 0), (1, 0), 2, 3, 0),
    ((0, 1), (2, 1), 1, 1, 0),
    ((0, 1), (1, 1), 1, 3, 0),
    ((2, 0), (3, 0), 1, 1, 0),
    ((1, 0), (3, 0), 2, 3, 0),
    ((2, 0), (2, 1), 2, 0, 1),
    ((1, 0), (1, 1), 2, 0, 1),
    ((2, 1), (3, 1), 1, 1, 0),
    ((1, 1), (3, 1), 2, 3, 0),
)
FIRST = (0, 2, 5, 1, 3, 4)
ONWARD = {0: (6, 7), 2: (8,), 3: (10,), 5: (9, 11), 6: (12,), 11: (13,)}
SERVE = (0, 2, 5, 3, 11, 6, 1, 4, 7, 8, 9, 10, 12, 13)
WHOLE = {1: (0, 1), 3: (2, 0), 4: (1, 0), 7: (1, 1), 9: (3, 0), 10: (2, 1), 13: (3, 1)}
HOPS_FAR = tuple(HOPS[k] for k in (13, 12, 9, 8))
RING = (
    ((0, 0), (2, 0), 0, 1, 0),
    ((0, 0), (1, 0), 0, 3, 0),
    ((2, 0), (3, 0), 1, 1, 0),
    ((1, 0), (3, 0), 2, 3, 0),
)
RING_ONWARD = {0: (2,), 1: (3,)}


def gather_tree(wire, device_of, hops, own, slot, cut, absolute):
    copies = []
    for source, target, part, dx, mirror in hops:
        src = own if source == (0, 0) else slot(*source)
        dst = slot(*(source if absolute else target))
        copies.append(wire.copy(cut(src, part), cut(dst, part), device_of(dx, mirror)))
    return copies


def arrive(tree, k, after=ONWARD):
    tree[k].wait_recv()
    for n in after.get(k, ()):
        tree[n].start()


def add_into(target, source):
    target[...] = (target[...].astype(jnp.float32) + source[...].astype(jnp.float32)).astype(
        target.dtype
    )


class SumTree:
    def __init__(self, wire, device_of, hops, slot, cut, landings):
        self.hops, self.slot, self.cut, self.landings = hops, slot, cut, landings
        self.copies = [
            wire.copy(cut(slot(*target), part), landing, device_of((4 - dx) % 4, mirror))
            for (_, target, part, dx, mirror), landing in zip(hops, landings)
        ]

    def start(self, *hops):
        for k in hops:
            self.copies[k].start()

    def absorb(self, *hops):
        for k in hops:
            source, _, part, _, _ = self.hops[k]
            self.copies[k].wait_recv()
            add_into(self.cut(self.slot(*source), part), self.landings[k])

    def send_far(self):
        self.start(13, 12, 9, 8)

    def send_mid(self):
        self.start(7, 4, 10)

    def send_near(self):
        self.absorb(13)
        self.start(11)
        self.absorb(12)
        self.start(6)
        self.absorb(8)
        self.start(2)

    def send_next(self):
        self.absorb(9, 11)
        self.start(5)
        self.absorb(10)
        self.start(3)

    def send_last(self):
        self.absorb(6, 7)
        self.start(0)

    def finish(self, axis):
        halves = []
        for part in (1, 2):
            total = self.cut(self.slot(0, 0), part)[...].astype(jnp.float32)
            for k in (4, 2, 0):
                self.copies[k + part - 1].wait_recv()
                total = total + self.landings[k + part - 1][...].astype(jnp.float32)
            halves.append(total)
        return jnp.concatenate(halves, axis=axis)


def front_kernel(
    tokens, cot, misc, freq, w_query, w_keyval, w_out, w_gate, w_up,
    o_misc, o_qkv, o_wo, o_gu, o_gb, o_normed1, o_q, o_kv, o_probs, o_att, o_middle, o_normed2, o_rope,
    x_ref, cot_ref, miscs, freq_ref, wqkv, wo, gate, up, packed, gb_own, normed1, q_ref, kv_ref,
    bias, probs, att, middle, normed2, rope,
    local_sems, send_sems, recv_sems,
):
    place = Place()
    wire = Wire(send_sems, recv_sems)
    core, me, y = place.core, place.shard, place.y
    rows, width = tokens.shape
    at = place.shard_at
    others = [(j, p) for p in (0, 1) for j in range(4) if (j, p) != (0, 0)]
    group = [place.device(dx=STEPS[j], mirror=p) for j, p in others]
    sequence = [(place.rep, at(j, p)) for j, p in others]
    sibling = place.device(sibling=1)
    column = [place.device(dy=d) for d in (1, 3, 2)]
    locals_ = []

    def local(src, dst):
        copy = pltpu.make_async_copy(src, dst, local_sems.at[len(locals_)])
        copy.start()
        locals_.append(copy)
        return copy

    load_x = local(tokens, x_ref)
    load_cot = local(cot, cot_ref)
    load_misc = local(misc, miscs.at[me])
    load_freq = local(freq, freq_ref)
    load_gate = local(w_gate, gate)
    load_up = local(w_up, up)
    load_own = [
        local(w_query, wqkv.at[me, :, pl.ds(0, 1024)]),
        local(w_keyval, wqkv.at[me, :, pl.ds(1024, 512)]),
        local(w_out, wo.at[me]),
    ]
    greet([sibling] + group + [d for d, (j, p) in zip(sequence, others) if p == 1] + column)

    def lanes_from(base, size):
        def cut(ref, part):
            start, count = ((0, size), (0, size // 2), (size // 2, size // 2))[part]
            start = pl.multiple_of(core * size + (base + start), 128)
            return ref.at[:, pl.ds(start, count)]

        return cut

    def cut_wo(ref, part):
        start, size = ((0, 64), (0, 32), (32, 32))[part]
        return ref.at[pl.ds(pl.multiple_of(core * 64 + start, 32), size)]

    def cut_gb(ref, part):
        return ref if part == 0 else ref.at[pl.ds((part - 1) * 96, 96)]

    def cut_gu(ref):
        return ref.at[:, pl.ds(pl.multiple_of(core * FF_PAD, 128), FF_PAD)]

    cut_q, cut_kv = lanes_from(0, 512), lanes_from(1024, 256)
    slot_qkv = lambda j, p: wqkv.at[at(j, p)]
    slot_wo = lambda j, p: wo.at[at(j, p)]
    slot_gb = lambda j, p: o_gb.at[j, p]
    misc_copies = [wire.copy(misc, miscs.at[me], device) for device in sequence]
    for copy in misc_copies:
        copy.start()
    for load in load_own:
        load.wait()
    own = wqkv.at[me]
    trees = [
        gather_tree(wire, place.over_group, HOPS, own, slot_qkv, cut_q, True),
        gather_tree(wire, place.over_group, HOPS, own, slot_qkv, cut_kv, True),
        gather_tree(wire, place.over_group, HOPS, wo.at[me], slot_wo, cut_wo, True),
    ]
    cuts = [cut_q, cut_kv, cut_wo]
    slots = [slot_qkv, slot_qkv, slot_wo]
    passes = [
        {k: wire.copy(cut(slot(*jp), 0), cut(slot(*jp), 0), sibling) for k, jp in WHOLE.items()}
        for cut, slot in zip(cuts, slots)
    ]
    for tree in trees:
        for k in FIRST:
            tree[k].start()

    load_x.wait()
    inputs = x_ref[...].astype(jnp.float32)
    inverse1 = lax.rsqrt(jnp.mean(inputs * inputs, axis=1, keepdims=True) + EPSILON)
    middle[...] = inputs * inverse1
    load_gate.wait()
    load_up.wait()
    for d in range(8):
        for t in range(PAIRS):
            start = FF_DEV * d + 128 * t
            size = min(128, FF_DEV - 128 * t)
            for k, weight in enumerate((gate, up)):
                block = weight[:, start : start + size]
                if size < 128:
                    block = jnp.concatenate(
                        [block, jnp.zeros((block.shape[0], 128 - size), block.dtype)], axis=1
                    )
                packed[d, :, 256 * t + 128 * k : 256 * t + 128 * (k + 1)] = block

    def attn(*hops):
        for k in hops:
            for tree, onward in zip(trees, passes):
                arrive(tree, k)
                if k in onward:
                    onward[k].start()

    z_of = lambda p: (place.z_hi + p) % 2
    shard_from = lambda d, p: z_of(p) * 4 + (place.x + y + d) % 4
    turn = []
    for p in (0, 1):
        target = z_of(p) * 4 + (place.x - y + 4) % 4
        turn.append(
            wire.copy(
                cut_gu(packed.at[target]), cut_gu(o_gu.at[me]), place.device(dx=4 - y, mirror=p)
            )
        )
    away, home = y > 0, y == 0
    keep_own = pltpu.make_async_copy(
        cut_gu(packed.at[me]), cut_gu(o_gu.at[me]), local_sems.at[len(locals_)]
    )
    locals_.append(None)
    turn[1].start()
    pl.when(away)(turn[0].start)
    pl.when(home)(keep_own.start)

    def over_y(dx, mirror):
        return place.device(dy=dx)

    def cut_block(ref, part):
        start, size = ((0, 144), (0, 80), (80, 64))[part]
        return ref.at[pl.ds(start, size), pl.ds(pl.multiple_of(core * FF_PAD, 128), FF_PAD)]

    gu_slots = [lambda j, _, p=p: o_gu.at[shard_from(STEPS[j], p)] for p in (0, 1)]
    gu_trees = [
        gather_tree(wire, over_y, RING, slot(0, 0), slot, cut_block, True) for slot in gu_slots
    ]
    gu_passes = {
        (j, p): wire.copy(
            cut_gu(o_gu.at[shard_from(STEPS[j], p)]),
            cut_gu(o_gu.at[shard_from(STEPS[j], p)]),
            sibling,
        )
        for j in range(4)
        for p in (0, 1)
    }

    def over(k, j):
        for p in (0, 1):
            arrive(gu_trees[p], k, RING_ONWARD)
            if j:
                gu_passes[j, p].start()

    attn(0, 2, 5)
    load_cot.wait()
    load_misc.wait()
    load_freq.wait()
    live_col = (
        lax.broadcasted_iota(jnp.int32, (rows, 1), 0).astype(jnp.float32)
        < miscs[me].astype(jnp.float32)[2:3, :1]
    )
    gb_own[...] = jnp.where(live_col, cot_ref[...].astype(jnp.float32), 0.0).astype(jnp.bfloat16)
    gb_tree = gather_tree(wire, place.over_group, HOPS, gb_own, slot_gb, cut_gb, False)
    attn(3, 11, 6)
    pl.when(away)(turn[0].wait_recv)
    turn[1].wait_recv()
    pl.when(home)(keep_own.wait)
    for p in (0, 1):
        gu_trees[p][0].start()
        gu_trees[p][1].start()
        gu_passes[0, p].start()
    for k in FIRST:
        gb_tree[k].start()
    local(gb_own, o_gb.at[0, 0])
    attn(1, 4, 7, 8, 9, 10, 12, 13)

    for copy in misc_copies:
        copy.wait_recv()
    as_float = [miscs[s].astype(jnp.float32) for s in range(8)]
    gain1 = jnp.concatenate([m[0:1, :144] for m in as_float], axis=1)
    gain2 = jnp.concatenate([m[1:2, :144] for m in as_float], axis=1)
    normed = (middle[...] * gain1).astype(jnp.bfloat16)
    normed1[...] = normed
    for k in WHOLE:
        passes[0][k].wait_recv()
        passes[1][k].wait_recv()
    live = [m[2:3, :1] for m in as_float]
    start_of = []
    for i in range(BEHIND + 1):
        total = jnp.zeros((1, 1), jnp.float32)
        for s in range(8):
            total = total + jnp.where(s < me - i, 1.0, 0.0) * live[s]
        start_of.append(total)
    row = lax.broadcasted_iota(jnp.int32, (rows, 1), 0).astype(jnp.float32)
    query_pos = start_of[0] + row
    angles = query_pos * freq_ref[0:1, :]
    cosine, sine_part = jnp.cos(angles), jnp.sin(angles)
    rope[:, :128] = cosine
    rope[:, 128:] = sine_part
    weights = wqkv.reshape(width, 1536)

    def turned(vectors):
        first, second = vectors[:, :128], vectors[:, 128:]
        return jnp.concatenate(
            [first * cosine - second * sine_part, second * cosine + first * sine_part], axis=1
        )

    projected = matmul(normed, weights[:, 1024:1536])
    kv_ref[0, :, :256] = turned(projected[:, :256]).astype(jnp.bfloat16)
    kv_ref[0, :, 256:] = projected[:, 256:].astype(jnp.bfloat16)
    x, upper = place.x, place.z_hi == 1
    cross_kv = wire.copy(kv_ref.at[0], kv_ref.at[BEHIND], (place.rep, at(0, 1)))
    near_kv, far_kv = [], []
    for i in range(1, BEHIND):
        target = (place.rep, 4 * place.z_hi + (x + i) % 4)
        near_kv.append(wire.copy(kv_ref.at[0], kv_ref.at[i], target))
        far_kv.append(wire.copy(kv_ref.at[BEHIND], kv_ref.at[i], target))
    pl.when(jnp.logical_not(upper))(cross_kv.start)
    for i, copy in enumerate(near_kv):
        pl.when(x + (i + 1) < 4)(copy.start)
    for i in range(1, BEHIND + 1):

        @pl.when(me < i)
        def _():
            kv_ref[i] = jnp.zeros(kv_ref.shape[1:], kv_ref.dtype)

    def pass_kv():
        pl.when(upper)(cross_kv.wait_recv)
        for i, copy in enumerate(far_kv):
            pl.when(jnp.logical_and(upper, x + (i + 1) > 3))(copy.start)

    def have_kv():
        for i, (near, far) in enumerate(zip(near_kv, far_kv)):
            pl.when(x >= i + 1)(near.wait_recv)
            pl.when(jnp.logical_and(upper, x < i + 1))(far.wait_recv)

    scaling = 256 ** (-0.5)
    for h in range(4):
        heads = matmul(normed, weights[:, 256 * h : 256 * (h + 1)])
        q_ref[h] = (turned(heads) * scaling).astype(jnp.bfloat16)

    index = lax.broadcasted_iota(jnp.int32, (1, (BEHIND + 1) * rows), 1)
    key_pos = jnp.zeros(index.shape, jnp.float32)
    key_live = jnp.zeros(index.shape, jnp.float32)
    for i in range(BEHIND + 1):
        inside = jnp.logical_and(index >= i * rows, index < (i + 1) * rows)
        within = (index - i * rows).astype(jnp.float32)
        live_i = jnp.zeros((1, 1), jnp.float32)
        for s in range(8):
            live_i = live_i + jnp.where(me - i == s, 1.0, 0.0) * live[s]
        key_pos = jnp.where(inside, start_of[i] + within, key_pos)
        key_live = jnp.where(inside, jnp.where(within < live_i, 1.0, 0.0), key_live)
    ahead = query_pos - key_pos
    allowed = jnp.logical_and(
        jnp.logical_and(ahead >= 0.0, ahead < float(WINDOW)), key_live > 0.5
    )
    bias[...] = jnp.where(allowed, 0.0, MASKED)
    pass_kv()

    over(0, 2)
    over(1, 1)
    for k in SERVE[:4]:
        arrive(gb_tree, k)
    have_kv()
    all_kv = kv_ref.reshape((BEHIND + 1) * rows, 512)
    for h in range(4):
        scores = trail_product(q_ref[h], all_kv[:, :256]) + bias[...]
        raised = jnp.exp(scores - jnp.max(scores, axis=1, keepdims=True))
        share = raised * (1.0 / jnp.sum(raised, axis=1, keepdims=True))
        probs[h] = share
        att[:, 256 * h : 256 * (h + 1)] = matmul(
            share.astype(jnp.bfloat16), all_kv[:, 256:]
        ).astype(jnp.bfloat16)
        if h == 1:
            for k in SERVE[4:6]:
                arrive(gb_tree, k)
    for k in WHOLE:
        passes[2][k].wait_recv()
    keep = jnp.where(live_col, 1.0, 0.0)
    mid = x_ref[...].astype(jnp.float32) + keep * matmul(att[...], wo.reshape(1024, width)[...])
    middle[...] = mid
    inverse2 = lax.rsqrt(jnp.mean(mid * mid, axis=1, keepdims=True) + EPSILON)
    normed2[...] = (mid * inverse2 * gain2).astype(jnp.bfloat16)
    for src, dst in (
        (miscs, o_misc),
        (wqkv, o_qkv),
        (wo, o_wo),
        (normed1, o_normed1),
        (q_ref, o_q),
        (kv_ref, o_kv),
        (probs, o_probs),
        (att, o_att),
        (middle, o_middle),
        (normed2, o_normed2),
        (rope, o_rope),
    ):
        local(src, dst)
    over(2, 0)
    over(3, 3)
    for k in SERVE[6:]:
        arrive(gb_tree, k)
    for copy in gu_passes.values():
        copy.wait_recv()
    waited = [id(copy) for copy in near_kv + far_kv + [cross_kv, turn[0]]]
    for copy in locals_[9:]:
        if copy is not None:
            copy.wait()
    pl.when(away)(turn[0].wait_send)
    pl.when(jnp.logical_not(upper))(cross_kv.wait_send)
    for i, (near, far) in enumerate(zip(near_kv, far_kv)):
        pl.when(x + (i + 1) < 4)(near.wait_send)
        pl.when(jnp.logical_and(upper, x + (i + 1) > 3))(far.wait_send)
    for copy in wire.made:
        if id(copy) not in waited:
            copy.wait_send()


ANY = pl.BlockSpec(memory_space=pl.ANY)


def comm_params(collective_id):
    return pltpu.CompilerParams(
        collective_id=collective_id, has_side_effects=True, vmem_limit_bytes=VMEM_LIMIT
    )


def front(tokens, cot, misc, freq, w_query, w_keyval, w_out, w_gate, w_up):
    bf, f32 = jnp.bfloat16, jnp.float32
    rows, width = tokens.shape
    keys = (BEHIND + 1) * rows
    outs = [
        ((8, 16, 256), bf),
        ((8, 144, 1536), bf),
        ((8, 128, width), bf),
        ((8, 144, 2 * FF_PAD), bf),
        ((4, 2, rows, width), bf),
        ((rows, width), bf),
        ((4, rows, 256), bf),
        ((BEHIND + 1, rows, 512), bf),
        ((4, rows, keys), f32),
        ((rows, 1024), bf),
        ((rows, width), f32),
        ((rows, width), bf),
        ((rows, 256), f32),
    ]
    scratch = [
        ((rows, width), bf),
        ((rows, width), bf),
        ((8, 16, 256), bf),
        ((8, 128), f32),
        ((8, 144, 1536), bf),
        ((8, 128, width), bf),
        (w_gate.shape, bf),
        (w_up.shape, bf),
        ((8, 144, 2 * FF_PAD), bf),
        ((rows, width), bf),
        ((rows, width), bf),
        ((4, rows, 256), bf),
        ((BEHIND + 1, rows, 512), bf),
        ((rows, keys), f32),
        ((4, rows, keys), f32),
        ((rows, 1024), bf),
        ((rows, width), f32),
        ((rows, width), bf),
        ((rows, 256), f32),
    ]
    return pl.pallas_call(
        front_kernel,
        out_shape=tuple(jax.ShapeDtypeStruct(*o) for o in outs),
        in_specs=[ANY] * 9,
        out_specs=(ANY,) * len(outs),
        scratch_shapes=[pltpu.VMEM(*v) for v in scratch]
        + [
            pltpu.SemaphoreType.DMA((32,)),
            pltpu.SemaphoreType.DMA((136,)),
            pltpu.SemaphoreType.DMA((136,)),
        ],
        compiler_params=comm_params(1),
        name="attention_forward",
    )(tokens, cot, misc, freq, w_query, w_keyval, w_out, w_gate, w_up)


def finish_kernel(both, d_in, q_in, kv_in, wo_in, gate, up, d_out, q_out, kv_out, wo_out):
    for k, out in enumerate((gate, up)):
        parts = []
        for d in range(8):
            for t in range(PAIRS):
                half, q, first = (k, 3, 0) if t == 3 else (t // 4, t % 4, 128 * k)
                size = min(128, FF_DEV - 128 * t)
                parts.append(both[half, q, d, :, first : first + size])
        out[...] = jnp.concatenate(parts, axis=1).astype(jnp.float32)
    d_out[...] = d_in[...].astype(jnp.float32)
    q_out[...] = q_in[...].astype(jnp.float32)
    for c in range(2):
        for q in range(2):
            start = 256 * c + 128 * q
            kv_out[:, start : start + 128] = kv_in[c, q].astype(jnp.float32)

    @pl.when(pl.program_id(0) == 0)
    def _():
        wo_out[...] = wo_in[...].astype(jnp.float32)


def finish(both, d_in, q_in, kv_in, wo_in):
    rows, width = both.shape[3], d_in.shape[1]
    steps = rows // 16
    shapes = [(rows, 8 * FF_DEV)] * 2 + [(FF_DEV, width), (rows, 1024), (rows, 512), wo_in.shape]
    blocks = [(16, 8 * FF_DEV)] * 2 + [(FF_DEV // steps, width), (16, 1024), (16, 512)]
    by_row = lambda i: (i, 0)
    fixed = pl.BlockSpec(wo_in.shape, lambda i: (0, 0))
    return pl.pallas_call(
        finish_kernel,
        grid=(steps,),
        out_shape=[jax.ShapeDtypeStruct(shape, jnp.float32) for shape in shapes],
        in_specs=[
            pl.BlockSpec((2, 4, 8, 16, 256), lambda i: (0, 0, 0, i, 0)),
            pl.BlockSpec((FF_DEV // steps, width), by_row),
            pl.BlockSpec((16, 1024), by_row),
            pl.BlockSpec((2, 4, 16, 128), lambda i: (0, 0, i, 0)),
            fixed,
        ],
        out_specs=[pl.BlockSpec(block, by_row) for block in blocks] + [fixed],
        compiler_params=pltpu.CompilerParams(vmem_limit_bytes=VMEM_LIMIT),
        name="finish",
    )(both, d_in, q_in, kv_in, wo_in)


ROOT = 0.7978845608028654
CUBE = 0.044715


def ff_kernel(
    own_n, gb_all, wgu_all, wd_all,
    o_gn, o_pb, o_pgu, o_pd,
    nbuf, gb, wgu, wd, gh, hid, ggu, part_g, part_b, out_f32, dgu,
    g_half, dd, r_d, d_whole, d_half_a, d_half_b, z_d,
    r_gu, gu_half, n_turned, b_half,
    local_sems, send_sems, recv_sems,
):
    place = Place()
    wire = Wire(send_sems, recv_sems)
    loads = [
        pltpu.make_async_copy(src, dst, local_sems.at[k])
        for k, (src, dst) in enumerate(
            [(own_n, nbuf.at[0, 0]), (wd_all, wd.at[pl.ds(0, FF_DEV)]), (gb_all, gb), (wgu_all, wgu)]
        )
    ]
    for load in loads:
        load.start()
    core, y = place.core, place.y
    sibling, low = place.device(sibling=1), place.device(swap_lo=1)
    greet(
        [place.device(dx=1), place.device(dx=3), place.device(mirror=1), sibling, low]
        + [place.device(dy=1), place.device(dy=3)]
    )

    def cut(ref, part):
        return ref if part == 0 else ref.at[pl.ds((part - 1) * 96, 96)]

    slot_n = lambda j, p: nbuf.at[j, p]
    tree = gather_tree(wire, place.over_group, HOPS, nbuf.at[0, 0], slot_n, cut, False)
    sum_g = SumTree(
        wire, place.over_group, HOPS, lambda j, p: part_g.at[j, p], cut,
        [g_half.at[k] for k in range(14)],
    )

    def cut_d(ref, part):
        start, size = ((0, 1152), (0, 640), (640, 512))[part]
        return ref.at[:, pl.ds(start, size)]

    quarter_d = dd.at[core, y]
    swap_d = wire.copy(dd.at[1 - core], r_d, sibling)
    sum_d = SumTree(
        wire, lambda dx, mirror: place.device(dy=dx), RING,
        lambda j, p: dd.at[core, (y + STEPS[j]) % 4], cut_d,
        [d_whole.at[0], d_whole.at[1], d_half_a, d_half_b],
    )
    cross_d = wire.copy(quarter_d, z_d, low)

    def cut_lead(ref, part):
        return ref if part == 0 else ref.at[pl.ds((part - 1) * 4, 4)]

    swap_gu = wire.copy(dgu.at[1 - core], r_gu, sibling)
    far_b = SumTree(
        wire, place.over_group, HOPS_FAR, lambda j, p: part_b.at[j, p], cut,
        [b_half.at[k] for k in range(4)],
    )
    far_gu = [
        wire.copy(
            cut_lead(dgu.at[core, (y + 2) % 4], part),
            gu_half.at[part - 1],
            place.device(dy=(3, 1)[part - 1]),
        )
        for part in (1, 2)
    ]
    loads[0].wait()
    for k in FIRST:
        tree[k].start()
    wd[FF_DEV:] = jnp.zeros((FF_PAD - FF_DEV, wd.shape[1]), wd.dtype)
    loads[1].wait()
    loads[2].wait()

    def back_hidden(j):
        rows = jnp.concatenate([gb[j, 0], gb[j, 1]], axis=0)
        gh[j] = trail_product(rows, wd[...])

    def forward(j, first=0, count=384):
        blocks = [nbuf[j, p] for p in (0, 1) if first <= 192 * p < first + count]
        rows = jnp.concatenate(blocks, axis=0) if len(blocks) > 1 else blocks[0]
        span = pl.ds(first, count)

        def tile(t, carry):
            columns = pl.ds(pl.multiple_of(t * 256, 256), 256)
            narrow = pl.ds(pl.multiple_of(t * 128, 128), 128)
            both = matmul(rows, wgu[:, columns])
            gate, up = both[:, :128], both[:, 128:]
            square = gate * gate
            curve = jnp.tanh(gate * (ROOT + ROOT * CUBE * square))
            half_up = 0.5 + 0.5 * curve
            active = gate * half_up
            slope = half_up + active * (1.0 - curve) * (ROOT + 3.0 * ROOT * CUBE * square)
            back = gh[j, span, narrow]
            hid[j, span, narrow] = (active * up).astype(jnp.bfloat16)
            ggu[j, span, columns] = jnp.concatenate(
                [(back * up * slope).astype(jnp.bfloat16), (back * active).astype(jnp.bfloat16)],
                axis=1,
            )
            return carry

        lax.fori_loop(0, PAIRS, tile, 0, unroll=True)

    def back_normed(j, first=0, count=384):
        for start, size in ((0, 512), (512, 512), (1024, 128)):
            block = trail_product(
                ggu[j, first : first + count], wgu[start : start + size, :]
            ).astype(jnp.bfloat16)
            for p in (0, 1):
                if first <= 192 * p < first + count:
                    low = 192 * p - first
                    part_g[j, p, :, start : start + size] = block[low : low + 192]

    def down(j):
        for start, size in ((0, 512), (512, 512), (1024, 128)):
            block = matmul(hid[j], wd[:, start : start + size]).astype(jnp.bfloat16)
            part_b[j, 0, :, start : start + size] = block[:192]
            part_b[j, 1, :, start : start + size] = block[192:]

    hid_rows = hid.reshape(4 * 384, FF_PAD)
    ggu_rows = ggu.reshape(4 * 384, 2 * FF_PAD)
    gb_rows = gb.reshape(4 * 384, 1152)
    dd_rows = dd.reshape(FF_PAD, 1152)
    dgu_rows = dgu.reshape(2, 4, 1152, 256)

    def turn_rows(j):
        rows = jnp.concatenate([nbuf[j, 0], nbuf[j, 1]], axis=0)
        n_turned[:, 384 * j : 384 * (j + 1)] = rows.T

    def grad_half(half):
        def tile(q, carry):
            columns = pl.ds(pl.multiple_of((half * 4 + q) * 256, 256), 256)
            dgu_rows[half, q] = matmul(n_turned[...], ggu_rows[:, columns]).astype(jnp.bfloat16)
            return carry

        lax.fori_loop(0, 3, tile, 0)

    dgu[:, 3, :, :, 128:] = jnp.zeros((2, 8, 144, 128), jnp.bfloat16)
    back_hidden(0)
    back_hidden(1)
    back_hidden(2)
    for k in SERVE[:3]:
        arrive(tree, k)
    back_hidden(3)
    for k in SERVE[3:7]:
        arrive(tree, k)
    loads[3].wait()
    forward(0)
    turn_rows(0)
    for k in SERVE[7:9]:
        arrive(tree, k)
    forward(1)
    for k in SERVE[9:12]:
        arrive(tree, k)
    forward(2)
    turn_rows(1)
    turn_rows(2)
    forward(3, 0, 192)
    back_normed(3, 0, 192)
    sum_g.start(9, 8)
    for k in SERVE[12:]:
        arrive(tree, k)
    forward(3, 192, 192)
    back_normed(3, 192, 192)
    sum_g.start(13, 12)
    back_normed(1)
    back_normed(2)
    sum_g.send_mid()
    for start, size in ((0, 512), (512, 512), (1024, 128)):
        dd_rows[:, start : start + size] = lead_product(
            hid_rows[...], gb_rows[:, start : start + size]
        ).astype(jnp.bfloat16)
    swap_d.start()
    sum_g.send_near()
    back_normed(0)
    sum_g.start(1)
    turn_rows(3)
    middle_tile = matmul(n_turned[...], ggu_rows[:, 768:1024]).astype(jnp.bfloat16)
    dgu_rows[0, 3, :, :128] = middle_tile[:, :128]
    dgu_rows[1, 3, :, :128] = middle_tile[:, 128:]
    down(3)
    swap_d.wait_recv()

    def add_d(i, carry):
        add_into(dd.at[core, i], r_d.at[i])
        return carry

    lax.fori_loop(0, 4, add_d, 0)
    sum_d.start(2, 3)
    sum_g.send_next()
    grad_half(1 - core)
    swap_gu.start()
    sum_g.send_last()
    far_b.start(0, 1, 2, 3)
    sum_d.absorb(2, 3)
    sum_d.start(0, 1)
    grad_half(core)
    down(0)
    swap_gu.wait_recv()

    def add_gu(i, carry):
        add_into(dgu.reshape(2, 32, 144, 256).at[core, i], r_gu.reshape(32, 144, 256).at[i])
        return carry

    lax.fori_loop(0, 32, add_gu, 0)
    for copy in far_gu:
        copy.start()
    sum_d.absorb(0, 1)
    cross_d.start()
    down(1)
    down(2)
    out_f32[...] = sum_g.finish(0)
    store_g = pltpu.make_async_copy(out_f32, o_gn, local_sems.at[6])
    store_g.start()
    cross_d.wait_recv()
    cross_d.wait_send()
    add_into(quarter_d, z_d)
    store_d = pltpu.make_async_copy(quarter_d, o_pd, local_sems.at[7])
    store_d.start()
    far_b.absorb(0, 1, 2, 3)
    store_b = pltpu.make_async_copy(part_b, o_pb, local_sems.at[5])
    store_b.start()
    for part, j in ((1, 2), (2, 1)):
        far_gu[part - 1].wait_recv()
        add_into(
            cut_lead(dgu.at[core, (y + STEPS[j]) % 4], part), gu_half.at[part - 1]
        )
    store_gu = pltpu.make_async_copy(dgu.at[core], o_pgu, local_sems.at[4])
    store_gu.start()
    for store in (store_b, store_gu, store_g, store_d):
        store.wait()
    for copy in wire.made:
        if copy is not cross_d:
            copy.wait_send()


def feed_forward(own_n, gb_all, wgu_all, wd_all):
    bf, f32 = jnp.bfloat16, jnp.float32
    vm = pltpu.VMEM
    tokens, width = own_n.shape
    sums = [vm((14, tokens // 2, width), bf)]
    return pl.pallas_call(
        ff_kernel,
        out_shape=(
            jax.ShapeDtypeStruct((tokens, width), f32),
            jax.ShapeDtypeStruct((4, 2, tokens, width), bf),
            jax.ShapeDtypeStruct((4, 8, 144, 256), bf),
            jax.ShapeDtypeStruct((112, width), bf),
        ),
        in_specs=[ANY] * 4,
        out_specs=(ANY,) * 4,
        scratch_shapes=[
            vm((4, 2, tokens, width), bf),
            vm((4, 2, tokens, width), bf),
            vm(wgu_all.shape, bf),
            vm((FF_PAD, width), bf),
            vm((4, 2 * tokens, FF_PAD), f32),
            vm((4, 2 * tokens, FF_PAD), bf),
            vm((4, 2 * tokens, 2 * FF_PAD), bf),
            vm((4, 2, tokens, width), bf),
            vm((4, 2, tokens, width), bf),
            vm((tokens, width), f32),
            vm((2, 4, 8, 144, 256), bf),
        ]
        + sums
        + [
            vm((2, 4, 112, width), bf),
            vm((4, 112, width), bf),
            vm((2, 112, width), bf),
            vm((112, 640), bf),
            vm((112, 512), bf),
            vm((112, width), bf),
            vm((4, 8, 144, 256), bf),
            vm((2, 4, 144, 256), bf),
            vm((width, 8 * tokens), bf),
            vm((4, tokens // 2, width), bf),
        ]
        + [
            pltpu.SemaphoreType.DMA((8,)),
            pltpu.SemaphoreType.DMA((48,)),
            pltpu.SemaphoreType.DMA((48,)),
        ],
        compiler_params=comm_params(2),
        name="feed_forward",
    )(own_n, gb_all, wgu_all, wd_all)


def back_kernel(
    p_gu, p_d, part_b_all, gn2_all, middle_all, miscs_all, tokens, cot, rope_all, q_all, kv_all,
    probs_all, att_all, wqkv_all, wo_all, normed1_all,
    o_gu, o_d, o_q, o_kv, o_wo, o_out, o_grad,
    h_gu, gu_whole, z_gu, f_gu, piece_d,
    part_b, b_half, gn2, middle, miscs, x_ref, cot_ref, rope, q_ref, kv_ref, probs, att,
    wqkv, wo, normed1, dq, r_q, q_whole, q_half, q_parts, dkv, r_kv, kv_parts, dwo, r_wo, w_whole, w_half, w_parts,
    gkv, kv_out, kv_in, gproj, gmid, out_bf,
    s_wo, z_wo, s_q, z_q, s_kv, y_kv, z_kv,
    local_sems, send_sems, recv_sems,
):
    place = Place()
    wire = Wire(send_sems, recv_sems)
    core, me, y, rep = place.core, place.shard, place.y, place.rep
    rows, width = tokens.shape
    at = place.shard_at
    others = [(j, p) for p in (0, 1) for j in range(4) if (j, p) != (0, 0)]
    group = [place.device(dx=STEPS[j], mirror=p) for j, p in others]
    sequence = [(rep, at(j, 1)) for j in range(4)]
    sibling = place.device(sibling=1)
    column = [place.device(dy=d) for d in (1, 3, 2)]
    low = place.device(swap_lo=1)
    locals_ = []

    def local(src, dst):
        copy = pltpu.make_async_copy(src, dst, local_sems.at[len(locals_)])
        copy.start()
        locals_.append(copy)
        return copy

    loads = [
        local(src, dst)
        for src, dst in (
            (miscs_all, miscs),
            (gn2_all, gn2),
            (middle_all, middle),
            (cot, cot_ref),
            (att_all, att),
            (wo_all, wo),
        )
    ]
    load_gu = local(p_gu, h_gu)
    load_d = local(p_d, piece_d)
    load_b = local(part_b_all, part_b)
    both_cores = [place.device(dy=d, sibling=1) for d in (1, 3, 2)]
    greet([sibling, low] + group + column + sequence + both_cores)
    loads_heads = [
        local(src, dst)
        for src, dst in ((q_all, q_ref), (kv_all, kv_ref), (probs_all, probs), (rope_all, rope))
    ]
    load_x = local(tokens, x_ref)
    load_n = local(normed1_all, normed1)
    load_w = local(wqkv_all, wqkv)
    loaded = len(locals_)

    def over_y(dx, mirror):
        return place.device(dy=dx)

    def cut_lead(ref, part):
        return ref if part == 0 else ref.at[pl.ds((part - 1) * 4, 4)]

    def cut_rows(size):
        def cut(ref, part):
            return ref if part == 0 else ref.at[pl.ds((part - 1) * size, size)]

        return cut

    def cut_lanes(size):
        def cut(ref, part):
            return ref if part == 0 else ref.at[:, pl.ds((part - 1) * size, size)]

        return cut

    def cut_d(ref, part):
        start, size = ((0, width), (0, 640), (640, 512))[part]
        return ref.at[:, pl.ds(start, size)]

    def added(target, source, count):
        def one(i, carry):
            add_into(target.at[i], source.at[i])
            return carry

        lax.fori_loop(0, count, one, 0)

    chunks = [pl.ds(0, 80), pl.ds(80, 64)]
    near_gu = [
        [
            wire.copy(
                h_gu.at[(y + STEPS[j]) % 4, :, c],
                gu_whole.at[k, :, c],
                place.device(dy=(3, 1)[k]),
            )
            for k, j in enumerate((2, 1))
        ]
        for c in chunks
    ]
    quarters = [h_gu.at[y, :, c] for c in chunks]
    crossings_gu = [wire.copy(h_gu.at[y, :, c], z_gu.at[:, c], low) for c in chunks]
    turns = [
        [
            wire.copy(h_gu.at[y, at(j, p), c], f_gu.at[me, c], device)
            for (j, p), device in zip(others, group)
        ]
        for c in chunks
    ]
    slots_gu = [lambda j, p, c=c: o_gu.at[core, (y + STEPS[j]) % 4, :, c] for c in chunks]
    trees_gu = [
        gather_tree(wire, over_y, RING, f_gu.at[:, c], slot, cut_lead, True)
        for c, slot in zip(chunks, slots_gu)
    ]
    passes_gu = [
        [
            wire.copy(f_gu.at[:, c] if j == 0 else slot(j, 0), slot(j, 0), sibling)
            for j in range(4)
        ]
        for c, slot in zip(chunks, slots_gu)
    ]

    def cross(i):
        for k, copy in enumerate(near_gu[i]):
            copy.wait_recv()
            added(quarters[i], gu_whole.at[k, :, chunks[i]], 8)
        crossings_gu[i].start()

    def turn(i):
        crossings_gu[i].wait_recv()
        crossings_gu[i].wait_send()
        added(quarters[i], z_gu.at[:, chunks[i]], 8)
        for copy in turns[i]:
            copy.start()
        f_gu[me, chunks[i]] = h_gu[y, me, chunks[i]]

    def spread(i):
        for copy in turns[i]:
            copy.wait_recv()
        for copy in (trees_gu[i][0], trees_gu[i][1], passes_gu[i][0]):
            copy.start()
        local(f_gu.at[:, chunks[i]], slots_gu[i](0, 0))

    def spread_on(i, k):
        arrive(trees_gu[i], k, RING_ONWARD)
        if k != 2:
            passes_gu[i][(2, 1, None, 3)[k]].start()

    load_gu.wait()
    for copy in near_gu[0] + near_gu[1]:
        copy.start()

    sum_b = SumTree(
        wire, place.over_group, HOPS, lambda j, p: part_b.at[j, p], cut_rows(96),
        [b_half.at[k] for k in range(14)],
    )
    load_b.wait()
    sum_b.start(7, 6, 4, 2, 11, 10, 1)

    load_d.wait()
    slot_d = lambda j, p: o_d.at[core, (y + STEPS[j]) % 4]
    tree_d = gather_tree(wire, over_y, RING, piece_d, slot_d, cut_d, True)
    pass_d = [
        wire.copy(piece_d if j == 0 else slot_d(j, 0), slot_d(j, 0), sibling) for j in range(4)
    ]

    for load in loads:
        load.wait()
    as_float = [miscs[s].astype(jnp.float32) for s in range(8)]
    gain1 = jnp.concatenate([m[0:1, :144] for m in as_float], axis=1)
    gain2 = jnp.concatenate([m[1:2, :144] for m in as_float], axis=1)
    row = lax.broadcasted_iota(jnp.int32, (rows, 1), 0).astype(jnp.float32)
    keep = jnp.where(row < miscs[me].astype(jnp.float32)[2:3, :1], 1.0, 0.0)
    mid = middle[...]
    inverse2 = lax.rsqrt(jnp.mean(mid * mid, axis=1, keepdims=True) + EPSILON)
    scaled2 = mid * inverse2
    grad2 = gn2[...]
    grad_gain2 = jnp.sum(grad2 * scaled2, axis=0, keepdims=True)
    grad2 = grad2 * gain2
    grad_mid = cot_ref[...].astype(jnp.float32) + inverse2 * (
        grad2 - scaled2 * jnp.mean(grad2 * scaled2, axis=1, keepdims=True)
    )
    gmid[...] = grad_mid
    grad_attn = (keep * grad_mid).astype(jnp.bfloat16)
    for start in range(0, width, 384):
        block = lead_product(att[...], grad_attn[:, start : start + 384]).astype(jnp.bfloat16)
        block = block.reshape(8, 2, 4, 16, 384)
        for c in range(2):
            for q in range(4):
                dwo[c, q, :, :, start : start + 384] = block[:, c, q]
    swap_wo = wire.copy(dwo.at[1 - core], r_wo, sibling)
    swap_wo.start()
    grad_att = trail_product(grad_attn, wo.reshape(1024, width)[...]).astype(jnp.bfloat16)

    for load in loads_heads:
        load.wait()
    keys = (BEHIND + 1) * rows
    all_kv = kv_ref.reshape(keys, 512)
    flat = gkv.reshape(keys, 512)
    cosine, sine_part = rope[:, :128], rope[:, 128:]
    scaling = 256 ** (-0.5)

    def turned_back(vectors):
        first, second = vectors[:, :128], vectors[:, 128:]
        return jnp.concatenate(
            [first * cosine + second * sine_part, second * cosine - first * sine_part], axis=1
        )

    for h in range(4):
        share = probs[h]
        share_low = share.astype(jnp.bfloat16)
        grad_h = grad_att[:, 256 * h : 256 * (h + 1)]
        grad_probs = trail_product(grad_h, all_kv[:, 256:])
        delta = jnp.sum(share * grad_probs, axis=1, keepdims=True)
        grad_scores = (share * (grad_probs - delta)).astype(jnp.bfloat16)
        grad_keys = lead_product(grad_scores, q_ref[h])
        grad_values = lead_product(share_low, grad_h)
        if h == 0:
            flat[:, :256] = grad_keys
            flat[:, 256:] = grad_values
        else:
            flat[:, :256] += grad_keys
            flat[:, 256:] += grad_values
        grad_q = matmul(grad_scores, all_kv[:, :256])
        gproj[:, 256 * h : 256 * (h + 1)] = (turned_back(grad_q) * scaling).astype(jnp.bfloat16)
        if h == 1:
            cross(0)
            for copy in (tree_d[0], tree_d[1], pass_d[0]):
                copy.start()
            local(piece_d, slot_d(0, 0))
    x, upper = place.x, place.z_hi == 1
    sends = []
    for i in range(1, BEHIND):
        kv_out[i - 1] = gkv[i].astype(jnp.bfloat16)
        target = (rep, 4 * place.z_hi + (x + (4 - i)) % 4)
        sends.append(wire.copy(kv_out.at[i - 1], kv_in.at[i - 1], target))
        pl.when(jnp.logical_or(upper, x >= i))(sends[-1].start)

        @pl.when(jnp.logical_not(jnp.logical_or(upper, x + i <= 3)))
        def _():
            kv_in[i - 1] = jnp.zeros(kv_in.shape[1:], kv_in.dtype)

    plane_kv = wire.copy(kv_out.at[BEHIND - 1], kv_in.at[BEHIND - 1], (rep, at(0, 1)))

    @pl.when(upper)
    def _():
        kv_in[BEHIND - 1] = jnp.zeros(kv_in.shape[1:], kv_in.dtype)

    def collect_kv():
        through = gkv[BEHIND]
        for i, copy in enumerate(sends):
            pl.when(jnp.logical_or(upper, x + (i + 1) <= 3))(copy.wait_recv)
            through = through + jnp.where(x + (i + 1) > 3, 1.0, 0.0) * kv_in[i].astype(jnp.float32)
        kv_out[BEHIND - 1] = through.astype(jnp.bfloat16)
        pl.when(upper)(plane_kv.start)

    def over_ring(blocks, whole, half):
        return SumTree(
            wire, over_y, RING, lambda j, p: blocks.at[core, (y + STEPS[j]) % 4], cut_lead,
            [whole.at[0], whole.at[1], half.at[0], half.at[1]],
        )

    def near_ring(tree):
        tree.absorb(2, 3)
        tree.start(0, 1)

    def to_owners(tree, blocks, parts):
        tree.absorb(0, 1)
        copies = [
            wire.copy(blocks.at[core, y, at(j, p)], parts.at[i], device)
            for i, ((j, p), device) in enumerate(zip(others, group))
        ]
        for copy in copies:
            copy.start()
        return copies

    def to_low(copies, blocks, parts, piece, other):
        total = blocks[core, y, me].astype(jnp.float32)
        for i, copy in enumerate(copies):
            copy.wait_recv()
            total = total + parts[i].astype(jnp.float32)
        piece[y] = total.astype(jnp.bfloat16)
        crossing = wire.copy(piece.at[y], other, low)
        crossing.start()
        return crossing

    load_n.wait()
    dq_rows = dq.reshape(2, 4, width, 128)
    for t in range(4):
        block = lead_product(normed1[...], gproj[:, 256 * t : 256 * (t + 1)]).astype(jnp.bfloat16)
        dq_rows[t // 2, 2 * (t % 2)] = block[:, :128]
        dq_rows[t // 2, 2 * (t % 2) + 1] = block[:, 128:]
    swap_q = wire.copy(dq.at[1 - core], r_q, sibling)
    swap_q.start()
    cross(1)
    swap_wo.wait_recv()
    added(dwo.reshape(2, 32, 16, width).at[core], r_wo.reshape(32, 16, width), 32)
    sum_wo = over_ring(dwo, w_whole, w_half)
    sum_wo.start(2, 3)
    load_x.wait()
    load_w.wait()
    weights = wqkv.reshape(width, 1536)
    gn2[...] = trail_product(gproj[:, :1024], weights[:, :1024])
    turn(0)
    swap_q.wait_recv()
    added(dq.reshape(2, 32, 144, 128).at[core], r_q.reshape(32, 144, 128), 32)
    sum_q = over_ring(dq, q_whole, q_half)
    sum_q.start(2, 3)
    collect_kv()
    near_ring(sum_wo)
    turn(1)
    near_ring(sum_q)
    spread(0)

    pl.when(jnp.logical_not(upper))(plane_kv.wait_recv)
    grad_kv = gkv[0] + kv_in[BEHIND - 1].astype(jnp.float32)
    for i in range(BEHIND - 1):
        grad_kv = grad_kv + jnp.where(x + (i + 1) <= 3, 1.0, 0.0) * kv_in[i].astype(jnp.float32)
    gproj[:, 1024:1280] = turned_back(grad_kv[:, :256]).astype(jnp.bfloat16)
    gproj[:, 1280:1536] = grad_kv[:, 256:].astype(jnp.bfloat16)
    for t in range(2):
        dkv[t, :, :144] = (
            lead_product(normed1[...], gproj[:, 1024 + 256 * t : 1280 + 256 * t])
            .astype(jnp.bfloat16)
            .reshape(8, 144, 256)
        )
    inputs = x_ref[...].astype(jnp.float32)
    inverse1 = lax.rsqrt(jnp.mean(inputs * inputs, axis=1, keepdims=True) + EPSILON)
    scaled1 = inputs * inverse1
    grad1 = gn2[...] + trail_product(gproj[:, 1024:], weights[:, 1024:])
    grad_gain1 = jnp.sum(grad1 * scaled1, axis=0, keepdims=True)
    for s in range(8):
        cols = slice(144 * s, 144 * (s + 1))
        both = jnp.concatenate(
            [grad_gain1[:, cols], grad_gain2[:, cols], jnp.zeros((14, 144), jnp.float32)], axis=0
        )
        both = jnp.concatenate([both, jnp.zeros((16, 112), jnp.float32)], axis=1)
        dkv[0, s, 144:] = both.astype(jnp.bfloat16)
        dkv[1, s, 144:] = both.astype(jnp.bfloat16)
    swap_kv = wire.copy(dkv.at[1 - core], r_kv, sibling)
    swap_kv.start()
    direct_wo = to_owners(sum_wo, dwo, w_parts)
    spread(1)
    def over_column(source, landing):
        copies = [
            wire.copy(source.at[(y + d) % 4], landing.at[i], device)
            for i, (d, device) in enumerate(zip((1, 3, 2), column))
        ]
        for copy in copies:
            copy.start()
        return copies

    def over_low(copies, source, landing, other):
        for copy in copies:
            copy.wait_recv()
        mine = source[y].astype(jnp.float32)
        for i in range(3):
            mine = mine + landing[i].astype(jnp.float32)
        source[y] = mine.astype(jnp.bfloat16)
        crossing = wire.copy(source.at[y], other, low)
        crossing.start()
        return crossing

    def to_all(crossing, source, other, slot):
        crossing.wait_recv()
        crossing.wait_send()
        add_into(source.at[y], other)
        made = [wire.copy(source.at[y], slot(core, y), device) for device in column + [sibling]]
        for copy in made:
            copy.start()
        local(source.at[y], slot(core, y))
        return made

    def to_both(crossing, source, other, slot):
        made = to_all(crossing, source, other, slot)
        made += [
            wire.copy(source.at[y], slot(core, y), place.device(dy=d, sibling=1)) for d in (1, 3, 2)
        ]
        for copy in made[4:]:
            copy.start()
        return made

    def pass_on(made, slot):
        ends = [made[3]]
        for d, copy in zip((3, 1, 2), made):
            copy.wait_recv()
            held = slot(core, (y + d) % 4)
            ends.append(wire.copy(held, held, sibling))
            ends[-1].start()
        return ends

    slot_wo = lambda c, q: o_wo.at[c, q]
    slot_q = lambda c, q: o_q.at[:, pl.ds(pl.multiple_of(c * 512 + q * 128, 128), 128)]
    slot_kv = lambda c, q: o_kv.at[c, q]
    swap_kv.wait_recv()
    added(dkv.at[core], r_kv, 8)
    direct_kv = [
        wire.copy(dkv.at[core, at(j, p)], kv_parts.at[i], device)
        for i, ((j, p), device) in enumerate(zip(others, group))
    ]
    for copy in direct_kv:
        copy.start()
    direct_q = to_owners(sum_q, dq, q_parts)
    grad1 = grad1 * gain1
    gmid[...] += inverse1 * (grad1 - scaled1 * jnp.mean(grad1 * scaled1, axis=1, keepdims=True))
    local(gmid, o_grad)
    for k in (0, 1):
        arrive(tree_d, k, RING_ONWARD)
        pass_d[(2, 1)[k]].start()
    cross_wo = to_low(direct_wo, dwo, w_parts, s_wo, z_wo)
    for k in (0, 1):
        spread_on(0, k)
    cross_q = to_low(direct_q, dq, q_parts, s_q, z_q)
    total = dkv[core, me].astype(jnp.float32)
    for i, copy in enumerate(direct_kv):
        copy.wait_recv()
        total = total + kv_parts[i].astype(jnp.float32)
    s_kv[0] = total[:144, :128].astype(jnp.bfloat16)
    s_kv[1] = total[:144, 128:].astype(jnp.bfloat16)
    s_kv[2] = jnp.concatenate(
        [total[144:, :128], total[144:, 128:], jnp.zeros((112, 128), jnp.float32)], axis=0
    ).astype(jnp.bfloat16)
    s_kv[3] = jnp.zeros((144, 128), jnp.bfloat16)
    over_kv = over_column(s_kv, y_kv)
    sum_b.absorb(10)
    sum_b.start(3)
    sum_b.absorb(11)
    sum_b.start(5)
    sum_b.send_last()
    all_wo = to_all(cross_wo, s_wo, z_wo, slot_wo)
    all_q = to_all(cross_q, s_q, z_q, slot_q)
    cross_kv = over_low(over_kv, s_kv, y_kv, z_kv)
    for k in (0, 1):
        spread_on(1, k)
    for k in (2, 3):
        arrive(tree_d, k, RING_ONWARD)
    pass_d[3].start()
    all_kv_sum = to_both(cross_kv, s_kv, z_kv, slot_kv)
    ends = pass_on(all_wo, slot_wo) + pass_on(all_q, slot_q)
    for i in (0, 1):
        for k in (2, 3):
            spread_on(i, k)
    out_bf[...] = (middle[...] + keep * sum_b.finish(0)).astype(jnp.bfloat16)
    local(out_bf, o_out)
    ends += all_kv_sum
    for copy in pass_d + passes_gu[0] + passes_gu[1] + ends:
        copy.wait_recv()
    for copy in locals_[loaded:]:
        copy.wait()
    for i, copy in enumerate(sends):
        pl.when(jnp.logical_or(upper, x >= i + 1))(copy.wait_send)
    pl.when(upper)(plane_kv.wait_send)
    waited = [id(copy) for copy in sends + [plane_kv] + crossings_gu + [cross_wo, cross_q, cross_kv]]
    waited += [id(sum_b.copies[k]) for k in (8, 9, 12, 13)]
    for copy in wire.made:
        if id(copy) not in waited:
            copy.wait_send()


def back(*args):
    bf, f32 = jnp.bfloat16, jnp.float32
    width = 1152
    rows = args[6].shape[0]
    outs = [
        ((2, 4, 8, 144, 256), bf),
        ((2, 4, 112, width), bf),
        ((144, 1024), bf),
        ((2, 4, 144, 128), bf),
        ((2, 4, 16, width), bf),
        ((rows, width), bf),
        ((rows, width), f32),
    ]
    scratch = [
        ((4, 8, 144, 256), bf),
        ((2, 8, 144, 256), bf),
        ((8, 144, 256), bf),
        ((8, 144, 256), bf),
        ((112, width), bf),
        ((4, 2, rows, width), bf),
        ((14, rows // 2, width), bf),
    ]
    scratch += [(a.shape, a.dtype) for a in args[3:16]]
    ring = lambda *b: [(2, 4, 8, *b), (4, 8, *b), (2, 8, *b), (2, 4, *b), (7, *b)]
    parts = ring(144, 128) + [(2, 8, 160, 256), (8, 160, 256), (7, 160, 256)] + ring(16, width)
    scratch += [(part, bf) for part in parts]
    scratch += [
        ((BEHIND + 1, rows, 512), f32),
        ((BEHIND, rows, 512), bf),
        ((BEHIND, rows, 512), bf),
        ((rows, 1536), bf),
        ((rows, width), f32),
        ((rows, width), bf),
    ]
    pieces = [(4, 16, width), (16, width), (4, 144, 128), (144, 128)]
    pieces += [(4, 144, 128), (3, 144, 128), (144, 128)]
    scratch += [(piece, bf) for piece in pieces]
    return pl.pallas_call(
        back_kernel,
        out_shape=tuple(jax.ShapeDtypeStruct(*o) for o in outs),
        in_specs=[ANY] * 16,
        out_specs=(ANY,) * len(outs),
        scratch_shapes=[pltpu.VMEM(*v) for v in scratch]
        + [
            pltpu.SemaphoreType.DMA((40,)),
            pltpu.SemaphoreType.DMA((176,)),
            pltpu.SemaphoreType.DMA((176,)),
        ],
        compiler_params=comm_params(3),
        name="attention_backward",
    )(*args)


def on_device(
    tokens, lengths, attn_gain, w_query, w_keyval, w_out, mlp_gain, w_gate, w_up, w_down, cotangent
):
    width = tokens.shape[1]
    live_count = lengths[0, 0]
    row = lax.broadcasted_iota(jnp.int32, (16, 256), 0)
    wide = lambda gain: jnp.pad(gain, (0, 112))[None]
    misc = jnp.where(
        row == 0,
        wide(attn_gain),
        jnp.where(row == 1, wide(mlp_gain), live_count.astype(jnp.bfloat16)),
    )
    frequency = np.power(10000.0, -2.0 * np.arange(128) / 256).astype(np.float32)
    (
        miscs, qkv_all, out_all, gu_all, branch_all,
        normed1, queries, all_kv, probs, attended, middle, normed2, rope,
    ) = front(
        tokens, cotangent, misc, jnp.asarray(np.tile(frequency[None], (8, 1))),
        w_query, w_keyval, w_out, w_gate, w_up,
    )
    grad_normed2, branch, grad_gu, grad_d = feed_forward(
        normed2, branch_all, gu_all.reshape(width, -1), w_down
    )
    sum_gu, sum_d, sum_q, sum_kv, sum_wo, outputs, grad_inputs = back(
        grad_gu, grad_d, branch, grad_normed2, middle, miscs, tokens, cotangent,
        rope, queries, all_kv, probs, attended, qkv_all, out_all, normed1,
    )
    grad_gate_w, grad_up_w, grad_down, grad_q, grad_kv, grad_wo = finish(
        sum_gu, sum_d.reshape(FF_PAD, width), sum_q, sum_kv, sum_wo.reshape(128, width)
    )
    gains = sum_kv[0, 2]
    gains = jnp.concatenate([gains[:2], gains[16:18, :16]], axis=1).astype(jnp.float32)
    return (
        outputs,
        grad_inputs,
        gains[0],
        grad_q,
        grad_kv,
        grad_wo,
        gains[1],
        grad_gate_w,
        grad_up_w,
        grad_down,
    )


def solution(mesh):
    placed = (
        P(("rep", "shard"), None),
        P("rep", "shard"),
        P("shard"),
        P("shard", None),
        P("shard", None),
        P("shard", None),
        P("shard"),
        P("shard", None),
        P("shard", None),
        P("shard", None),
        P(("rep", "shard"), None),
    )
    return jax.shard_map(
        on_device,
        mesh=mesh,
        in_specs=placed,
        out_specs=(
            P(("rep", "shard"), None),
            P(("rep", "shard"), None),
            P("shard"),
            P("shard", None),
            P("shard", None),
            P("shard", None),
            P("shard"),
            P("shard", None),
            P("shard", None),
            P("shard", None),
        ),
        check_vma=False,
    )
```

```python
import functools

import jax
import jax.numpy as jnp
import numpy as np
from jax import lax
from jax.experimental import pallas as pl
from jax.experimental.pallas import tpu as pltpu
from jax.sharding import PartitionSpec as P

MESH = pl.DeviceIdType.MESH
WINDOW = 512
EPSILON = 1e-06
MASKED = -1e30
VMEM_LIMIT = 60 * 2**20
FF_DEV = 864
FF_PAD = 896
PAIRS = FF_PAD // 128
BEHIND = 4


def matmul(former, latter):
    return jnp.dot(former, latter, preferred_element_type=jnp.float32)


def lead_product(former, latter):
    return lax.dot_general(
        former, latter, (((0,), (0,)), ((), ())), preferred_element_type=jnp.float32
    )


def trail_product(former, latter):
    return lax.dot_general(
        former, latter, (((1,), (1,)), ((), ())), preferred_element_type=jnp.float32
    )


class Place:
    def __init__(self):
        rep, shard = lax.axis_index("rep"), lax.axis_index("shard")
        self.rep, self.shard = rep, shard
        self.y, self.z_lo, self.core = rep // 4, (rep // 2) % 2, rep % 2
        self.z_hi, self.x = shard // 4, shard % 4

    def device(self, dx=0, dy=0, mirror=0, swap_lo=0, sibling=0):
        z_lo = (self.z_lo + mirror + swap_lo) % 2
        rep = (((self.y + dy) % 4) * 2 + z_lo) * 2 + (self.core + sibling) % 2
        return (rep, ((self.z_hi + mirror) % 2) * 4 + (self.x + dx) % 4)

    def over_group(self, dx, mirror):
        return self.device(dx=dx, mirror=mirror)

    def shard_at(self, j, p):
        return ((self.z_hi + p) % 2) * 4 + (self.x + STEPS[j]) % 4


STEPS = (0, 1, 3, 2)


class Wire:
    def __init__(self, send_sems, recv_sems):
        self.send_sems, self.recv_sems, self.made = send_sems, recv_sems, []

    def copy(self, src, dst, device):
        k = len(self.made)
        made = pltpu.make_async_remote_copy(
            src_ref=src,
            dst_ref=dst,
            send_sem=self.send_sems.at[k],
            recv_sem=self.recv_sems.at[k],
            device_id=device,
            device_id_type=MESH,
        )
        self.made.append(made)
        return made

    def drain(self):
        for made in self.made:
            made.wait_send()


def greet(devices):
    barrier = pltpu.get_barrier_semaphore()
    for device in devices:
        pl.semaphore_signal(barrier, inc=1, device_id=device, device_id_type=MESH)
    pl.semaphore_wait(barrier, len(devices))


HOPS = (
    ((0, 0), (0, 1), 1, 0, 1),
    ((0, 0), (0, 1), 2, 0, 1),
    ((0, 0), (2, 0), 1, 1, 0),
    ((0, 0), (2, 0), 2, 1, 0),
    ((0, 0), (1, 0), 1, 3, 0),
    ((0, 0), (1, 0), 2, 3, 0),
    ((0, 1), (2, 1), 1, 1, 0),
    ((0, 1), (1, 1), 1, 3, 0),
    ((2, 0), (3, 0), 1, 1, 0),
    ((1, 0), (3, 0), 2, 3, 0),
    ((2, 0), (2, 1), 2, 0, 1),
    ((1, 0), (1, 1), 2, 0, 1),
    ((2, 1), (3, 1), 1, 1, 0),
    ((1, 1), (3, 1), 2, 3, 0),
)
FIRST = (0, 2, 5, 1, 3, 4)
ONWARD = {0: (6, 7), 2: (8,), 3: (10,), 5: (9, 11), 6: (12,), 11: (13,)}
SERVE = (0, 2, 5, 3, 11, 6, 1, 4, 7, 8, 9, 10, 12, 13)
WHOLE = {1: (0, 1), 3: (2, 0), 4: (1, 0), 7: (1, 1), 9: (3, 0), 10: (2, 1), 13: (3, 1)}
HOPS_FAR = tuple(HOPS[k] for k in (13, 12, 9, 8))
RING = (
    ((0, 0), (2, 0), 0, 1, 0),
    ((0, 0), (1, 0), 0, 3, 0),
    ((2, 0), (3, 0), 1, 1, 0),
    ((1, 0), (3, 0), 2, 3, 0),
)
RING_ONWARD = {0: (2,), 1: (3,)}


def gather_tree(wire, device_of, hops, own, slot, cut, absolute):
    copies = []
    for source, target, part, dx, mirror in hops:
        src = own if source == (0, 0) else slot(*source)
        dst = slot(*(source if absolute else target))
        copies.append(wire.copy(cut(src, part), cut(dst, part), device_of(dx, mirror)))
    return copies


def arrive(tree, k, after=ONWARD):
    tree[k].wait_recv()
    for n in after.get(k, ()):
        tree[n].start()


def add_into(target, source):
    target[...] = (target[...].astype(jnp.float32) + source[...].astype(jnp.float32)).astype(
        target.dtype
    )


class SumTree:
    def __init__(self, wire, device_of, hops, slot, cut, landings):
        self.hops, self.slot, self.cut, self.landings = hops, slot, cut, landings
        self.copies = [
            wire.copy(cut(slot(*target), part), landing, device_of((4 - dx) % 4, mirror))
            for (_, target, part, dx, mirror), landing in zip(hops, landings)
        ]

    def start(self, *hops):
        for k in hops:
            self.copies[k].start()

    def absorb(self, *hops):
        for k in hops:
            source, _, part, _, _ = self.hops[k]
            self.copies[k].wait_recv()
            add_into(self.cut(self.slot(*source), part), self.landings[k])

    def send_far(self):
        self.start(13, 12, 9, 8)

    def send_mid(self):
        self.start(7, 4, 10)

    def send_near(self):
        self.absorb(13)
        self.start(11)
        self.absorb(12)
        self.start(6)
        self.absorb(8)
        self.start(2)

    def send_next(self):
        self.absorb(9, 11)
        self.start(5)
        self.absorb(10)
        self.start(3)

    def send_last(self):
        self.absorb(6, 7)
        self.start(0)

    def finish(self, axis):
        halves = []
        for part in (1, 2):
            total = self.cut(self.slot(0, 0), part)[...].astype(jnp.float32)
            for k in (4, 2, 0):
                self.copies[k + part - 1].wait_recv()
                total = total + self.landings[k + part - 1][...].astype(jnp.float32)
            halves.append(total)
        return jnp.concatenate(halves, axis=axis)


def front_kernel(
    tokens, cot, misc, freq, w_query, w_keyval, w_out, w_gate, w_up,
    o_misc, o_qkv, o_wo, o_gu, o_gb, o_normed1, o_q, o_kv, o_probs, o_att, o_middle, o_normed2, o_rope,
    x_ref, cot_ref, miscs, freq_ref, wqkv, wo, gate, up, packed, gb_own, normed1, q_ref, kv_ref,
    bias, probs, att, middle, normed2, rope, wo_own,
    local_sems, send_sems, recv_sems,
):
    place = Place()
    wire = Wire(send_sems, recv_sems)
    core, me, y = place.core, place.shard, place.y
    rows, width = tokens.shape
    at = place.shard_at
    others = [(j, p) for p in (0, 1) for j in range(4) if (j, p) != (0, 0)]
    group = [place.device(dx=STEPS[j], mirror=p) for j, p in others]
    sequence = [(place.rep, at(j, p)) for j, p in others]
    sibling = place.device(sibling=1)
    column = [place.device(dy=d) for d in (1, 3, 2)]
    locals_ = []

    def local(src, dst):
        copy = pltpu.make_async_copy(src, dst, local_sems.at[len(locals_)])
        copy.start()
        locals_.append(copy)
        return copy

    load_x = local(tokens, x_ref)
    load_cot = local(cot, cot_ref)
    load_misc = local(misc, miscs.at[me])
    load_freq = local(freq, freq_ref)
    load_gate = local(w_gate, gate)
    load_up = local(w_up, up)
    load_own = [
        local(w_query, wqkv.at[me, :, pl.ds(0, 1024)]),
        local(w_keyval, wqkv.at[me, :, pl.ds(1024, 512)]),
        local(w_out, wo_own),
    ]
    greet([sibling] + group + [d for d, (j, p) in zip(sequence, others) if p == 1] + column)

    def lanes_from(base, size):
        def cut(ref, part):
            start, count = ((0, size), (0, size // 2), (size // 2, size // 2))[part]
            start = pl.multiple_of(core * size + (base + start), 128)
            return ref.at[:, pl.ds(start, count)]

        return cut

    def cut_wo(ref, part):
        start, size = ((0, 64), (0, 32), (32, 32))[part]
        return ref.at[pl.ds(pl.multiple_of(core * 64 + start, 32), size)]

    def cut_gb(ref, part):
        return ref if part == 0 else ref.at[pl.ds((part - 1) * 96, 96)]

    def cut_gu(ref):
        return ref.at[:, pl.ds(pl.multiple_of(core * FF_PAD, 128), FF_PAD)]

    cut_q, cut_kv = lanes_from(0, 512), lanes_from(1024, 256)
    slot_qkv = lambda j, p: wqkv.at[at(j, p)]
    slot_gb = lambda j, p: o_gb.at[j, p]
    misc_copies = [wire.copy(misc, miscs.at[me], device) for device in sequence]
    for copy in misc_copies:
        copy.start()
    for load in load_own:
        load.wait()
    own = wqkv.at[me]
    trees = [
        gather_tree(wire, place.over_group, HOPS, own, slot_qkv, cut_q, True),
        gather_tree(wire, place.over_group, HOPS, own, slot_qkv, cut_kv, True),
    ]
    cuts = [cut_q, cut_kv]
    slots = [slot_qkv, slot_qkv]
    passes = [
        {k: wire.copy(cut(slot(*jp), 0), cut(slot(*jp), 0), sibling) for k, jp in WHOLE.items()}
        for cut, slot in zip(cuts, slots)
    ]
    for tree in trees:
        for k in FIRST:
            tree[k].start()

    load_x.wait()
    inputs = x_ref[...].astype(jnp.float32)
    inverse1 = lax.rsqrt(jnp.mean(inputs * inputs, axis=1, keepdims=True) + EPSILON)
    middle[...] = inputs * inverse1
    load_gate.wait()
    load_up.wait()
    for d in range(8):
        for t in range(PAIRS):
            start = FF_DEV * d + 128 * t
            size = min(128, FF_DEV - 128 * t)
            for k, weight in enumerate((gate, up)):
                block = weight[:, start : start + size]
                if size < 128:
                    block = jnp.concatenate(
                        [block, jnp.zeros((block.shape[0], 128 - size), block.dtype)], axis=1
                    )
                packed[d, :, 256 * t + 128 * k : 256 * t + 128 * (k + 1)] = block

    def attn(*hops):
        for k in hops:
            for tree, onward in zip(trees, passes):
                arrive(tree, k)
                if k in onward:
                    onward[k].start()

    z_of = lambda p: (place.z_hi + p) % 2
    shard_from = lambda d, p: z_of(p) * 4 + (place.x + y + d) % 4
    turn = []
    for p in (0, 1):
        target = z_of(p) * 4 + (place.x - y + 4) % 4
        turn.append(
            wire.copy(
                cut_gu(packed.at[target]), cut_gu(o_gu.at[me]), place.device(dx=4 - y, mirror=p)
            )
        )
    away, home = y > 0, y == 0
    keep_own = pltpu.make_async_copy(
        cut_gu(packed.at[me]), cut_gu(o_gu.at[me]), local_sems.at[len(locals_)]
    )
    locals_.append(None)
    held_wo = lambda j, p: cut_wo(wo.at[shard_from(STEPS[j], p)], 0)
    turn_wo = wire.copy(cut_wo(wo_own, 0), cut_wo(wo.at[me], 0), place.device(dx=4 - y))
    keep_wo = pltpu.make_async_copy(
        cut_wo(wo_own, 0), cut_wo(wo.at[me], 0), local_sems.at[len(locals_)]
    )
    locals_.append(None)
    pl.when(away)(turn_wo.start)
    pl.when(home)(keep_wo.start)
    turn[1].start()
    pl.when(away)(turn[0].start)
    pl.when(home)(keep_own.start)

    def over_y(dx, mirror):
        return place.device(dy=dx)

    def cut_block(ref, part):
        start, size = ((0, 144), (0, 80), (80, 64))[part]
        return ref.at[pl.ds(start, size), pl.ds(pl.multiple_of(core * FF_PAD, 128), FF_PAD)]

    gu_slots = [lambda j, _, p=p: o_gu.at[shard_from(STEPS[j], p)] for p in (0, 1)]
    gu_trees = [
        gather_tree(wire, over_y, RING, slot(0, 0), slot, cut_block, True) for slot in gu_slots
    ]
    gu_passes = {
        (j, p): wire.copy(
            cut_gu(o_gu.at[shard_from(STEPS[j], p)]),
            cut_gu(o_gu.at[shard_from(STEPS[j], p)]),
            sibling,
        )
        for j in range(4)
        for p in (0, 1)
    }

    wo_slots = [lambda j, _, p=p: wo.at[shard_from(STEPS[j], p)] for p in (0, 1)]
    wo_trees = [
        gather_tree(wire, over_y, RING, slot(0, 0), slot, cut_wo, True) for slot in wo_slots
    ]
    mirror_wo = wire.copy(held_wo(0, 0), held_wo(0, 0), place.device(mirror=1))
    wo_passes = {
        (j, p): wire.copy(held_wo(j, p), held_wo(j, p), sibling)
        for j in range(4)
        for p in (0, 1)
    }

    def start_wo(p):
        for copy in (wo_trees[p][0], wo_trees[p][1], wo_passes[0, p]):
            copy.start()

    def over_wo(k, j):
        for p in (0, 1):
            arrive(wo_trees[p], k, RING_ONWARD)
            if j:
                wo_passes[j, p].start()

    def over(k, j):
        for p in (0, 1):
            arrive(gu_trees[p], k, RING_ONWARD)
            if j:
                gu_passes[j, p].start()

    attn(0, 2, 5)
    load_cot.wait()
    load_misc.wait()
    load_freq.wait()
    live_col = (
        lax.broadcasted_iota(jnp.int32, (rows, 1), 0).astype(jnp.float32)
        < miscs[me].astype(jnp.float32)[2:3, :1]
    )
    gb_own[...] = jnp.where(live_col, cot_ref[...].astype(jnp.float32), 0.0).astype(jnp.bfloat16)
    gb_tree = gather_tree(wire, place.over_group, HOPS, gb_own, slot_gb, cut_gb, False)
    pl.when(away)(turn_wo.wait_recv)
    pl.when(home)(keep_wo.wait)
    mirror_wo.start()
    start_wo(0)
    attn(3, 11, 6)
    mirror_wo.wait_recv()
    start_wo(1)
    pl.when(away)(turn[0].wait_recv)
    turn[1].wait_recv()
    pl.when(home)(keep_own.wait)
    for p in (0, 1):
        gu_trees[p][0].start()
        gu_trees[p][1].start()
        gu_passes[0, p].start()
    for k in FIRST:
        gb_tree[k].start()
    local(gb_own, o_gb.at[0, 0])
    attn(1, 4, 7, 8, 9, 10, 12, 13)

    for copy in misc_copies:
        copy.wait_recv()
    as_float = [miscs[s].astype(jnp.float32) for s in range(8)]
    gain1 = jnp.concatenate([m[0:1, :144] for m in as_float], axis=1)
    gain2 = jnp.concatenate([m[1:2, :144] for m in as_float], axis=1)
    normed = (middle[...] * gain1).astype(jnp.bfloat16)
    normed1[...] = normed
    for k in WHOLE:
        passes[0][k].wait_recv()
        passes[1][k].wait_recv()
    live = [m[2:3, :1] for m in as_float]
    start_of = []
    for i in range(BEHIND + 1):
        total = jnp.zeros((1, 1), jnp.float32)
        for s in range(8):
            total = total + jnp.where(s < me - i, 1.0, 0.0) * live[s]
        start_of.append(total)
    row = lax.broadcasted_iota(jnp.int32, (rows, 1), 0).astype(jnp.float32)
    query_pos = start_of[0] + row
    angles = query_pos * freq_ref[0:1, :]
    cosine, sine_part = jnp.cos(angles), jnp.sin(angles)
    rope[:, :128] = cosine
    rope[:, 128:] = sine_part
    weights = wqkv.reshape(width, 1536)

    def turned(vectors):
        first, second = vectors[:, :128], vectors[:, 128:]
        return jnp.concatenate(
            [first * cosine - second * sine_part, second * cosine + first * sine_part], axis=1
        )

    projected = matmul(normed, weights[:, 1024:1536])
    kv_ref[0, :, :256] = turned(projected[:, :256]).astype(jnp.bfloat16)
    kv_ref[0, :, 256:] = projected[:, 256:].astype(jnp.bfloat16)
    x, upper = place.x, place.z_hi == 1
    cross_kv = wire.copy(kv_ref.at[0], kv_ref.at[BEHIND], (place.rep, at(0, 1)))
    near_kv, far_kv = [], []
    for i in range(1, BEHIND):
        target = (place.rep, 4 * place.z_hi + (x + i) % 4)
        near_kv.append(wire.copy(kv_ref.at[0], kv_ref.at[i], target))
        far_kv.append(wire.copy(kv_ref.at[BEHIND], kv_ref.at[i], target))
    pl.when(jnp.logical_not(upper))(cross_kv.start)
    for i, copy in enumerate(near_kv):
        pl.when(x + (i + 1) < 4)(copy.start)
    for i in range(1, BEHIND + 1):

        @pl.when(me < i)
        def _():
            kv_ref[i] = jnp.zeros(kv_ref.shape[1:], kv_ref.dtype)

    def pass_kv():
        pl.when(upper)(cross_kv.wait_recv)
        for i, copy in enumerate(far_kv):
            pl.when(jnp.logical_and(upper, x + (i + 1) > 3))(copy.start)

    def have_kv():
        for i, (near, far) in enumerate(zip(near_kv, far_kv)):
            pl.when(x >= i + 1)(near.wait_recv)
            pl.when(jnp.logical_and(upper, x < i + 1))(far.wait_recv)

    scaling = 256 ** (-0.5)
    for h in range(4):
        heads = matmul(normed, weights[:, 256 * h : 256 * (h + 1)])
        q_ref[h] = (turned(heads) * scaling).astype(jnp.bfloat16)

    index = lax.broadcasted_iota(jnp.int32, (1, (BEHIND + 1) * rows), 1)
    key_pos = jnp.zeros(index.shape, jnp.float32)
    key_live = jnp.zeros(index.shape, jnp.float32)
    for i in range(BEHIND + 1):
        inside = jnp.logical_and(index >= i * rows, index < (i + 1) * rows)
        within = (index - i * rows).astype(jnp.float32)
        live_i = jnp.zeros((1, 1), jnp.float32)
        for s in range(8):
            live_i = live_i + jnp.where(me - i == s, 1.0, 0.0) * live[s]
        key_pos = jnp.where(inside, start_of[i] + within, key_pos)
        key_live = jnp.where(inside, jnp.where(within < live_i, 1.0, 0.0), key_live)
    ahead = query_pos - key_pos
    allowed = jnp.logical_and(
        jnp.logical_and(ahead >= 0.0, ahead < float(WINDOW)), key_live > 0.5
    )
    bias[...] = jnp.where(allowed, 0.0, MASKED)
    pass_kv()

    over_wo(0, 2)
    over_wo(1, 1)
    over(0, 2)
    over(1, 1)
    for k in SERVE[:4]:
        arrive(gb_tree, k)
    have_kv()
    all_kv = kv_ref.reshape((BEHIND + 1) * rows, 512)
    for h in range(4):
        scores = trail_product(q_ref[h], all_kv[:, :256]) + bias[...]
        raised = jnp.exp(scores - jnp.max(scores, axis=1, keepdims=True))
        share = raised * (1.0 / jnp.sum(raised, axis=1, keepdims=True))
        probs[h] = share
        att[:, 256 * h : 256 * (h + 1)] = matmul(
            share.astype(jnp.bfloat16), all_kv[:, 256:]
        ).astype(jnp.bfloat16)
        if h == 1:
            for k in SERVE[4:6]:
                arrive(gb_tree, k)
    over_wo(2, 0)
    over_wo(3, 3)
    for copy in wo_passes.values():
        copy.wait_recv()
    keep = jnp.where(live_col, 1.0, 0.0)
    mid = x_ref[...].astype(jnp.float32) + keep * matmul(att[...], wo.reshape(1024, width)[...])
    middle[...] = mid
    inverse2 = lax.rsqrt(jnp.mean(mid * mid, axis=1, keepdims=True) + EPSILON)
    normed2[...] = (mid * inverse2 * gain2).astype(jnp.bfloat16)
    for src, dst in (
        (miscs, o_misc),
        (wqkv, o_qkv),
        (wo, o_wo),
        (normed1, o_normed1),
        (q_ref, o_q),
        (kv_ref, o_kv),
        (probs, o_probs),
        (att, o_att),
        (middle, o_middle),
        (normed2, o_normed2),
        (rope, o_rope),
    ):
        local(src, dst)
    over(2, 0)
    over(3, 3)
    for k in SERVE[6:]:
        arrive(gb_tree, k)
    for copy in gu_passes.values():
        copy.wait_recv()
    waited = [id(copy) for copy in near_kv + far_kv + [cross_kv, turn[0], turn_wo]]
    for copy in locals_[9:]:
        if copy is not None:
            copy.wait()
    pl.when(away)(turn[0].wait_send)
    pl.when(away)(turn_wo.wait_send)
    pl.when(jnp.logical_not(upper))(cross_kv.wait_send)
    for i, (near, far) in enumerate(zip(near_kv, far_kv)):
        pl.when(x + (i + 1) < 4)(near.wait_send)
        pl.when(jnp.logical_and(upper, x + (i + 1) > 3))(far.wait_send)
    for copy in wire.made:
        if id(copy) not in waited:
            copy.wait_send()


ANY = pl.BlockSpec(memory_space=pl.ANY)


def comm_params(collective_id):
    return pltpu.CompilerParams(
        collective_id=collective_id, has_side_effects=True, vmem_limit_bytes=VMEM_LIMIT
    )


def front(tokens, cot, misc, freq, w_query, w_keyval, w_out, w_gate, w_up):
    bf, f32 = jnp.bfloat16, jnp.float32
    rows, width = tokens.shape
    keys = (BEHIND + 1) * rows
    outs = [
        ((8, 16, 256), bf),
        ((8, 144, 1536), bf),
        ((8, 128, width), bf),
        ((8, 144, 2 * FF_PAD), bf),
        ((4, 2, rows, width), bf),
        ((rows, width), bf),
        ((4, rows, 256), bf),
        ((BEHIND + 1, rows, 512), bf),
        ((4, rows, keys), f32),
        ((rows, 1024), bf),
        ((rows, width), f32),
        ((rows, width), bf),
        ((rows, 256), f32),
    ]
    scratch = [
        ((rows, width), bf),
        ((rows, width), bf),
        ((8, 16, 256), bf),
        ((8, 128), f32),
        ((8, 144, 1536), bf),
        ((8, 128, width), bf),
        (w_gate.shape, bf),
        (w_up.shape, bf),
        ((8, 144, 2 * FF_PAD), bf),
        ((rows, width), bf),
        ((rows, width), bf),
        ((4, rows, 256), bf),
        ((BEHIND + 1, rows, 512), bf),
        ((rows, keys), f32),
        ((4, rows, keys), f32),
        ((rows, 1024), bf),
        ((rows, width), f32),
        ((rows, width), bf),
        ((rows, 256), f32),
        (w_out.shape, bf),
    ]
    return pl.pallas_call(
        front_kernel,
        out_shape=tuple(jax.ShapeDtypeStruct(*o) for o in outs),
        in_specs=[ANY] * 9,
        out_specs=(ANY,) * len(outs),
        scratch_shapes=[pltpu.VMEM(*v) for v in scratch]
        + [
            pltpu.SemaphoreType.DMA((32,)),
            pltpu.SemaphoreType.DMA((136,)),
            pltpu.SemaphoreType.DMA((136,)),
        ],
        compiler_params=comm_params(1),
        name="attention_forward",
    )(tokens, cot, misc, freq, w_query, w_keyval, w_out, w_gate, w_up)


def finish_kernel(both, d_in, q_in, kv_in, wo_in, gate, up, d_out, q_out, kv_out, wo_out):
    for k, out in enumerate((gate, up)):
        parts = []
        for d in range(8):
            for t in range(PAIRS):
                half, q, first = (k, 3, 0) if t == 3 else (t // 4, t % 4, 128 * k)
                size = min(128, FF_DEV - 128 * t)
                parts.append(both[half, q, d, :, first : first + size])
        out[...] = jnp.concatenate(parts, axis=1).astype(jnp.float32)
    d_out[...] = d_in[...].astype(jnp.float32)
    q_out[...] = q_in[...].astype(jnp.float32)
    for c in range(2):
        for q in range(2):
            start = 256 * c + 128 * q
            kv_out[:, start : start + 128] = kv_in[c, q].astype(jnp.float32)

    @pl.when(pl.program_id(0) == 0)
    def _():
        wo_out[...] = wo_in[...].astype(jnp.float32)


def finish(both, d_in, q_in, kv_in, wo_in):
    rows, width = both.shape[3], d_in.shape[1]
    steps = rows // 16
    shapes = [(rows, 8 * FF_DEV)] * 2 + [(FF_DEV, width), (rows, 1024), (rows, 512), wo_in.shape]
    blocks = [(16, 8 * FF_DEV)] * 2 + [(FF_DEV // steps, width), (16, 1024), (16, 512)]
    by_row = lambda i: (i, 0)
    fixed = pl.BlockSpec(wo_in.shape, lambda i: (0, 0))
    return pl.pallas_call(
        finish_kernel,
        grid=(steps,),
        out_shape=[jax.ShapeDtypeStruct(shape, jnp.float32) for shape in shapes],
        in_specs=[
            pl.BlockSpec((2, 4, 8, 16, 256), lambda i: (0, 0, 0, i, 0)),
            pl.BlockSpec((FF_DEV // steps, width), by_row),
            pl.BlockSpec((16, 1024), by_row),
            pl.BlockSpec((2, 4, 16, 128), lambda i: (0, 0, i, 0)),
            fixed,
        ],
        out_specs=[pl.BlockSpec(block, by_row) for block in blocks] + [fixed],
        compiler_params=pltpu.CompilerParams(vmem_limit_bytes=VMEM_LIMIT),
        name="finish",
    )(both, d_in, q_in, kv_in, wo_in)


ROOT = 0.7978845608028654
CUBE = 0.044715


def ff_kernel(
    own_n, gb_all, wgu_all, wd_all,
    o_gn, o_pb, o_pgu, o_pd,
    nbuf, gb, wgu, wd, gh, hid, ggu, part_g, part_b, out_f32, dgu,
    g_half, dd, r_d, d_whole, d_half_a, d_half_b, z_d,
    r_gu, gu_half, n_turned, b_half,
    local_sems, send_sems, recv_sems,
):
    place = Place()
    wire = Wire(send_sems, recv_sems)
    loads = [
        pltpu.make_async_copy(src, dst, local_sems.at[k])
        for k, (src, dst) in enumerate(
            [(own_n, nbuf.at[0, 0]), (wd_all, wd.at[pl.ds(0, FF_DEV)]), (gb_all, gb), (wgu_all, wgu)]
        )
    ]
    for load in loads:
        load.start()
    core, y = place.core, place.y
    sibling, low = place.device(sibling=1), place.device(swap_lo=1)
    greet(
        [place.device(dx=1), place.device(dx=3), place.device(mirror=1), sibling, low]
        + [place.device(dy=1), place.device(dy=3)]
    )

    def cut(ref, part):
        return ref if part == 0 else ref.at[pl.ds((part - 1) * 96, 96)]

    slot_n = lambda j, p: nbuf.at[j, p]
    tree = gather_tree(wire, place.over_group, HOPS, nbuf.at[0, 0], slot_n, cut, False)
    sum_g = SumTree(
        wire, place.over_group, HOPS, lambda j, p: part_g.at[j, p], cut,
        [g_half.at[k] for k in range(14)],
    )

    def cut_d(ref, part):
        start, size = ((0, 1152), (0, 640), (640, 512))[part]
        return ref.at[:, pl.ds(start, size)]

    quarter_d = dd.at[core, y]
    swap_d = wire.copy(dd.at[1 - core], r_d, sibling)
    sum_d = SumTree(
        wire, lambda dx, mirror: place.device(dy=dx), RING,
        lambda j, p: dd.at[core, (y + STEPS[j]) % 4], cut_d,
        [d_whole.at[0], d_whole.at[1], d_half_a, d_half_b],
    )
    cross_d = wire.copy(quarter_d, z_d, low)

    def cut_lead(ref, part):
        return ref if part == 0 else ref.at[pl.ds((part - 1) * 4, 4)]

    swap_gu = wire.copy(dgu.at[1 - core], r_gu, sibling)
    far_b = SumTree(
        wire, place.over_group, HOPS_FAR, lambda j, p: part_b.at[j, p], cut,
        [b_half.at[k] for k in range(4)],
    )
    far_gu = [
        wire.copy(
            cut_lead(dgu.at[core, (y + 2) % 4], part),
            gu_half.at[part - 1],
            place.device(dy=(3, 1)[part - 1]),
        )
        for part in (1, 2)
    ]
    loads[0].wait()
    for k in FIRST:
        tree[k].start()
    wd[FF_DEV:] = jnp.zeros((FF_PAD - FF_DEV, wd.shape[1]), wd.dtype)
    loads[1].wait()
    loads[2].wait()

    def back_hidden(j):
        rows = jnp.concatenate([gb[j, 0], gb[j, 1]], axis=0)
        gh[j] = trail_product(rows, wd[...])

    def forward(j, first=0, count=384):
        blocks = [nbuf[j, p] for p in (0, 1) if first <= 192 * p < first + count]
        rows = jnp.concatenate(blocks, axis=0) if len(blocks) > 1 else blocks[0]
        span = pl.ds(first, count)

        def tile(t, carry):
            columns = pl.ds(pl.multiple_of(t * 256, 256), 256)
            narrow = pl.ds(pl.multiple_of(t * 128, 128), 128)
            both = matmul(rows, wgu[:, columns])
            gate, up = both[:, :128], both[:, 128:]
            square = gate * gate
            curve = jnp.tanh(gate * (ROOT + ROOT * CUBE * square))
            half_up = 0.5 + 0.5 * curve
            active = gate * half_up
            slope = half_up + active * (1.0 - curve) * (ROOT + 3.0 * ROOT * CUBE * square)
            back = gh[j, span, narrow]
            hid[j, span, narrow] = (active * up).astype(jnp.bfloat16)
            ggu[j, span, columns] = jnp.concatenate(
                [(back * up * slope).astype(jnp.bfloat16), (back * active).astype(jnp.bfloat16)],
                axis=1,
            )
            return carry

        lax.fori_loop(0, PAIRS, tile, 0, unroll=True)

    def back_normed(j, first=0, count=384):
        for start, size in ((0, 512), (512, 512), (1024, 128)):
            block = trail_product(
                ggu[j, first : first + count], wgu[start : start + size, :]
            ).astype(jnp.bfloat16)
            for p in (0, 1):
                if first <= 192 * p < first + count:
                    low = 192 * p - first
                    part_g[j, p, :, start : start + size] = block[low : low + 192]

    def down(j):
        for start, size in ((0, 512), (512, 512), (1024, 128)):
            block = matmul(hid[j], wd[:, start : start + size]).astype(jnp.bfloat16)
            part_b[j, 0, :, start : start + size] = block[:192]
            part_b[j, 1, :, start : start + size] = block[192:]

    hid_rows = hid.reshape(4 * 384, FF_PAD)
    ggu_rows = ggu.reshape(4 * 384, 2 * FF_PAD)
    gb_rows = gb.reshape(4 * 384, 1152)
    dd_rows = dd.reshape(FF_PAD, 1152)
    dgu_rows = dgu.reshape(2, 4, 1152, 256)

    def turn_rows(j):
        rows = jnp.concatenate([nbuf[j, 0], nbuf[j, 1]], axis=0)
        n_turned[:, 384 * j : 384 * (j + 1)] = rows.T

    def grad_half(half):
        def tile(q, carry):
            columns = pl.ds(pl.multiple_of((half * 4 + q) * 256, 256), 256)
            dgu_rows[half, q] = matmul(n_turned[...], ggu_rows[:, columns]).astype(jnp.bfloat16)
            return carry

        lax.fori_loop(0, 3, tile, 0)

    dgu[:, 3, :, :, 128:] = jnp.zeros((2, 8, 144, 128), jnp.bfloat16)
    back_hidden(0)
    back_hidden(1)
    back_hidden(2)
    for k in SERVE[:3]:
        arrive(tree, k)
    back_hidden(3)
    for k in SERVE[3:7]:
        arrive(tree, k)
    loads[3].wait()
    forward(0)
    turn_rows(0)
    for k in SERVE[7:9]:
        arrive(tree, k)
    forward(1)
    for k in SERVE[9:12]:
        arrive(tree, k)
    forward(2)
    turn_rows(1)
    turn_rows(2)
    forward(3, 0, 192)
    back_normed(3, 0, 192)
    sum_g.start(9, 8)
    for k in SERVE[12:]:
        arrive(tree, k)
    forward(3, 192, 192)
    back_normed(3, 192, 192)
    sum_g.start(13, 12)
    back_normed(1)
    back_normed(2)
    sum_g.send_mid()
    for start, size in ((0, 512), (512, 512), (1024, 128)):
        dd_rows[:, start : start + size] = lead_product(
            hid_rows[...], gb_rows[:, start : start + size]
        ).astype(jnp.bfloat16)
    swap_d.start()
    sum_g.send_near()
    back_normed(0)
    sum_g.start(1)
    turn_rows(3)
    middle_tile = matmul(n_turned[...], ggu_rows[:, 768:1024]).astype(jnp.bfloat16)
    dgu_rows[0, 3, :, :128] = middle_tile[:, :128]
    dgu_rows[1, 3, :, :128] = middle_tile[:, 128:]
    down(3)
    swap_d.wait_recv()

    def add_d(i, carry):
        add_into(dd.at[core, i], r_d.at[i])
        return carry

    lax.fori_loop(0, 4, add_d, 0)
    sum_d.start(2, 3)
    sum_g.send_next()
    grad_half(1 - core)
    swap_gu.start()
    sum_g.send_last()
    far_b.start(0, 1, 2, 3)
    sum_d.absorb(2, 3)
    sum_d.start(0, 1)
    grad_half(core)
    down(0)
    swap_gu.wait_recv()

    def add_gu(i, carry):
        add_into(dgu.reshape(2, 32, 144, 256).at[core, i], r_gu.reshape(32, 144, 256).at[i])
        return carry

    lax.fori_loop(0, 32, add_gu, 0)
    for copy in far_gu:
        copy.start()
    sum_d.absorb(0, 1)
    cross_d.start()
    down(1)
    down(2)
    out_f32[...] = sum_g.finish(0)
    store_g = pltpu.make_async_copy(out_f32, o_gn, local_sems.at[6])
    store_g.start()
    cross_d.wait_recv()
    cross_d.wait_send()
    add_into(quarter_d, z_d)
    store_d = pltpu.make_async_copy(quarter_d, o_pd, local_sems.at[7])
    store_d.start()
    far_b.absorb(0, 1, 2, 3)
    store_b = pltpu.make_async_copy(part_b, o_pb, local_sems.at[5])
    store_b.start()
    for part, j in ((1, 2), (2, 1)):
        far_gu[part - 1].wait_recv()
        add_into(
            cut_lead(dgu.at[core, (y + STEPS[j]) % 4], part), gu_half.at[part - 1]
        )
    store_gu = pltpu.make_async_copy(dgu.at[core], o_pgu, local_sems.at[4])
    store_gu.start()
    for store in (store_b, store_gu, store_g, store_d):
        store.wait()
    for copy in wire.made:
        if copy is not cross_d:
            copy.wait_send()


def feed_forward(own_n, gb_all, wgu_all, wd_all):
    bf, f32 = jnp.bfloat16, jnp.float32
    vm = pltpu.VMEM
    tokens, width = own_n.shape
    sums = [vm((14, tokens // 2, width), bf)]
    return pl.pallas_call(
        ff_kernel,
        out_shape=(
            jax.ShapeDtypeStruct((tokens, width), f32),
            jax.ShapeDtypeStruct((4, 2, tokens, width), bf),
            jax.ShapeDtypeStruct((4, 8, 144, 256), bf),
            jax.ShapeDtypeStruct((112, width), bf),
        ),
        in_specs=[ANY] * 4,
        out_specs=(ANY,) * 4,
        scratch_shapes=[
            vm((4, 2, tokens, width), bf),
            vm((4, 2, tokens, width), bf),
            vm(wgu_all.shape, bf),
            vm((FF_PAD, width), bf),
            vm((4, 2 * tokens, FF_PAD), f32),
            vm((4, 2 * tokens, FF_PAD), bf),
            vm((4, 2 * tokens, 2 * FF_PAD), bf),
            vm((4, 2, tokens, width), bf),
            vm((4, 2, tokens, width), bf),
            vm((tokens, width), f32),
            vm((2, 4, 8, 144, 256), bf),
        ]
        + sums
        + [
            vm((2, 4, 112, width), bf),
            vm((4, 112, width), bf),
            vm((2, 112, width), bf),
            vm((112, 640), bf),
            vm((112, 512), bf),
            vm((112, width), bf),
            vm((4, 8, 144, 256), bf),
            vm((2, 4, 144, 256), bf),
            vm((width, 8 * tokens), bf),
            vm((4, tokens // 2, width), bf),
        ]
        + [
            pltpu.SemaphoreType.DMA((8,)),
            pltpu.SemaphoreType.DMA((48,)),
            pltpu.SemaphoreType.DMA((48,)),
        ],
        compiler_params=comm_params(2),
        name="feed_forward",
    )(own_n, gb_all, wgu_all, wd_all)


def back_kernel(
    p_gu, p_d, part_b_all, gn2_all, middle_all, miscs_all, tokens, cot, rope_all, q_all, kv_all,
    probs_all, att_all, wqkv_all, wo_all, normed1_all,
    o_gu, o_d, o_q, o_kv, o_wo, o_out, o_grad,
    h_gu, gu_whole, z_gu, f_gu, piece_d,
    part_b, b_half, gn2, middle, miscs, x_ref, cot_ref, rope, q_ref, kv_ref, probs, att,
    wqkv, wo, normed1, dq, r_q, q_whole, q_half, q_parts, dkv, r_kv, kv_parts, dwo, r_wo, w_whole, w_half, w_parts,
    gkv, kv_out, kv_in, gproj, gmid, out_bf,
    s_wo, z_wo, s_q, z_q, s_kv, y_kv, z_kv,
    local_sems, send_sems, recv_sems,
):
    place = Place()
    wire = Wire(send_sems, recv_sems)
    core, me, y, rep = place.core, place.shard, place.y, place.rep
    rows, width = tokens.shape
    at = place.shard_at
    others = [(j, p) for p in (0, 1) for j in range(4) if (j, p) != (0, 0)]
    group = [place.device(dx=STEPS[j], mirror=p) for j, p in others]
    sequence = [(rep, at(j, 1)) for j in range(4)]
    sibling = place.device(sibling=1)
    column = [place.device(dy=d) for d in (1, 3, 2)]
    low = place.device(swap_lo=1)
    locals_ = []

    def local(src, dst):
        copy = pltpu.make_async_copy(src, dst, local_sems.at[len(locals_)])
        copy.start()
        locals_.append(copy)
        return copy

    loads = [
        local(src, dst)
        for src, dst in (
            (miscs_all, miscs),
            (gn2_all, gn2),
            (middle_all, middle),
            (cot, cot_ref),
            (att_all, att),
            (wo_all, wo),
        )
    ]
    load_gu = local(p_gu, h_gu)
    load_d = local(p_d, piece_d)
    load_b = local(part_b_all, part_b)
    both_cores = [place.device(dy=d, sibling=1) for d in (1, 3, 2)]
    greet([sibling, low] + group + column + sequence + both_cores)
    loads_heads = [
        local(src, dst)
        for src, dst in ((q_all, q_ref), (kv_all, kv_ref), (probs_all, probs), (rope_all, rope))
    ]
    load_x = local(tokens, x_ref)
    load_n = local(normed1_all, normed1)
    load_w = local(wqkv_all, wqkv)
    loaded = len(locals_)

    def over_y(dx, mirror):
        return place.device(dy=dx)

    def cut_lead(ref, part):
        return ref if part == 0 else ref.at[pl.ds((part - 1) * 4, 4)]

    def cut_rows(size):
        def cut(ref, part):
            return ref if part == 0 else ref.at[pl.ds((part - 1) * size, size)]

        return cut

    def cut_lanes(size):
        def cut(ref, part):
            return ref if part == 0 else ref.at[:, pl.ds((part - 1) * size, size)]

        return cut

    def cut_d(ref, part):
        start, size = ((0, width), (0, 640), (640, 512))[part]
        return ref.at[:, pl.ds(start, size)]

    def added(target, source, count):
        def one(i, carry):
            add_into(target.at[i], source.at[i])
            return carry

        lax.fori_loop(0, count, one, 0)

    chunks = [pl.ds(0, 80), pl.ds(80, 64)]
    near_gu = [
        [
            wire.copy(
                h_gu.at[(y + STEPS[j]) % 4, :, c],
                gu_whole.at[k, :, c],
                place.device(dy=(3, 1)[k]),
            )
            for k, j in enumerate((2, 1))
        ]
        for c in chunks
    ]
    quarters = [h_gu.at[y, :, c] for c in chunks]
    crossings_gu = [wire.copy(h_gu.at[y, :, c], z_gu.at[:, c], low) for c in chunks]
    turns = [
        [
            wire.copy(h_gu.at[y, at(j, p), c], f_gu.at[me, c], device)
            for (j, p), device in zip(others, group)
        ]
        for c in chunks
    ]
    slots_gu = [lambda j, p, c=c: o_gu.at[core, (y + STEPS[j]) % 4, :, c] for c in chunks]
    trees_gu = [
        gather_tree(wire, over_y, RING, f_gu.at[:, c], slot, cut_lead, True)
        for c, slot in zip(chunks, slots_gu)
    ]
    passes_gu = [
        [
            wire.copy(f_gu.at[:, c] if j == 0 else slot(j, 0), slot(j, 0), sibling)
            for j in range(4)
        ]
        for c, slot in zip(chunks, slots_gu)
    ]

    def cross(i):
        for k, copy in enumerate(near_gu[i]):
            copy.wait_recv()
            added(quarters[i], gu_whole.at[k, :, chunks[i]], 8)
        crossings_gu[i].start()

    def turn(i):
        crossings_gu[i].wait_recv()
        crossings_gu[i].wait_send()
        added(quarters[i], z_gu.at[:, chunks[i]], 8)
        for copy in turns[i]:
            copy.start()
        f_gu[me, chunks[i]] = h_gu[y, me, chunks[i]]

    def spread(i):
        for copy in turns[i]:
            copy.wait_recv()
        for copy in (trees_gu[i][0], trees_gu[i][1], passes_gu[i][0]):
            copy.start()
        local(f_gu.at[:, chunks[i]], slots_gu[i](0, 0))

    def spread_on(i, k):
        arrive(trees_gu[i], k, RING_ONWARD)
        if k != 2:
            passes_gu[i][(2, 1, None, 3)[k]].start()

    load_gu.wait()
    for copy in near_gu[0] + near_gu[1]:
        copy.start()

    sum_b = SumTree(
        wire, place.over_group, HOPS, lambda j, p: part_b.at[j, p], cut_rows(96),
        [b_half.at[k] for k in range(14)],
    )
    load_b.wait()
    sum_b.start(7, 6, 4, 2, 11, 10, 1)

    load_d.wait()
    slot_d = lambda j, p: o_d.at[core, (y + STEPS[j]) % 4]
    tree_d = gather_tree(wire, over_y, RING, piece_d, slot_d, cut_d, True)
    pass_d = [
        wire.copy(piece_d if j == 0 else slot_d(j, 0), slot_d(j, 0), sibling) for j in range(4)
    ]

    for load in loads:
        load.wait()
    as_float = [miscs[s].astype(jnp.float32) for s in range(8)]
    gain1 = jnp.concatenate([m[0:1, :144] for m in as_float], axis=1)
    gain2 = jnp.concatenate([m[1:2, :144] for m in as_float], axis=1)
    row = lax.broadcasted_iota(jnp.int32, (rows, 1), 0).astype(jnp.float32)
    keep = jnp.where(row < miscs[me].astype(jnp.float32)[2:3, :1], 1.0, 0.0)
    mid = middle[...]
    inverse2 = lax.rsqrt(jnp.mean(mid * mid, axis=1, keepdims=True) + EPSILON)
    scaled2 = mid * inverse2
    grad2 = gn2[...]
    grad_gain2 = jnp.sum(grad2 * scaled2, axis=0, keepdims=True)
    grad2 = grad2 * gain2
    grad_mid = cot_ref[...].astype(jnp.float32) + inverse2 * (
        grad2 - scaled2 * jnp.mean(grad2 * scaled2, axis=1, keepdims=True)
    )
    gmid[...] = grad_mid
    grad_attn = (keep * grad_mid).astype(jnp.bfloat16)
    for start in range(0, width, 384):
        block = lead_product(att[...], grad_attn[:, start : start + 384]).astype(jnp.bfloat16)
        block = block.reshape(8, 2, 4, 16, 384)
        for c in range(2):
            for q in range(4):
                dwo[c, q, :, :, start : start + 384] = block[:, c, q]
    swap_wo = wire.copy(dwo.at[1 - core], r_wo, sibling)
    swap_wo.start()
    grad_att = trail_product(grad_attn, wo.reshape(1024, width)[...]).astype(jnp.bfloat16)

    for load in loads_heads:
        load.wait()
    keys = (BEHIND + 1) * rows
    all_kv = kv_ref.reshape(keys, 512)
    flat = gkv.reshape(keys, 512)
    cosine, sine_part = rope[:, :128], rope[:, 128:]
    scaling = 256 ** (-0.5)

    def turned_back(vectors):
        first, second = vectors[:, :128], vectors[:, 128:]
        return jnp.concatenate(
            [first * cosine + second * sine_part, second * cosine - first * sine_part], axis=1
        )

    for h in range(4):
        share = probs[h]
        share_low = share.astype(jnp.bfloat16)
        grad_h = grad_att[:, 256 * h : 256 * (h + 1)]
        grad_probs = trail_product(grad_h, all_kv[:, 256:])
        delta = jnp.sum(share * grad_probs, axis=1, keepdims=True)
        grad_scores = (share * (grad_probs - delta)).astype(jnp.bfloat16)
        grad_keys = lead_product(grad_scores, q_ref[h])
        grad_values = lead_product(share_low, grad_h)
        if h == 0:
            flat[:, :256] = grad_keys
            flat[:, 256:] = grad_values
        else:
            flat[:, :256] += grad_keys
            flat[:, 256:] += grad_values
        grad_q = matmul(grad_scores, all_kv[:, :256])
        gproj[:, 256 * h : 256 * (h + 1)] = (turned_back(grad_q) * scaling).astype(jnp.bfloat16)
        if h == 1:
            cross(0)
            for copy in (tree_d[0], tree_d[1], pass_d[0]):
                copy.start()
            local(piece_d, slot_d(0, 0))
    x, upper = place.x, place.z_hi == 1
    sends = []
    for i in range(1, BEHIND):
        kv_out[i - 1] = gkv[i].astype(jnp.bfloat16)
        target = (rep, 4 * place.z_hi + (x + (4 - i)) % 4)
        sends.append(wire.copy(kv_out.at[i - 1], kv_in.at[i - 1], target))
        pl.when(jnp.logical_or(upper, x >= i))(sends[-1].start)

        @pl.when(jnp.logical_not(jnp.logical_or(upper, x + i <= 3)))
        def _():
            kv_in[i - 1] = jnp.zeros(kv_in.shape[1:], kv_in.dtype)

    plane_kv = wire.copy(kv_out.at[BEHIND - 1], kv_in.at[BEHIND - 1], (rep, at(0, 1)))

    @pl.when(upper)
    def _():
        kv_in[BEHIND - 1] = jnp.zeros(kv_in.shape[1:], kv_in.dtype)

    def collect_kv():
        through = gkv[BEHIND]
        for i, copy in enumerate(sends):
            pl.when(jnp.logical_or(upper, x + (i + 1) <= 3))(copy.wait_recv)
            through = through + jnp.where(x + (i + 1) > 3, 1.0, 0.0) * kv_in[i].astype(jnp.float32)
        kv_out[BEHIND - 1] = through.astype(jnp.bfloat16)
        pl.when(upper)(plane_kv.start)

    def over_ring(blocks, whole, half):
        return SumTree(
            wire, over_y, RING, lambda j, p: blocks.at[core, (y + STEPS[j]) % 4], cut_lead,
            [whole.at[0], whole.at[1], half.at[0], half.at[1]],
        )

    def near_ring(tree):
        tree.absorb(2, 3)
        tree.start(0, 1)

    def to_owners(tree, blocks, parts):
        tree.absorb(0, 1)
        copies = [
            wire.copy(blocks.at[core, y, at(j, p)], parts.at[i], device)
            for i, ((j, p), device) in enumerate(zip(others, group))
        ]
        for copy in copies:
            copy.start()
        return copies

    def to_low(copies, blocks, parts, piece, other):
        total = blocks[core, y, me].astype(jnp.float32)
        for i, copy in enumerate(copies):
            copy.wait_recv()
            total = total + parts[i].astype(jnp.float32)
        piece[y] = total.astype(jnp.bfloat16)
        crossing = wire.copy(piece.at[y], other, low)
        crossing.start()
        return crossing

    load_n.wait()
    dq_rows = dq.reshape(2, 4, width, 128)
    for t in range(4):
        block = lead_product(normed1[...], gproj[:, 256 * t : 256 * (t + 1)]).astype(jnp.bfloat16)
        dq_rows[t // 2, 2 * (t % 2)] = block[:, :128]
        dq_rows[t // 2, 2 * (t % 2) + 1] = block[:, 128:]
    swap_q = wire.copy(dq.at[1 - core], r_q, sibling)
    swap_q.start()
    cross(1)
    swap_wo.wait_recv()
    added(dwo.reshape(2, 32, 16, width).at[core], r_wo.reshape(32, 16, width), 32)
    sum_wo = over_ring(dwo, w_whole, w_half)
    sum_wo.start(2, 3)
    load_x.wait()
    load_w.wait()
    weights = wqkv.reshape(width, 1536)
    gn2[...] = trail_product(gproj[:, :1024], weights[:, :1024])
    turn(0)
    swap_q.wait_recv()
    added(dq.reshape(2, 32, 144, 128).at[core], r_q.reshape(32, 144, 128), 32)
    sum_q = over_ring(dq, q_whole, q_half)
    sum_q.start(2, 3)
    collect_kv()
    near_ring(sum_wo)
    turn(1)
    near_ring(sum_q)
    spread(0)

    pl.when(jnp.logical_not(upper))(plane_kv.wait_recv)
    grad_kv = gkv[0] + kv_in[BEHIND - 1].astype(jnp.float32)
    for i in range(BEHIND - 1):
        grad_kv = grad_kv + jnp.where(x + (i + 1) <= 3, 1.0, 0.0) * kv_in[i].astype(jnp.float32)
    gproj[:, 1024:1280] = turned_back(grad_kv[:, :256]).astype(jnp.bfloat16)
    gproj[:, 1280:1536] = grad_kv[:, 256:].astype(jnp.bfloat16)
    for t in range(2):
        dkv[t, :, :144] = (
            lead_product(normed1[...], gproj[:, 1024 + 256 * t : 1280 + 256 * t])
            .astype(jnp.bfloat16)
            .reshape(8, 144, 256)
        )
    inputs = x_ref[...].astype(jnp.float32)
    inverse1 = lax.rsqrt(jnp.mean(inputs * inputs, axis=1, keepdims=True) + EPSILON)
    scaled1 = inputs * inverse1
    grad1 = gn2[...] + trail_product(gproj[:, 1024:], weights[:, 1024:])
    grad_gain1 = jnp.sum(grad1 * scaled1, axis=0, keepdims=True)
    for s in range(8):
        cols = slice(144 * s, 144 * (s + 1))
        both = jnp.concatenate(
            [grad_gain1[:, cols], grad_gain2[:, cols], jnp.zeros((14, 144), jnp.float32)], axis=0
        )
        both = jnp.concatenate([both, jnp.zeros((16, 112), jnp.float32)], axis=1)
        dkv[0, s, 144:] = both.astype(jnp.bfloat16)
        dkv[1, s, 144:] = both.astype(jnp.bfloat16)
    swap_kv = wire.copy(dkv.at[1 - core], r_kv, sibling)
    swap_kv.start()
    direct_wo = to_owners(sum_wo, dwo, w_parts)
    spread(1)
    def over_column(source, landing):
        copies = [
            wire.copy(source.at[(y + d) % 4], landing.at[i], device)
            for i, (d, device) in enumerate(zip((1, 3, 2), column))
        ]
        for copy in copies:
            copy.start()
        return copies

    def over_low(copies, source, landing, other):
        for copy in copies:
            copy.wait_recv()
        mine = source[y].astype(jnp.float32)
        for i in range(3):
            mine = mine + landing[i].astype(jnp.float32)
        source[y] = mine.astype(jnp.bfloat16)
        crossing = wire.copy(source.at[y], other, low)
        crossing.start()
        return crossing

    def to_all(crossing, source, other, slot):
        crossing.wait_recv()
        crossing.wait_send()
        add_into(source.at[y], other)
        made = [wire.copy(source.at[y], slot(core, y), device) for device in column + [sibling]]
        for copy in made:
            copy.start()
        local(source.at[y], slot(core, y))
        return made

    def to_both(crossing, source, other, slot):
        made = to_all(crossing, source, other, slot)
        made += [
            wire.copy(source.at[y], slot(core, y), place.device(dy=d, sibling=1)) for d in (1, 3, 2)
        ]
        for copy in made[4:]:
            copy.start()
        return made

    def pass_on(made, slot):
        ends = [made[3]]
        for d, copy in zip((3, 1, 2), made):
            copy.wait_recv()
            held = slot(core, (y + d) % 4)
            ends.append(wire.copy(held, held, sibling))
            ends[-1].start()
        return ends

    slot_wo = lambda c, q: o_wo.at[c, q]
    slot_q = lambda c, q: o_q.at[:, pl.ds(pl.multiple_of(c * 512 + q * 128, 128), 128)]
    slot_kv = lambda c, q: o_kv.at[c, q]
    swap_kv.wait_recv()
    added(dkv.at[core], r_kv, 8)
    direct_kv = [
        wire.copy(dkv.at[core, at(j, p)], kv_parts.at[i], device)
        for i, ((j, p), device) in enumerate(zip(others, group))
    ]
    for copy in direct_kv:
        copy.start()
    direct_q = to_owners(sum_q, dq, q_parts)
    grad1 = grad1 * gain1
    gmid[...] += inverse1 * (grad1 - scaled1 * jnp.mean(grad1 * scaled1, axis=1, keepdims=True))
    local(gmid, o_grad)
    for k in (0, 1):
        arrive(tree_d, k, RING_ONWARD)
        pass_d[(2, 1)[k]].start()
    cross_wo = to_low(direct_wo, dwo, w_parts, s_wo, z_wo)
    for k in (0, 1):
        spread_on(0, k)
    cross_q = to_low(direct_q, dq, q_parts, s_q, z_q)
    total = dkv[core, me].astype(jnp.float32)
    for i, copy in enumerate(direct_kv):
        copy.wait_recv()
        total = total + kv_parts[i].astype(jnp.float32)
    s_kv[0] = total[:144, :128].astype(jnp.bfloat16)
    s_kv[1] = total[:144, 128:].astype(jnp.bfloat16)
    s_kv[2] = jnp.concatenate(
        [total[144:, :128], total[144:, 128:], jnp.zeros((112, 128), jnp.float32)], axis=0
    ).astype(jnp.bfloat16)
    s_kv[3] = jnp.zeros((144, 128), jnp.bfloat16)
    over_kv = over_column(s_kv, y_kv)
    sum_b.absorb(10)
    sum_b.start(3)
    sum_b.absorb(11)
    sum_b.start(5)
    sum_b.send_last()
    all_wo = to_all(cross_wo, s_wo, z_wo, slot_wo)
    all_q = to_all(cross_q, s_q, z_q, slot_q)
    cross_kv = over_low(over_kv, s_kv, y_kv, z_kv)
    for k in (0, 1):
        spread_on(1, k)
    for k in (2, 3):
        arrive(tree_d, k, RING_ONWARD)
    pass_d[3].start()
    all_kv_sum = to_both(cross_kv, s_kv, z_kv, slot_kv)
    ends = pass_on(all_wo, slot_wo) + pass_on(all_q, slot_q)
    for i in (0, 1):
        for k in (2, 3):
            spread_on(i, k)
    out_bf[...] = (middle[...] + keep * sum_b.finish(0)).astype(jnp.bfloat16)
    local(out_bf, o_out)
    ends += all_kv_sum
    for copy in pass_d + passes_gu[0] + passes_gu[1] + ends:
        copy.wait_recv()
    for copy in locals_[loaded:]:
        copy.wait()
    for i, copy in enumerate(sends):
        pl.when(jnp.logical_or(upper, x >= i + 1))(copy.wait_send)
    pl.when(upper)(plane_kv.wait_send)
    waited = [id(copy) for copy in sends + [plane_kv] + crossings_gu + [cross_wo, cross_q, cross_kv]]
    waited += [id(sum_b.copies[k]) for k in (8, 9, 12, 13)]
    for copy in wire.made:
        if id(copy) not in waited:
            copy.wait_send()


def back(*args):
    bf, f32 = jnp.bfloat16, jnp.float32
    width = 1152
    rows = args[6].shape[0]
    outs = [
        ((2, 4, 8, 144, 256), bf),
        ((2, 4, 112, width), bf),
        ((144, 1024), bf),
        ((2, 4, 144, 128), bf),
        ((2, 4, 16, width), bf),
        ((rows, width), bf),
        ((rows, width), f32),
    ]
    scratch = [
        ((4, 8, 144, 256), bf),
        ((2, 8, 144, 256), bf),
        ((8, 144, 256), bf),
        ((8, 144, 256), bf),
        ((112, width), bf),
        ((4, 2, rows, width), bf),
        ((14, rows // 2, width), bf),
    ]
    scratch += [(a.shape, a.dtype) for a in args[3:16]]
    ring = lambda *b: [(2, 4, 8, *b), (4, 8, *b), (2, 8, *b), (2, 4, *b), (7, *b)]
    parts = ring(144, 128) + [(2, 8, 160, 256), (8, 160, 256), (7, 160, 256)] + ring(16, width)
    scratch += [(part, bf) for part in parts]
    scratch += [
        ((BEHIND + 1, rows, 512), f32),
        ((BEHIND, rows, 512), bf),
        ((BEHIND, rows, 512), bf),
        ((rows, 1536), bf),
        ((rows, width), f32),
        ((rows, width), bf),
    ]
    pieces = [(4, 16, width), (16, width), (4, 144, 128), (144, 128)]
    pieces += [(4, 144, 128), (3, 144, 128), (144, 128)]
    scratch += [(piece, bf) for piece in pieces]
    return pl.pallas_call(
        back_kernel,
        out_shape=tuple(jax.ShapeDtypeStruct(*o) for o in outs),
        in_specs=[ANY] * 16,
        out_specs=(ANY,) * len(outs),
        scratch_shapes=[pltpu.VMEM(*v) for v in scratch]
        + [
            pltpu.SemaphoreType.DMA((40,)),
            pltpu.SemaphoreType.DMA((176,)),
            pltpu.SemaphoreType.DMA((176,)),
        ],
        compiler_params=comm_params(3),
        name="attention_backward",
    )(*args)


def on_device(
    tokens, lengths, attn_gain, w_query, w_keyval, w_out, mlp_gain, w_gate, w_up, w_down, cotangent
):
    width = tokens.shape[1]
    live_count = lengths[0, 0]
    row = lax.broadcasted_iota(jnp.int32, (16, 256), 0)
    wide = lambda gain: jnp.pad(gain, (0, 112))[None]
    misc = jnp.where(
        row == 0,
        wide(attn_gain),
        jnp.where(row == 1, wide(mlp_gain), live_count.astype(jnp.bfloat16)),
    )
    frequency = np.power(10000.0, -2.0 * np.arange(128) / 256).astype(np.float32)
    (
        miscs, qkv_all, out_all, gu_all, branch_all,
        normed1, queries, all_kv, probs, attended, middle, normed2, rope,
    ) = front(
        tokens, cotangent, misc, jnp.asarray(np.tile(frequency[None], (8, 1))),
        w_query, w_keyval, w_out, w_gate, w_up,
    )
    grad_normed2, branch, grad_gu, grad_d = feed_forward(
        normed2, branch_all, gu_all.reshape(width, -1), w_down
    )
    sum_gu, sum_d, sum_q, sum_kv, sum_wo, outputs, grad_inputs = back(
        grad_gu, grad_d, branch, grad_normed2, middle, miscs, tokens, cotangent,
        rope, queries, all_kv, probs, attended, qkv_all, out_all, normed1,
    )
    grad_gate_w, grad_up_w, grad_down, grad_q, grad_kv, grad_wo = finish(
        sum_gu, sum_d.reshape(FF_PAD, width), sum_q, sum_kv, sum_wo.reshape(128, width)
    )
    gains = sum_kv[0, 2]
    gains = jnp.concatenate([gains[:2], gains[16:18, :16]], axis=1).astype(jnp.float32)
    return (
        outputs,
        grad_inputs,
        gains[0],
        grad_q,
        grad_kv,
        grad_wo,
        gains[1],
        grad_gate_w,
        grad_up_w,
        grad_down,
    )


def solution(mesh):
    placed = (
        P(("rep", "shard"), None),
        P("rep", "shard"),
        P("shard"),
        P("shard", None),
        P("shard", None),
        P("shard", None),
        P("shard"),
        P("shard", None),
        P("shard", None),
        P("shard", None),
        P(("rep", "shard"), None),
    )
    return jax.shard_map(
        on_device,
        mesh=mesh,
        in_specs=placed,
        out_specs=(
            P(("rep", "shard"), None),
            P(("rep", "shard"), None),
            P("shard"),
            P("shard", None),
            P("shard", None),
            P("shard", None),
            P("shard"),
            P("shard", None),
            P("shard", None),
            P("shard", None),
        ),
        check_vma=False,
    )
```

```python
import functools

import jax
import jax.numpy as jnp
import numpy as np
from jax import lax
from jax.experimental import pallas as pl
from jax.experimental.pallas import tpu as pltpu
from jax.sharding import PartitionSpec as P

MESH = pl.DeviceIdType.MESH
WINDOW = 512
EPSILON = 1e-06
MASKED = -1e30
VMEM_LIMIT = 60 * 2**20
FF_DEV = 864
FF_PAD = 896
PAIRS = FF_PAD // 128
BEHIND = 4


def matmul(former, latter):
    return jnp.dot(former, latter, preferred_element_type=jnp.float32)


def lead_product(former, latter):
    return lax.dot_general(
        former, latter, (((0,), (0,)), ((), ())), preferred_element_type=jnp.float32
    )


def trail_product(former, latter):
    return lax.dot_general(
        former, latter, (((1,), (1,)), ((), ())), preferred_element_type=jnp.float32
    )


class Place:
    def __init__(self):
        rep, shard = lax.axis_index("rep"), lax.axis_index("shard")
        self.rep, self.shard = rep, shard
        self.y, self.z_lo, self.core = rep // 4, (rep // 2) % 2, rep % 2
        self.z_hi, self.x = shard // 4, shard % 4

    def device(self, dx=0, dy=0, mirror=0, swap_lo=0, sibling=0):
        z_lo = (self.z_lo + mirror + swap_lo) % 2
        rep = (((self.y + dy) % 4) * 2 + z_lo) * 2 + (self.core + sibling) % 2
        return (rep, ((self.z_hi + mirror) % 2) * 4 + (self.x + dx) % 4)

    def over_group(self, dx, mirror):
        return self.device(dx=dx, mirror=mirror)

    def shard_at(self, j, p):
        return ((self.z_hi + p) % 2) * 4 + (self.x + STEPS[j]) % 4


STEPS = (0, 1, 3, 2)


class Wire:
    def __init__(self, send_sems, recv_sems):
        self.send_sems, self.recv_sems, self.made = send_sems, recv_sems, []

    def copy(self, src, dst, device):
        k = len(self.made)
        made = pltpu.make_async_remote_copy(
            src_ref=src,
            dst_ref=dst,
            send_sem=self.send_sems.at[k],
            recv_sem=self.recv_sems.at[k],
            device_id=device,
            device_id_type=MESH,
        )
        self.made.append(made)
        return made

    def drain(self):
        for made in self.made:
            made.wait_send()


def greet(devices):
    barrier = pltpu.get_barrier_semaphore()
    for device in devices:
        pl.semaphore_signal(barrier, inc=1, device_id=device, device_id_type=MESH)
    pl.semaphore_wait(barrier, len(devices))


HOPS = (
    ((0, 0), (0, 1), 1, 0, 1),
    ((0, 0), (0, 1), 2, 0, 1),
    ((0, 0), (2, 0), 1, 1, 0),
    ((0, 0), (2, 0), 2, 1, 0),
    ((0, 0), (1, 0), 1, 3, 0),
    ((0, 0), (1, 0), 2, 3, 0),
    ((0, 1), (2, 1), 1, 1, 0),
    ((0, 1), (1, 1), 1, 3, 0),
    ((2, 0), (3, 0), 1, 1, 0),
    ((1, 0), (3, 0), 2, 3, 0),
    ((2, 0), (2, 1), 2, 0, 1),
    ((1, 0), (1, 1), 2, 0, 1),
    ((2, 1), (3, 1), 1, 1, 0),
    ((1, 1), (3, 1), 2, 3, 0),
)
FIRST = (0, 2, 5, 1, 3, 4)
ONWARD = {0: (6, 7), 2: (8,), 3: (10,), 5: (9, 11), 6: (12,), 11: (13,)}
SERVE = (0, 2, 5, 3, 11, 6, 1, 4, 7, 8, 9, 10, 12, 13)
WHOLE = {1: (0, 1), 3: (2, 0), 4: (1, 0), 7: (1, 1), 9: (3, 0), 10: (2, 1), 13: (3, 1)}
HOPS_FAR = tuple(HOPS[k] for k in (13, 12, 9, 8))
RING = (
    ((0, 0), (2, 0), 0, 1, 0),
    ((0, 0), (1, 0), 0, 3, 0),
    ((2, 0), (3, 0), 1, 1, 0),
    ((1, 0), (3, 0), 2, 3, 0),
)
RING_ONWARD = {0: (2,), 1: (3,)}


def gather_tree(wire, device_of, hops, own, slot, cut, absolute):
    copies = []
    for source, target, part, dx, mirror in hops:
        src = own if source == (0, 0) else slot(*source)
        dst = slot(*(source if absolute else target))
        copies.append(wire.copy(cut(src, part), cut(dst, part), device_of(dx, mirror)))
    return copies


def arrive(tree, k, after=ONWARD):
    tree[k].wait_recv()
    for n in after.get(k, ()):
        tree[n].start()


def add_into(target, source):
    target[...] = (target[...].astype(jnp.float32) + source[...].astype(jnp.float32)).astype(
        target.dtype
    )


class SumTree:
    def __init__(self, wire, device_of, hops, slot, cut, landings):
        self.hops, self.slot, self.cut, self.landings = hops, slot, cut, landings
        self.copies = [
            wire.copy(cut(slot(*target), part), landing, device_of((4 - dx) % 4, mirror))
            for (_, target, part, dx, mirror), landing in zip(hops, landings)
        ]

    def start(self, *hops):
        for k in hops:
            self.copies[k].start()

    def absorb(self, *hops):
        for k in hops:
            source, _, part, _, _ = self.hops[k]
            self.copies[k].wait_recv()
            add_into(self.cut(self.slot(*source), part), self.landings[k])

    def send_far(self):
        self.start(13, 12, 9, 8)

    def send_mid(self):
        self.start(7, 4, 10)

    def send_near(self):
        self.absorb(13)
        self.start(11)
        self.absorb(12)
        self.start(6)
        self.absorb(8)
        self.start(2)

    def send_next(self):
        self.absorb(9, 11)
        self.start(5)
        self.absorb(10)
        self.start(3)

    def send_last(self):
        self.absorb(6, 7)
        self.start(0)

    def finish(self, axis):
        halves = []
        for part in (1, 2):
            total = self.cut(self.slot(0, 0), part)[...].astype(jnp.float32)
            for k in (4, 2, 0):
                self.copies[k + part - 1].wait_recv()
                total = total + self.landings[k + part - 1][...].astype(jnp.float32)
            halves.append(total)
        return jnp.concatenate(halves, axis=axis)


def front_kernel(
    tokens, cot, misc, freq, w_query, w_keyval, w_out, w_gate, w_up,
    o_misc, o_qkv, o_wo, o_gu, o_gb, o_normed1, o_q, o_kv, o_probs, o_att, o_middle, o_normed2, o_rope,
    x_ref, cot_ref, miscs, freq_ref, wqkv, wo, gate, up, packed, gb_own, normed1, q_ref, kv_ref,
    bias, probs, att, middle, normed2, rope, wo_own,
    local_sems, send_sems, recv_sems,
):
    place = Place()
    wire = Wire(send_sems, recv_sems)
    core, me, y = place.core, place.shard, place.y
    rows, width = tokens.shape
    at = place.shard_at
    others = [(j, p) for p in (0, 1) for j in range(4) if (j, p) != (0, 0)]
    group = [place.device(dx=STEPS[j], mirror=p) for j, p in others]
    sequence = [(place.rep, at(j, p)) for j, p in others]
    sibling = place.device(sibling=1)
    column = [place.device(dy=d) for d in (1, 3, 2)]
    locals_ = []

    def local(src, dst):
        copy = pltpu.make_async_copy(src, dst, local_sems.at[len(locals_)])
        copy.start()
        locals_.append(copy)
        return copy

    load_x = local(tokens, x_ref)
    load_cot = local(cot, cot_ref)
    load_misc = local(misc, miscs.at[me])
    load_freq = local(freq, freq_ref)
    load_gate = local(w_gate, gate)
    load_up = local(w_up, up)
    load_own = [
        local(w_query, wqkv.at[me, :, pl.ds(0, 1024)]),
        local(w_keyval, wqkv.at[me, :, pl.ds(1024, 512)]),
        local(w_out, wo_own),
    ]
    greet([sibling] + group + [d for d, (j, p) in zip(sequence, others) if p == 1] + column)

    def lanes_from(base, size):
        def cut(ref, part):
            start, count = ((0, size), (0, size // 2), (size // 2, size // 2))[part]
            start = pl.multiple_of(core * size + (base + start), 128)
            return ref.at[:, pl.ds(start, count)]

        return cut

    def cut_wo(ref, part):
        start, size = ((0, 64), (0, 32), (32, 32))[part]
        return ref.at[pl.ds(pl.multiple_of(core * 64 + start, 32), size)]

    def cut_gb(ref, part):
        return ref if part == 0 else ref.at[pl.ds((part - 1) * 96, 96)]

    def cut_gu(ref):
        return ref.at[:, pl.ds(pl.multiple_of(core * FF_PAD, 128), FF_PAD)]

    cut_q, cut_kv = lanes_from(0, 512), lanes_from(1024, 256)
    slot_qkv = lambda j, p: wqkv.at[at(j, p)]
    slot_gb = lambda j, p: o_gb.at[j, p]
    misc_copies = [wire.copy(misc, miscs.at[me], device) for device in sequence]
    for copy in misc_copies:
        copy.start()
    for load in load_own:
        load.wait()
    own = wqkv.at[me]
    trees = [
        gather_tree(wire, place.over_group, HOPS, own, slot_qkv, cut_q, True),
        gather_tree(wire, place.over_group, HOPS, own, slot_qkv, cut_kv, True),
    ]
    cuts = [cut_q, cut_kv]
    slots = [slot_qkv, slot_qkv]
    passes = [
        {k: wire.copy(cut(slot(*jp), 0), cut(slot(*jp), 0), sibling) for k, jp in WHOLE.items()}
        for cut, slot in zip(cuts, slots)
    ]
    for tree in trees:
        for k in FIRST:
            tree[k].start()

    load_x.wait()
    inputs = x_ref[...].astype(jnp.float32)
    inverse1 = lax.rsqrt(jnp.mean(inputs * inputs, axis=1, keepdims=True) + EPSILON)
    middle[...] = inputs * inverse1
    load_gate.wait()
    load_up.wait()
    for d in range(8):
        for t in range(PAIRS):
            start = FF_DEV * d + 128 * t
            size = min(128, FF_DEV - 128 * t)
            for k, weight in enumerate((gate, up)):
                block = weight[:, start : start + size]
                if size < 128:
                    block = jnp.concatenate(
                        [block, jnp.zeros((block.shape[0], 128 - size), block.dtype)], axis=1
                    )
                packed[d, :, 256 * t + 128 * k : 256 * t + 128 * (k + 1)] = block

    def attn(*hops):
        for k in hops:
            for tree, onward in zip(trees, passes):
                arrive(tree, k)
                if k in onward:
                    onward[k].start()

    z_of = lambda p: (place.z_hi + p) % 2
    shard_from = lambda d, p: z_of(p) * 4 + (place.x + y + d) % 4
    turn = []
    for p in (0, 1):
        target = z_of(p) * 4 + (place.x - y + 4) % 4
        turn.append(
            wire.copy(
                cut_gu(packed.at[target]), cut_gu(o_gu.at[me]), place.device(dx=4 - y, mirror=p)
            )
        )
    away, home = y > 0, y == 0
    keep_own = pltpu.make_async_copy(
        cut_gu(packed.at[me]), cut_gu(o_gu.at[me]), local_sems.at[len(locals_)]
    )
    locals_.append(None)
    held_wo = lambda j, p: cut_wo(wo.at[shard_from(STEPS[j], p)], 0)
    turn_wo = wire.copy(cut_wo(wo_own, 0), cut_wo(wo.at[me], 0), place.device(dx=4 - y))
    keep_wo = pltpu.make_async_copy(
        cut_wo(wo_own, 0), cut_wo(wo.at[me], 0), local_sems.at[len(locals_)]
    )
    locals_.append(None)
    pl.when(away)(turn_wo.start)
    pl.when(home)(keep_wo.start)
    turn[1].start()
    pl.when(away)(turn[0].start)
    pl.when(home)(keep_own.start)

    def over_y(dx, mirror):
        return place.device(dy=dx)

    def cut_block(ref, part):
        start, size = ((0, 144), (0, 80), (80, 64))[part]
        return ref.at[pl.ds(start, size), pl.ds(pl.multiple_of(core * FF_PAD, 128), FF_PAD)]

    gu_slots = [lambda j, _, p=p: o_gu.at[shard_from(STEPS[j], p)] for p in (0, 1)]
    gu_trees = [
        gather_tree(wire, over_y, RING, slot(0, 0), slot, cut_block, True) for slot in gu_slots
    ]
    gu_passes = {
        (j, p): wire.copy(
            cut_gu(o_gu.at[shard_from(STEPS[j], p)]),
            cut_gu(o_gu.at[shard_from(STEPS[j], p)]),
            sibling,
        )
        for j in range(4)
        for p in (0, 1)
    }

    wo_slots = [lambda j, _, p=p: wo.at[shard_from(STEPS[j], p)] for p in (0, 1)]
    wo_trees = [
        gather_tree(wire, over_y, RING, slot(0, 0), slot, cut_wo, True) for slot in wo_slots
    ]
    mirror_wo = wire.copy(held_wo(0, 0), held_wo(0, 0), place.device(mirror=1))
    wo_passes = {
        (j, p): wire.copy(held_wo(j, p), held_wo(j, p), sibling)
        for j in range(4)
        for p in (0, 1)
    }

    def start_wo(p):
        for copy in (wo_trees[p][0], wo_trees[p][1], wo_passes[0, p]):
            copy.start()

    def over_wo(k, j):
        for p in (0, 1):
            arrive(wo_trees[p], k, RING_ONWARD)
            if j:
                wo_passes[j, p].start()

    def over(k, j):
        for p in (0, 1):
            arrive(gu_trees[p], k, RING_ONWARD)
            if j:
                gu_passes[j, p].start()

    attn(0, 2, 5)
    load_cot.wait()
    load_misc.wait()
    load_freq.wait()
    live_col = (
        lax.broadcasted_iota(jnp.int32, (rows, 1), 0).astype(jnp.float32)
        < miscs[me].astype(jnp.float32)[2:3, :1]
    )
    gb_own[...] = jnp.where(live_col, cot_ref[...].astype(jnp.float32), 0.0).astype(jnp.bfloat16)
    gb_tree = gather_tree(wire, place.over_group, HOPS, gb_own, slot_gb, cut_gb, False)
    pl.when(away)(turn_wo.wait_recv)
    pl.when(home)(keep_wo.wait)
    mirror_wo.start()
    start_wo(0)
    attn(3, 11, 6)
    mirror_wo.wait_recv()
    start_wo(1)
    pl.when(away)(turn[0].wait_recv)
    turn[1].wait_recv()
    pl.when(home)(keep_own.wait)
    for p in (0, 1):
        gu_trees[p][0].start()
        gu_trees[p][1].start()
        gu_passes[0, p].start()
    for k in FIRST:
        gb_tree[k].start()
    local(gb_own, o_gb.at[0, 0])
    attn(1, 4, 7, 8, 9, 10, 12, 13)

    for copy in misc_copies:
        copy.wait_recv()
    as_float = [miscs[s].astype(jnp.float32) for s in range(8)]
    gain1 = jnp.concatenate([m[0:1, :144] for m in as_float], axis=1)
    gain2 = jnp.concatenate([m[1:2, :144] for m in as_float], axis=1)
    normed = (middle[...] * gain1).astype(jnp.bfloat16)
    normed1[...] = normed
    for k in WHOLE:
        passes[0][k].wait_recv()
        passes[1][k].wait_recv()
    live = [m[2:3, :1] for m in as_float]
    start_of = []
    for i in range(BEHIND + 1):
        total = jnp.zeros((1, 1), jnp.float32)
        for s in range(8):
            total = total + jnp.where(s < me - i, 1.0, 0.0) * live[s]
        start_of.append(total)
    row = lax.broadcasted_iota(jnp.int32, (rows, 1), 0).astype(jnp.float32)
    query_pos = start_of[0] + row
    angles = query_pos * freq_ref[0:1, :]
    cosine, sine_part = jnp.cos(angles), jnp.sin(angles)
    rope[:, :128] = cosine
    rope[:, 128:] = sine_part
    weights = wqkv.reshape(width, 1536)

    def turned(vectors):
        first, second = vectors[:, :128], vectors[:, 128:]
        return jnp.concatenate(
            [first * cosine - second * sine_part, second * cosine + first * sine_part], axis=1
        )

    projected = matmul(normed, weights[:, 1024:1536])
    kv_ref[0, :, :256] = turned(projected[:, :256]).astype(jnp.bfloat16)
    kv_ref[0, :, 256:] = projected[:, 256:].astype(jnp.bfloat16)
    x, upper = place.x, place.z_hi == 1
    cross_kv = wire.copy(kv_ref.at[0], kv_ref.at[BEHIND], (place.rep, at(0, 1)))
    near_kv, far_kv = [], []
    for i in range(1, BEHIND):
        target = (place.rep, 4 * place.z_hi + (x + i) % 4)
        near_kv.append(wire.copy(kv_ref.at[0], kv_ref.at[i], target))
        far_kv.append(wire.copy(kv_ref.at[BEHIND], kv_ref.at[i], target))
    pl.when(jnp.logical_not(upper))(cross_kv.start)
    for i, copy in enumerate(near_kv):
        pl.when(x + (i + 1) < 4)(copy.start)
    for i in range(1, BEHIND + 1):

        @pl.when(me < i)
        def _():
            kv_ref[i] = jnp.zeros(kv_ref.shape[1:], kv_ref.dtype)

    def pass_kv():
        pl.when(upper)(cross_kv.wait_recv)
        for i, copy in enumerate(far_kv):
            pl.when(jnp.logical_and(upper, x + (i + 1) > 3))(copy.start)

    def have_kv():
        for i, (near, far) in enumerate(zip(near_kv, far_kv)):
            pl.when(x >= i + 1)(near.wait_recv)
            pl.when(jnp.logical_and(upper, x < i + 1))(far.wait_recv)

    scaling = 256 ** (-0.5)
    for h in range(4):
        heads = matmul(normed, weights[:, 256 * h : 256 * (h + 1)])
        q_ref[h] = (turned(heads) * scaling).astype(jnp.bfloat16)

    index = lax.broadcasted_iota(jnp.int32, (1, (BEHIND + 1) * rows), 1)
    key_pos = jnp.zeros(index.shape, jnp.float32)
    key_live = jnp.zeros(index.shape, jnp.float32)
    for i in range(BEHIND + 1):
        inside = jnp.logical_and(index >= i * rows, index < (i + 1) * rows)
        within = (index - i * rows).astype(jnp.float32)
        live_i = jnp.zeros((1, 1), jnp.float32)
        for s in range(8):
            live_i = live_i + jnp.where(me - i == s, 1.0, 0.0) * live[s]
        key_pos = jnp.where(inside, start_of[i] + within, key_pos)
        key_live = jnp.where(inside, jnp.where(within < live_i, 1.0, 0.0), key_live)
    ahead = query_pos - key_pos
    allowed = jnp.logical_and(
        jnp.logical_and(ahead >= 0.0, ahead < float(WINDOW)), key_live > 0.5
    )
    bias[...] = jnp.where(allowed, 0.0, MASKED)
    pass_kv()

    over_wo(0, 2)
    over_wo(1, 1)
    over(0, 2)
    over(1, 1)
    for k in SERVE[:4]:
        arrive(gb_tree, k)
    have_kv()
    all_kv = kv_ref.reshape((BEHIND + 1) * rows, 512)
    for h in range(4):
        scores = trail_product(q_ref[h], all_kv[:, :256]) + bias[...]
        raised = jnp.exp(scores - jnp.max(scores, axis=1, keepdims=True))
        share = raised * (1.0 / jnp.sum(raised, axis=1, keepdims=True))
        probs[h] = share
        att[:, 256 * h : 256 * (h + 1)] = matmul(
            share.astype(jnp.bfloat16), all_kv[:, 256:]
        ).astype(jnp.bfloat16)
        if h == 1:
            for k in SERVE[4:6]:
                arrive(gb_tree, k)
    over_wo(2, 0)
    over_wo(3, 3)
    for copy in wo_passes.values():
        copy.wait_recv()
    keep = jnp.where(live_col, 1.0, 0.0)
    mid = x_ref[...].astype(jnp.float32) + keep * matmul(att[...], wo.reshape(1024, width)[...])
    middle[...] = mid
    inverse2 = lax.rsqrt(jnp.mean(mid * mid, axis=1, keepdims=True) + EPSILON)
    normed2[...] = (mid * inverse2 * gain2).astype(jnp.bfloat16)
    for src, dst in (
        (miscs, o_misc),
        (wqkv, o_qkv),
        (wo, o_wo),
        (normed1, o_normed1),
        (q_ref, o_q),
        (kv_ref, o_kv),
        (probs, o_probs),
        (att, o_att),
        (middle, o_middle),
        (normed2, o_normed2),
        (rope, o_rope),
    ):
        local(src, dst)
    over(2, 0)
    over(3, 3)
    for k in SERVE[6:]:
        arrive(gb_tree, k)
    for copy in gu_passes.values():
        copy.wait_recv()
    waited = [id(copy) for copy in near_kv + far_kv + [cross_kv, turn[0], turn_wo]]
    for copy in locals_[9:]:
        if copy is not None:
            copy.wait()
    pl.when(away)(turn[0].wait_send)
    pl.when(away)(turn_wo.wait_send)
    pl.when(jnp.logical_not(upper))(cross_kv.wait_send)
    for i, (near, far) in enumerate(zip(near_kv, far_kv)):
        pl.when(x + (i + 1) < 4)(near.wait_send)
        pl.when(jnp.logical_and(upper, x + (i + 1) > 3))(far.wait_send)
    for copy in wire.made:
        if id(copy) not in waited:
            copy.wait_send()


ANY = pl.BlockSpec(memory_space=pl.ANY)


def comm_params(collective_id):
    return pltpu.CompilerParams(
        collective_id=collective_id, has_side_effects=True, vmem_limit_bytes=VMEM_LIMIT
    )


def front(tokens, cot, misc, freq, w_query, w_keyval, w_out, w_gate, w_up):
    bf, f32 = jnp.bfloat16, jnp.float32
    rows, width = tokens.shape
    keys = (BEHIND + 1) * rows
    outs = [
        ((8, 16, 256), bf),
        ((8, 144, 1536), bf),
        ((8, 128, width), bf),
        ((8, 144, 2 * FF_PAD), bf),
        ((4, 2, rows, width), bf),
        ((rows, width), bf),
        ((4, rows, 256), bf),
        ((BEHIND + 1, rows, 512), bf),
        ((4, rows, keys), f32),
        ((rows, 1024), bf),
        ((rows, width), f32),
        ((rows, width), bf),
        ((rows, 256), f32),
    ]
    scratch = [
        ((rows, width), bf),
        ((rows, width), bf),
        ((8, 16, 256), bf),
        ((8, 128), f32),
        ((8, 144, 1536), bf),
        ((8, 128, width), bf),
        (w_gate.shape, bf),
        (w_up.shape, bf),
        ((8, 144, 2 * FF_PAD), bf),
        ((rows, width), bf),
        ((rows, width), bf),
        ((4, rows, 256), bf),
        ((BEHIND + 1, rows, 512), bf),
        ((rows, keys), f32),
        ((4, rows, keys), f32),
        ((rows, 1024), bf),
        ((rows, width), f32),
        ((rows, width), bf),
        ((rows, 256), f32),
        (w_out.shape, bf),
    ]
    return pl.pallas_call(
        front_kernel,
        out_shape=tuple(jax.ShapeDtypeStruct(*o) for o in outs),
        in_specs=[ANY] * 9,
        out_specs=(ANY,) * len(outs),
        scratch_shapes=[pltpu.VMEM(*v) for v in scratch]
        + [
            pltpu.SemaphoreType.DMA((32,)),
            pltpu.SemaphoreType.DMA((136,)),
            pltpu.SemaphoreType.DMA((136,)),
        ],
        compiler_params=comm_params(1),
        name="attention_forward",
    )(tokens, cot, misc, freq, w_query, w_keyval, w_out, w_gate, w_up)


def finish_kernel(both, d_in, q_in, kv_in, wo_in, gate, up, d_out, q_out, kv_out, wo_out):
    for k, out in enumerate((gate, up)):
        parts = []
        for d in range(8):
            for t in range(PAIRS):
                half, q, first = (k, 3, 0) if t == 3 else (t // 4, t % 4, 128 * k)
                size = min(128, FF_DEV - 128 * t)
                parts.append(both[half, q, d, :, first : first + size])
        out[...] = jnp.concatenate(parts, axis=1).astype(jnp.float32)
    d_out[...] = d_in[...].astype(jnp.float32)
    q_out[...] = q_in[...].astype(jnp.float32)
    for c in range(2):
        for q in range(2):
            start = 256 * c + 128 * q
            kv_out[:, start : start + 128] = kv_in[c, q].astype(jnp.float32)

    @pl.when(pl.program_id(0) == 0)
    def _():
        wo_out[...] = wo_in[...].astype(jnp.float32)


def finish(both, d_in, q_in, kv_in, wo_in):
    rows, width = both.shape[3], d_in.shape[1]
    tall = 48
    steps = rows // tall
    shapes = [(rows, 8 * FF_DEV)] * 2 + [(FF_DEV, width), (rows, 1024), (rows, 512), wo_in.shape]
    blocks = [(tall, 8 * FF_DEV)] * 2 + [(FF_DEV // steps, width), (tall, 1024), (tall, 512)]
    by_row = lambda i: (i, 0)
    fixed = pl.BlockSpec(wo_in.shape, lambda i: (0, 0))
    return pl.pallas_call(
        finish_kernel,
        grid=(steps,),
        out_shape=[jax.ShapeDtypeStruct(shape, jnp.float32) for shape in shapes],
        in_specs=[
            pl.BlockSpec((2, 4, 8, tall, 256), lambda i: (0, 0, 0, i, 0)),
            pl.BlockSpec((FF_DEV // steps, width), by_row),
            pl.BlockSpec((tall, 1024), by_row),
            pl.BlockSpec((2, 4, tall, 128), lambda i: (0, 0, i, 0)),
            fixed,
        ],
        out_specs=[pl.BlockSpec(block, by_row) for block in blocks] + [fixed],
        compiler_params=pltpu.CompilerParams(vmem_limit_bytes=VMEM_LIMIT),
        name="finish",
    )(both, d_in, q_in, kv_in, wo_in)


ROOT = 0.7978845608028654
CUBE = 0.044715


def ff_kernel(
    own_n, gb_all, wgu_all, wd_all,
    o_gn, o_pb, o_pgu, o_pd,
    nbuf, gb, wgu, wd, gh, hid, ggu, part_g, part_b, out_f32, dgu,
    g_half, dd, r_d, d_whole, d_half_a, d_half_b, z_d,
    r_gu, gu_half, n_turned, b_half,
    local_sems, send_sems, recv_sems,
):
    place = Place()
    wire = Wire(send_sems, recv_sems)
    loads = [
        pltpu.make_async_copy(src, dst, local_sems.at[k])
        for k, (src, dst) in enumerate(
            [(own_n, nbuf.at[0, 0]), (wd_all, wd.at[pl.ds(0, FF_DEV)]), (gb_all, gb), (wgu_all, wgu)]
        )
    ]
    for load in loads:
        load.start()
    core, y = place.core, place.y
    sibling, low = place.device(sibling=1), place.device(swap_lo=1)
    greet(
        [place.device(dx=1), place.device(dx=3), place.device(mirror=1), sibling, low]
        + [place.device(dy=1), place.device(dy=3)]
    )

    def cut(ref, part):
        return ref if part == 0 else ref.at[pl.ds((part - 1) * 96, 96)]

    slot_n = lambda j, p: nbuf.at[j, p]
    tree = gather_tree(wire, place.over_group, HOPS, nbuf.at[0, 0], slot_n, cut, False)
    sum_g = SumTree(
        wire, place.over_group, HOPS, lambda j, p: part_g.at[j, p], cut,
        [g_half.at[k] for k in range(14)],
    )

    def cut_d(ref, part):
        start, size = ((0, 1152), (0, 640), (640, 512))[part]
        return ref.at[:, pl.ds(start, size)]

    quarter_d = dd.at[core, y]
    swap_d = wire.copy(dd.at[1 - core], r_d, sibling)
    sum_d = SumTree(
        wire, lambda dx, mirror: place.device(dy=dx), RING,
        lambda j, p: dd.at[core, (y + STEPS[j]) % 4], cut_d,
        [d_whole.at[0], d_whole.at[1], d_half_a, d_half_b],
    )
    cross_d = wire.copy(quarter_d, z_d, low)

    def cut_lead(ref, part):
        return ref if part == 0 else ref.at[pl.ds((part - 1) * 4, 4)]

    swap_gu = wire.copy(dgu.at[1 - core], r_gu, sibling)
    far_b = SumTree(
        wire, place.over_group, HOPS_FAR, lambda j, p: part_b.at[j, p], cut,
        [b_half.at[k] for k in range(4)],
    )
    far_gu = [
        wire.copy(
            cut_lead(dgu.at[core, (y + 2) % 4], part),
            gu_half.at[part - 1],
            place.device(dy=(3, 1)[part - 1]),
        )
        for part in (1, 2)
    ]
    loads[0].wait()
    for k in FIRST:
        tree[k].start()
    wd[FF_DEV:] = jnp.zeros((FF_PAD - FF_DEV, wd.shape[1]), wd.dtype)
    loads[1].wait()
    loads[2].wait()

    def back_hidden(j):
        rows = jnp.concatenate([gb[j, 0], gb[j, 1]], axis=0)
        gh[j] = trail_product(rows, wd[...])

    def forward(j, first=0, count=384):
        blocks = [nbuf[j, p] for p in (0, 1) if first <= 192 * p < first + count]
        rows = jnp.concatenate(blocks, axis=0) if len(blocks) > 1 else blocks[0]
        span = pl.ds(first, count)

        def tile(t, carry):
            columns = pl.ds(pl.multiple_of(t * 256, 256), 256)
            narrow = pl.ds(pl.multiple_of(t * 128, 128), 128)
            both = matmul(rows, wgu[:, columns])
            gate, up = both[:, :128], both[:, 128:]
            square = gate * gate
            curve = jnp.tanh(gate * (ROOT + ROOT * CUBE * square))
            half_up = 0.5 + 0.5 * curve
            active = gate * half_up
            slope = half_up + active * (1.0 - curve) * (ROOT + 3.0 * ROOT * CUBE * square)
            back = gh[j, span, narrow]
            hid[j, span, narrow] = (active * up).astype(jnp.bfloat16)
            ggu[j, span, columns] = jnp.concatenate(
                [(back * up * slope).astype(jnp.bfloat16), (back * active).astype(jnp.bfloat16)],
                axis=1,
            )
            return carry

        lax.fori_loop(0, PAIRS, tile, 0, unroll=True)

    def back_normed(j, first=0, count=384):
        for start, size in ((0, 512), (512, 512), (1024, 128)):
            block = trail_product(
                ggu[j, first : first + count], wgu[start : start + size, :]
            ).astype(jnp.bfloat16)
            for p in (0, 1):
                if first <= 192 * p < first + count:
                    low = 192 * p - first
                    part_g[j, p, :, start : start + size] = block[low : low + 192]

    def down(j):
        for start, size in ((0, 512), (512, 512), (1024, 128)):
            block = matmul(hid[j], wd[:, start : start + size]).astype(jnp.bfloat16)
            part_b[j, 0, :, start : start + size] = block[:192]
            part_b[j, 1, :, start : start + size] = block[192:]

    hid_rows = hid.reshape(4 * 384, FF_PAD)
    ggu_rows = ggu.reshape(4 * 384, 2 * FF_PAD)
    gb_rows = gb.reshape(4 * 384, 1152)
    dd_rows = dd.reshape(FF_PAD, 1152)
    dgu_rows = dgu.reshape(2, 4, 1152, 256)

    def turn_rows(j):
        rows = jnp.concatenate([nbuf[j, 0], nbuf[j, 1]], axis=0)
        n_turned[:, 384 * j : 384 * (j + 1)] = rows.T

    def grad_half(half):
        def tile(q, carry):
            columns = pl.ds(pl.multiple_of((half * 4 + q) * 256, 256), 256)
            dgu_rows[half, q] = matmul(n_turned[...], ggu_rows[:, columns]).astype(jnp.bfloat16)
            return carry

        lax.fori_loop(0, 3, tile, 0)

    dgu[:, 3, :, :, 128:] = jnp.zeros((2, 8, 144, 128), jnp.bfloat16)
    back_hidden(0)
    back_hidden(1)
    back_hidden(2)
    for k in SERVE[:3]:
        arrive(tree, k)
    back_hidden(3)
    for k in SERVE[3:7]:
        arrive(tree, k)
    loads[3].wait()
    forward(0)
    turn_rows(0)
    for k in SERVE[7:9]:
        arrive(tree, k)
    forward(1)
    for k in SERVE[9:12]:
        arrive(tree, k)
    forward(2)
    turn_rows(1)
    turn_rows(2)
    forward(3, 0, 192)
    back_normed(3, 0, 192)
    sum_g.start(9, 8)
    for k in SERVE[12:]:
        arrive(tree, k)
    forward(3, 192, 192)
    back_normed(3, 192, 192)
    sum_g.start(13, 12)
    back_normed(1)
    back_normed(2)
    sum_g.send_mid()
    for start, size in ((0, 512), (512, 512), (1024, 128)):
        dd_rows[:, start : start + size] = lead_product(
            hid_rows[...], gb_rows[:, start : start + size]
        ).astype(jnp.bfloat16)
    swap_d.start()
    sum_g.send_near()
    back_normed(0)
    sum_g.start(1)
    turn_rows(3)
    middle_tile = matmul(n_turned[...], ggu_rows[:, 768:1024]).astype(jnp.bfloat16)
    dgu_rows[0, 3, :, :128] = middle_tile[:, :128]
    dgu_rows[1, 3, :, :128] = middle_tile[:, 128:]
    down(3)
    swap_d.wait_recv()

    def add_d(i, carry):
        add_into(dd.at[core, i], r_d.at[i])
        return carry

    lax.fori_loop(0, 4, add_d, 0)
    sum_d.start(2, 3)
    sum_g.send_next()
    grad_half(1 - core)
    swap_gu.start()
    sum_g.send_last()
    far_b.start(0, 1, 2, 3)
    sum_d.absorb(2, 3)
    sum_d.start(0, 1)
    grad_half(core)
    down(0)
    swap_gu.wait_recv()

    def add_gu(i, carry):
        add_into(dgu.reshape(2, 32, 144, 256).at[core, i], r_gu.reshape(32, 144, 256).at[i])
        return carry

    lax.fori_loop(0, 32, add_gu, 0)
    for copy in far_gu:
        copy.start()
    sum_d.absorb(0, 1)
    cross_d.start()
    down(1)
    down(2)
    out_f32[...] = sum_g.finish(0)
    store_g = pltpu.make_async_copy(out_f32, o_gn, local_sems.at[6])
    store_g.start()
    cross_d.wait_recv()
    cross_d.wait_send()
    add_into(quarter_d, z_d)
    store_d = pltpu.make_async_copy(quarter_d, o_pd, local_sems.at[7])
    store_d.start()
    far_b.absorb(0, 1, 2, 3)
    store_b = pltpu.make_async_copy(part_b, o_pb, local_sems.at[5])
    store_b.start()
    for part, j in ((1, 2), (2, 1)):
        far_gu[part - 1].wait_recv()
        add_into(
            cut_lead(dgu.at[core, (y + STEPS[j]) % 4], part), gu_half.at[part - 1]
        )
    store_gu = pltpu.make_async_copy(dgu.at[core], o_pgu, local_sems.at[4])
    store_gu.start()
    for store in (store_b, store_gu, store_g, store_d):
        store.wait()
    for copy in wire.made:
        if copy is not cross_d:
            copy.wait_send()


def feed_forward(own_n, gb_all, wgu_all, wd_all):
    bf, f32 = jnp.bfloat16, jnp.float32
    vm = pltpu.VMEM
    tokens, width = own_n.shape
    sums = [vm((14, tokens // 2, width), bf)]
    return pl.pallas_call(
        ff_kernel,
        out_shape=(
            jax.ShapeDtypeStruct((tokens, width), f32),
            jax.ShapeDtypeStruct((4, 2, tokens, width), bf),
            jax.ShapeDtypeStruct((4, 8, 144, 256), bf),
            jax.ShapeDtypeStruct((112, width), bf),
        ),
        in_specs=[ANY] * 4,
        out_specs=(ANY,) * 4,
        scratch_shapes=[
            vm((4, 2, tokens, width), bf),
            vm((4, 2, tokens, width), bf),
            vm(wgu_all.shape, bf),
            vm((FF_PAD, width), bf),
            vm((4, 2 * tokens, FF_PAD), f32),
            vm((4, 2 * tokens, FF_PAD), bf),
            vm((4, 2 * tokens, 2 * FF_PAD), bf),
            vm((4, 2, tokens, width), bf),
            vm((4, 2, tokens, width), bf),
            vm((tokens, width), f32),
            vm((2, 4, 8, 144, 256), bf),
        ]
        + sums
        + [
            vm((2, 4, 112, width), bf),
            vm((4, 112, width), bf),
            vm((2, 112, width), bf),
            vm((112, 640), bf),
            vm((112, 512), bf),
            vm((112, width), bf),
            vm((4, 8, 144, 256), bf),
            vm((2, 4, 144, 256), bf),
            vm((width, 8 * tokens), bf),
            vm((4, tokens // 2, width), bf),
        ]
        + [
            pltpu.SemaphoreType.DMA((8,)),
            pltpu.SemaphoreType.DMA((48,)),
            pltpu.SemaphoreType.DMA((48,)),
        ],
        compiler_params=comm_params(2),
        name="feed_forward",
    )(own_n, gb_all, wgu_all, wd_all)


def back_kernel(
    p_gu, p_d, part_b_all, gn2_all, middle_all, miscs_all, tokens, cot, rope_all, q_all, kv_all,
    probs_all, att_all, wqkv_all, wo_all, normed1_all,
    o_gu, o_d, o_q, o_kv, o_wo, o_out, o_grad,
    h_gu, gu_whole, z_gu, f_gu, piece_d,
    part_b, b_half, gn2, middle, miscs, x_ref, cot_ref, rope, q_ref, kv_ref, probs, att,
    wqkv, wo, normed1, dq, r_q, q_whole, q_half, q_parts, dkv, r_kv, kv_parts, dwo, r_wo, w_whole, w_half, w_parts,
    gkv, kv_out, kv_in, gproj, gmid, out_bf,
    s_wo, z_wo, s_q, z_q, s_kv, y_kv, z_kv,
    local_sems, send_sems, recv_sems,
):
    place = Place()
    wire = Wire(send_sems, recv_sems)
    core, me, y, rep = place.core, place.shard, place.y, place.rep
    rows, width = tokens.shape
    at = place.shard_at
    others = [(j, p) for p in (0, 1) for j in range(4) if (j, p) != (0, 0)]
    group = [place.device(dx=STEPS[j], mirror=p) for j, p in others]
    sequence = [(rep, at(j, 1)) for j in range(4)]
    sibling = place.device(sibling=1)
    column = [place.device(dy=d) for d in (1, 3, 2)]
    low = place.device(swap_lo=1)
    locals_ = []

    def local(src, dst):
        copy = pltpu.make_async_copy(src, dst, local_sems.at[len(locals_)])
        copy.start()
        locals_.append(copy)
        return copy

    loads = [
        local(src, dst)
        for src, dst in (
            (miscs_all, miscs),
            (gn2_all, gn2),
            (middle_all, middle),
            (cot, cot_ref),
            (att_all, att),
            (wo_all, wo),
        )
    ]
    load_gu = local(p_gu, h_gu)
    load_d = local(p_d, piece_d)
    load_b = local(part_b_all, part_b)
    both_cores = [place.device(dy=d, sibling=1) for d in (1, 3, 2)]
    greet([sibling, low] + group + column + sequence + both_cores)
    loads_heads = [
        local(src, dst)
        for src, dst in ((q_all, q_ref), (kv_all, kv_ref), (probs_all, probs), (rope_all, rope))
    ]
    load_x = local(tokens, x_ref)
    load_n = local(normed1_all, normed1)
    load_w = local(wqkv_all, wqkv)
    loaded = len(locals_)

    def over_y(dx, mirror):
        return place.device(dy=dx)

    def cut_lead(ref, part):
        return ref if part == 0 else ref.at[pl.ds((part - 1) * 4, 4)]

    def cut_rows(size):
        def cut(ref, part):
            return ref if part == 0 else ref.at[pl.ds((part - 1) * size, size)]

        return cut

    def cut_lanes(size):
        def cut(ref, part):
            return ref if part == 0 else ref.at[:, pl.ds((part - 1) * size, size)]

        return cut

    def cut_d(ref, part):
        start, size = ((0, width), (0, 640), (640, 512))[part]
        return ref.at[:, pl.ds(start, size)]

    def added(target, source, count):
        def one(i, carry):
            add_into(target.at[i], source.at[i])
            return carry

        lax.fori_loop(0, count, one, 0)

    chunks = [pl.ds(0, 80), pl.ds(80, 64)]
    near_gu = [
        [
            wire.copy(
                h_gu.at[(y + STEPS[j]) % 4, :, c],
                gu_whole.at[k, :, c],
                place.device(dy=(3, 1)[k]),
            )
            for k, j in enumerate((2, 1))
        ]
        for c in chunks
    ]
    quarters = [h_gu.at[y, :, c] for c in chunks]
    crossings_gu = [wire.copy(h_gu.at[y, :, c], z_gu.at[:, c], low) for c in chunks]
    turns = [
        [
            wire.copy(h_gu.at[y, at(j, p), c], f_gu.at[me, c], device)
            for (j, p), device in zip(others, group)
        ]
        for c in chunks
    ]
    slots_gu = [lambda j, p, c=c: o_gu.at[core, (y + STEPS[j]) % 4, :, c] for c in chunks]
    trees_gu = [
        gather_tree(wire, over_y, RING, f_gu.at[:, c], slot, cut_lead, True)
        for c, slot in zip(chunks, slots_gu)
    ]
    passes_gu = [
        [
            wire.copy(f_gu.at[:, c] if j == 0 else slot(j, 0), slot(j, 0), sibling)
            for j in range(4)
        ]
        for c, slot in zip(chunks, slots_gu)
    ]

    def cross(i):
        for k, copy in enumerate(near_gu[i]):
            copy.wait_recv()
            added(quarters[i], gu_whole.at[k, :, chunks[i]], 8)
        crossings_gu[i].start()

    def turn(i):
        crossings_gu[i].wait_recv()
        crossings_gu[i].wait_send()
        added(quarters[i], z_gu.at[:, chunks[i]], 8)
        for copy in turns[i]:
            copy.start()
        f_gu[me, chunks[i]] = h_gu[y, me, chunks[i]]

    def spread(i):
        for copy in turns[i]:
            copy.wait_recv()
        for copy in (trees_gu[i][0], trees_gu[i][1], passes_gu[i][0]):
            copy.start()
        local(f_gu.at[:, chunks[i]], slots_gu[i](0, 0))

    def spread_on(i, k):
        arrive(trees_gu[i], k, RING_ONWARD)
        if k != 2:
            passes_gu[i][(2, 1, None, 3)[k]].start()

    load_gu.wait()
    for copy in near_gu[0] + near_gu[1]:
        copy.start()

    sum_b = SumTree(
        wire, place.over_group, HOPS, lambda j, p: part_b.at[j, p], cut_rows(96),
        [b_half.at[k] for k in range(14)],
    )
    load_b.wait()
    sum_b.start(7, 6, 4, 2, 11, 10, 1)

    load_d.wait()
    slot_d = lambda j, p: o_d.at[core, (y + STEPS[j]) % 4]
    tree_d = gather_tree(wire, over_y, RING, piece_d, slot_d, cut_d, True)
    pass_d = [
        wire.copy(piece_d if j == 0 else slot_d(j, 0), slot_d(j, 0), sibling) for j in range(4)
    ]

    for load in loads:
        load.wait()
    as_float = [miscs[s].astype(jnp.float32) for s in range(8)]
    gain1 = jnp.concatenate([m[0:1, :144] for m in as_float], axis=1)
    gain2 = jnp.concatenate([m[1:2, :144] for m in as_float], axis=1)
    row = lax.broadcasted_iota(jnp.int32, (rows, 1), 0).astype(jnp.float32)
    keep = jnp.where(row < miscs[me].astype(jnp.float32)[2:3, :1], 1.0, 0.0)
    mid = middle[...]
    inverse2 = lax.rsqrt(jnp.mean(mid * mid, axis=1, keepdims=True) + EPSILON)
    scaled2 = mid * inverse2
    grad2 = gn2[...]
    grad_gain2 = jnp.sum(grad2 * scaled2, axis=0, keepdims=True)
    grad2 = grad2 * gain2
    grad_mid = cot_ref[...].astype(jnp.float32) + inverse2 * (
        grad2 - scaled2 * jnp.mean(grad2 * scaled2, axis=1, keepdims=True)
    )
    gmid[...] = grad_mid
    grad_attn = (keep * grad_mid).astype(jnp.bfloat16)
    for start in range(0, width, 384):
        block = lead_product(att[...], grad_attn[:, start : start + 384]).astype(jnp.bfloat16)
        block = block.reshape(8, 2, 4, 16, 384)
        for c in range(2):
            for q in range(4):
                dwo[c, q, :, :, start : start + 384] = block[:, c, q]
    swap_wo = wire.copy(dwo.at[1 - core], r_wo, sibling)
    swap_wo.start()
    grad_att = trail_product(grad_attn, wo.reshape(1024, width)[...]).astype(jnp.bfloat16)

    for load in loads_heads:
        load.wait()
    keys = (BEHIND + 1) * rows
    all_kv = kv_ref.reshape(keys, 512)
    flat = gkv.reshape(keys, 512)
    cosine, sine_part = rope[:, :128], rope[:, 128:]
    scaling = 256 ** (-0.5)

    def turned_back(vectors):
        first, second = vectors[:, :128], vectors[:, 128:]
        return jnp.concatenate(
            [first * cosine + second * sine_part, second * cosine - first * sine_part], axis=1
        )

    for h in range(4):
        share = probs[h]
        share_low = share.astype(jnp.bfloat16)
        grad_h = grad_att[:, 256 * h : 256 * (h + 1)]
        grad_probs = trail_product(grad_h, all_kv[:, 256:])
        delta = jnp.sum(share * grad_probs, axis=1, keepdims=True)
        grad_scores = (share * (grad_probs - delta)).astype(jnp.bfloat16)
        grad_keys = lead_product(grad_scores, q_ref[h])
        grad_values = lead_product(share_low, grad_h)
        if h == 0:
            flat[:, :256] = grad_keys
            flat[:, 256:] = grad_values
        else:
            flat[:, :256] += grad_keys
            flat[:, 256:] += grad_values
        grad_q = matmul(grad_scores, all_kv[:, :256])
        gproj[:, 256 * h : 256 * (h + 1)] = (turned_back(grad_q) * scaling).astype(jnp.bfloat16)
        if h == 1:
            cross(0)
            for copy in (tree_d[0], tree_d[1], pass_d[0]):
                copy.start()
            local(piece_d, slot_d(0, 0))
    x, upper = place.x, place.z_hi == 1
    sends = []
    for i in range(1, BEHIND):
        kv_out[i - 1] = gkv[i].astype(jnp.bfloat16)
        target = (rep, 4 * place.z_hi + (x + (4 - i)) % 4)
        sends.append(wire.copy(kv_out.at[i - 1], kv_in.at[i - 1], target))
        pl.when(jnp.logical_or(upper, x >= i))(sends[-1].start)

        @pl.when(jnp.logical_not(jnp.logical_or(upper, x + i <= 3)))
        def _():
            kv_in[i - 1] = jnp.zeros(kv_in.shape[1:], kv_in.dtype)

    plane_kv = wire.copy(kv_out.at[BEHIND - 1], kv_in.at[BEHIND - 1], (rep, at(0, 1)))

    @pl.when(upper)
    def _():
        kv_in[BEHIND - 1] = jnp.zeros(kv_in.shape[1:], kv_in.dtype)

    def collect_kv():
        through = gkv[BEHIND]
        for i, copy in enumerate(sends):
            pl.when(jnp.logical_or(upper, x + (i + 1) <= 3))(copy.wait_recv)
            through = through + jnp.where(x + (i + 1) > 3, 1.0, 0.0) * kv_in[i].astype(jnp.float32)
        kv_out[BEHIND - 1] = through.astype(jnp.bfloat16)
        pl.when(upper)(plane_kv.start)

    def over_ring(blocks, whole, half):
        return SumTree(
            wire, over_y, RING, lambda j, p: blocks.at[core, (y + STEPS[j]) % 4], cut_lead,
            [whole.at[0], whole.at[1], half.at[0], half.at[1]],
        )

    def near_ring(tree):
        tree.absorb(2, 3)
        tree.start(0, 1)

    def to_owners(tree, blocks, parts):
        tree.absorb(0, 1)
        copies = [
            wire.copy(blocks.at[core, y, at(j, p)], parts.at[i], device)
            for i, ((j, p), device) in enumerate(zip(others, group))
        ]
        for copy in copies:
            copy.start()
        return copies

    def to_low(copies, blocks, parts, piece, other):
        total = blocks[core, y, me].astype(jnp.float32)
        for i, copy in enumerate(copies):
            copy.wait_recv()
            total = total + parts[i].astype(jnp.float32)
        piece[y] = total.astype(jnp.bfloat16)
        crossing = wire.copy(piece.at[y], other, low)
        crossing.start()
        return crossing

    load_n.wait()
    dq_rows = dq.reshape(2, 4, width, 128)
    for t in range(4):
        block = lead_product(normed1[...], gproj[:, 256 * t : 256 * (t + 1)]).astype(jnp.bfloat16)
        dq_rows[t // 2, 2 * (t % 2)] = block[:, :128]
        dq_rows[t // 2, 2 * (t % 2) + 1] = block[:, 128:]
    swap_q = wire.copy(dq.at[1 - core], r_q, sibling)
    swap_q.start()
    cross(1)
    swap_wo.wait_recv()
    added(dwo.reshape(2, 32, 16, width).at[core], r_wo.reshape(32, 16, width), 32)
    sum_wo = over_ring(dwo, w_whole, w_half)
    sum_wo.start(2, 3)
    load_x.wait()
    load_w.wait()
    weights = wqkv.reshape(width, 1536)
    gn2[...] = trail_product(gproj[:, :1024], weights[:, :1024])
    turn(0)
    swap_q.wait_recv()
    added(dq.reshape(2, 32, 144, 128).at[core], r_q.reshape(32, 144, 128), 32)
    sum_q = over_ring(dq, q_whole, q_half)
    sum_q.start(2, 3)
    collect_kv()
    near_ring(sum_wo)
    turn(1)
    near_ring(sum_q)
    spread(0)

    pl.when(jnp.logical_not(upper))(plane_kv.wait_recv)
    grad_kv = gkv[0] + kv_in[BEHIND - 1].astype(jnp.float32)
    for i in range(BEHIND - 1):
        grad_kv = grad_kv + jnp.where(x + (i + 1) <= 3, 1.0, 0.0) * kv_in[i].astype(jnp.float32)
    gproj[:, 1024:1280] = turned_back(grad_kv[:, :256]).astype(jnp.bfloat16)
    gproj[:, 1280:1536] = grad_kv[:, 256:].astype(jnp.bfloat16)
    for t in range(2):
        dkv[t, :, :144] = (
            lead_product(normed1[...], gproj[:, 1024 + 256 * t : 1280 + 256 * t])
            .astype(jnp.bfloat16)
            .reshape(8, 144, 256)
        )
    inputs = x_ref[...].astype(jnp.float32)
    inverse1 = lax.rsqrt(jnp.mean(inputs * inputs, axis=1, keepdims=True) + EPSILON)
    scaled1 = inputs * inverse1
    grad1 = gn2[...] + trail_product(gproj[:, 1024:], weights[:, 1024:])
    grad_gain1 = jnp.sum(grad1 * scaled1, axis=0, keepdims=True)
    for s in range(8):
        cols = slice(144 * s, 144 * (s + 1))
        both = jnp.concatenate(
            [grad_gain1[:, cols], grad_gain2[:, cols], jnp.zeros((14, 144), jnp.float32)], axis=0
        )
        both = jnp.concatenate([both, jnp.zeros((16, 112), jnp.float32)], axis=1)
        dkv[0, s, 144:] = both.astype(jnp.bfloat16)
        dkv[1, s, 144:] = both.astype(jnp.bfloat16)
    swap_kv = wire.copy(dkv.at[1 - core], r_kv, sibling)
    swap_kv.start()
    direct_wo = to_owners(sum_wo, dwo, w_parts)
    spread(1)
    def over_column(source, landing):
        copies = [
            wire.copy(source.at[(y + d) % 4], landing.at[i], device)
            for i, (d, device) in enumerate(zip((1, 3, 2), column))
        ]
        for copy in copies:
            copy.start()
        return copies

    def over_low(copies, source, landing, other):
        for copy in copies:
            copy.wait_recv()
        mine = source[y].astype(jnp.float32)
        for i in range(3):
            mine = mine + landing[i].astype(jnp.float32)
        source[y] = mine.astype(jnp.bfloat16)
        crossing = wire.copy(source.at[y], other, low)
        crossing.start()
        return crossing

    def to_all(crossing, source, other, slot):
        crossing.wait_recv()
        crossing.wait_send()
        add_into(source.at[y], other)
        made = [wire.copy(source.at[y], slot(core, y), device) for device in column + [sibling]]
        for copy in made:
            copy.start()
        local(source.at[y], slot(core, y))
        return made

    def to_both(crossing, source, other, slot):
        made = to_all(crossing, source, other, slot)
        made += [
            wire.copy(source.at[y], slot(core, y), place.device(dy=d, sibling=1)) for d in (1, 3, 2)
        ]
        for copy in made[4:]:
            copy.start()
        return made

    def pass_on(made, slot):
        ends = [made[3]]
        for d, copy in zip((3, 1, 2), made):
            copy.wait_recv()
            held = slot(core, (y + d) % 4)
            ends.append(wire.copy(held, held, sibling))
            ends[-1].start()
        return ends

    slot_wo = lambda c, q: o_wo.at[c, q]
    slot_q = lambda c, q: o_q.at[:, pl.ds(pl.multiple_of(c * 512 + q * 128, 128), 128)]
    slot_kv = lambda c, q: o_kv.at[c, q]
    swap_kv.wait_recv()
    added(dkv.at[core], r_kv, 8)
    direct_kv = [
        wire.copy(dkv.at[core, at(j, p)], kv_parts.at[i], device)
        for i, ((j, p), device) in enumerate(zip(others, group))
    ]
    for copy in direct_kv:
        copy.start()
    direct_q = to_owners(sum_q, dq, q_parts)
    grad1 = grad1 * gain1
    gmid[...] += inverse1 * (grad1 - scaled1 * jnp.mean(grad1 * scaled1, axis=1, keepdims=True))
    local(gmid, o_grad)
    for k in (0, 1):
        arrive(tree_d, k, RING_ONWARD)
        pass_d[(2, 1)[k]].start()
    cross_wo = to_low(direct_wo, dwo, w_parts, s_wo, z_wo)
    for k in (0, 1):
        spread_on(0, k)
    cross_q = to_low(direct_q, dq, q_parts, s_q, z_q)
    total = dkv[core, me].astype(jnp.float32)
    for i, copy in enumerate(direct_kv):
        copy.wait_recv()
        total = total + kv_parts[i].astype(jnp.float32)
    s_kv[0] = total[:144, :128].astype(jnp.bfloat16)
    s_kv[1] = total[:144, 128:].astype(jnp.bfloat16)
    s_kv[2] = jnp.concatenate(
        [total[144:, :128], total[144:, 128:], jnp.zeros((112, 128), jnp.float32)], axis=0
    ).astype(jnp.bfloat16)
    s_kv[3] = jnp.zeros((144, 128), jnp.bfloat16)
    over_kv = over_column(s_kv, y_kv)
    sum_b.absorb(10)
    sum_b.start(3)
    sum_b.absorb(11)
    sum_b.start(5)
    sum_b.send_last()
    all_wo = to_all(cross_wo, s_wo, z_wo, slot_wo)
    all_q = to_all(cross_q, s_q, z_q, slot_q)
    cross_kv = over_low(over_kv, s_kv, y_kv, z_kv)
    for k in (0, 1):
        spread_on(1, k)
    for k in (2, 3):
        arrive(tree_d, k, RING_ONWARD)
    pass_d[3].start()
    all_kv_sum = to_both(cross_kv, s_kv, z_kv, slot_kv)
    ends = pass_on(all_wo, slot_wo) + pass_on(all_q, slot_q)
    for i in (0, 1):
        for k in (2, 3):
            spread_on(i, k)
    out_bf[...] = (middle[...] + keep * sum_b.finish(0)).astype(jnp.bfloat16)
    local(out_bf, o_out)
    ends += all_kv_sum
    for copy in pass_d + passes_gu[0] + passes_gu[1] + ends:
        copy.wait_recv()
    for copy in locals_[loaded:]:
        copy.wait()
    for i, copy in enumerate(sends):
        pl.when(jnp.logical_or(upper, x >= i + 1))(copy.wait_send)
    pl.when(upper)(plane_kv.wait_send)
    waited = [id(copy) for copy in sends + [plane_kv] + crossings_gu + [cross_wo, cross_q, cross_kv]]
    waited += [id(sum_b.copies[k]) for k in (8, 9, 12, 13)]
    for copy in wire.made:
        if id(copy) not in waited:
            copy.wait_send()


def back(*args):
    bf, f32 = jnp.bfloat16, jnp.float32
    width = 1152
    rows = args[6].shape[0]
    outs = [
        ((2, 4, 8, 144, 256), bf),
        ((2, 4, 112, width), bf),
        ((144, 1024), bf),
        ((2, 4, 144, 128), bf),
        ((2, 4, 16, width), bf),
        ((rows, width), bf),
        ((rows, width), f32),
    ]
    scratch = [
        ((4, 8, 144, 256), bf),
        ((2, 8, 144, 256), bf),
        ((8, 144, 256), bf),
        ((8, 144, 256), bf),
        ((112, width), bf),
        ((4, 2, rows, width), bf),
        ((14, rows // 2, width), bf),
    ]
    scratch += [(a.shape, a.dtype) for a in args[3:16]]
    ring = lambda *b: [(2, 4, 8, *b), (4, 8, *b), (2, 8, *b), (2, 4, *b), (7, *b)]
    parts = ring(144, 128) + [(2, 8, 160, 256), (8, 160, 256), (7, 160, 256)] + ring(16, width)
    scratch += [(part, bf) for part in parts]
    scratch += [
        ((BEHIND + 1, rows, 512), f32),
        ((BEHIND, rows, 512), bf),
        ((BEHIND, rows, 512), bf),
        ((rows, 1536), bf),
        ((rows, width), f32),
        ((rows, width), bf),
    ]
    pieces = [(4, 16, width), (16, width), (4, 144, 128), (144, 128)]
    pieces += [(4, 144, 128), (3, 144, 128), (144, 128)]
    scratch += [(piece, bf) for piece in pieces]
    return pl.pallas_call(
        back_kernel,
        out_shape=tuple(jax.ShapeDtypeStruct(*o) for o in outs),
        in_specs=[ANY] * 16,
        out_specs=(ANY,) * len(outs),
        scratch_shapes=[pltpu.VMEM(*v) for v in scratch]
        + [
            pltpu.SemaphoreType.DMA((40,)),
            pltpu.SemaphoreType.DMA((176,)),
            pltpu.SemaphoreType.DMA((176,)),
        ],
        compiler_params=comm_params(3),
        name="attention_backward",
    )(*args)


def on_device(
    tokens, lengths, attn_gain, w_query, w_keyval, w_out, mlp_gain, w_gate, w_up, w_down, cotangent
):
    width = tokens.shape[1]
    live_count = lengths[0, 0]
    row = lax.broadcasted_iota(jnp.int32, (16, 256), 0)
    wide = lambda gain: jnp.pad(gain, (0, 112))[None]
    misc = jnp.where(
        row == 0,
        wide(attn_gain),
        jnp.where(row == 1, wide(mlp_gain), live_count.astype(jnp.bfloat16)),
    )
    frequency = np.power(10000.0, -2.0 * np.arange(128) / 256).astype(np.float32)
    (
        miscs, qkv_all, out_all, gu_all, branch_all,
        normed1, queries, all_kv, probs, attended, middle, normed2, rope,
    ) = front(
        tokens, cotangent, misc, jnp.asarray(np.tile(frequency[None], (8, 1))),
        w_query, w_keyval, w_out, w_gate, w_up,
    )
    grad_normed2, branch, grad_gu, grad_d = feed_forward(
        normed2, branch_all, gu_all.reshape(width, -1), w_down
    )
    sum_gu, sum_d, sum_q, sum_kv, sum_wo, outputs, grad_inputs = back(
        grad_gu, grad_d, branch, grad_normed2, middle, miscs, tokens, cotangent,
        rope, queries, all_kv, probs, attended, qkv_all, out_all, normed1,
    )
    grad_gate_w, grad_up_w, grad_down, grad_q, grad_kv, grad_wo = finish(
        sum_gu, sum_d.reshape(FF_PAD, width), sum_q, sum_kv, sum_wo.reshape(128, width)
    )
    gains = sum_kv[0, 2]
    gains = jnp.concatenate([gains[:2], gains[16:18, :16]], axis=1).astype(jnp.float32)
    return (
        outputs,
        grad_inputs,
        gains[0],
        grad_q,
        grad_kv,
        grad_wo,
        gains[1],
        grad_gate_w,
        grad_up_w,
        grad_down,
    )


def solution(mesh):
    placed = (
        P(("rep", "shard"), None),
        P("rep", "shard"),
        P("shard"),
        P("shard", None),
        P("shard", None),
        P("shard", None),
        P("shard"),
        P("shard", None),
        P("shard", None),
        P("shard", None),
        P(("rep", "shard"), None),
    )
    return jax.shard_map(
        on_device,
        mesh=mesh,
        in_specs=placed,
        out_specs=(
            P(("rep", "shard"), None),
            P(("rep", "shard"), None),
            P("shard"),
            P("shard", None),
            P("shard", None),
            P("shard", None),
            P("shard"),
            P("shard", None),
            P("shard", None),
            P("shard", None),
        ),
        check_vma=False,
    )
```
